32 devices in a mesh: dp: 16 (over z, x, core), seq: 2 (over y).
Axes of the slice: x: 2, y: 2, z: 4, core: 2. Of those that a mesh axis runs over, the one named last changes fastest.
Arguments:
- tokens: bfloat16 [2, 16, 1024, 1152], P(None, 'dp', 'seq'), may hold values from -6 to 6
- conditioning: bfloat16 [2, 16, 1152], P(None, 'dp'), may hold values from -6 to 6
- heights: int32 [2, 16], P(None, 'dp'), may hold values from 8 to 32, as said below
- widths: int32 [2, 16], P(None, 'dp'), may hold values from 8 to 32
- upstream: bfloat16 [2, 16, 1024, 1152], P(None, 'dp', 'seq'), may hold values from -6 to 6
- w_qkv: float32 [1152, 3456], P('seq', 'dp'), may hold values from -0.1875 to 0.1875
- w_proj: float32 [1152, 1152], P('seq', 'dp'), may hold values from -0.5 to 0.5
- w_fc1: float32 [1152, 4608], P('seq', 'dp'), may hold values from -0.1875 to 0.1875
- w_fc2: float32 [4608, 1152], P('seq', 'dp'), may hold values from -0.09375 to 0.09375
- w_ada: float32 [1152, 6912], P('seq', 'dp'), may hold values from -0.25 to 0.25
- mom_qkv: float32 [1152, 3456], P('seq', 'dp')
- mom_proj: float32 [1152, 1152], P('seq', 'dp')
- mom_fc1: float32 [1152, 4608], P('seq', 'dp')
- mom_fc2: float32 [4608, 1152], P('seq', 'dp')
- mom_ada: float32 [1152, 6912], P('seq', 'dp')
- biases: float32 [16128], P(('dp', 'seq')), may hold values from -1.2 to 1.2
- bias_first: float32 [16128], P(('dp', 'seq'))
- bias_second: float32 [16128], P(('dp', 'seq'))
Outputs:
- output: bfloat16 [2, 16, 1024, 1152], P(None, 'dp', 'seq')
- grad_tokens: bfloat16 [2, 16, 1024, 1152], P(None, 'dp', 'seq')
- grad_conditioning: float32 [2, 16, 1152], P(None, 'dp')
- new_qkv: float32 [1152, 3456], P('seq', 'dp')
- new_proj: float32 [1152, 1152], P('seq', 'dp')
- new_fc1: float32 [1152, 4608], P('seq', 'dp')
- new_fc2: float32 [4608, 1152], P('seq', 'dp')
- new_ada: float32 [1152, 6912], P('seq', 'dp')
- next_mom_qkv: float32 [1152, 3456], P('seq', 'dp')
- next_mom_proj: float32 [1152, 1152], P('seq', 'dp')
- next_mom_fc1: float32 [1152, 4608], P('seq', 'dp')
- next_mom_fc2: float32 [4608, 1152], P('seq', 'dp')
- next_mom_ada: float32 [1152, 6912], P('seq', 'dp')
- new_biases: float32 [16128], P(('dp', 'seq'))
- next_first: float32 [16128], P(('dp', 'seq'))
- next_second: float32 [16128], P(('dp', 'seq'))
The draws below stay inside these ranges and needn't reach their ends.
Inputs may be any that keep to these rules, and one draw needn't show every extreme that they name: `heights`: among the 2 samples that one index of dp holds over all micro-batches, one (drawn from the seed) has a full 32 x 32 grid; the other sides are drawn independently.
All inputs are finite; a program needn't handle non-finite values.
Results may differ from the reference program's by a relative error of at most 0.028.
The reference program's roundings to bfloat16 on the way count: a program that leaves them out, or rounds other values in their place, can miss the bound.
Values may be sent and summed in bfloat16 or wider, within the bound.
No kernel may reach another device: no remote copies, remote signals or barrier semaphores. Data moves between devices by JAX's collectives and lax.ppermute only.
A program may use at most 240 MiB of HBM per device.

```python
import math
import jax
import jax.numpy as jnp
from jax import lax

D = 1152
HEADS = 16
HEAD_DIM = 72
FF = 4608
ADA = 6912
NB = 16128
GRID = 32
LEN = 1024
SMB = 1
MB = 2
SAMPLES = 16
TOKENS_ALL = 32768
ROW_BLOCK = 144
NS_STEPS = 5
STEP_COUNT = 10


def grid_sides(key):
    key_h, key_w, key_f = jax.random.split(key, 3)
    sides_h = jax.random.randint(key_h, (MB, SAMPLES), GRID // 4, GRID + 1)
    sides_w = jax.random.randint(key_w, (MB, SAMPLES), GRID // 4, GRID + 1)
    owners = SAMPLES // SMB
    chosen = jax.random.randint(key_f, (owners,), 0, MB * SMB)
    slots = jnp.arange(MB)[:, None] * SMB + (jnp.arange(SAMPLES) % SMB)[None, :]
    owner_of = jnp.arange(SAMPLES) // SMB
    full = slots == chosen[owner_of][None, :]
    return (jnp.where(full, GRID, sides_h).astype(jnp.int32), jnp.where(full, GRID, sides_w).astype(jnp.int32))


def draw_heights(key, part):
    return grid_sides(key)[0]


def draw_widths(key, part):
    return grid_sides(key)[1]


def moment_field(entries, key, rows, cols, base, level):
    key_r, key_c = jax.random.split(key)
    row_scale = jnp.exp(jax.random.uniform(key_r, (rows, 1), jnp.float32, 0.0, math.log(10.0)))
    ramp = base ** (jnp.arange(cols, dtype=jnp.float32) / cols)
    col_scale = ramp * jnp.exp(jax.random.uniform(key_c, (cols,), jnp.float32, 0.0, math.log(3.0)))
    return entries * row_scale * col_scale[None, :] * (level * TOKENS_ALL ** 0.5)


def draw_mom_qkv(key, part):
    key = jax.random.fold_in(key, 11)
    key_e, key_s = jax.random.split(key)
    entries = jax.random.truncated_normal(key_e, -4.0, 4.0, (D, 3 * D), jnp.float32)
    base = 3.0
    return moment_field(entries, key_s, D, 3 * D, base, 0.1)


def draw_mom_proj(key, part):
    key = jax.random.fold_in(key, 12)
    key_e, key_s = jax.random.split(key)
    entries = jax.random.truncated_normal(key_e, -4.0, 4.0, (D, D), jnp.float32)
    base = 3.0
    return moment_field(entries, key_s, D, D, base, 0.15)


def draw_mom_fc1(key, part):
    key = jax.random.fold_in(key, 13)
    key_e, key_s = jax.random.split(key)
    entries = jax.random.truncated_normal(key_e, -4.0, 4.0, (D, FF), jnp.float32)
    base = 3.0
    return moment_field(entries, key_s, D, FF, base, 0.5)


def draw_mom_fc2(key, part):
    key = jax.random.fold_in(key, 14)
    key_e, key_s = jax.random.split(key)
    entries = jax.random.truncated_normal(key_e, -4.0, 4.0, (FF, D), jnp.float32)
    base = 3.0
    return moment_field(entries, key_s, FF, D, base, 0.6)


def draw_mom_ada(key, part):
    key = jax.random.fold_in(key, 15)
    key_e, key_s = jax.random.split(key)
    entries = jax.random.truncated_normal(key_e, -4.0, 4.0, (D, 6 * D), jnp.float32)
    base = 3.0
    return moment_field(entries, key_s, D, 6 * D, base, 0.6)


def bias_levels():
    pieces = [(6 * D, 0.5), (D, 0.1), (D, 0.2), (D, 1.0), (FF, 0.4), (D, 1.0)]
    levels = jnp.concatenate([jnp.full((count,), level, jnp.float32) for count, level in pieces])
    return levels * TOKENS_ALL ** 0.5


def draw_bias_first(key, part):
    key = jax.random.fold_in(key, 21)
    entries = jax.random.truncated_normal(key, -4.0, 4.0, (10 * D + FF,), jnp.float32)
    return 0.11 * entries * bias_levels()


def draw_bias_second(key, part):
    key = jax.random.fold_in(key, 22)
    key_a, key_b = jax.random.split(key)
    spread = jax.random.uniform(key_a, (10 * D + FF,), jnp.float32, 1.0, 4.0)
    factor = jnp.exp(jax.random.uniform(key_b, (10 * D + FF,), jnp.float32, math.log(0.5), math.log(2.0)))
    levels = bias_levels()
    return 0.001 * levels * levels * spread * factor


def shard_levels(stream_key, shape, shards, low, top_value):
    factor_of = 1.0
    for position, blocks in shards:
        steps = jax.random.uniform(jax.random.fold_in(jax.random.fold_in(stream_key, 6), position), (blocks,), jnp.float32, low / len(shards), top_value / len(shards))
        factor_of = factor_of * jnp.repeat(jnp.exp(steps), shape[position] // blocks).reshape((-1,) + (1,) * (len(shape) - 1 - position))
    return factor_of


def normal_values(stream_key, extent, scale, reach, cuts=(), kind=jnp.bfloat16):
    values = scale * jax.random.normal(stream_key, extent, jnp.float32)
    if cuts:
        values = values * shard_levels(stream_key, extent, cuts, -0.22, 0.18)
    return jnp.clip(values, -reach, reach).astype(kind)


def setup_inputs(seed: int = 0) -> dict:
    arg_keys = jax.random.split(jax.random.key(seed), 19)
    return {
        "tokens": normal_values(arg_keys[0], (MB, SAMPLES, LEN, D), 1.0, 6.0, ((1, 16), (2, 2))),
        "conditioning": normal_values(arg_keys[1], (MB, SAMPLES, D), 1.0, 6.0, ((1, 16),)),
        "heights": draw_heights(jax.random.fold_in(arg_keys[18], 71), 0),
        "widths": draw_widths(jax.random.fold_in(arg_keys[18], 71), 0),
        "upstream": normal_values(arg_keys[4], (MB, SAMPLES, LEN, D), 1.0, 6.0, ((1, 16), (2, 2))),
        "w_qkv": normal_values(arg_keys[5], (D, 3 * D), D ** -0.5, 0.1875, ((0, 2), (1, 16)), jnp.float32),
        "w_proj": normal_values(arg_keys[6], (D, D), (D // 8) ** -0.5, 0.5, ((0, 2), (1, 16)), jnp.float32),
        "w_fc1": normal_values(arg_keys[7], (D, FF), D ** -0.5, 0.1875, ((0, 2), (1, 16)), jnp.float32),
        "w_fc2": normal_values(arg_keys[8], (FF, D), FF ** -0.5, 0.09375, ((0, 2), (1, 16)), jnp.float32),
        "w_ada": normal_values(arg_keys[9], (D, ADA), (D // 2) ** -0.5, 0.25, ((0, 2), (1, 16)), jnp.float32),
        "mom_qkv": draw_mom_qkv(jax.random.fold_in(arg_keys[18], 71), 0),
        "mom_proj": draw_mom_proj(jax.random.fold_in(arg_keys[18], 71), 0),
        "mom_fc1": draw_mom_fc1(jax.random.fold_in(arg_keys[18], 71), 0),
        "mom_fc2": draw_mom_fc2(jax.random.fold_in(arg_keys[18], 71), 0),
        "mom_ada": draw_mom_ada(jax.random.fold_in(arg_keys[18], 71), 0),
        "biases": normal_values(arg_keys[15], (NB,), 0.2, 1.2, ((0, 32),), jnp.float32),
        "bias_first": draw_bias_first(jax.random.fold_in(arg_keys[18], 71), 0),
        "bias_second": draw_bias_second(jax.random.fold_in(arg_keys[18], 71), 0),
    }


@jax.custom_vjp
def low(v):
    return lax.optimization_barrier(v.astype(jnp.bfloat16)).astype(jnp.float32)

@jax.custom_vjp
def low_back(v):
    return v

def low_keep(v):
    return (low(v), None)

def low_pass(kept, grad):
    return (grad,)

def back_keep(v):
    return (v, None)

def back_low(kept, grad):
    return (low(grad),)
low.defvjp(low_keep, low_pass)
low_back.defvjp(back_keep, back_low)
PRECISE = lax.Precision.HIGHEST
LN_EPS = 1e-06
MASKED = -1e+30
NS_A = 3.4445
NS_B = -4.775
NS_C = 2.0315
MUON_DECAY = 0.5
WEIGHT_SHRINK = 0.0001
NORM_EPS = 1e-07
BETA_FIRST = 0.9
BETA_SECOND = 0.999
ADAM_RATE = 0.1
ADAM_DECAY = 0.01
ADAM_EPS = 1e-08

def product(left, right):
    return jnp.dot(left, right, precision=PRECISE, preferred_element_type=jnp.float32)

def layer_norm(values):
    centered = values - lax.optimization_barrier(jnp.mean(values, axis=-1, keepdims=True))
    return centered * lax.rsqrt(lax.optimization_barrier(jnp.mean(centered * centered, axis=-1, keepdims=True)) + LN_EPS)

def sigmoid_linear(values):
    return values * jax.nn.sigmoid(values)

def sample_layer(weights, bias_parts, inputs):
    w_qkv, w_proj, w_fc1, w_fc2 = weights
    b_q, b_v, b_proj, b_fc1, b_fc2 = bias_parts
    tokens, modulation, length = inputs
    width = tokens.shape[-1]
    shift_one, scale_one, gate_one, shift_two, scale_two, gate_two = jnp.split(modulation, 6)
    normed_one = layer_norm(tokens)
    attn_in = low(normed_one * (1.0 + scale_one) + shift_one)
    projected = product(attn_in, w_qkv)
    queries = low(low_back(projected[:, :width] + b_q))
    keys = low(low_back(projected[:, width:2 * width]))
    values = low(low_back(projected[:, 2 * width:] + b_v))
    query_heads = queries.reshape(LEN, HEADS, HEAD_DIM)
    key_heads = keys.reshape(LEN, HEADS, HEAD_DIM)
    value_heads = values.reshape(LEN, HEADS, HEAD_DIM)
    scores = jnp.einsum('qhd,khd->hqk', query_heads, key_heads, precision=PRECISE) * HEAD_DIM ** (-0.5)
    valid = jnp.arange(LEN, dtype=jnp.int32) < length
    scores = low_back(jnp.where(valid[None, None, :], scores, MASKED))
    peak = lax.optimization_barrier(jnp.max(scores, axis=-1, keepdims=True))
    exponents = jnp.exp(scores - peak)
    probs = low(exponents / lax.optimization_barrier(jnp.sum(exponents, axis=-1, keepdims=True)))
    attended = jnp.einsum('hqk,khd->qhd', probs, value_heads, precision=PRECISE).reshape(LEN, width)
    attended = low(low_back(attended))
    branch_one = low_back(product(attended, w_proj) + b_proj)
    mixed_one = tokens + gate_one * branch_one
    normed_two = layer_norm(mixed_one)
    ffn_in = low(normed_two * (1.0 + scale_two) + shift_two)
    pre_act = low_back(product(ffn_in, w_fc1) + b_fc1)
    activated = low(jax.nn.gelu(pre_act, approximate=True))
    branch_two = low_back(product(activated, w_fc2) + b_fc2)
    return mixed_one + gate_two * branch_two

def muon_update(weight, moment, grad, rate):
    moment_new = MUON_DECAY * moment + grad
    blocks = moment_new.reshape(moment_new.shape[0] // ROW_BLOCK, ROW_BLOCK, moment_new.shape[1])
    norms = jnp.sqrt(lax.optimization_barrier(jnp.sum(blocks * blocks, axis=(1, 2)))) + NORM_EPS
    current = blocks / norms[:, None, None]
    for step in range(NS_STEPS):
        gram = jnp.einsum('nrc,nsc->nrs', current, current, precision=PRECISE)
        poly = NS_B * gram + NS_C * jnp.einsum('nrs,nst->nrt', gram, gram, precision=PRECISE)
        current = NS_A * current + jnp.einsum('nrs,nsc->nrc', poly, current, precision=PRECISE)
    new_weight = weight * (1.0 - WEIGHT_SHRINK) - rate * current.reshape(weight.shape)
    return (new_weight, moment_new)

def reference(tokens, conditioning, heights, widths, upstream, w_qkv, w_proj, w_fc1, w_fc2, w_ada, mom_qkv, mom_proj, mom_fc1, mom_fc2, mom_ada, biases, bias_first, bias_second):
    width = tokens.shape[-1]
    lengths = (heights * widths).reshape(-1).astype(jnp.int32)
    flat_tokens = tokens.astype(jnp.float32).reshape(-1, LEN, width)
    flat_cond = conditioning.astype(jnp.float32).reshape(-1, width)
    flat_upstream = upstream.astype(jnp.float32).reshape(-1, LEN, width)
    bounds = [0, 6 * D, 7 * D, 8 * D, 9 * D, 9 * D + FF, 10 * D + FF]

    def forward(tok, cond, m_qkv, m_proj, m_fc1, m_fc2, m_ada, bias_all):
        parts = [bias_all[bounds[i]:bounds[i + 1]] for i in range(6)]
        cond_act = low(sigmoid_linear(cond))
        mods = low_back(product(cond_act, low(m_ada))) + parts[0]
        weights = (low(m_qkv), low(m_proj), low(m_fc1), low(m_fc2))
        bias_parts = (parts[1], parts[2], parts[3], parts[4], parts[5])

        def one_sample(inputs):
            return sample_layer(weights, bias_parts, inputs)
        return lax.map(jax.checkpoint(one_sample), (tok, mods, lengths))
    result, pullback = jax.vjp(forward, flat_tokens, flat_cond, w_qkv, w_proj, w_fc1, w_fc2, w_ada, biases)
    grad_tok, grad_cond, g_qkv, g_proj, g_fc1, g_fc2, g_ada, g_bias = pullback(flat_upstream)
    rates = (math.sqrt(3.0), 1.0, math.sqrt(FF / D), math.sqrt(D / FF), math.sqrt(6.0))
    updated = [muon_update(weight, moment, grad, rate) for weight, moment, grad, rate in zip((w_qkv, w_proj, w_fc1, w_fc2, w_ada), (mom_qkv, mom_proj, mom_fc1, mom_fc2, mom_ada), (g_qkv, g_proj, g_fc1, g_fc2, g_ada), rates)]
    next_first = BETA_FIRST * bias_first + (1.0 - BETA_FIRST) * g_bias
    next_second = BETA_SECOND * bias_second + (1.0 - BETA_SECOND) * g_bias * g_bias
    first_hat = next_first / (1.0 - BETA_FIRST ** STEP_COUNT)
    second_hat = next_second / (1.0 - BETA_SECOND ** STEP_COUNT)
    new_biases = biases * (1.0 - ADAM_RATE * ADAM_DECAY) - ADAM_RATE * first_hat / (jnp.sqrt(second_hat) + ADAM_EPS)
    output = result.reshape(tokens.shape).astype(jnp.bfloat16)
    grad_tokens = grad_tok.reshape(tokens.shape).astype(jnp.bfloat16)
    grad_conditioning = grad_cond.reshape(conditioning.shape)
    return (output, grad_tokens, grad_conditioning, updated[0][0], updated[1][0], updated[2][0], updated[3][0], updated[4][0], updated[0][1], updated[1][1], updated[2][1], updated[3][1], updated[4][1], new_biases, next_first, next_second)
```

```python
import functools
import math

import jax
import jax.numpy as jnp
from jax import lax
from jax.experimental import pallas as pl
from jax.experimental.pallas import tpu as pltpu
from jax.sharding import PartitionSpec as P

HEADS = 16
ROW_BLOCK = 144
NS_STEPS = 5
STEP_COUNT = 10

PRECISE = lax.Precision.HIGHEST
LN_EPS = 1e-06
MASKED = -1e30
NS_A = 3.4445
NS_B = -4.775
NS_C = 2.0315
MUON_DECAY = 0.5
WEIGHT_SHRINK = 0.0001
NORM_EPS = 1e-07
BETA_FIRST = 0.9
BETA_SECOND = 0.999
ADAM_RATE = 0.1
ADAM_DECAY = 0.01
ADAM_EPS = 1e-08
BF = jnp.bfloat16
F32 = jnp.float32


class Ring:
    def __init__(self, name, total, stride, size):
        self.name, self.total, self.stride, self.size = name, total, stride, size

    def digit(self):
        return (lax.axis_index(self.name) // self.stride) % self.size

    def send(self, value, shift):
        pairs = []
        for i in range(self.total):
            d = (i // self.stride) % self.size
            pairs.append((i, i + ((d + shift) % self.size - d) * self.stride))
        return lax.ppermute(value, self.name, pairs)

    def gather(self, value):
        n, rows = self.size, value.shape[0]
        pieces = [(0, 0, rows, value)]
        if n == 1:
            return pieces
        if n == 2:
            return pieces + [(1, 0, rows, self.send(value, 1))]
        low = high = value
        for t in range(1, n // 2):
            low, high = self.send(low, 1), self.send(high, -1)
            pieces += [(n - t, 0, rows, low), (t, 0, rows, high)]
        cut = rows // 2
        pieces.append((n // 2, 0, cut, self.send(low[:cut], 1)))
        pieces.append((n // 2, cut, rows, self.send(high[cut:], -1)))
        return pieces

    def gather_list(self, value):
        blocks = [[] for _ in range(self.size)]
        for shift, start, _, array in self.gather(value):
            blocks[shift].append((start, array))
        merged = []
        for block in blocks:
            arrays = [array for _, array in sorted(block, key=lambda item: item[0])]
            merged.append(arrays[0] if len(arrays) == 1 else jnp.concatenate(arrays, axis=0))
        return merged

    def scatter_sum(self, block_of):
        n = self.size
        own = block_of(0).astype(F32)
        if n == 1:
            return own
        if n == 2:
            return own + self.send(block_of(1), 1).astype(F32)
        far = block_of(n // 2)
        kind, cut = far.dtype, far.shape[0] // 2
        low, high = self.send(far[:cut], 1), self.send(far[cut:], -1)
        for t in range(n // 2 - 1, 0, -1):
            up, down = block_of(t), block_of(n - t)
            if t == n // 2 - 1:
                up = jnp.concatenate([(up[:cut].astype(F32) + low.astype(F32)).astype(kind), up[cut:]], axis=0)
                down = jnp.concatenate(
                    [down[:cut], (down[cut:].astype(F32) + high.astype(F32)).astype(kind)], axis=0
                )
            else:
                up = (up.astype(F32) + low.astype(F32)).astype(kind)
                down = (down.astype(F32) + high.astype(F32)).astype(kind)
            low, high = self.send(up, 1), self.send(down, -1)
        return own + low.astype(F32) + high.astype(F32)


def place_kernel(moves, count, *refs):
    spots, sources, out, sems = refs[0], refs[1 : 1 + count], refs[1 + count], refs[2 + count]
    copies = []
    for n, (source, index, target) in enumerate(moves):
        copies.append(
            pltpu.make_async_copy(sources[source].at[index], out.at[target(spots)], sems.at[n])
        )
    for copy in copies:
        copy.start()
    for copy in copies:
        copy.wait()


def place(spots, sources, moves, shape, dtype):
    return pl.pallas_call(
        functools.partial(place_kernel, moves, len(sources)),
        out_shape=jax.ShapeDtypeStruct(shape, dtype),
        in_specs=[pl.BlockSpec(memory_space=pltpu.SMEM)]
        + [pl.BlockSpec(memory_space=pl.ANY)] * len(sources),
        out_specs=pl.BlockSpec(memory_space=pl.ANY),
        scratch_shapes=[pltpu.SemaphoreType.DMA((len(moves),))],
        cost_estimate=pl.CostEstimate(
            flops=0, bytes_accessed=2 * math.prod(shape) * jnp.dtype(dtype).itemsize, transcendentals=0
        ),
        name="place",
    )(spots, *sources)


class Net:
    def __init__(self, mesh):
        dp, seq = mesh.shape["dp"], mesh.shape["seq"]
        self.dp, self.seq = dp, seq
        self.core = Ring("dp", dp, 1, 2)
        self.x = Ring("dp", dp, 2, 2)
        self.z = Ring("dp", dp, 4, dp // 4)
        self.y = Ring("seq", seq, 1, seq)

    def spots(self):
        return jnp.stack([self.z.digit(), self.x.digit(), self.core.digit()]).astype(jnp.int32)


    def rows_joined(self, shard):
        turned = shard.astype(BF).T
        blocks = self.y.gather_list(turned)
        if self.seq == 2:
            own, other = blocks
            full = jnp.where(
                self.y.digit() == 0,
                jnp.concatenate([own, other], axis=1),
                jnp.concatenate([other, own], axis=1),
            )
        else:
            order = (jnp.arange(self.seq) - self.y.digit()) % self.seq
            full = jnp.take(jnp.stack(blocks), order, axis=0)
            full = jnp.transpose(full, (1, 0, 2)).reshape(turned.shape[0], -1)
        unit = math.gcd(full.shape[0], 8)
        return full.reshape(full.shape[0] // unit, unit, full.shape[1])

    def gather_weight(self, units):
        g, unit, depth = units.shape
        zs = self.z.size
        ga = max(1, (4 * g) // 9)
        gb = g - ga
        first, second = units[:ga], units[ga:]
        line = jnp.stack(self.z.gather_list(first))
        line_x = self.x.send(line, 1)
        pair = jnp.stack([second, self.x.send(second, 1)])
        pieces = self.z.gather(pair)
        sources, moves = [], []

        def spot(sz, sx, sc, start, stop):
            def target(spots):
                return (
                    lax.rem(spots[0] + sz, zs),
                    lax.rem(spots[1] + sx, 2),
                    lax.rem(spots[2] + sc, 2),
                    pl.ds(start, stop - start),
                )

            return target

        for sc in range(2):
            for sx, array in ((0, line), (1, line_x)):
                array = array if sc == 0 else self.core.send(array, 1)
                for sz in range(zs):
                    moves.append((len(sources), (sz,), spot(sz, sx, sc, 0, ga)))
                sources.append(array)
            for sz, start, stop, array in pieces:
                array = array if sc == 0 else self.core.send(array, 1)
                for sx in range(start, stop):
                    moves.append((len(sources), (sx - start,), spot(sz, sx, sc, ga, g)))
                sources.append(array)
        full = place(self.spots(), sources, moves, (zs, 2, 2, g, unit, depth), BF)
        return full.reshape(self.dp * g * unit, depth)

    def scatter_weight(self, term, rows):
        depth = term.shape[1]
        n = term.shape[0] // self.dp
        unit = math.gcd(n, 8)
        g = n // unit
        zs = self.z.size
        ga = max(1, (4 * g) // 9)
        blocks = term.reshape(zs, 2, 2, g, unit, depth)
        core, x, z = self.core.digit(), self.x.digit(), self.z.digit()
        half = self.core.scatter_sum(
            lambda s: lax.dynamic_index_in_dim(blocks, (core + s) % 2, 2, keepdims=False)
        ).astype(BF)
        first, second = half[:, :, :ga], half[:, :, ga:]
        line = self.x.scatter_sum(
            lambda s: lax.dynamic_index_in_dim(first, (x + s) % 2, 1, keepdims=False)
        ).astype(BF)
        first = self.z.scatter_sum(
            lambda s: lax.dynamic_index_in_dim(line, (z + s) % zs, 0, keepdims=False)
        )
        pair = self.z.scatter_sum(
            lambda s: lax.dynamic_index_in_dim(second, (z + s) % zs, 0, keepdims=False)
        ).astype(BF)
        second = self.x.scatter_sum(
            lambda s: lax.dynamic_index_in_dim(pair, (x + s) % 2, 0, keepdims=False)
        )
        joined = jnp.concatenate([first, second], axis=0).astype(BF).reshape(n, depth)
        y = self.y.digit()
        total = self.y.scatter_sum(
            lambda s: lax.dynamic_slice_in_dim(joined, ((y + s) % self.seq) * rows, rows, 1)
        )
        return total.T


    def gather_dp(self, value):
        z, x, core = self.z.digit(), self.x.digit(), self.core.digit()
        blocks = self.z.gather_list(value)
        line = jnp.zeros((self.z.size,) + value.shape, value.dtype)
        for s, block in enumerate(blocks):
            line = lax.dynamic_update_index_in_dim(line, block, (z + s) % self.z.size, 0)
        other = self.x.send(line, 1)
        plane = jnp.where(x == 0, jnp.stack([line, other], 1), jnp.stack([other, line], 1))
        other = self.core.send(plane, 1)
        both = jnp.where(core == 0, jnp.stack([plane, other], 2), jnp.stack([other, plane], 2))
        return both.reshape((self.dp,) + value.shape)

    def scatter_dp(self, value):
        z, x, core, zs = self.z.digit(), self.x.digit(), self.core.digit(), self.z.size
        blocks = value.reshape((zs, 2, 2) + value.shape[1:])
        half = self.core.scatter_sum(
            lambda s: lax.dynamic_index_in_dim(blocks, (core + s) % 2, 2, keepdims=False)
        )
        line = self.x.scatter_sum(
            lambda s: lax.dynamic_index_in_dim(half, (x + s) % 2, 1, keepdims=False)
        )
        return self.z.scatter_sum(
            lambda s: lax.dynamic_index_in_dim(line, (z + s) % zs, 0, keepdims=False)
        )


def layer_norm(values):
    centered = values - jnp.mean(values, axis=-1, keepdims=True)
    inverse = lax.rsqrt(jnp.mean(centered * centered, axis=-1, keepdims=True) + LN_EPS)
    return (centered * inverse, inverse)


def norm_back(normed, inverse, grad):
    mean_grad = jnp.mean(grad, axis=-1, keepdims=True)
    mean_cross = jnp.mean(grad * normed, axis=-1, keepdims=True)
    return inverse * (grad - mean_grad - normed * mean_cross)


def sigmoid_linear(values):
    return values * jax.nn.sigmoid(values)


def gelu_tanh(values):
    return jax.nn.gelu(values, approximate=True)


def dot_t(left, right):
    return jnp.einsum("srk,nk->srn", left, right, preferred_element_type=F32)


def dot(left, right):
    return jnp.einsum("srn,nk->srk", left, right, preferred_element_type=F32)


def outer(left, right):
    return jnp.einsum("srn,srk->nk", left, right, preferred_element_type=F32).astype(BF)


def attention_scores(queries, keys, valid):
    head_dim = queries.shape[-1]
    scores = jnp.einsum("qhd,khd->hqk", queries, keys, preferred_element_type=F32) * head_dim**-0.5
    return jnp.where(valid[None, None, :], scores, MASKED)


def attention_one(queries, keys, values, valid):
    scores = attention_scores(queries, keys, valid)
    peak = jnp.max(scores, axis=-1)
    weights = jnp.exp(scores - peak[..., None])
    total = jnp.sum(weights, axis=-1)
    mixed = jnp.einsum("hqk,khd->hqd", weights.astype(BF), values, preferred_element_type=F32)
    heads = jnp.transpose(mixed / total[..., None], (1, 0, 2))
    return heads, peak + jnp.log(total)


def attention_one_back(queries, keys, values, valid, heads, log_total, grad_heads):
    head_dim = queries.shape[-1]
    delta = jnp.einsum("qhd,qhd->hq", grad_heads.astype(F32), heads)
    scores = attention_scores(queries, keys, valid)
    probs = jnp.exp(scores - log_total[..., None])
    grad_probs = jnp.einsum("qhd,khd->hqk", grad_heads, values, preferred_element_type=F32)
    grad_scores = (probs * (grad_probs - delta[..., None])).astype(BF)
    scale = head_dim**-0.5
    grad_q = jnp.einsum("hqk,khd->qhd", grad_scores, keys, preferred_element_type=F32) * scale
    grad_k = jnp.einsum("hqk,qhd->khd", grad_scores, queries, preferred_element_type=F32) * scale
    grad_v = jnp.einsum("hqk,qhd->khd", probs.astype(BF), grad_heads, preferred_element_type=F32)
    return grad_q.astype(BF), grad_k.astype(BF), grad_v.astype(BF)


def gram_of(moment):
    block = moment.reshape(moment.shape[0] // ROW_BLOCK, ROW_BLOCK, moment.shape[1])
    return jnp.einsum("nrc,nsc->nrs", block, block, precision=PRECISE)


def polynomial(gram):
    eye = jnp.eye(ROW_BLOCK, dtype=F32)
    square = jnp.sum(gram * eye, axis=(1, 2))
    scale = 1.0 / (jnp.sqrt(square) + NORM_EPS)
    current = gram * (scale * scale)[:, None, None]
    mul = functools.partial(jnp.einsum, "nrs,nst->nrt", precision=PRECISE)
    total = None
    for step in range(NS_STEPS):
        factor = NS_A * eye + NS_B * current + NS_C * mul(current, current)
        total = factor if total is None else mul(factor, total)
        if step + 1 < NS_STEPS:
            current = mul(mul(factor, current), factor)
    return total * scale[:, None, None]


def body(net, tokens, conditioning, heights, widths, upstream, *state):
    masters, momenta = state[0:5], state[5:10]
    biases, bias_first, bias_second = state[10:13]
    w_qkv, w_proj, w_fc1, w_fc2, w_ada = masters
    micro, local, rows, width = tokens.shape
    count = micro * local
    head_dim = width // HEADS
    hidden = w_fc1.shape[1] * net.dp
    seq, dp = net.seq, net.dp
    y = net.y.digit()

    units_qkv = net.rows_joined(w_qkv)
    units_proj = net.rows_joined(w_proj)
    units_fc1 = net.rows_joined(w_fc1)
    units_fc2 = net.rows_joined(w_fc2)
    own_tokens = tokens.reshape(count, rows, width)
    all_tokens = jnp.concatenate(net.y.gather_list(own_tokens), axis=1)
    t_qkv = net.gather_weight(units_qkv)
    t_proj = net.gather_weight(units_proj)
    t_fc1 = net.gather_weight(units_fc1)
    t_fc2 = net.gather_weight(units_fc2)

    low_ada = w_ada.astype(BF)
    ada_rows, ada_cols = w_ada.shape
    cond = conditioning.astype(F32).reshape(count, width)
    cond_act, silu_back = jax.vjp(sigmoid_linear, cond)
    cond_low = cond_act.astype(BF)
    cond_rows = lax.dynamic_slice_in_dim(cond_low, y * ada_rows, ada_rows, 1)
    cond_all = net.gather_dp(cond_rows).reshape(dp * count, ada_rows)
    partial = jnp.dot(cond_all, low_ada, preferred_element_type=F32)
    partial = lax.psum(partial, "seq").reshape(dp, count, ada_cols)
    received = lax.all_to_all(partial, "dp", 0, 0, tiled=True)
    bias_full = lax.all_to_all(
        jnp.broadcast_to(biases[None], (dp * seq,) + biases.shape), ("dp", "seq"), 0, 0, tiled=True
    ).reshape(-1)
    bounds = [0, 6 * width, 7 * width, 8 * width, 9 * width, 9 * width + hidden, 10 * width + hidden]
    b_ada, b_q, b_v, b_proj, b_fc1, b_fc2 = [bias_full[bounds[i] : bounds[i + 1]] for i in range(6)]
    modulation = jnp.transpose(received, (1, 0, 2)).reshape(count, dp * ada_cols) + b_ada
    shift_one, scale_one, gate_one, shift_two, scale_two, gate_two = jnp.split(
        modulation[:, None, :], 6, axis=-1
    )

    lengths = (heights * widths).reshape(count)
    places = jnp.concatenate([((y + s) % seq) * rows + jnp.arange(rows) for s in range(seq)])
    valid = places[None, :] < lengths[:, None]
    normed_all, inverse_all = layer_norm(all_tokens.astype(F32))
    attn_all = (normed_all * (1.0 + scale_one) + shift_one).astype(BF)
    attn_own = attn_all[:, :rows]
    queries = (dot_t(attn_own, t_qkv[:width]) + b_q).astype(BF)
    keys = dot_t(attn_all, t_qkv[width : 2 * width]).astype(BF)
    values = (dot_t(attn_all, t_qkv[2 * width :]) + b_v).astype(BF)
    queries = queries.reshape(count, rows, HEADS, head_dim)
    keys = keys.reshape(count, rows * seq, HEADS, head_dim)
    values = values.reshape(count, rows * seq, HEADS, head_dim)
    mixed_heads = [attention_one(queries[i], keys[i], values[i], valid[i]) for i in range(count)]
    attended_low = jnp.stack([heads for heads, _ in mixed_heads]).reshape(count, rows, width).astype(BF)
    inputs = own_tokens.astype(F32)
    branch_one = dot_t(attended_low, t_proj) + b_proj
    mixed_one = inputs + gate_one * branch_one
    normed_two, inverse_two = layer_norm(mixed_one)
    ffn_in = (normed_two * (1.0 + scale_two) + shift_two).astype(BF)
    pre_act = dot_t(ffn_in, t_fc1) + b_fc1
    activated, gelu_back = jax.vjp(gelu_tanh, pre_act)
    activated_low = activated.astype(BF)
    branch_two = dot_t(activated_low, t_fc2) + b_fc2
    result = (mixed_one + gate_two * branch_two).astype(BF)

    grad_out = upstream.reshape(count, rows, width).astype(F32)
    grad_branch_two = (gate_two * grad_out).astype(BF)
    grad_gate_two = jnp.sum(branch_two * grad_out, axis=1)
    shard_fc2 = net.scatter_weight(outer(grad_branch_two, activated_low), w_fc2.shape[0])
    bias_fc2 = jnp.sum(grad_branch_two.astype(F32), axis=(0, 1))
    grad_pre = gelu_back(dot(grad_branch_two, t_fc2))[0].astype(BF)
    shard_fc1 = net.scatter_weight(outer(grad_pre, ffn_in), w_fc1.shape[0])
    bias_fc1 = jnp.sum(grad_pre.astype(F32), axis=(0, 1))
    grad_ffn_in = dot(grad_pre, t_fc1)
    grad_shift_two = jnp.sum(grad_ffn_in, axis=1)
    grad_scale_two = jnp.sum(grad_ffn_in * normed_two, axis=1)
    grad_mixed = grad_out + norm_back(normed_two, inverse_two, grad_ffn_in * (1.0 + scale_two))
    grad_gate_one = jnp.sum(branch_one * grad_mixed, axis=1)
    grad_branch_one = (gate_one * grad_mixed).astype(BF)
    shard_proj = net.scatter_weight(outer(grad_branch_one, attended_low), w_proj.shape[0])
    bias_proj = jnp.sum(grad_branch_one.astype(F32), axis=(0, 1))
    grad_attended = dot(grad_branch_one, t_proj).astype(BF).reshape(count, rows, HEADS, head_dim)

    parts = [
        attention_one_back(
            queries[i], keys[i], values[i], valid[i], mixed_heads[i][0], mixed_heads[i][1], grad_attended[i]
        )
        for i in range(count)
    ]
    grad_q = jnp.stack([part[0] for part in parts]).reshape(count, rows, width)
    grad_kv = jnp.concatenate(
        [jnp.stack([part[k] for part in parts]).reshape(count, rows * seq, width) for k in (1, 2)], axis=-1
    )
    term_qkv = jnp.concatenate([outer(grad_q, attn_own), outer(grad_kv, attn_all)], axis=0)
    shard_qkv = net.scatter_weight(term_qkv, w_qkv.shape[0])
    bias_q = jnp.sum(grad_q.astype(F32), axis=(0, 1))
    bias_v = jnp.sum(grad_kv[..., width:].astype(F32), axis=(0, 1))
    part_in = dot(grad_kv, t_qkv[width:])
    own_part = part_in[:, :rows] + dot(grad_q, t_qkv[:width])
    grad_attn_in = net.y.scatter_sum(
        lambda s: own_part if s == 0 else part_in[:, s * rows : (s + 1) * rows].astype(BF)
    )
    normed_one, inverse_one = normed_all[:, :rows], inverse_all[:, :rows]
    grad_shift_one = jnp.sum(grad_attn_in, axis=1)
    grad_scale_one = jnp.sum(grad_attn_in * normed_one, axis=1)
    grad_inputs = grad_mixed + norm_back(normed_one, inverse_one, grad_attn_in * (1.0 + scale_one))

    grad_mod_local = jnp.concatenate(
        [grad_shift_one, grad_scale_one, grad_gate_one, grad_shift_two, grad_scale_two, grad_gate_two], axis=-1
    )
    bias_ada = jnp.sum(grad_mod_local, axis=0)
    grad_mod = lax.psum(grad_mod_local, "seq").astype(BF)
    grad_mod = jnp.transpose(grad_mod.reshape(count, dp, ada_cols), (1, 0, 2))
    mod_cols = lax.all_to_all(grad_mod, "dp", 0, 0, tiled=True).reshape(dp * count, ada_cols)
    shard_ada = jnp.einsum("sr,sc->rc", cond_all, mod_cols, preferred_element_type=F32)
    cond_part = jnp.einsum("sc,rc->sr", mod_cols, low_ada, preferred_element_type=F32)
    cond_part = lax.all_to_all(cond_part.reshape(dp, count, ada_rows), "dp", 0, 0, tiled=True)
    cond_part = jnp.sum(cond_part, axis=0)
    grad_cond_act = lax.all_gather(cond_part, "seq", axis=1, tiled=True)
    grad_cond = silu_back(grad_cond_act)[0]

    term_bias = jnp.concatenate([bias_ada, bias_q, bias_v, bias_proj, bias_fc1, bias_fc2])
    grad_bias = jnp.sum(
        lax.all_to_all(term_bias.reshape(dp * seq, -1), ("dp", "seq"), 0, 0, tiled=True), axis=0
    )
    next_first = BETA_FIRST * bias_first + (1.0 - BETA_FIRST) * grad_bias
    next_second = BETA_SECOND * bias_second + (1.0 - BETA_SECOND) * grad_bias * grad_bias
    first_hat = next_first / (1.0 - BETA_FIRST**STEP_COUNT)
    second_hat = next_second / (1.0 - BETA_SECOND**STEP_COUNT)
    new_biases = biases * (1.0 - ADAM_RATE * ADAM_DECAY) - ADAM_RATE * first_hat / (
        jnp.sqrt(second_hat) + ADAM_EPS
    )

    shards = (shard_qkv, shard_proj, shard_fc1, shard_fc2, shard_ada)
    moments = [MUON_DECAY * momentum + shard for momentum, shard in zip(momenta, shards)]
    grams = [gram_of(moment) for moment in moments]
    directions = [None] * 5
    for group in ((3, 2, 1), (0, 4)):
        stack = jnp.concatenate([grams[i] for i in group], axis=0)
        blocks = stack.shape[0]
        each = -(-blocks // dp)
        stack = jnp.pad(stack, ((0, each * dp - blocks), (0, 0), (0, 0)))
        mine = net.scatter_dp(stack.reshape(dp, each, ROW_BLOCK, ROW_BLOCK))
        factors = net.gather_dp(polynomial(mine)).reshape(dp * each, ROW_BLOCK, ROW_BLOCK)
        start = 0
        for i in group:
            size = grams[i].shape[0]
            block = moments[i].reshape(size, ROW_BLOCK, -1)
            direction = jnp.einsum("nrs,nsc->nrc", factors[start : start + size], block, precision=PRECISE)
            directions[i] = direction.reshape(moments[i].shape)
            start += size
    rates = (math.sqrt(3.0), 1.0, math.sqrt(hidden / width), math.sqrt(width / hidden), math.sqrt(6.0))
    new_weights = [
        weight * (1.0 - WEIGHT_SHRINK) - rate * direction
        for weight, rate, direction in zip(masters, rates, directions)
    ]
    return (
        result.reshape(tokens.shape),
        grad_inputs.astype(BF).reshape(tokens.shape),
        grad_cond.reshape(conditioning.shape),
        *new_weights,
        *moments,
        new_biases,
        next_first,
        next_second,
    )


def solution(mesh):
    rows = P(None, "dp", "seq", None)
    matrix = P("seq", "dp")
    flat = P(("dp", "seq"))
    in_specs = (rows, P(None, "dp", None), P(None, "dp"), P(None, "dp"), rows) + (matrix,) * 10 + (flat,) * 3
    out_specs = (rows, rows, P(None, "dp", None)) + (matrix,) * 10 + (flat,) * 3
    return jax.shard_map(
        functools.partial(body, Net(mesh)), mesh=mesh, in_specs=in_specs, out_specs=out_specs, check_vma=False
    )
```

```python
import functools
import math

import jax
import jax.numpy as jnp
from jax import lax
from jax.experimental import pallas as pl
from jax.experimental.pallas import tpu as pltpu
from jax.sharding import PartitionSpec as P

HEADS = 16
ROW_BLOCK = 144
NS_STEPS = 5
STEP_COUNT = 10

PRECISE = lax.Precision.HIGHEST
LN_EPS = 1e-06
MASKED = -1e30
NS_A = 3.4445
NS_B = -4.775
NS_C = 2.0315
MUON_DECAY = 0.5
WEIGHT_SHRINK = 0.0001
NORM_EPS = 1e-07
BETA_FIRST = 0.9
BETA_SECOND = 0.999
ADAM_RATE = 0.1
ADAM_DECAY = 0.01
ADAM_EPS = 1e-08
BF = jnp.bfloat16
F32 = jnp.float32
VMEM_LIMIT = 60 * 2**20


class Ring:
    def __init__(self, name, total, stride, size):
        self.name, self.total, self.stride, self.size = name, total, stride, size

    def digit(self):
        return (lax.axis_index(self.name) // self.stride) % self.size

    def send(self, value, shift):
        pairs = []
        for i in range(self.total):
            d = (i // self.stride) % self.size
            pairs.append((i, i + ((d + shift) % self.size - d) * self.stride))
        return lax.ppermute(value, self.name, pairs)

    def gather(self, value, far=1):
        n = self.size
        blocks = [value] + [None] * (n - 1)
        if n == 2:
            blocks[1] = self.send(value, 1)
        elif n > 2:
            low = high = value
            for t in range(1, n // 2):
                low, high = self.send(low, 1), self.send(high, -1)
                blocks[n - t], blocks[t] = low, high
            blocks[n // 2] = self.send(low, 1) if far == 1 else self.send(high, -1)
        return blocks

    def scatter_sum(self, block_of, far=1):
        n = self.size
        own = block_of(0).astype(F32)
        if n == 1:
            return own
        if n == 2:
            return own + self.send(block_of(1), 1).astype(F32)
        low = high = None
        if far == 1:
            low = self.send(block_of(n // 2), 1)
        else:
            high = self.send(block_of(n // 2), -1)
        for t in range(n // 2 - 1, 0, -1):
            up, down = block_of(t), block_of(n - t)
            if low is not None:
                up = (up.astype(F32) + low.astype(F32)).astype(up.dtype)
            if high is not None:
                down = (down.astype(F32) + high.astype(F32)).astype(down.dtype)
            low, high = self.send(up, 1), self.send(down, -1)
        return own + low.astype(F32) + high.astype(F32)


def place_kernel(moves, outs, count, parts, *refs):
    spots, sources = refs[0], refs[1 : 1 + count]
    outputs, (full, in_sems, out_sems) = refs[1 + count : 1 + count + parts], refs[1 + count + parts :]
    arrivals = []
    for n, (source, index, target) in enumerate(moves):
        arrivals.append(
            pltpu.make_async_copy(sources[source].at[index], full.at[target(spots)], in_sems.at[n])
        )
    for copy in arrivals:
        copy.start()
    for copy in arrivals:
        copy.wait()
    exits = []
    for n, (start, output, target) in enumerate(outs):
        exits.append(pltpu.make_async_copy(full.at[start], outputs[output].at[target], out_sems.at[n]))
    for copy in exits:
        copy.start()
    for copy in exits:
        copy.wait()


def place(spots, sources, moves, shape, outs, shapes):
    moved = math.prod(shape) * 2
    return pl.pallas_call(
        functools.partial(place_kernel, moves, outs, len(sources), len(shapes)),
        out_shape=[jax.ShapeDtypeStruct(each, BF) for each in shapes],
        in_specs=[pl.BlockSpec(memory_space=pltpu.SMEM)]
        + [pl.BlockSpec(memory_space=pl.ANY)] * len(sources),
        out_specs=[pl.BlockSpec(memory_space=pl.ANY)] * len(shapes),
        scratch_shapes=[
            pltpu.VMEM(shape, BF),
            pltpu.SemaphoreType.DMA((len(moves),)),
            pltpu.SemaphoreType.DMA((len(outs),)),
        ],
        compiler_params=pltpu.CompilerParams(vmem_limit_bytes=VMEM_LIMIT),
        cost_estimate=pl.CostEstimate(flops=0, bytes_accessed=2 * moved, transcendentals=0),
        name="place",
    )(spots, *sources)


class Net:
    def __init__(self, mesh):
        dp, seq = mesh.shape["dp"], mesh.shape["seq"]
        self.dp, self.seq = dp, seq
        self.core = Ring("dp", dp, 1, 2)
        self.x = Ring("dp", dp, 2, 2)
        self.z = Ring("dp", dp, 4, dp // 4)
        self.y = Ring("seq", seq, 1, seq)

    def spots(self):
        return jnp.stack([self.z.digit(), self.x.digit(), self.core.digit()]).astype(jnp.int32)


    def rows_joined(self, shards, unit, depth):
        turned = [shard.astype(BF).T for shard in shards]
        wire = jnp.concatenate([t.reshape(-1) for t in turned]) if len(turned) > 1 else turned[0]
        wires = self.y.gather(wire)
        joined = []
        start = 0
        for t in turned:
            if len(turned) > 1:
                blocks = [w[start : start + t.size].reshape(t.shape) for w in wires]
            else:
                blocks = wires
            start += t.size
            if self.seq == 2:
                own, other = blocks
                full = jnp.where(
                    self.y.digit() == 0,
                    jnp.concatenate([own, other], axis=1),
                    jnp.concatenate([other, own], axis=1),
                )
            else:
                order = (jnp.arange(self.seq) - self.y.digit()) % self.seq
                full = jnp.take(jnp.stack(blocks), order, axis=0)
                full = jnp.transpose(full, (1, 0, 2)).reshape(t.shape[0], -1)
            full = full.reshape(t.shape[0] // unit, unit, full.shape[1] // depth, depth)
            joined.append(jnp.transpose(full, (2, 0, 1, 3)).reshape(-1, unit, depth))
        return joined[0] if len(joined) == 1 else jnp.concatenate(joined, axis=0)

    def gather_weights(self, units, layout):
        g, unit, depth = units.shape
        zs = self.z.size
        ga = max(1, (4 * g) // 9)
        first, second = units[:ga], units[ga:]
        line = jnp.stack(self.z.gather(first, 1))
        pair = jnp.stack([second, self.x.send(second, 1)])
        line_x = self.x.send(line, 1)
        pieces = self.z.gather(pair, -1)
        arrived = [line_x] + pieces[1:]
        sources, moves = [], []

        def spot(sz, sx, sc, start, stop):
            def target(spots):
                return (
                    lax.rem(spots[0] + sz, zs),
                    lax.rem(spots[1] + sx, 2),
                    lax.rem(spots[2] + sc, 2),
                    pl.ds(start, stop - start),
                )

            return target

        for sc in range(2):
            for sx, array in ((0, line), (1, line_x)):
                array = array if sc == 0 else self.core.send(array, 1)
                for sz in range(zs):
                    moves.append((len(sources), (sz,), spot(sz, sx, sc, 0, ga)))
                sources.append(array)
            for sz, array in enumerate(pieces):
                array = array if sc == 0 else self.core.send(array, 1)
                for sx in range(2):
                    moves.append((len(sources), (sx,), spot(sz, sx, sc, ga, g)))
                sources.append(array)
        outs, shapes, start = [], [], 0
        for n, (rows, blocks) in enumerate(layout):
            size = rows // unit
            shapes.append((zs, 2, 2, size, unit, blocks * depth))
            for j in range(blocks):
                window = (slice(None),) * 3 + (pl.ds(start, size),)
                target = (slice(None),) * 5 + (pl.ds(j * depth, depth),)
                outs.append((window, n, target))
                start += size
        full = place(self.spots(), sources, moves, (zs, 2, 2, g, unit, depth), outs, shapes)
        return [f.reshape(-1, f.shape[-1]) for f in full], arrived

    def scatter_weights(self, terms, unit, depth, layout):
        zs = self.z.size
        blocks = [term.reshape(zs, 2, 2, -1, unit, depth) for term in terms]
        g = sum(block.shape[3] for block in blocks)
        ga = max(1, (4 * g) // 9)
        core, x, z = self.core.digit(), self.x.digit(), self.z.digit()

        def half_of(s):
            parts = [lax.dynamic_index_in_dim(block, (core + s) % 2, 2, keepdims=False) for block in blocks]
            return parts[0] if len(parts) == 1 else jnp.concatenate(parts, axis=2)

        half = self.core.scatter_sum(half_of).astype(BF)
        first, second = half[:, :, :ga], half[:, :, ga:]
        line = self.x.scatter_sum(
            lambda s: lax.dynamic_index_in_dim(first, (x + s) % 2, 1, keepdims=False)
        ).astype(BF)
        pair = self.z.scatter_sum(
            lambda s: lax.dynamic_index_in_dim(second, (z + s) % zs, 0, keepdims=False), -1
        ).astype(BF)
        first = self.z.scatter_sum(
            lambda s: lax.dynamic_index_in_dim(line, (z + s) % zs, 0, keepdims=False), 1
        )
        second = self.x.scatter_sum(
            lambda s: lax.dynamic_index_in_dim(pair, (x + s) % 2, 0, keepdims=False)
        )
        joined = jnp.concatenate([first, second], axis=0).astype(BF)
        y = self.y.digit()
        wire, start = [], 0
        for rows, count in layout:
            size = rows // unit * count
            full = joined[start : start + size].reshape(count, rows // unit, unit, depth)
            full = jnp.transpose(full, (1, 2, 0, 3)).reshape(rows, count * depth)
            wire.append(full.reshape(rows, self.seq, -1))
            start += size
        own = [lax.dynamic_index_in_dim(w, y, 1, keepdims=False).astype(F32) for w in wire]
        if len(wire) == 1:
            total = [
                self.y.scatter_sum(
                    lambda s: lax.dynamic_index_in_dim(wire[0], (y + s) % self.seq, 1, keepdims=False)
                )
            ]
        else:

            def flat_of(s):
                parts = [lax.dynamic_index_in_dim(w, (y + s) % self.seq, 1, keepdims=False) for w in wire]
                return jnp.concatenate([part.reshape(-1) for part in parts])

            summed = self.y.scatter_sum(flat_of)
            total, start = [], 0
            for part in own:
                total.append(summed[start : start + part.size].reshape(part.shape))
                start += part.size
        return [t.T for t in total]


    def to_all(self, value):
        flat = value.reshape((self.dp * self.seq,) + value.shape[2:])
        return lax.all_to_all(flat, ("dp", "seq"), 0, 0, tiled=True).reshape(value.shape)

    def to_dp(self, value):
        return lax.all_to_all(value, "dp", 0, 0, tiled=True)


def after(value, *earlier):
    return lax.optimization_barrier((value,) + earlier)[0]


def layer_norm(values):
    centered = values - jnp.mean(values, axis=-1, keepdims=True)
    inverse = lax.rsqrt(jnp.mean(centered * centered, axis=-1, keepdims=True) + LN_EPS)
    return (centered * inverse, inverse)


def norm_back(normed, inverse, grad):
    mean_grad = jnp.mean(grad, axis=-1, keepdims=True)
    mean_cross = jnp.mean(grad * normed, axis=-1, keepdims=True)
    return inverse * (grad - mean_grad - normed * mean_cross)


def sigmoid_linear(values):
    return values * jax.nn.sigmoid(values)


def gelu_tanh(values):
    return jax.nn.gelu(values, approximate=True)


def dot_t(left, right):
    return jnp.einsum("srk,nk->srn", left, right, preferred_element_type=F32)


def dot(left, right):
    return jnp.einsum("srn,nk->srk", left, right, preferred_element_type=F32)


def outer(left, right):
    return jnp.einsum("srn,srk->nk", left, right, preferred_element_type=F32).astype(BF)


LANES = 128
LOG2E = math.log2(math.e)


def padded(block, column=None):
    rows, depth = block.shape
    if column is None:
        return jnp.concatenate([block, jnp.zeros((rows, LANES - depth), block.dtype)], axis=1)
    rest = jnp.zeros((rows, LANES - depth - 1), block.dtype)
    return jnp.concatenate([block, column.astype(block.dtype), rest], axis=1)


def mask_column(lengths_ref, offsets_ref, sample, total, rows):
    place = lax.broadcasted_iota(jnp.int32, (total, 1), 0)
    position = place
    for s in range(total // rows):
        position = jnp.where(place // rows == s, place - s * rows + offsets_ref[s], position)
    return jnp.where(position < lengths_ref[sample], 0.0, MASKED)


def nt(left, right):
    return lax.dot_general(left, right, (((1,), (1,)), ((), ())), preferred_element_type=F32)


def nn(left, right):
    return jnp.dot(left, right, preferred_element_type=F32)


def attend_kernel(heads, chunk, lengths_ref, offsets_ref, q_ref, k_ref, v_ref, o_ref, lse_ref, q_s, k_s, vt_s, o_s):
    rows, width = q_ref.shape[1:]
    total = k_ref.shape[1]
    depth = width // heads
    factor = depth**-0.5 * LOG2E
    mask = mask_column(lengths_ref, offsets_ref, pl.program_id(0), total, rows)
    ones = jnp.ones((rows, 1), F32)
    for h in range(heads):
        span = slice(h * depth, (h + 1) * depth)
        q_s[h] = padded(q_ref[0, :, span], ones)
        k_s[h] = padded(k_ref[0, :, span], mask)
        vt_s[h] = jnp.transpose(v_ref[0, :, span])

    def one_head(h, carry):
        peak = jnp.full((1, rows), MASKED, F32)
        sums = jnp.zeros((1, rows), F32)
        mixed = jnp.zeros((depth, rows), F32)
        for c in range(total // chunk):
            part = slice(c * chunk, (c + 1) * chunk)
            scores = nt(k_s[h, part], q_s[h])
            higher = jnp.maximum(peak, jnp.max(scores, axis=0, keepdims=True))
            weights = jnp.exp2((scores - higher) * factor)
            if c == 0:
                sums = jnp.sum(weights, axis=0, keepdims=True)
                mixed = nn(vt_s[h, :, part], weights.astype(BF))
            else:
                shrink = jnp.exp2((peak - higher) * factor)
                sums = sums * shrink + jnp.sum(weights, axis=0, keepdims=True)
                mixed = mixed * shrink + nn(vt_s[h, :, part], weights.astype(BF))
            peak = higher
        o_s[h] = jnp.transpose(mixed / sums)
        lse_ref[0, h] = peak * factor + jnp.log2(sums)
        return carry

    lax.fori_loop(0, heads, one_head, 0)
    for h in range(heads):
        o_ref[0, :, h * depth : (h + 1) * depth] = o_s[h].astype(BF)


def attend(lengths, offsets, queries, keys, values, heads, tile):
    count, rows, width = queries.shape
    total = keys.shape[1]
    depth = width // heads
    tile = min(tile, total)
    pick = lambda i, *_: (i, 0, 0)
    return pl.pallas_call(
        functools.partial(attend_kernel, heads, tile),
        grid_spec=pltpu.PrefetchScalarGridSpec(
            num_scalar_prefetch=2,
            grid=(count,),
            in_specs=[
                pl.BlockSpec((1, rows, width), pick),
                pl.BlockSpec((1, total, width), pick),
                pl.BlockSpec((1, total, width), pick),
            ],
            out_specs=[
                pl.BlockSpec((1, rows, width), pick),
                pl.BlockSpec((1, heads, 1, rows), lambda i, *_: (i, 0, 0, 0)),
            ],
            scratch_shapes=[
                pltpu.VMEM((heads, rows, LANES), BF),
                pltpu.VMEM((heads, total, LANES), BF),
                pltpu.VMEM((heads, depth, total), BF),
                pltpu.VMEM((heads, rows, depth), F32),
            ],
        ),
        out_shape=[
            jax.ShapeDtypeStruct((count, rows, width), BF),
            jax.ShapeDtypeStruct((count, heads, 1, rows), F32),
        ],
        compiler_params=pltpu.CompilerParams(vmem_limit_bytes=VMEM_LIMIT),
        cost_estimate=pl.CostEstimate(
            flops=4 * count * heads * rows * total * LANES,
            bytes_accessed=2 * count * width * (2 * rows + 2 * total),
            transcendentals=count * heads * rows * total,
        ),
        name="attend",
    )(lengths, offsets, queries, keys, values)


def attend_back_kernel(
    heads, chunk, lengths_ref, offsets_ref, q_ref, k_ref, v_ref, o_ref, g_ref, lse_ref,
    dq_ref, dk_ref, dv_ref, q_s, k_s, kt_s, v_s, g_s, delta_s, dq_s, dk_s, dv_s
):
    rows, width = q_ref.shape[1:]
    total = k_ref.shape[1]
    depth = width // heads
    scale = depth**-0.5
    factor = scale * LOG2E
    mask = mask_column(lengths_ref, offsets_ref, pl.program_id(0), total, rows)
    ones = jnp.ones((rows, 1), F32)
    cross = jnp.transpose(g_ref[0].astype(F32) * o_ref[0].astype(F32))
    for h in range(heads):
        span = slice(h * depth, (h + 1) * depth)
        delta_s[h] = jnp.sum(cross[span], axis=0, keepdims=True)
        q_s[h] = padded(q_ref[0, :, span], ones)
        k_s[h] = padded(k_ref[0, :, span], mask)
        kt_s[h] = jnp.transpose(k_ref[0, :, span])
        g_s[h] = padded(g_ref[0, :, span])
        v_s[h] = padded(v_ref[0, :, span])

    def one_head(h, carry):
        dq = jnp.zeros((depth, rows), F32)
        for c in range(total // chunk):
            part = slice(c * chunk, (c + 1) * chunk)
            probs = jnp.exp2(nt(k_s[h, part], q_s[h]) * factor - lse_ref[0, h])
            slopes = (probs * (nt(v_s[h, part], g_s[h]) - delta_s[h])).astype(BF)
            dv_s[h, part] = nn(probs.astype(BF), g_s[h]).astype(BF)
            dk_s[h, part] = (nn(slopes, q_s[h]) * scale).astype(BF)
            dq = dq + nn(kt_s[h, :, part], slopes)
        dq_s[h] = jnp.transpose(dq * scale)
        return carry

    lax.fori_loop(0, heads, one_head, 0)
    for h in range(heads):
        span = slice(h * depth, (h + 1) * depth)
        dq_ref[0, :, span] = dq_s[h].astype(BF)
        dk_ref[0, :, span] = dk_s[h][:, :depth]
        dv_ref[0, :, span] = dv_s[h][:, :depth]


def attend_back(lengths, offsets, queries, keys, values, mixed, grads, lse, heads, tile):
    count, rows, width = queries.shape
    total = keys.shape[1]
    depth = width // heads
    tile = min(tile, total)
    pick = lambda i, *_: (i, 0, 0)
    near = pl.BlockSpec((1, rows, width), pick)
    far = pl.BlockSpec((1, total, width), pick)
    return pl.pallas_call(
        functools.partial(attend_back_kernel, heads, tile),
        grid_spec=pltpu.PrefetchScalarGridSpec(
            num_scalar_prefetch=2,
            grid=(count,),
            in_specs=[near, far, far, near, near, pl.BlockSpec((1, heads, 1, rows), lambda i, *_: (i, 0, 0, 0))],
            out_specs=[near, far, far],
            scratch_shapes=[
                pltpu.VMEM((heads, rows, LANES), BF),
                pltpu.VMEM((heads, total, LANES), BF),
                pltpu.VMEM((heads, depth, total), BF),
                pltpu.VMEM((heads, total, LANES), BF),
                pltpu.VMEM((heads, rows, LANES), BF),
                pltpu.VMEM((heads, 1, rows), F32),
                pltpu.VMEM((heads, rows, depth), F32),
                pltpu.VMEM((heads, total, LANES), BF),
                pltpu.VMEM((heads, total, LANES), BF),
            ],
        ),
        out_shape=[
            jax.ShapeDtypeStruct((count, rows, width), BF),
            jax.ShapeDtypeStruct((count, total, width), BF),
            jax.ShapeDtypeStruct((count, total, width), BF),
        ],
        compiler_params=pltpu.CompilerParams(vmem_limit_bytes=VMEM_LIMIT),
        cost_estimate=pl.CostEstimate(
            flops=10 * count * heads * rows * total * LANES,
            bytes_accessed=2 * count * width * (4 * rows + 4 * total),
            transcendentals=count * heads * rows * total,
        ),
        name="attend_back",
    )(lengths, offsets, queries, keys, values, mixed, grads, lse)


def gram_of(moment):
    block = moment.reshape(moment.shape[0] // ROW_BLOCK, ROW_BLOCK, moment.shape[1])
    return jnp.einsum("nrc,nsc->nrs", block, block, precision=PRECISE)


def polynomial(gram):
    eye = jnp.eye(ROW_BLOCK, dtype=F32)
    square = jnp.sum(gram * eye, axis=(1, 2))
    scale = 1.0 / (jnp.sqrt(square) + NORM_EPS)
    current = gram * (scale * scale)[:, None, None]
    mul = functools.partial(jnp.einsum, "nrs,nst->nrt", precision=PRECISE)
    total = None
    for step in range(NS_STEPS):
        factor = NS_A * eye + NS_B * current + NS_C * mul(current, current)
        total = factor if total is None else mul(factor, total)
        if step + 1 < NS_STEPS:
            current = mul(mul(factor, current), factor)
    return total * scale[:, None, None]


def body(net, tokens, conditioning, heights, widths, upstream, *state):
    masters, momenta = state[0:5], state[5:10]
    biases, bias_first, bias_second = state[10:13]
    w_qkv, w_proj, w_fc1, w_fc2, w_ada = masters
    micro, local, rows, width = tokens.shape
    count = micro * local
    head_dim = width // HEADS
    hidden = w_fc1.shape[1] * net.dp
    seq, dp = net.seq, net.dp
    y = net.y.digit()

    bounds = [0, 6 * width, 7 * width, 8 * width, 9 * width, 9 * width + hidden, 10 * width + hidden]

    ada_rows, ada_cols = w_ada.shape
    cond = conditioning.astype(F32).reshape(count, width)
    cond_act, silu_back = jax.vjp(sigmoid_linear, cond)
    cond_low = cond_act.astype(BF)
    cond_rows = lax.dynamic_slice_in_dim(cond_low, y * ada_rows, ada_rows, 1)
    cond_all = net.to_dp(jnp.broadcast_to(cond_rows[None], (dp,) + cond_rows.shape))
    cond_all = cond_all.reshape(dp * count, ada_rows)
    bias_full = net.to_all(jnp.broadcast_to(biases, (dp, seq) + biases.shape)).reshape(-1)
    b_ada, b_q, b_v, b_proj, b_fc1, b_fc2 = [bias_full[bounds[i] : bounds[i + 1]] for i in range(6)]

    n_qkv, n_proj, n_fc1, n_fc2 = [w.shape[1] for w in (w_qkv, w_proj, w_fc1, w_fc2)]
    unit_qkv = math.gcd(n_qkv, 8)
    unit = math.gcd(math.gcd(n_proj, n_fc1), math.gcd(n_fc2, 8))
    fold = hidden // width
    layout_qkv = [(n_qkv, 1)]
    layout = [(n_proj, 1), (n_fc1, 1), (n_fc2, fold)]
    own_tokens = tokens.reshape(count, rows, width)
    units_qkv = net.rows_joined([w_qkv], unit_qkv, width)
    first_tokens = net.y.gather(after(own_tokens[0], units_qkv))
    units = net.rows_joined(
        [after(w, first_tokens[-1]) for w in (w_proj, w_fc1, w_fc2)], unit, width
    )
    other_tokens = [net.y.gather(after(own_tokens[i], units)) for i in range(1, count)]
    all_tokens = jnp.stack([jnp.concatenate(t, axis=0) for t in [first_tokens] + other_tokens])
    (t_qkv,), arrived = net.gather_weights(units_qkv, layout_qkv)
    (t_proj, t_fc1, t_fc2), _ = net.gather_weights(after(units, *arrived), layout)

    low_ada = w_ada.astype(BF)
    partial = jnp.dot(cond_all, low_ada, preferred_element_type=F32).reshape(dp, 1, count, ada_cols)
    received = jnp.sum(net.to_all(jnp.broadcast_to(partial, (dp, seq, count, ada_cols))), axis=1)
    modulation = jnp.transpose(received, (1, 0, 2)).reshape(count, dp * ada_cols) + b_ada
    shift_one, scale_one, gate_one, shift_two, scale_two, gate_two = jnp.split(
        modulation[:, None, :], 6, axis=-1
    )

    lengths = (heights * widths).reshape(count).astype(jnp.int32)
    offsets = jnp.stack([((y + s) % seq) * rows for s in range(seq)]).astype(jnp.int32)
    normed_all, inverse_all, attn_all, queries, keys, values, attended_low, log_total = [[] for _ in range(8)]
    for i in range(count):
        normed, inverse = layer_norm(all_tokens[i].astype(F32))
        attn = (normed * (1.0 + scale_one[i]) + shift_one[i]).astype(BF)
        queries.append((dot_t(attn[None, :rows], t_qkv[:width]) + b_q).astype(BF))
        keys.append(dot_t(attn[None], t_qkv[width : 2 * width]).astype(BF))
        values.append((dot_t(attn[None], t_qkv[2 * width :]) + b_v).astype(BF))
        mixed, lse = attend(lengths[i : i + 1], offsets, queries[i], keys[i], values[i], HEADS, 512)
        normed_all.append(normed[:rows])
        inverse_all.append(inverse[:rows])
        attn_all.append(attn)
        attended_low.append(mixed[0])
        log_total.append(lse)
    attended_low = jnp.stack(attended_low)
    attn_all = jnp.stack(attn_all)
    attn_own = attn_all[:, :rows]
    inputs = own_tokens.astype(F32)
    branch_one = dot_t(attended_low, t_proj) + b_proj
    mixed_one = inputs + gate_one * branch_one
    normed_two, inverse_two = layer_norm(mixed_one)
    ffn_in = (normed_two * (1.0 + scale_two) + shift_two).astype(BF)
    pre_act = dot_t(ffn_in, t_fc1) + b_fc1
    activated, gelu_back = jax.vjp(gelu_tanh, pre_act)
    activated_low = activated.astype(BF)
    branch_two = dot_t(activated_low, t_fc2) + b_fc2
    result = (mixed_one + gate_two * branch_two).astype(BF)

    grad_out = upstream.reshape(count, rows, width).astype(F32)
    grad_branch_two = (gate_two * grad_out).astype(BF)
    grad_gate_two = jnp.sum(branch_two * grad_out, axis=1)
    terms_fc2 = [
        outer(grad_branch_two, activated_low[..., j * width : (j + 1) * width]) for j in range(fold)
    ]
    bias_fc2 = jnp.sum(grad_branch_two.astype(F32), axis=(0, 1))
    grad_pre = gelu_back(dot(grad_branch_two, t_fc2))[0].astype(BF)
    term_fc1 = outer(grad_pre, ffn_in)
    bias_fc1 = jnp.sum(grad_pre.astype(F32), axis=(0, 1))
    grad_ffn_in = dot(grad_pre, t_fc1)
    grad_shift_two = jnp.sum(grad_ffn_in, axis=1)
    grad_scale_two = jnp.sum(grad_ffn_in * normed_two, axis=1)
    grad_mixed = grad_out + norm_back(normed_two, inverse_two, grad_ffn_in * (1.0 + scale_two))
    grad_gate_one = jnp.sum(branch_one * grad_mixed, axis=1)
    grad_branch_one = (gate_one * grad_mixed).astype(BF)
    term_proj = outer(grad_branch_one, attended_low)
    shard_proj, shard_fc1, shard_fc2 = net.scatter_weights([term_proj, term_fc1, *terms_fc2], unit, width, layout)
    bias_proj = jnp.sum(grad_branch_one.astype(F32), axis=(0, 1))
    grad_attended = dot(grad_branch_one, t_proj).astype(BF)

    parts = [
        attend_back(
            lengths[i : i + 1], offsets, queries[i], keys[i], values[i], attended_low[i : i + 1],
            grad_attended[i : i + 1], log_total[i], HEADS, 512,
        )
        for i in range(count)
    ]
    grad_q, grad_k, grad_v = [jnp.concatenate([part[k] for part in parts], axis=0) for k in range(3)]
    term_qkv = jnp.concatenate(
        [outer(grad_q, attn_own), outer(grad_k, attn_all), outer(grad_v, attn_all)], axis=0
    )
    (shard_qkv,) = net.scatter_weights([term_qkv], unit_qkv, width, layout_qkv)
    bias_q = jnp.sum(grad_q.astype(F32), axis=(0, 1))
    bias_v = jnp.sum(grad_v.astype(F32), axis=(0, 1))
    part_in = dot(grad_k, t_qkv[width : 2 * width]) + dot(grad_v, t_qkv[2 * width :])
    own_part = part_in[:, :rows] + dot(grad_q, t_qkv[:width])
    grad_attn_in = net.y.scatter_sum(
        lambda s: own_part if s == 0 else part_in[:, s * rows : (s + 1) * rows].astype(BF)
    )
    normed_one, inverse_one = jnp.stack(normed_all), jnp.stack(inverse_all)
    grad_shift_one = jnp.sum(grad_attn_in, axis=1)
    grad_scale_one = jnp.sum(grad_attn_in * normed_one, axis=1)
    grad_inputs = grad_mixed + norm_back(normed_one, inverse_one, grad_attn_in * (1.0 + scale_one))

    grad_mod_local = jnp.concatenate(
        [grad_shift_one, grad_scale_one, grad_gate_one, grad_shift_two, grad_scale_two, grad_gate_two], axis=-1
    )
    bias_ada = jnp.sum(grad_mod_local, axis=0)
    sent = jnp.transpose(grad_mod_local.reshape(count, dp, 1, ada_cols), (1, 2, 0, 3))
    sent = jnp.broadcast_to(sent, (dp, seq, count, ada_cols))
    mod_cols = jnp.sum(net.to_all(sent), axis=1).astype(BF).reshape(dp * count, ada_cols)
    shard_ada = jnp.einsum("sr,sc->rc", cond_all, mod_cols, preferred_element_type=F32)
    cond_part = jnp.einsum("sc,rc->sr", mod_cols, low_ada, preferred_element_type=F32)
    cond_part = cond_part.reshape(dp, 1, count, ada_rows)
    cond_part = jnp.sum(net.to_all(jnp.broadcast_to(cond_part, (dp, seq, count, ada_rows))), axis=0)
    grad_cond = silu_back(jnp.transpose(cond_part, (1, 0, 2)).reshape(count, width))[0]

    term_bias = jnp.concatenate([bias_ada, bias_q, bias_v, bias_proj, bias_fc1, bias_fc2])
    grad_bias = jnp.sum(net.to_all(term_bias.reshape(dp, seq, -1)), axis=(0, 1))
    next_first = BETA_FIRST * bias_first + (1.0 - BETA_FIRST) * grad_bias
    next_second = BETA_SECOND * bias_second + (1.0 - BETA_SECOND) * grad_bias * grad_bias
    first_hat = next_first / (1.0 - BETA_FIRST**STEP_COUNT)
    second_hat = next_second / (1.0 - BETA_SECOND**STEP_COUNT)
    new_biases = biases * (1.0 - ADAM_RATE * ADAM_DECAY) - ADAM_RATE * first_hat / (
        jnp.sqrt(second_hat) + ADAM_EPS
    )

    shards = (shard_qkv, shard_proj, shard_fc1, shard_fc2, shard_ada)
    moments = [MUON_DECAY * momentum + shard for momentum, shard in zip(momenta, shards)]
    grams = [gram_of(moment) for moment in moments]
    directions = [None] * 5
    for group in ((3, 2, 1), (0, 4)):
        stack = jnp.concatenate([grams[i] for i in group], axis=0)
        blocks = stack.shape[0]
        each = -(-blocks // dp)
        stack = jnp.pad(stack, ((0, each * dp - blocks), (0, 0), (0, 0)))
        mine = jnp.sum(net.to_dp(stack.reshape(dp, each, ROW_BLOCK, ROW_BLOCK)), axis=0)
        factors = jnp.broadcast_to(polynomial(mine)[None], (dp, each, ROW_BLOCK, ROW_BLOCK))
        factors = net.to_dp(factors).reshape(dp * each, ROW_BLOCK, ROW_BLOCK)
        start = 0
        for i in group:
            size = grams[i].shape[0]
            block = moments[i].reshape(size, ROW_BLOCK, -1)
            direction = jnp.einsum("nrs,nsc->nrc", factors[start : start + size], block, precision=PRECISE)
            directions[i] = direction.reshape(moments[i].shape)
            start += size
    rates = (math.sqrt(3.0), 1.0, math.sqrt(hidden / width), math.sqrt(width / hidden), math.sqrt(6.0))
    new_weights = [
        weight * (1.0 - WEIGHT_SHRINK) - rate * direction
        for weight, rate, direction in zip(masters, rates, directions)
    ]
    return (
        result.reshape(tokens.shape),
        grad_inputs.astype(BF).reshape(tokens.shape),
        grad_cond.reshape(conditioning.shape),
        *new_weights,
        *moments,
        new_biases,
        next_first,
        next_second,
    )


def solution(mesh):
    rows = P(None, "dp", "seq", None)
    matrix = P("seq", "dp")
    flat = P(("dp", "seq"))
    in_specs = (rows, P(None, "dp", None), P(None, "dp"), P(None, "dp"), rows) + (matrix,) * 10 + (flat,) * 3
    out_specs = (rows, rows, P(None, "dp", None)) + (matrix,) * 10 + (flat,) * 3
    return jax.shard_map(
        functools.partial(body, Net(mesh)), mesh=mesh, in_specs=in_specs, out_specs=out_specs, check_vma=False
    )
```

```python
import functools
import math

import jax
import jax.numpy as jnp
from jax import lax
from jax.experimental import pallas as pl
from jax.experimental.pallas import tpu as pltpu
from jax.sharding import PartitionSpec as P

HEADS = 16
ROW_BLOCK = 144
NS_STEPS = 5
STEP_COUNT = 10

PRECISE = lax.Precision.HIGHEST
LN_EPS = 1e-06
MASKED = -1e30
NS_A = 3.4445
NS_B = -4.775
NS_C = 2.0315
MUON_DECAY = 0.5
WEIGHT_SHRINK = 0.0001
NORM_EPS = 1e-07
BETA_FIRST = 0.9
BETA_SECOND = 0.999
ADAM_RATE = 0.1
ADAM_DECAY = 0.01
ADAM_EPS = 1e-08
BF = jnp.bfloat16
F32 = jnp.float32
VMEM_LIMIT = 60 * 2**20


class Ring:
    def __init__(self, name, total, stride, size):
        self.name, self.total, self.stride, self.size = name, total, stride, size

    def digit(self):
        return (lax.axis_index(self.name) // self.stride) % self.size

    def send(self, value, shift):
        pairs = []
        for i in range(self.total):
            d = (i // self.stride) % self.size
            pairs.append((i, i + ((d + shift) % self.size - d) * self.stride))
        return lax.ppermute(value, self.name, pairs)

    def gather(self, value, far=1):
        n = self.size
        blocks = [value] + [None] * (n - 1)
        if n == 2:
            blocks[1] = self.send(value, 1)
        elif n > 2:
            low = high = value
            for t in range(1, n // 2):
                low, high = self.send(low, 1), self.send(high, -1)
                blocks[n - t], blocks[t] = low, high
            blocks[n // 2] = self.send(low, 1) if far == 1 else self.send(high, -1)
        return blocks

    def gather_steps(self, value, far=1):
        n = self.size
        blocks = [value] + [None] * (n - 1)
        if n == 2:
            blocks[1] = self.send(value, 1)
            anchor = yield [value]
            blocks[1] = tie(blocks[1], anchor)
            return blocks
        low = high = value
        for t in range(1, n // 2):
            sent = [low, high]
            low, high = self.send(low, 1), self.send(high, -1)
            anchor = yield sent
            low, high = tie(low, anchor), tie(high, anchor)
            blocks[n - t], blocks[t] = low, high
        sent = [low if far == 1 else high]
        last = self.send(sent[0], far)
        anchor = yield sent
        blocks[n // 2] = tie(last, anchor)
        return blocks

    def scatter_steps(self, block_of, far=1):
        n = self.size
        if n == 1:
            return block_of(0).astype(F32)
        if n == 2:
            sent = block_of(1)
            got = self.send(sent, 1)
            anchor = yield [sent]
            return block_of(0).astype(F32) + tie(got, anchor).astype(F32)
        sent = block_of(n // 2)
        got = self.send(sent, far)
        anchor = yield [sent]
        low, high = (tie(got, anchor), None) if far == 1 else (None, tie(got, anchor))
        for t in range(n // 2 - 1, 0, -1):
            up, down = block_of(t), block_of(n - t)
            if low is not None:
                up = (up.astype(F32) + low.astype(F32)).astype(up.dtype)
            if high is not None:
                down = (down.astype(F32) + high.astype(F32)).astype(down.dtype)
            low, high = self.send(up, 1), self.send(down, -1)
            anchor = yield [up, down]
            low, high = tie(low, anchor), tie(high, anchor)
        return block_of(0).astype(F32) + low.astype(F32) + high.astype(F32)


def tie(value, *earlier):
    earlier = [array for array in earlier if array is not None]
    if not earlier:
        return value
    anywhere = pl.BlockSpec(memory_space=pl.ANY)
    return pl.pallas_call(
        lambda *refs: None,
        out_shape=jax.ShapeDtypeStruct(value.shape, value.dtype),
        in_specs=[anywhere] * (1 + len(earlier)),
        out_specs=anywhere,
        input_output_aliases={0: 0},
        name="tie",
    )(value, *earlier)


def lockstep(*steps):
    results = [None] * len(steps)
    alive = dict(enumerate(steps))
    anchor = None
    while alive:
        sent = []
        for n, step in list(alive.items()):
            try:
                sent += step.send(anchor)
            except StopIteration as stop:
                results[n] = stop.value
                del alive[n]
        if alive:
            anchor = yield sent
    return results


class Staged:
    def __init__(self, steps):
        self.steps, self.result, self.started, self.done = steps, None, False, False

    def advance(self, anchor=None):
        if self.done:
            return []
        try:
            sent = self.steps.send(anchor if self.started else None)
            self.started = True
            return sent
        except StopIteration as stop:
            self.result, self.done = stop.value, True
            return []

    def finish(self, anchor=None):
        while not self.done:
            self.advance(anchor)
        return self.result


def place_kernel(moves, outs, count, parts, *refs):
    spots, sources = refs[0], refs[1 : 1 + count]
    outputs, (full, in_sems, out_sems) = refs[1 + count : 1 + count + parts], refs[1 + count + parts :]
    arrivals = []
    for n, (source, index, target) in enumerate(moves):
        arrivals.append(
            pltpu.make_async_copy(sources[source].at[index], full.at[target(spots)], in_sems.at[n])
        )
    for copy in arrivals:
        copy.start()
    for copy in arrivals:
        copy.wait()
    exits = []
    for n, (start, output, target) in enumerate(outs):
        exits.append(pltpu.make_async_copy(full.at[start], outputs[output].at[target], out_sems.at[n]))
    for copy in exits:
        copy.start()
    for copy in exits:
        copy.wait()


def place(spots, sources, moves, shape, outs, shapes):
    moved = math.prod(shape) * 2
    return pl.pallas_call(
        functools.partial(place_kernel, moves, outs, len(sources), len(shapes)),
        out_shape=[jax.ShapeDtypeStruct(each, BF) for each in shapes],
        in_specs=[pl.BlockSpec(memory_space=pltpu.SMEM)]
        + [pl.BlockSpec(memory_space=pl.ANY)] * len(sources),
        out_specs=[pl.BlockSpec(memory_space=pl.ANY)] * len(shapes),
        scratch_shapes=[
            pltpu.VMEM(shape, BF),
            pltpu.SemaphoreType.DMA((len(moves),)),
            pltpu.SemaphoreType.DMA((len(outs),)),
        ],
        compiler_params=pltpu.CompilerParams(vmem_limit_bytes=VMEM_LIMIT),
        cost_estimate=pl.CostEstimate(flops=0, bytes_accessed=2 * moved, transcendentals=0),
        name="place",
    )(spots, *sources)


class Net:
    def __init__(self, mesh):
        dp, seq = mesh.shape["dp"], mesh.shape["seq"]
        self.dp, self.seq = dp, seq
        self.core = Ring("dp", dp, 1, 2)
        self.x = Ring("dp", dp, 2, 2)
        self.z = Ring("dp", dp, 4, dp // 4)
        self.y = Ring("seq", seq, 1, seq)

    def spots(self):
        return jnp.stack([self.z.digit(), self.x.digit(), self.core.digit()]).astype(jnp.int32)


    def wire(self, shards):
        turned = [shard.astype(BF).T for shard in shards]
        return turned[0] if len(turned) == 1 else jnp.concatenate(turned, axis=0)

    def joined(self, wires, unit, depth):
        if self.seq == 2:
            own, other = wires
            full = jnp.where(
                self.y.digit() == 0,
                jnp.concatenate([own, other], axis=1),
                jnp.concatenate([other, own], axis=1),
            )
        else:
            order = (jnp.arange(self.seq) - self.y.digit()) % self.seq
            full = jnp.take(jnp.stack(wires), order, axis=0)
            full = jnp.transpose(full, (1, 0, 2)).reshape(full.shape[1], -1)
        full = full.reshape(full.shape[0] // unit, unit, full.shape[1] // depth, depth)
        return jnp.transpose(full, (2, 0, 1, 3)).reshape(-1, unit, depth)

    def gather_steps(self, units, layout, part):
        g, unit, depth = units.shape
        zs = self.z.size
        ga = max(1, int(part * g))
        first, second = units[:ga], units[ga:]

        def line_steps():
            blocks = yield from self.z.gather_steps(first, 1)
            line = jnp.stack(blocks)
            return (yield from self.x.gather_steps(line))

        def pair_steps():
            blocks = yield from self.x.gather_steps(second)
            return (yield from self.z.gather_steps(jnp.stack(blocks), -1))

        lines, pairs = yield from lockstep(line_steps(), pair_steps())
        pieces = lines + pairs
        others = [self.core.send(piece, 1) for piece in pieces]
        anchor = yield pieces
        sources, moves = pieces + [tie(other, anchor) for other in others], []

        def spot(sz, sx, sc, start, stop):
            def target(spots):
                return (
                    lax.rem(spots[0] + sz, zs),
                    lax.rem(spots[1] + sx, 2),
                    lax.rem(spots[2] + sc, 2),
                    pl.ds(start, stop - start),
                )

            return target

        for sc in range(2):
            base = sc * len(pieces)
            for sx in range(2):
                for sz in range(zs):
                    moves.append((base + sx, (sz,), spot(sz, sx, sc, 0, ga)))
                    moves.append((base + 2 + sz, (sx,), spot(sz, sx, sc, ga, g)))
        outs, shapes, start = [], [], 0
        for n, (rows, blocks) in enumerate(layout):
            size = rows // unit
            shapes.append((zs, 2, 2, size, unit, blocks * depth))
            for j in range(blocks):
                window = (slice(None),) * 3 + (pl.ds(start, size),)
                target = (slice(None),) * 5 + (pl.ds(j * depth, depth),)
                outs.append((window, n, target))
                start += size
        full = place(self.spots(), sources, moves, (zs, 2, 2, g, unit, depth), outs, shapes)
        return [f.reshape(-1, f.shape[-1]) for f in full], lines[1:] + pairs[1:]

    def scatter_steps(self, terms, unit, depth, layout, part):
        zs = self.z.size
        blocks = [term.reshape(zs, 2, 2, -1, unit, depth) for term in terms]
        g = sum(block.shape[3] for block in blocks)
        ga = max(1, int(part * g))
        core, x, z = self.core.digit(), self.x.digit(), self.z.digit()

        def half_of(s):
            parts = [lax.dynamic_index_in_dim(block, (core + s) % 2, 2, keepdims=False) for block in blocks]
            return parts[0] if len(parts) == 1 else jnp.concatenate(parts, axis=2)

        half = (yield from self.core.scatter_steps(half_of)).astype(BF)

        def line_steps():
            line = yield from self.x.scatter_steps(
                lambda s: lax.dynamic_index_in_dim(half[:, :, :ga], (x + s) % 2, 1, keepdims=False)
            )
            line = line.astype(BF)
            return (
                yield from self.z.scatter_steps(
                    lambda s: lax.dynamic_index_in_dim(line, (z + s) % zs, 0, keepdims=False), 1
                )
            )

        def pair_steps():
            pair = yield from self.z.scatter_steps(
                lambda s: lax.dynamic_index_in_dim(half[:, :, ga:], (z + s) % zs, 0, keepdims=False), -1
            )
            pair = pair.astype(BF)
            return (
                yield from self.x.scatter_steps(
                    lambda s: lax.dynamic_index_in_dim(pair, (x + s) % 2, 0, keepdims=False)
                )
            )

        line, pair = yield from lockstep(line_steps(), pair_steps())
        joined = jnp.concatenate([line, pair], axis=0).astype(BF)
        count = layout[0][1]
        if count > 1:
            joined = jnp.transpose(joined.reshape(count, -1, unit, depth), (1, 2, 0, 3))
        joined = joined.reshape(-1, self.seq, count * depth // self.seq)
        y = self.y.digit()
        return (
            yield from self.y.scatter_steps(
                lambda s: lax.dynamic_index_in_dim(joined, (y + s) % self.seq, 1, keepdims=False)
            )
        )


    def muon_steps(self, groups, masters, rates):
        momenta, own, other = muon_gram(self.spots(), groups)
        got = self.core.send(other, 1)
        anchor = yield [other]
        half = own + tie(got, anchor)
        sent, kept = half[1], half[0]
        got = self.x.send(sent, 1)
        anchor = yield [sent]
        blocks = yield from self.z.gather_steps(kept + tie(got, anchor))
        factor = polynomial(blocks)
        got = self.x.send(factor, 1)
        anchor = yield [factor]
        got = tie(got, anchor)
        pair = [factor, got]
        others = [self.core.send(each, 1) for each in pair]
        anchor = yield pair
        factors = pair + [tie(each, anchor) for each in others]
        return momenta, muon_apply(self.spots(), factors, momenta, masters, rates)


    def to_all(self, value):
        flat = value.reshape((self.dp * self.seq,) + value.shape[2:])
        return lax.all_to_all(flat, ("dp", "seq"), 0, 0, tiled=True).reshape(value.shape)

    def to_dp(self, value):
        return lax.all_to_all(value, "dp", 0, 0, tiled=True)


def layer_norm(values):
    centered = values - jnp.mean(values, axis=-1, keepdims=True)
    inverse = lax.rsqrt(jnp.mean(centered * centered, axis=-1, keepdims=True) + LN_EPS)
    return (centered * inverse, inverse)


def norm_back(normed, inverse, grad):
    mean_grad = jnp.mean(grad, axis=-1, keepdims=True)
    mean_cross = jnp.mean(grad * normed, axis=-1, keepdims=True)
    return inverse * (grad - mean_grad - normed * mean_cross)


def sigmoid_linear(values):
    return values * jax.nn.sigmoid(values)


def gelu_tanh(values):
    return jax.nn.gelu(values, approximate=True)


def dot_t(left, right):
    return jnp.einsum("srk,nk->srn", left, right, preferred_element_type=F32)


def dot(left, right):
    return jnp.einsum("srn,nk->srk", left, right, preferred_element_type=F32)


def outer(left, right):
    return jnp.einsum("srn,srk->nk", left, right, preferred_element_type=F32).astype(BF)


LANES = 128
LOG2E = math.log2(math.e)


def padded(block, column=None):
    rows, depth = block.shape
    if column is None:
        return jnp.concatenate([block, jnp.zeros((rows, LANES - depth), block.dtype)], axis=1)
    rest = jnp.zeros((rows, LANES - depth - 1), block.dtype)
    return jnp.concatenate([block, column.astype(block.dtype), rest], axis=1)


def mask_column(lengths_ref, offsets_ref, sample, total, rows):
    place = lax.broadcasted_iota(jnp.int32, (total, 1), 0)
    position = place
    for s in range(total // rows):
        position = jnp.where(place // rows == s, place - s * rows + offsets_ref[s], position)
    return jnp.where(position < lengths_ref[sample], 0.0, MASKED)


def nt(left, right):
    return lax.dot_general(left, right, (((1,), (1,)), ((), ())), preferred_element_type=F32)


def nn(left, right):
    return jnp.dot(left, right, preferred_element_type=F32)


def without(kernel, start, count, *fixed):
    def run(*refs):
        kernel(*fixed, *refs[:start], *refs[start + count :])

    return run


def attend_kernel(heads, chunk, lengths_ref, offsets_ref, q_ref, k_ref, v_ref, o_ref, lse_ref, q_s, k_s, vt_s, o_s):
    rows, width = q_ref.shape[1:]
    total = k_ref.shape[1]
    depth = width // heads
    factor = depth**-0.5 * LOG2E
    mask = mask_column(lengths_ref, offsets_ref, pl.program_id(0), total, rows)
    ones = jnp.ones((rows, 1), F32)
    for h in range(heads):
        span = slice(h * depth, (h + 1) * depth)
        q_s[h] = padded(q_ref[0, :, span], ones)
        k_s[h] = padded(k_ref[0, :, span], mask)
        vt_s[h] = jnp.transpose(v_ref[0, :, span])

    def one_head(h, carry):
        peak = jnp.full((1, rows), MASKED, F32)
        sums = jnp.zeros((1, rows), F32)
        mixed = jnp.zeros((depth, rows), F32)
        for c in range(total // chunk):
            part = slice(c * chunk, (c + 1) * chunk)
            scores = nt(k_s[h, part], q_s[h])
            higher = jnp.maximum(peak, jnp.max(scores, axis=0, keepdims=True))
            weights = jnp.exp2((scores - higher) * factor)
            if c == 0:
                sums = jnp.sum(weights, axis=0, keepdims=True)
                mixed = nn(vt_s[h, :, part], weights.astype(BF))
            else:
                shrink = jnp.exp2((peak - higher) * factor)
                sums = sums * shrink + jnp.sum(weights, axis=0, keepdims=True)
                mixed = mixed * shrink + nn(vt_s[h, :, part], weights.astype(BF))
            peak = higher
        o_s[h] = jnp.transpose(mixed / sums)
        lse_ref[0, h] = peak * factor + jnp.log2(sums)
        return carry

    lax.fori_loop(0, heads, one_head, 0)
    for h in range(heads):
        o_ref[0, :, h * depth : (h + 1) * depth] = o_s[h].astype(BF)


def attend(lengths, offsets, queries, keys, values, heads, tile, deps=()):
    count, rows, width = queries.shape
    total = keys.shape[1]
    depth = width // heads
    tile = min(tile, total)
    pick = lambda i, *_: (i, 0, 0)
    return pl.pallas_call(
        without(attend_kernel, 5, len(deps), heads, tile),
        grid_spec=pltpu.PrefetchScalarGridSpec(
            num_scalar_prefetch=2,
            grid=(count,),
            in_specs=[
                pl.BlockSpec((1, rows, width), pick),
                pl.BlockSpec((1, total, width), pick),
                pl.BlockSpec((1, total, width), pick),
            ]
            + [pl.BlockSpec(memory_space=pl.ANY)] * len(deps),
            out_specs=[
                pl.BlockSpec((1, rows, width), pick),
                pl.BlockSpec((1, heads, 1, rows), lambda i, *_: (i, 0, 0, 0)),
            ],
            scratch_shapes=[
                pltpu.VMEM((heads, rows, LANES), BF),
                pltpu.VMEM((heads, total, LANES), BF),
                pltpu.VMEM((heads, depth, total), BF),
                pltpu.VMEM((heads, rows, depth), F32),
            ],
        ),
        out_shape=[
            jax.ShapeDtypeStruct((count, rows, width), BF),
            jax.ShapeDtypeStruct((count, heads, 1, rows), F32),
        ],
        compiler_params=pltpu.CompilerParams(vmem_limit_bytes=VMEM_LIMIT),
        cost_estimate=pl.CostEstimate(
            flops=4 * count * heads * rows * total * LANES,
            bytes_accessed=2 * count * width * (2 * rows + 2 * total),
            transcendentals=count * heads * rows * total,
        ),
        name="attend",
    )(lengths, offsets, queries, keys, values, *deps)


def attend_back_kernel(
    heads, chunk, lengths_ref, offsets_ref, q_ref, k_ref, v_ref, o_ref, g_ref, lse_ref,
    dq_ref, dk_ref, dv_ref, q_s, k_s, kt_s, v_s, g_s, delta_s, dq_s, dk_s, dv_s
):
    rows, width = q_ref.shape[1:]
    total = k_ref.shape[1]
    depth = width // heads
    scale = depth**-0.5
    factor = scale * LOG2E
    mask = mask_column(lengths_ref, offsets_ref, pl.program_id(0), total, rows)
    ones = jnp.ones((rows, 1), F32)
    cross = jnp.transpose(g_ref[0].astype(F32) * o_ref[0].astype(F32))
    for h in range(heads):
        span = slice(h * depth, (h + 1) * depth)
        delta_s[h] = jnp.sum(cross[span], axis=0, keepdims=True)
        q_s[h] = padded(q_ref[0, :, span], ones)
        k_s[h] = padded(k_ref[0, :, span], mask)
        kt_s[h] = jnp.transpose(k_ref[0, :, span])
        g_s[h] = padded(g_ref[0, :, span])
        v_s[h] = padded(v_ref[0, :, span])

    def one_head(h, carry):
        dq = jnp.zeros((depth, rows), F32)
        for c in range(total // chunk):
            part = slice(c * chunk, (c + 1) * chunk)
            probs = jnp.exp2(nt(k_s[h, part], q_s[h]) * factor - lse_ref[0, h])
            slopes = (probs * (nt(v_s[h, part], g_s[h]) - delta_s[h])).astype(BF)
            dv_s[h, part] = nn(probs.astype(BF), g_s[h]).astype(BF)
            dk_s[h, part] = (nn(slopes, q_s[h]) * scale).astype(BF)
            dq = dq + nn(kt_s[h, :, part], slopes)
        dq_s[h] = jnp.transpose(dq * scale)
        return carry

    lax.fori_loop(0, heads, one_head, 0)
    for h in range(heads):
        span = slice(h * depth, (h + 1) * depth)
        dq_ref[0, :, span] = dq_s[h].astype(BF)
        dk_ref[0, :, span] = dk_s[h][:, :depth]
        dv_ref[0, :, span] = dv_s[h][:, :depth]


def attend_back(lengths, offsets, queries, keys, values, mixed, grads, lse, heads, tile, deps=()):
    count, rows, width = queries.shape
    total = keys.shape[1]
    depth = width // heads
    tile = min(tile, total)
    pick = lambda i, *_: (i, 0, 0)
    near = pl.BlockSpec((1, rows, width), pick)
    far = pl.BlockSpec((1, total, width), pick)
    return pl.pallas_call(
        without(attend_back_kernel, 8, len(deps), heads, tile),
        grid_spec=pltpu.PrefetchScalarGridSpec(
            num_scalar_prefetch=2,
            grid=(count,),
            in_specs=[near, far, far, near, near, pl.BlockSpec((1, heads, 1, rows), lambda i, *_: (i, 0, 0, 0))]
            + [pl.BlockSpec(memory_space=pl.ANY)] * len(deps),
            out_specs=[near, far, far],
            scratch_shapes=[
                pltpu.VMEM((heads, rows, LANES), BF),
                pltpu.VMEM((heads, total, LANES), BF),
                pltpu.VMEM((heads, depth, total), BF),
                pltpu.VMEM((heads, total, LANES), BF),
                pltpu.VMEM((heads, rows, LANES), BF),
                pltpu.VMEM((heads, 1, rows), F32),
                pltpu.VMEM((heads, rows, depth), F32),
                pltpu.VMEM((heads, total, LANES), BF),
                pltpu.VMEM((heads, total, LANES), BF),
            ],
        ),
        out_shape=[
            jax.ShapeDtypeStruct((count, rows, width), BF),
            jax.ShapeDtypeStruct((count, total, width), BF),
            jax.ShapeDtypeStruct((count, total, width), BF),
        ],
        compiler_params=pltpu.CompilerParams(vmem_limit_bytes=VMEM_LIMIT),
        cost_estimate=pl.CostEstimate(
            flops=10 * count * heads * rows * total * LANES,
            bytes_accessed=2 * count * width * (4 * rows + 4 * total),
            transcendentals=count * heads * rows * total,
        ),
        name="attend_back",
    )(lengths, offsets, queries, keys, values, mixed, grads, lse, *deps)


def block_spots(counts):
    total = sum(counts)
    per = -(-total // 4)
    spots = []
    for matrix, count in enumerate(counts):
        for block in range(count):
            n = len(spots)
            spots.append((matrix, block, n // per // 2, n // per % 2, n % per))
    return spots, per


def precise(left, right, dims):
    return lax.dot_general(left, right, (dims, ((), ())), precision=PRECISE, preferred_element_type=F32)


def muon_gram_kernel(groups, spots_ref, *refs):
    count = sum(matrices for _, matrices in groups)
    sums, momenta = refs[: len(groups)], refs[len(groups) : len(groups) + count]
    outs = refs[len(groups) + count : len(groups) + 2 * count]
    own_ref, other_ref = refs[len(groups) + 2 * count :]
    n = 0
    for (turned, matrices), sum_ref in zip(groups, sums):
        grads = jnp.transpose(sum_ref[...]) if turned else sum_ref[...]
        start = 0
        for _ in range(matrices):
            width = momenta[n].shape[1]
            outs[n][...] = MUON_DECAY * momenta[n][...] + grads[:, start : start + width]
            start += width
            n += 1
    spots, per = block_spots([out.shape[0] // ROW_BLOCK for out in outs])
    if len(spots) < 4 * per:
        own_ref[...] = jnp.zeros_like(own_ref)
        other_ref[...] = jnp.zeros_like(other_ref)
    for matrix, block, core, x, place_in in spots:
        rows = outs[matrix][block * ROW_BLOCK : (block + 1) * ROW_BLOCK]
        gram = precise(rows, rows, ((1,), (1,)))
        away = lax.rem(spots_ref[1] + x, 2)

        @pl.when(spots_ref[2] == core)
        def _():
            own_ref[away, place_in] = gram

        @pl.when(spots_ref[2] != core)
        def _():
            other_ref[away, place_in] = gram


def muon_gram(spots, groups):
    momenta = [momentum for _, _, each in groups for momentum in each]
    _, per = block_spots([momentum.shape[0] // ROW_BLOCK for momentum in momenta])
    grams = jax.ShapeDtypeStruct((2, per, ROW_BLOCK, ROW_BLOCK), F32)
    vmem = pl.BlockSpec(memory_space=pltpu.VMEM)
    outs = pl.pallas_call(
        functools.partial(muon_gram_kernel, [(turned, len(each)) for _, turned, each in groups]),
        out_shape=[jax.ShapeDtypeStruct(momentum.shape, F32) for momentum in momenta] + [grams, grams],
        in_specs=[pl.BlockSpec(memory_space=pltpu.SMEM)] + [vmem] * (len(groups) + len(momenta)),
        out_specs=[vmem] * (len(momenta) + 2),
        compiler_params=pltpu.CompilerParams(vmem_limit_bytes=VMEM_LIMIT),
        name="muon_gram",
    )(spots, *[group[0] for group in groups], *momenta)
    return outs[:-2], outs[-2], outs[-1]


def polynomial_kernel(count, *refs):
    out = refs[count]
    shape = (ROW_BLOCK, ROW_BLOCK)
    eye = (lax.broadcasted_iota(jnp.int32, shape, 0) == lax.broadcasted_iota(jnp.int32, shape, 1)).astype(F32)
    mul = lambda left, right: precise(left, right, ((1,), (0,)))
    blocks = range(out.shape[0])
    currents, scales, totals = [], [], []
    for n in blocks:
        gram = refs[0][n]
        for ref in refs[1:count]:
            gram = gram + ref[n]
        square = jnp.sum(jnp.sum(gram * eye, axis=1, keepdims=True), axis=0, keepdims=True)
        scale = 1.0 / (jnp.sqrt(square) + NORM_EPS)
        scales.append(scale)
        currents.append(gram * (scale * scale))
    for step in range(NS_STEPS):
        factors = [NS_A * eye + NS_B * a + NS_C * mul(a, a) for a in currents]
        totals = factors if step == 0 else [mul(f, t) for f, t in zip(factors, totals)]
        if step + 1 < NS_STEPS:
            currents = [mul(f, a) for f, a in zip(factors, currents)]
            currents = [mul(a, f) for f, a in zip(factors, currents)]
    for n in blocks:
        out[n] = totals[n] * scales[n]


def polynomial(parts):
    vmem = pl.BlockSpec(memory_space=pltpu.VMEM)
    return pl.pallas_call(
        functools.partial(polynomial_kernel, len(parts)),
        out_shape=jax.ShapeDtypeStruct(parts[0].shape, F32),
        in_specs=[vmem] * len(parts),
        out_specs=vmem,
        compiler_params=pltpu.CompilerParams(vmem_limit_bytes=VMEM_LIMIT),
        name="polynomial",
    )(*parts)


def muon_apply_kernel(rates, spots_ref, *refs):
    count = len(rates)
    parts, momenta, masters = refs[:4], refs[4 : 4 + count], refs[4 + count : 4 + 2 * count]
    outs, factors = refs[4 + 2 * count : 4 + 3 * count], refs[4 + 3 * count]
    for n in range(4):
        factors[n] = parts[n][...]
    spots, _ = block_spots([momentum.shape[0] // ROW_BLOCK for momentum in momenta])
    for matrix, block, core, x, place_in in spots:
        rows = slice(block * ROW_BLOCK, (block + 1) * ROW_BLOCK)
        away = 2 * lax.rem(spots_ref[2] + core, 2) + lax.rem(spots_ref[1] + x, 2)
        direction = precise(factors[away, place_in], momenta[matrix][rows], ((1,), (0,)))
        outs[matrix][rows] = masters[matrix][rows] * (1.0 - WEIGHT_SHRINK) - rates[matrix] * direction


def muon_apply(spots, factors, momenta, masters, rates):
    vmem = pl.BlockSpec(memory_space=pltpu.VMEM)
    return pl.pallas_call(
        functools.partial(muon_apply_kernel, rates),
        out_shape=[jax.ShapeDtypeStruct(master.shape, F32) for master in masters],
        in_specs=[pl.BlockSpec(memory_space=pltpu.SMEM)] + [vmem] * (4 + 2 * len(masters)),
        out_specs=[vmem] * len(masters),
        scratch_shapes=[pltpu.VMEM((4,) + factors[0].shape, F32)],
        compiler_params=pltpu.CompilerParams(vmem_limit_bytes=VMEM_LIMIT),
        name="muon_apply",
    )(spots, *factors, *momenta, *masters)


def body(net, tokens, conditioning, heights, widths, upstream, *state):
    masters, momenta = state[0:5], state[5:10]
    biases, bias_first, bias_second = state[10:13]
    w_qkv, w_proj, w_fc1, w_fc2, w_ada = masters
    micro, local, rows, width = tokens.shape
    count = micro * local
    head_dim = width // HEADS
    hidden = w_fc1.shape[1] * net.dp
    seq, dp = net.seq, net.dp
    y = net.y.digit()

    bounds = [0, 6 * width, 7 * width, 8 * width, 9 * width, 9 * width + hidden, 10 * width + hidden]

    n_qkv, n_proj, n_fc1, n_fc2 = [w.shape[1] for w in (w_qkv, w_proj, w_fc1, w_fc2)]
    unit_qkv, unit_fc2 = math.gcd(n_qkv, 8), math.gcd(n_fc2, 8)
    unit_mid = math.gcd(math.gcd(n_proj, n_fc1), 8)
    fold = hidden // width
    layout_qkv, layout_mid, layout_fc2 = [(n_qkv, 1)], [(n_proj, 1), (n_fc1, 1)], [(n_fc2, fold)]
    own_tokens = tokens.reshape(count, rows, width)
    wires = net.y.gather(net.wire([w_qkv]))
    units_qkv = net.joined(wires, unit_qkv, width)
    token_pieces = [net.y.gather(tie(own_tokens[0], wires[-1]))]
    wires = net.y.gather(tie(net.wire([w_proj, w_fc1]), token_pieces[0][-1]))
    units_mid = net.joined(wires, unit_mid, width)
    for i in range(1, count):
        token_pieces.append(net.y.gather(tie(own_tokens[i], wires[-1])))
    wires = net.y.gather(tie(net.wire([w_fc2]), token_pieces[-1][-1]))
    units_fc2 = net.joined(wires, unit_fc2, width)

    ada_rows, ada_cols = w_ada.shape
    cond = conditioning.astype(F32).reshape(count, width)
    cond_act, silu_back = jax.vjp(sigmoid_linear, cond)
    cond_low = cond_act.astype(BF).astype(F32)
    cond_parts = jnp.transpose(cond_low.reshape(count, seq, ada_rows), (1, 0, 2)).reshape(seq, -1)
    parcel = jnp.concatenate([jnp.broadcast_to(biases, (seq,) + biases.shape), cond_parts], axis=1)
    parcel = net.to_all(jnp.broadcast_to(parcel[None], (dp,) + parcel.shape))
    bias_full = parcel[:, :, : biases.shape[0]].reshape(-1)
    cond_all = parcel[:, 0, biases.shape[0] :].reshape(dp * count, ada_rows).astype(BF)
    b_ada, b_q, b_v, b_proj, b_fc1, b_fc2 = [bias_full[bounds[i] : bounds[i + 1]] for i in range(6)]

    low_ada = w_ada.astype(BF)
    partial = jnp.dot(cond_all, low_ada, preferred_element_type=F32).reshape(dp, 1, count, ada_cols)
    received = jnp.sum(net.to_all(jnp.broadcast_to(partial, (dp, seq, count, ada_cols))), axis=1)
    modulation = jnp.transpose(received, (1, 0, 2)).reshape(count, dp * ada_cols) + b_ada
    shift_one, scale_one, gate_one, shift_two, scale_two, gate_two = jnp.split(
        modulation[:, None, :], 6, axis=-1
    )

    (t_qkv,), arrived = Staged(net.gather_steps(units_qkv, layout_qkv, 0.45)).finish()
    mid = Staged(net.gather_steps(tie(units_mid, *arrived), layout_mid, 0.4))
    late = None

    lengths = (heights * widths).reshape(count).astype(jnp.int32)
    offsets = jnp.stack([((y + s) % seq) * rows for s in range(seq)]).astype(jnp.int32)
    normed_all, inverse_all, attn_all, queries, keys, values, attended_low, log_total = [[] for _ in range(8)]
    sent = mid.advance()
    for i in range(count):
        normed, inverse = layer_norm(jnp.concatenate(token_pieces[i], axis=0).astype(F32))
        attn = (normed * (1.0 + scale_one[i]) + shift_one[i]).astype(BF)
        attn = tie(attn, *sent)
        queries.append((dot_t(attn[None, :rows], t_qkv[:width]) + b_q).astype(BF))
        keys.append(dot_t(attn[None], t_qkv[width : 2 * width]).astype(BF))
        values.append((dot_t(attn[None], t_qkv[2 * width :]) + b_v).astype(BF))
        if i == 0:
            sent = mid.advance(keys[i])
        elif late is None:
            late = Staged(net.gather_steps(tie(units_fc2, keys[i]), layout_fc2, 0.4))
            sent = late.advance()
        mixed, lse = attend(lengths[i : i + 1], offsets, queries[i], keys[i], values[i], HEADS, 512, sent)
        sent = mid.advance(mixed)
        normed_all.append(normed[:rows])
        inverse_all.append(inverse[:rows])
        attn_all.append(attn)
        attended_low.append(mixed[0])
        log_total.append(lse)
    if late is None:
        late = Staged(net.gather_steps(tie(units_fc2, keys[-1]), layout_fc2, 0.4))
        late.advance()
    attended_low = jnp.stack(attended_low)
    attn_all = jnp.stack(attn_all)
    attn_own = attn_all[:, :rows]
    t_proj, t_fc1 = mid.finish(log_total[-1])[0]
    sent = late.advance(attended_low)

    inputs = own_tokens.astype(F32)
    branch_one = dot_t(tie(attended_low, *sent), t_proj) + b_proj
    mixed_one = inputs + gate_one * branch_one
    normed_two, inverse_two = layer_norm(mixed_one)
    ffn_in = (normed_two * (1.0 + scale_two) + shift_two).astype(BF)
    sent = late.advance(ffn_in)
    ffn_in = tie(ffn_in, *sent)
    pre_act = dot_t(ffn_in, t_fc1) + b_fc1
    activated, gelu_back = jax.vjp(gelu_tanh, pre_act)
    activated_low = activated.astype(BF)
    sent = late.advance(activated_low)
    grad_out = upstream.reshape(count, rows, width).astype(F32)
    grad_branch_two = (gate_two * grad_out).astype(BF)
    activated_low = tie(activated_low, *sent)
    terms_fc2 = [
        outer(grad_branch_two, activated_low[..., j * width : (j + 1) * width]) for j in range(fold)
    ]
    back_fc2 = Staged(net.scatter_steps(terms_fc2, unit_fc2, width, layout_fc2, 0.4))
    sent = back_fc2.advance()
    (t_fc2,) = late.finish(terms_fc2[-1])[0]
    branch_two = dot_t(tie(activated_low, *sent), t_fc2) + b_fc2
    result = (mixed_one + gate_two * branch_two).astype(BF)

    grad_gate_two = jnp.sum(branch_two * grad_out, axis=1)
    sent = back_fc2.advance(branch_two)
    grad_branch_two = tie(grad_branch_two, *sent)
    bias_fc2 = jnp.sum(grad_branch_two.astype(F32), axis=(0, 1))
    grad_pre = gelu_back(dot(grad_branch_two, t_fc2))[0].astype(BF)
    sent = back_fc2.advance(grad_pre)
    grad_pre = tie(grad_pre, *sent)
    term_fc1 = outer(grad_pre, ffn_in)
    sent = back_fc2.advance(term_fc1)
    grad_pre = tie(grad_pre, *sent)
    bias_fc1 = jnp.sum(grad_pre.astype(F32), axis=(0, 1))
    grad_ffn_in = dot(grad_pre, t_fc1)
    grad_shift_two = jnp.sum(grad_ffn_in, axis=1)
    grad_scale_two = jnp.sum(grad_ffn_in * normed_two, axis=1)
    grad_mixed = grad_out + norm_back(normed_two, inverse_two, grad_ffn_in * (1.0 + scale_two))
    grad_gate_one = jnp.sum(branch_one * grad_mixed, axis=1)
    grad_branch_one = (gate_one * grad_mixed).astype(BF)
    term_proj = outer(grad_branch_one, attended_low)
    back_mid = Staged(net.scatter_steps([term_proj, term_fc1], unit_mid, width, layout_mid, 0.4))
    sent = back_mid.advance() + back_fc2.advance(term_proj)
    grad_branch_one = tie(grad_branch_one, *sent)
    bias_proj = jnp.sum(grad_branch_one.astype(F32), axis=(0, 1))
    grad_attended = dot(grad_branch_one, t_proj).astype(BF)

    grad_q, grad_k, grad_v, far_parts = [], [], [], []
    sent = back_mid.advance(grad_attended)
    for i in range(count):
        dq, dk, dv = attend_back(
            lengths[i : i + 1], offsets, queries[i], keys[i], values[i], attended_low[i : i + 1],
            grad_attended[i : i + 1], log_total[i], HEADS, 512, sent,
        )
        sent = back_mid.advance(dq) + back_fc2.advance(dq)
        grad_q.append(dq)
        grad_k.append(dk)
        grad_v.append(dv)
        far_part = (
            dot(dk[:, rows:], t_qkv[width : 2 * width]) + dot(dv[:, rows:], t_qkv[2 * width :])
        ).astype(BF)[0]
        far_steps = Staged(
            net.y.scatter_steps(
                lambda s, p=far_part: (
                    jnp.zeros((rows, width), BF) if s == 0 else p[(s - 1) * rows : s * rows]
                )
            )
        )
        sent = sent + far_steps.advance()
        far_parts.append(far_steps)
    grad_q, grad_k, grad_v = [jnp.concatenate(each, axis=0) for each in (grad_q, grad_k, grad_v)]
    grad_q = tie(grad_q, *sent)
    term_qkv = jnp.concatenate(
        [outer(grad_q, attn_own), outer(grad_k, attn_all), outer(grad_v, attn_all)], axis=0
    )
    back_qkv = Staged(net.scatter_steps([term_qkv], unit_qkv, width, layout_qkv, 0.45))
    sent = back_qkv.advance() + back_mid.advance(term_qkv)
    grad_q = tie(grad_q, *sent)
    bias_q = jnp.sum(grad_q.astype(F32), axis=(0, 1))
    bias_v = jnp.sum(grad_v.astype(F32), axis=(0, 1))
    own_part = (
        dot(grad_q, t_qkv[:width])
        + dot(grad_k[:, :rows], t_qkv[width : 2 * width])
        + dot(grad_v[:, :rows], t_qkv[2 * width :])
    )
    sent = back_qkv.advance(own_part) + back_mid.advance(own_part)
    far_sum = jnp.stack([steps.finish() for steps in far_parts])
    grad_attn_in = tie(own_part, *sent) + far_sum
    normed_one, inverse_one = jnp.stack(normed_all), jnp.stack(inverse_all)
    grad_shift_one = jnp.sum(grad_attn_in, axis=1)
    grad_scale_one = jnp.sum(grad_attn_in * normed_one, axis=1)
    grad_inputs = grad_mixed + norm_back(normed_one, inverse_one, grad_attn_in * (1.0 + scale_one))
    grad_inputs = grad_inputs.astype(BF).reshape(tokens.shape)

    grad_mod_local = jnp.concatenate(
        [grad_shift_one, grad_scale_one, grad_gate_one, grad_shift_two, grad_scale_two, grad_gate_two], axis=-1
    )
    bias_ada = jnp.sum(grad_mod_local, axis=0)
    sent = jnp.transpose(grad_mod_local.reshape(count, dp, 1, ada_cols), (1, 2, 0, 3))
    sent = jnp.broadcast_to(sent, (dp, seq, count, ada_cols))
    mod_cols = jnp.sum(net.to_all(sent), axis=1).astype(BF).reshape(dp * count, ada_cols)
    shard_ada = jnp.einsum("sr,sc->rc", cond_all, mod_cols, preferred_element_type=F32)

    rate_of = {
        "qkv": math.sqrt(3.0), "proj": 1.0, "fc1": math.sqrt(hidden / width),
        "fc2": math.sqrt(width / hidden), "ada": math.sqrt(6.0),
    }
    sum_mid, sum_fc2 = back_mid.finish(), back_fc2.finish()
    early = Staged(
        net.muon_steps(
            [(sum_mid, True, [momenta[1], momenta[2]]), (sum_fc2, True, [momenta[3]])],
            [w_proj, w_fc1, w_fc2],
            [rate_of["proj"], rate_of["fc1"], rate_of["fc2"]],
        )
    )
    (next_proj, next_fc1, next_fc2), (new_proj, new_fc1, new_fc2) = early.finish()
    sum_qkv = back_qkv.finish()
    last = Staged(
        net.muon_steps(
            [(sum_qkv, True, [momenta[0]]), (shard_ada, False, [momenta[4]])],
            [w_qkv, w_ada],
            [rate_of["qkv"], rate_of["ada"]],
        )
    )
    (next_qkv, next_ada), (new_qkv, new_ada) = last.finish()

    cond_part = jnp.einsum("sc,rc->sr", mod_cols, low_ada, preferred_element_type=F32)
    cond_part = cond_part.reshape(dp, 1, count, ada_rows)
    cond_part = jnp.sum(net.to_all(jnp.broadcast_to(cond_part, (dp, seq, count, ada_rows))), axis=0)
    grad_cond = silu_back(jnp.transpose(cond_part, (1, 0, 2)).reshape(count, width))[0]

    term_bias = jnp.concatenate([bias_ada, bias_q, bias_v, bias_proj, bias_fc1, bias_fc2])
    grad_bias = jnp.sum(net.to_all(term_bias.reshape(dp, seq, -1)), axis=(0, 1))
    next_first = BETA_FIRST * bias_first + (1.0 - BETA_FIRST) * grad_bias
    next_second = BETA_SECOND * bias_second + (1.0 - BETA_SECOND) * grad_bias * grad_bias
    first_hat = next_first / (1.0 - BETA_FIRST**STEP_COUNT)
    second_hat = next_second / (1.0 - BETA_SECOND**STEP_COUNT)
    new_biases = biases * (1.0 - ADAM_RATE * ADAM_DECAY) - ADAM_RATE * first_hat / (
        jnp.sqrt(second_hat) + ADAM_EPS
    )
    return (
        result.reshape(tokens.shape),
        grad_inputs,
        grad_cond.reshape(conditioning.shape),
        new_qkv, new_proj, new_fc1, new_fc2, new_ada,
        next_qkv, next_proj, next_fc1, next_fc2, next_ada,
        new_biases,
        next_first,
        next_second,
    )


def solution(mesh):
    rows = P(None, "dp", "seq", None)
    matrix = P("seq", "dp")
    flat = P(("dp", "seq"))
    in_specs = (rows, P(None, "dp", None), P(None, "dp"), P(None, "dp"), rows) + (matrix,) * 10 + (flat,) * 3
    out_specs = (rows, rows, P(None, "dp", None)) + (matrix,) * 10 + (flat,) * 3
    return jax.shard_map(
        functools.partial(body, Net(mesh)), mesh=mesh, in_specs=in_specs, out_specs=out_specs, check_vma=False
    )
```

```python
import functools
import math

import jax
import jax.numpy as jnp
from jax import lax
from jax.experimental import pallas as pl
from jax.experimental.pallas import tpu as pltpu
from jax.sharding import PartitionSpec as P

HEADS = 16
ROW_BLOCK = 144
NS_STEPS = 5
STEP_COUNT = 10

PRECISE = lax.Precision.HIGHEST
LN_EPS = 1e-06
MASKED = -1e30
NS_A = 3.4445
NS_B = -4.775
NS_C = 2.0315
MUON_DECAY = 0.5
WEIGHT_SHRINK = 0.0001
NORM_EPS = 1e-07
BETA_FIRST = 0.9
BETA_SECOND = 0.999
ADAM_RATE = 0.1
ADAM_DECAY = 0.01
ADAM_EPS = 1e-08
BF = jnp.bfloat16
F32 = jnp.float32
VMEM_LIMIT = 60 * 2**20


class Ring:
    def __init__(self, name, total, stride, size):
        self.name, self.total, self.stride, self.size = name, total, stride, size

    def digit(self):
        return (lax.axis_index(self.name) // self.stride) % self.size

    def send(self, value, shift):
        pairs = []
        for i in range(self.total):
            d = (i // self.stride) % self.size
            pairs.append((i, i + ((d + shift) % self.size - d) * self.stride))
        return lax.ppermute(value, self.name, pairs)

    def gather(self, value, far=1):
        n = self.size
        blocks = [value] + [None] * (n - 1)
        if n == 2:
            blocks[1] = self.send(value, 1)
        elif n > 2:
            low = high = value
            for t in range(1, n // 2):
                low, high = self.send(low, 1), self.send(high, -1)
                blocks[n - t], blocks[t] = low, high
            blocks[n // 2] = self.send(low, 1) if far == 1 else self.send(high, -1)
        return blocks

    def gather_steps(self, value, far=1):
        n = self.size
        blocks = [value] + [None] * (n - 1)
        if n == 2:
            blocks[1] = self.send(value, 1)
            anchor = yield [value]
            blocks[1] = tie(blocks[1], anchor)
            return blocks
        low = high = value
        for t in range(1, n // 2):
            sent = [low, high]
            low, high = self.send(low, 1), self.send(high, -1)
            anchor = yield sent
            low, high = tie(low, anchor), tie(high, anchor)
            blocks[n - t], blocks[t] = low, high
        sent = [low if far == 1 else high]
        last = self.send(sent[0], far)
        anchor = yield sent
        blocks[n // 2] = tie(last, anchor)
        return blocks

    def scatter_steps(self, block_of, far=1):
        n = self.size
        if n == 1:
            return block_of(0).astype(F32)
        if n == 2:
            sent = block_of(1)
            got = self.send(sent, 1)
            anchor = yield [sent]
            return block_of(0).astype(F32) + tie(got, anchor).astype(F32)
        sent = block_of(n // 2)
        got = self.send(sent, far)
        anchor = yield [sent]
        low, high = (tie(got, anchor), None) if far == 1 else (None, tie(got, anchor))
        for t in range(n // 2 - 1, 0, -1):
            up, down = block_of(t), block_of(n - t)
            if low is not None:
                up = (up.astype(F32) + low.astype(F32)).astype(up.dtype)
            if high is not None:
                down = (down.astype(F32) + high.astype(F32)).astype(down.dtype)
            low, high = self.send(up, 1), self.send(down, -1)
            anchor = yield [up, down]
            low, high = tie(low, anchor), tie(high, anchor)
        return block_of(0).astype(F32) + low.astype(F32) + high.astype(F32)


def tie(value, *earlier):
    earlier = [array for array in earlier if array is not None]
    if not earlier:
        return value
    anywhere = pl.BlockSpec(memory_space=pl.ANY)
    return pl.pallas_call(
        lambda *refs: None,
        out_shape=jax.ShapeDtypeStruct(value.shape, value.dtype),
        in_specs=[anywhere] * (1 + len(earlier)),
        out_specs=anywhere,
        input_output_aliases={0: 0},
        name="tie",
    )(value, *earlier)


def lockstep(*steps):
    results = [None] * len(steps)
    alive = dict(enumerate(steps))
    anchor = None
    while alive:
        sent = []
        for n, step in list(alive.items()):
            try:
                sent += step.send(anchor)
            except StopIteration as stop:
                results[n] = stop.value
                del alive[n]
        if alive:
            anchor = yield sent
    return results


class Staged:
    def __init__(self, steps):
        self.steps, self.result, self.started, self.done = steps, None, False, False

    def advance(self, anchor=None):
        if self.done:
            return []
        try:
            sent = self.steps.send(anchor if self.started else None)
            self.started = True
            return sent
        except StopIteration as stop:
            self.result, self.done = stop.value, True
            return []

    def finish(self, anchor=None):
        while not self.done:
            self.advance(anchor)
        return self.result


def place_kernel(zs, ga, parts, count, outs, *refs):
    spots, sources = refs[0], refs[1 : 1 + count]
    outputs, (full, in_sems, out_sems) = refs[1 + count : 1 + count + outs], refs[1 + count + outs :]
    g = full.shape[3]
    half = count // 2
    shards = []
    for sc in range(2):
        for sx in range(2):
            for sz in range(zs):
                where = (lax.rem(spots[0] + sz, zs), lax.rem(spots[1] + sx, 2), lax.rem(spots[2] + sc, 2))
                n = 2 * len(shards)
                line, pair = sources[sc * half + sx].at[sz], sources[sc * half + 2 + sz].at[sx]
                copies = [
                    pltpu.make_async_copy(line, full.at[(*where, pl.ds(0, ga))], in_sems.at[n]),
                    pltpu.make_async_copy(pair, full.at[(*where, pl.ds(ga, g - ga))], in_sems.at[n + 1]),
                ]
                for copy in copies:
                    copy.start()
                shards.append((where, copies))
    exits = []
    for where, copies in shards:
        for copy in copies:
            copy.wait()
        for output, start, size, column, depth in parts:
            target = outputs[output].at[(*where, slice(None), slice(None), pl.ds(column, depth))]
            copy = pltpu.make_async_copy(
                full.at[(*where, pl.ds(start, size))], target, out_sems.at[len(exits)]
            )
            copy.start()
            exits.append(copy)
    for copy in exits:
        copy.wait()


def place(spots, sources, shape, ga, parts, shapes):
    zs = shape[0]
    moved = math.prod(shape) * 2
    return pl.pallas_call(
        functools.partial(place_kernel, zs, ga, parts, len(sources), len(shapes)),
        out_shape=[jax.ShapeDtypeStruct(each, BF) for each in shapes],
        in_specs=[pl.BlockSpec(memory_space=pltpu.SMEM)]
        + [pl.BlockSpec(memory_space=pl.ANY)] * len(sources),
        out_specs=[pl.BlockSpec(memory_space=pl.ANY)] * len(shapes),
        scratch_shapes=[
            pltpu.VMEM(shape, BF),
            pltpu.SemaphoreType.DMA((8 * zs,)),
            pltpu.SemaphoreType.DMA((4 * zs * len(parts),)),
        ],
        compiler_params=pltpu.CompilerParams(vmem_limit_bytes=VMEM_LIMIT),
        cost_estimate=pl.CostEstimate(flops=0, bytes_accessed=2 * moved, transcendentals=0),
        name="place",
    )(spots, *sources)


class Net:
    def __init__(self, mesh):
        dp, seq = mesh.shape["dp"], mesh.shape["seq"]
        self.dp, self.seq = dp, seq
        self.core = Ring("dp", dp, 1, 2)
        self.x = Ring("dp", dp, 2, 2)
        self.z = Ring("dp", dp, 4, dp // 4)
        self.y = Ring("seq", seq, 1, seq)

    def spots(self):
        return jnp.stack([self.z.digit(), self.x.digit(), self.core.digit()]).astype(jnp.int32)


    def wire(self, shards):
        turned = [shard.astype(BF).T for shard in shards]
        return turned[0] if len(turned) == 1 else jnp.concatenate(turned, axis=0)

    def rows(self, wires):
        if self.seq == 2:
            own, other = wires
            return jnp.where(
                self.y.digit() == 0,
                jnp.concatenate([own, other], axis=1),
                jnp.concatenate([other, own], axis=1),
            )
        order = (jnp.arange(self.seq) - self.y.digit()) % self.seq
        full = jnp.take(jnp.stack(wires), order, axis=0)
        return jnp.transpose(full, (1, 0, 2)).reshape(full.shape[1], -1)

    def joined(self, wires, unit, depth):
        full = self.rows(wires)
        return full.reshape(full.shape[0] // unit, unit, depth)

    def scatter(self, term):
        return lax.psum_scatter(term, "dp", scatter_dimension=0, tiled=True)

    def halves_steps(self, term):
        y = self.y.digit()
        blocks = term.reshape(term.shape[0], self.seq, -1)
        return (
            yield from self.y.scatter_steps(
                lambda s: lax.dynamic_index_in_dim(blocks, (y + s) % self.seq, 1, keepdims=False)
            )
        )

    def gather_steps(self, units, layout, part):
        g, unit, depth = units.shape
        zs = self.z.size
        ga = max(1, int(part * g))
        first, second = units[:ga], units[ga:]

        def line_steps():
            blocks = yield from self.z.gather_steps(first, 1)
            line = jnp.stack(blocks)
            return (yield from self.x.gather_steps(line))

        def pair_steps():
            blocks = yield from self.x.gather_steps(second)
            return (yield from self.z.gather_steps(jnp.stack(blocks), -1))

        lines, pairs = yield from lockstep(line_steps(), pair_steps())
        pieces = lines + pairs
        others = [self.core.send(piece, 1) for piece in pieces]
        anchor = yield pieces
        sources = pieces + [tie(other, anchor) for other in others]
        parts, shapes, start = [], [], 0
        for n, (rows, blocks) in enumerate(layout):
            size = rows // unit
            shapes.append((zs, 2, 2, size, unit, blocks * depth))
            for j in range(blocks):
                parts.append((n, start, size, j * depth, depth))
                start += size
        full = place(self.spots(), sources, (zs, 2, 2, g, unit, depth), ga, parts, shapes)
        return [f.reshape(-1, f.shape[-1]) for f in full], lines[1:] + pairs[1:]


    def muon_steps(self, groups, masters, rates):
        momenta, own, other = muon_gram(self.spots(), self.z.size, groups)
        got = self.core.send(other, 1)
        anchor = yield [other]
        half = own + tie(got, anchor)
        sent = half[1]
        got = self.x.send(sent, 1)
        anchor = yield [sent]
        kept = half[0] + tie(got, anchor)
        blocks = [kept[shift] for shift in range(self.z.size)]
        got = [self.z.send(blocks[shift], shift) for shift in range(1, self.z.size)]
        anchor = yield blocks[1:]
        factor = polynomial([blocks[0]] + [tie(each, anchor) for each in got])
        got = [self.z.send(factor, -shift) for shift in range(1, self.z.size)]
        anchor = yield [factor]
        line = jnp.stack([factor] + [tie(each, anchor) for each in got])
        got = self.x.send(line, 1)
        anchor = yield [line]
        pair = [line, tie(got, anchor)]
        others = [self.core.send(each, 1) for each in pair]
        anchor = yield pair
        factors = pair + [tie(each, anchor) for each in others]
        return momenta, muon_apply(self.spots(), factors, momenta, masters, rates)


    def to_all(self, value):
        flat = value.reshape((self.dp * self.seq,) + value.shape[2:])
        return lax.all_to_all(flat, ("dp", "seq"), 0, 0, tiled=True).reshape(value.shape)

    def to_dp(self, value):
        return lax.all_to_all(value, "dp", 0, 0, tiled=True)


def layer_norm(values):
    centered = values - jnp.mean(values, axis=-1, keepdims=True)
    inverse = lax.rsqrt(jnp.mean(centered * centered, axis=-1, keepdims=True) + LN_EPS)
    return (centered * inverse, inverse)


def norm_back(normed, inverse, grad):
    mean_grad = jnp.mean(grad, axis=-1, keepdims=True)
    mean_cross = jnp.mean(grad * normed, axis=-1, keepdims=True)
    return inverse * (grad - mean_grad - normed * mean_cross)


def sigmoid_linear(values):
    return values * jax.nn.sigmoid(values)


def gelu_tanh(values):
    return jax.nn.gelu(values, approximate=True)


def dot_t(left, right):
    return jnp.einsum("srk,nk->srn", left, right, preferred_element_type=F32)


def dot(left, right):
    return jnp.einsum("srn,nk->srk", left, right, preferred_element_type=F32)


def outer(left, right):
    return jnp.einsum("srn,srk->nk", left, right, preferred_element_type=F32).astype(BF)


def joined_outer_kernel(loads, parts, counts, tile, *refs):
    inputs, out = refs[: counts[0]], refs[counts[1]]
    buffers = refs[counts[1] + 1 : counts[1] + 1 + len(loads)]
    acc, in_sems, out_sems = refs[counts[1] + 1 + len(loads) :]
    arrivals = []
    for n, (sources, start, size) in enumerate(loads):
        row, copies = 0, []
        for m, source in enumerate(sources):
            rows = inputs[source].shape[0]
            window = inputs[source].at[:, pl.ds(start, size)]
            copies.append(pltpu.make_async_copy(window, buffers[n].at[pl.ds(row, rows)], in_sems.at[n, m]))
            row += rows
        arrivals.append(copies)
    order = [n for part in parts for n in part]
    for n in sorted(range(len(loads)), key=order.index):
        for copy in arrivals[n]:
            copy.start()
    ready, exits = set(), []
    for n, (left, right) in enumerate(parts):
        for m in (left, right):
            if m not in ready:
                for copy in arrivals[m]:
                    copy.wait()
                ready.add(m)
        width = buffers[left].shape[1]
        step = tile if width % tile == 0 else width

        @pl.loop(0, width // step)
        def _(t):
            spot = pl.multiple_of(t * step, step)
            product = lax.dot_general(
                buffers[left][:, pl.ds(spot, step)],
                buffers[right][...],
                (((0,), (0,)), ((), ())),
                preferred_element_type=F32,
            )
            acc[n, pl.ds(spot, step)] = product.astype(BF)

        exits.append(pltpu.make_async_copy(acc.at[n], out.at[pl.ds(n * width, width)], out_sems.at[n]))
        exits[-1].start()
    for copy in exits:
        copy.wait()


def joined_outer(inputs, loads, parts, deps=(), tile=384):
    heights = [sum(inputs[source].shape[0] for source in sources) for sources, _, _ in loads]
    width, depth = loads[parts[0][0]][2], loads[parts[0][1]][2]
    anywhere = pl.BlockSpec(memory_space=pl.ANY)
    return pl.pallas_call(
        functools.partial(joined_outer_kernel, loads, parts, (len(inputs), len(inputs) + len(deps)), tile),
        out_shape=jax.ShapeDtypeStruct((len(parts) * width, depth), BF),
        in_specs=[anywhere] * (len(inputs) + len(deps)),
        out_specs=anywhere,
        scratch_shapes=[pltpu.VMEM((height, load[2]), BF) for height, load in zip(heights, loads)]
        + [
            pltpu.VMEM((len(parts), width, depth), BF),
            pltpu.SemaphoreType.DMA((len(loads), max(len(load[0]) for load in loads))),
            pltpu.SemaphoreType.DMA((len(parts),)),
        ],
        compiler_params=pltpu.CompilerParams(vmem_limit_bytes=VMEM_LIMIT),
        cost_estimate=pl.CostEstimate(
            flops=sum(2 * heights[left] * width * depth for left, _ in parts),
            bytes_accessed=2 * sum(heights) * width + 2 * len(parts) * width * depth,
            transcendentals=0,
        ),
        name="joined_outer",
    )(*inputs, *deps)


LANES = 128
LOG2E = math.log2(math.e)


def padded(block, column=None):
    rows, depth = block.shape
    if column is None:
        return jnp.concatenate([block, jnp.zeros((rows, LANES - depth), block.dtype)], axis=1)
    rest = jnp.zeros((rows, LANES - depth - 1), block.dtype)
    return jnp.concatenate([block, column.astype(block.dtype), rest], axis=1)


def mask_column(lengths_ref, offsets_ref, sample, total, rows):
    place = lax.broadcasted_iota(jnp.int32, (total, 1), 0)
    position = place
    for s in range(total // rows):
        position = jnp.where(place // rows == s, place - s * rows + offsets_ref[s], position)
    return jnp.where(position < lengths_ref[sample], 0.0, MASKED)


def nt(left, right):
    return lax.dot_general(left, right, (((1,), (1,)), ((), ())), preferred_element_type=F32)


def nn(left, right):
    return jnp.dot(left, right, preferred_element_type=F32)


def without(kernel, start, count, *fixed):
    def run(*refs):
        kernel(*fixed, *refs[:start], *refs[start + count :])

    return run


def attend_kernel(heads, chunk, lengths_ref, offsets_ref, q_ref, k_ref, v_ref, o_ref, lse_ref, q_s, k_s, vt_s, o_s):
    rows, width = q_ref.shape[1:]
    total = k_ref.shape[1]
    depth = width // heads
    factor = depth**-0.5 * LOG2E
    mask = mask_column(lengths_ref, offsets_ref, pl.program_id(0), total, rows)
    ones = jnp.ones((rows, 1), F32)
    for h in range(heads):
        span = slice(h * depth, (h + 1) * depth)
        q_s[h] = padded(q_ref[0, :, span], ones)
        k_s[h] = padded(k_ref[0, :, span], mask)
        vt_s[h] = jnp.transpose(v_ref[0, :, span])

    def one_head(h, carry):
        peak = jnp.full((1, rows), MASKED, F32)
        sums = jnp.zeros((1, rows), F32)
        mixed = jnp.zeros((depth, rows), F32)
        for c in range(total // chunk):
            part = slice(c * chunk, (c + 1) * chunk)
            scores = nt(k_s[h, part], q_s[h])
            higher = jnp.maximum(peak, jnp.max(scores, axis=0, keepdims=True))
            weights = jnp.exp2((scores - higher) * factor)
            if c == 0:
                sums = jnp.sum(weights, axis=0, keepdims=True)
                mixed = nn(vt_s[h, :, part], weights.astype(BF))
            else:
                shrink = jnp.exp2((peak - higher) * factor)
                sums = sums * shrink + jnp.sum(weights, axis=0, keepdims=True)
                mixed = mixed * shrink + nn(vt_s[h, :, part], weights.astype(BF))
            peak = higher
        o_s[h] = jnp.transpose(mixed / sums)
        lse_ref[0, h] = peak * factor + jnp.log2(sums)
        return carry

    lax.fori_loop(0, heads, one_head, 0)
    for h in range(heads):
        o_ref[0, :, h * depth : (h + 1) * depth] = o_s[h].astype(BF)


def attend(lengths, offsets, queries, keys, values, heads, tile, deps=()):
    count, rows, width = queries.shape
    total = keys.shape[1]
    depth = width // heads
    tile = min(tile, total)
    pick = lambda i, *_: (i, 0, 0)
    return pl.pallas_call(
        without(attend_kernel, 5, len(deps), heads, tile),
        grid_spec=pltpu.PrefetchScalarGridSpec(
            num_scalar_prefetch=2,
            grid=(count,),
            in_specs=[
                pl.BlockSpec((1, rows, width), pick),
                pl.BlockSpec((1, total, width), pick),
                pl.BlockSpec((1, total, width), pick),
            ]
            + [pl.BlockSpec(memory_space=pl.ANY)] * len(deps),
            out_specs=[
                pl.BlockSpec((1, rows, width), pick),
                pl.BlockSpec((1, heads, 1, rows), lambda i, *_: (i, 0, 0, 0)),
            ],
            scratch_shapes=[
                pltpu.VMEM((heads, rows, LANES), BF),
                pltpu.VMEM((heads, total, LANES), BF),
                pltpu.VMEM((heads, depth, total), BF),
                pltpu.VMEM((heads, rows, depth), F32),
            ],
        ),
        out_shape=[
            jax.ShapeDtypeStruct((count, rows, width), BF),
            jax.ShapeDtypeStruct((count, heads, 1, rows), F32),
        ],
        compiler_params=pltpu.CompilerParams(vmem_limit_bytes=VMEM_LIMIT),
        cost_estimate=pl.CostEstimate(
            flops=4 * count * heads * rows * total * LANES,
            bytes_accessed=2 * count * width * (2 * rows + 2 * total),
            transcendentals=count * heads * rows * total,
        ),
        name="attend",
    )(lengths, offsets, queries, keys, values, *deps)


def attend_back_kernel(
    heads, chunk, lengths_ref, offsets_ref, q_ref, k_ref, v_ref, o_ref, g_ref, lse_ref,
    dq_ref, dk_ref, dv_ref, q_s, k_s, kt_s, v_s, g_s, delta_s, dq_s, dk_s, dv_s
):
    rows, width = q_ref.shape[1:]
    total = k_ref.shape[1]
    depth = width // heads
    scale = depth**-0.5
    factor = scale * LOG2E
    mask = mask_column(lengths_ref, offsets_ref, pl.program_id(0), total, rows)
    ones = jnp.ones((rows, 1), F32)
    cross = jnp.transpose(g_ref[0].astype(F32) * o_ref[0].astype(F32))
    for h in range(heads):
        span = slice(h * depth, (h + 1) * depth)
        delta_s[h] = jnp.sum(cross[span], axis=0, keepdims=True)
        q_s[h] = padded(q_ref[0, :, span], ones)
        k_s[h] = padded(k_ref[0, :, span], mask)
        kt_s[h] = jnp.transpose(k_ref[0, :, span])
        g_s[h] = padded(g_ref[0, :, span])
        v_s[h] = padded(v_ref[0, :, span])

    def one_head(h, carry):
        dq = jnp.zeros((depth, rows), F32)
        for c in range(total // chunk):
            part = slice(c * chunk, (c + 1) * chunk)
            probs = jnp.exp2(nt(k_s[h, part], q_s[h]) * factor - lse_ref[0, h])
            slopes = (probs * (nt(v_s[h, part], g_s[h]) - delta_s[h])).astype(BF)
            dv_s[h, part] = nn(probs.astype(BF), g_s[h]).astype(BF)
            dk_s[h, part] = (nn(slopes, q_s[h]) * scale).astype(BF)
            dq = dq + nn(kt_s[h, :, part], slopes)
        dq_s[h] = jnp.transpose(dq * scale)
        return carry

    lax.fori_loop(0, heads, one_head, 0)
    for h in range(heads):
        span = slice(h * depth, (h + 1) * depth)
        dq_ref[0, :, span] = dq_s[h].astype(BF)
        dk_ref[0, :, span] = dk_s[h][:, :depth]
        dv_ref[0, :, span] = dv_s[h][:, :depth]


def attend_back(lengths, offsets, queries, keys, values, mixed, grads, lse, heads, tile, deps=()):
    count, rows, width = queries.shape
    total = keys.shape[1]
    depth = width // heads
    tile = min(tile, total)
    pick = lambda i, *_: (i, 0, 0)
    near = pl.BlockSpec((1, rows, width), pick)
    far = pl.BlockSpec((1, total, width), pick)
    return pl.pallas_call(
        without(attend_back_kernel, 8, len(deps), heads, tile),
        grid_spec=pltpu.PrefetchScalarGridSpec(
            num_scalar_prefetch=2,
            grid=(count,),
            in_specs=[near, far, far, near, near, pl.BlockSpec((1, heads, 1, rows), lambda i, *_: (i, 0, 0, 0))]
            + [pl.BlockSpec(memory_space=pl.ANY)] * len(deps),
            out_specs=[near, far, far],
            scratch_shapes=[
                pltpu.VMEM((heads, rows, LANES), BF),
                pltpu.VMEM((heads, total, LANES), BF),
                pltpu.VMEM((heads, depth, total), BF),
                pltpu.VMEM((heads, total, LANES), BF),
                pltpu.VMEM((heads, rows, LANES), BF),
                pltpu.VMEM((heads, 1, rows), F32),
                pltpu.VMEM((heads, rows, depth), F32),
                pltpu.VMEM((heads, total, LANES), BF),
                pltpu.VMEM((heads, total, LANES), BF),
            ],
        ),
        out_shape=[
            jax.ShapeDtypeStruct((count, rows, width), BF),
            jax.ShapeDtypeStruct((count, total, width), BF),
            jax.ShapeDtypeStruct((count, total, width), BF),
        ],
        compiler_params=pltpu.CompilerParams(vmem_limit_bytes=VMEM_LIMIT),
        cost_estimate=pl.CostEstimate(
            flops=10 * count * heads * rows * total * LANES,
            bytes_accessed=2 * count * width * (4 * rows + 4 * total),
            transcendentals=count * heads * rows * total,
        ),
        name="attend_back",
    )(lengths, offsets, queries, keys, values, mixed, grads, lse, *deps)


def block_spots(counts, zs):
    per = -(-sum(counts) // (4 * zs))
    spots = []
    for matrix, count in enumerate(counts):
        for block in range(count):
            device, place_in = divmod(len(spots), per)
            spots.append((matrix, block, device // 4, device // 2 % 2, device % 2, place_in))
    return spots, per


def precise(left, right, dims):
    return lax.dot_general(left, right, (dims, ((), ())), precision=PRECISE, preferred_element_type=F32)


def muon_gram_kernel(groups, spots_ref, *refs):
    count = sum(groups)
    sums, momenta = refs[: len(groups)], refs[len(groups) : len(groups) + count]
    outs = refs[len(groups) + count : len(groups) + 2 * count]
    own_ref, other_ref = refs[len(groups) + 2 * count :]
    n = 0
    for matrices, sum_ref in zip(groups, sums):
        start = 0
        for _ in range(matrices):
            size = momenta[n].shape[0]
            outs[n][...] = MUON_DECAY * momenta[n][...] + sum_ref[start : start + size]
            start += size
            n += 1
    zs = own_ref.shape[1]
    spots, per = block_spots([out.shape[1] // ROW_BLOCK for out in outs], zs)
    if len(spots) < 4 * zs * per:
        own_ref[...] = jnp.zeros_like(own_ref)
        other_ref[...] = jnp.zeros_like(other_ref)
    for matrix, block, z, x, core, place_in in spots:
        turned = outs[matrix][:, block * ROW_BLOCK : (block + 1) * ROW_BLOCK]
        gram = precise(turned, turned, ((0,), (0,)))
        away = (lax.rem(spots_ref[1] + x, 2), lax.rem(zs + z - spots_ref[0], zs), place_in)

        @pl.when(spots_ref[2] == core)
        def _():
            own_ref[away] = gram

        @pl.when(spots_ref[2] != core)
        def _():
            other_ref[away] = gram


def muon_gram(spots, zs, groups):
    momenta = [momentum for _, each in groups for momentum in each]
    _, per = block_spots([momentum.shape[1] // ROW_BLOCK for momentum in momenta], zs)
    grams = jax.ShapeDtypeStruct((2, zs, per, ROW_BLOCK, ROW_BLOCK), F32)
    vmem = pl.BlockSpec(memory_space=pltpu.VMEM)
    outs = pl.pallas_call(
        functools.partial(muon_gram_kernel, [len(each) for _, each in groups]),
        out_shape=[jax.ShapeDtypeStruct(momentum.shape, F32) for momentum in momenta] + [grams, grams],
        in_specs=[pl.BlockSpec(memory_space=pltpu.SMEM)] + [vmem] * (len(groups) + len(momenta)),
        out_specs=[vmem] * (len(momenta) + 2),
        compiler_params=pltpu.CompilerParams(vmem_limit_bytes=VMEM_LIMIT),
        name="muon_gram",
    )(spots, *[group[0] for group in groups], *momenta)
    return outs[:-2], outs[-2], outs[-1]


def polynomial_kernel(count, *refs):
    out = refs[count]
    shape = (ROW_BLOCK, ROW_BLOCK)
    eye = (lax.broadcasted_iota(jnp.int32, shape, 0) == lax.broadcasted_iota(jnp.int32, shape, 1)).astype(F32)
    mul = lambda left, right: precise(left, right, ((1,), (0,)))
    blocks = range(out.shape[0])
    currents, scales, totals = [], [], []
    for n in blocks:
        gram = refs[0][n]
        for ref in refs[1:count]:
            gram = gram + ref[n]
        square = jnp.sum(jnp.sum(gram * eye, axis=1, keepdims=True), axis=0, keepdims=True)
        scale = 1.0 / (jnp.sqrt(square) + NORM_EPS)
        scales.append(scale)
        currents.append(gram * (scale * scale))
    for step in range(NS_STEPS):
        factors = [NS_A * eye + NS_B * a + NS_C * mul(a, a) for a in currents]
        totals = factors if step == 0 else [mul(f, t) for f, t in zip(factors, totals)]
        if step + 1 < NS_STEPS:
            currents = [mul(f, a) for f, a in zip(factors, currents)]
            currents = [mul(a, f) for f, a in zip(factors, currents)]
    for n in blocks:
        out[n] = totals[n] * scales[n]


def polynomial(parts):
    vmem = pl.BlockSpec(memory_space=pltpu.VMEM)
    return pl.pallas_call(
        functools.partial(polynomial_kernel, len(parts)),
        out_shape=jax.ShapeDtypeStruct(parts[0].shape, F32),
        in_specs=[vmem] * len(parts),
        out_specs=vmem,
        compiler_params=pltpu.CompilerParams(vmem_limit_bytes=VMEM_LIMIT),
        name="polynomial",
    )(*parts)


def muon_apply_kernel(rates, spots_ref, *refs):
    count = len(rates)
    parts, momenta, masters = refs[:4], refs[4 : 4 + count], refs[4 + count : 4 + 2 * count]
    outs, factors = refs[4 + 2 * count : 4 + 3 * count], refs[4 + 3 * count]
    for n in range(4):
        factors[n] = parts[n][...]
    zs = factors.shape[1]
    spots, _ = block_spots([momentum.shape[1] // ROW_BLOCK for momentum in momenta], zs)
    for matrix, block, z, x, core, place_in in spots:
        part = slice(block * ROW_BLOCK, (block + 1) * ROW_BLOCK)
        away = 2 * lax.rem(spots_ref[2] + core, 2) + lax.rem(spots_ref[1] + x, 2)
        factor = factors[away, lax.rem(zs + z - spots_ref[0], zs), place_in]
        direction = precise(momenta[matrix][:, part], factor, ((1,), (1,)))
        outs[matrix][:, part] = masters[matrix][:, part] * (1.0 - WEIGHT_SHRINK) - rates[matrix] * direction


def muon_apply(spots, factors, momenta, masters, rates):
    vmem = pl.BlockSpec(memory_space=pltpu.VMEM)
    return pl.pallas_call(
        functools.partial(muon_apply_kernel, rates),
        out_shape=[jax.ShapeDtypeStruct(master.shape, F32) for master in masters],
        in_specs=[pl.BlockSpec(memory_space=pltpu.SMEM)] + [vmem] * (4 + 2 * len(masters)),
        out_specs=[vmem] * len(masters),
        scratch_shapes=[pltpu.VMEM((4,) + factors[0].shape, F32)],
        compiler_params=pltpu.CompilerParams(vmem_limit_bytes=VMEM_LIMIT),
        name="muon_apply",
    )(spots, *factors, *momenta, *masters)


def body(net, tokens, conditioning, heights, widths, upstream, *state):
    masters, momenta = state[0:5], state[5:10]
    biases, bias_first, bias_second = state[10:13]
    w_qkv, w_proj, w_fc1, w_fc2, w_ada = masters
    micro, local, rows, width = tokens.shape
    count = micro * local
    head_dim = width // HEADS
    hidden = w_fc1.shape[1] * net.dp
    seq, dp = net.seq, net.dp
    y = net.y.digit()

    bounds = [0, 6 * width, 7 * width, 8 * width, 9 * width, 9 * width + hidden, 10 * width + hidden]

    n_qkv, n_proj, n_fc1, n_fc2 = [w.shape[1] for w in (w_qkv, w_proj, w_fc1, w_fc2)]
    unit_qkv, layout_qkv = math.gcd(n_qkv, 8), [(n_qkv, 1)]
    own_tokens = tokens.reshape(count, rows, width)
    wires = net.y.gather(net.wire([w_qkv]))
    units_qkv = net.joined(wires, unit_qkv, width)
    token_pieces = [net.y.gather(tie(own_tokens[0], wires[-1]))]
    wires = net.y.gather(tie(net.wire([w_proj, w_fc1]), token_pieces[0][-1]))
    for i in range(1, count):
        token_pieces.append(net.y.gather(tie(own_tokens[i], wires[-1])))
    rows_mid = net.rows(wires)
    t_proj = lax.all_gather(rows_mid[:n_proj], "dp", axis=0, tiled=True)
    t_fc1 = lax.all_gather(rows_mid[n_proj:], "dp", axis=0, tiled=True)
    wires = net.y.gather(tie(net.wire([w_fc2]), token_pieces[-1][-1]))
    t_fc2 = lax.all_gather(net.rows(wires), "dp", axis=0, tiled=True)

    ada_rows, ada_cols = w_ada.shape
    cond = conditioning.astype(F32).reshape(count, width)
    cond_act, silu_back = jax.vjp(sigmoid_linear, cond)
    cond_low = cond_act.astype(BF).astype(F32)
    cond_parts = jnp.transpose(cond_low.reshape(count, seq, ada_rows), (1, 0, 2)).reshape(seq, -1)
    parcel = jnp.concatenate([jnp.broadcast_to(biases, (seq,) + biases.shape), cond_parts], axis=1)
    parcel = net.to_all(jnp.broadcast_to(parcel[None], (dp,) + parcel.shape))
    bias_full = parcel[:, :, : biases.shape[0]].reshape(-1)
    cond_all = parcel[:, 0, biases.shape[0] :].reshape(dp * count, ada_rows).astype(BF)
    b_ada, b_q, b_v, b_proj, b_fc1, b_fc2 = [bias_full[bounds[i] : bounds[i + 1]] for i in range(6)]

    low_ada = w_ada.astype(BF)
    partial = jnp.dot(cond_all, low_ada, preferred_element_type=F32).reshape(dp, 1, count, ada_cols)
    received = jnp.sum(net.to_all(jnp.broadcast_to(partial, (dp, seq, count, ada_cols))), axis=1)
    (t_qkv,), _ = Staged(net.gather_steps(units_qkv, layout_qkv, 0.45)).finish()
    modulation = jnp.transpose(received, (1, 0, 2)).reshape(count, dp * ada_cols) + b_ada
    shift_one, scale_one, gate_one, shift_two, scale_two, gate_two = jnp.split(
        modulation[:, None, :], 6, axis=-1
    )

    lengths = (heights * widths).reshape(count).astype(jnp.int32)
    offsets = jnp.stack([((y + s) % seq) * rows for s in range(seq)]).astype(jnp.int32)
    normed_all, inverse_all, attn_all, queries, keys, values, attended_low, log_total = [[] for _ in range(8)]
    for i in range(count):
        normed, inverse = layer_norm(jnp.concatenate(token_pieces[i], axis=0).astype(F32))
        attn = (normed * (1.0 + scale_one[i]) + shift_one[i]).astype(BF)
        queries.append((dot_t(attn[None, :rows], t_qkv[:width]) + b_q).astype(BF))
        keys.append(dot_t(attn[None], t_qkv[width : 2 * width]).astype(BF))
        values.append((dot_t(attn[None], t_qkv[2 * width :]) + b_v).astype(BF))
        mixed, lse = attend(lengths[i : i + 1], offsets, queries[i], keys[i], values[i], HEADS, 512)
        normed_all.append(normed[:rows])
        inverse_all.append(inverse[:rows])
        attn_all.append(attn)
        attended_low.append(mixed[0])
        log_total.append(lse)
    attended_low = jnp.stack(attended_low)

    inputs = own_tokens.astype(F32)
    branch_one = dot_t(attended_low, t_proj) + b_proj
    mixed_one = inputs + gate_one * branch_one
    normed_two, inverse_two = layer_norm(mixed_one)
    ffn_in = (normed_two * (1.0 + scale_two) + shift_two).astype(BF)
    pre_act = dot_t(ffn_in, t_fc1) + b_fc1
    activated, gelu_back = jax.vjp(gelu_tanh, pre_act)
    activated_low = activated.astype(BF)
    grad_out = upstream.reshape(count, rows, width).astype(F32)
    grad_branch_two = (gate_two * grad_out).astype(BF)
    flat = lambda array: array.reshape(-1, array.shape[-1])
    sum_fc2 = net.scatter(outer(grad_branch_two, activated_low))
    branch_two = dot_t(activated_low, t_fc2) + b_fc2
    result = (mixed_one + gate_two * branch_two).astype(BF)

    grad_gate_two = jnp.sum(branch_two * grad_out, axis=1)
    bias_fc2 = jnp.sum(grad_branch_two.astype(F32), axis=(0, 1))
    grad_pre = gelu_back(dot(grad_branch_two, t_fc2))[0].astype(BF)
    term_fc1 = outer(grad_pre, ffn_in)
    sum_fc1 = net.scatter(term_fc1)
    grad_pre = tie(grad_pre, term_fc1)
    bias_fc1 = jnp.sum(grad_pre.astype(F32), axis=(0, 1))
    grad_ffn_in = dot(grad_pre, t_fc1)
    grad_shift_two = jnp.sum(grad_ffn_in, axis=1)
    grad_scale_two = jnp.sum(grad_ffn_in * normed_two, axis=1)
    grad_mixed = grad_out + norm_back(normed_two, inverse_two, grad_ffn_in * (1.0 + scale_two))
    grad_gate_one = jnp.sum(branch_one * grad_mixed, axis=1)
    grad_branch_one = (gate_one * grad_mixed).astype(BF)
    term_proj = outer(grad_branch_one, attended_low)
    sum_proj = net.scatter(term_proj)
    grad_branch_one = tie(grad_branch_one, term_proj)
    bias_proj = jnp.sum(grad_branch_one.astype(F32), axis=(0, 1))
    grad_attended = dot(grad_branch_one, t_proj).astype(BF)

    grad_q, grad_k, grad_v, far_parts = [], [], [], []
    turned = [momentum.T for momentum in momenta]
    sent = []
    for i in range(count):
        dq, dk, dv = attend_back(
            lengths[i : i + 1], offsets, queries[i], keys[i], values[i], attended_low[i : i + 1],
            grad_attended[i : i + 1], log_total[i], HEADS, 512, sent,
        )
        if i == 0:
            early = Staged(lockstep(*[net.halves_steps(tie(each, dq)) for each in (sum_proj, sum_fc1, sum_fc2)]))
            sent = early.advance()
        else:
            sent = early.advance(dq)
        grad_q.append(dq)
        grad_k.append(dk)
        grad_v.append(dv)
        far_part = (
            dot(dk[:, rows:], t_qkv[width : 2 * width]) + dot(dv[:, rows:], t_qkv[2 * width :])
        ).astype(BF)[0]
        far_steps = Staged(
            net.y.scatter_steps(
                lambda s, p=far_part: (
                    jnp.zeros((rows, width), BF) if s == 0 else p[(s - 1) * rows : s * rows]
                )
            )
        )
        sent = sent + far_steps.advance()
        far_parts.append(far_steps)
    term_qkv = joined_outer(
        [flat(each) for each in grad_q + grad_k + grad_v] + [attn[:rows] for attn in attn_all] + attn_all,
        [([n * count + i for i in range(count)], 0, width) for n in range(5)],
        [(0, 3), (1, 4), (2, 4)],
        sent,
    )
    sum_qkv = net.scatter(term_qkv)
    sums = early.finish(term_qkv)
    chain = Staged(
        net.muon_steps(
            [(sums[0], [turned[1]]), (sums[1], [turned[2]]), (sums[2], [turned[3]])],
            [w_proj.T, w_fc1.T, w_fc2.T],
            [1.0, math.sqrt(hidden / width), math.sqrt(width / hidden)],
        )
    )
    sent = chain.advance()
    grad_q[0] = tie(grad_q[0], *sent)
    bias_q = sum(jnp.sum(each.astype(F32), axis=(0, 1)) for each in grad_q)
    bias_v = sum(jnp.sum(each.astype(F32), axis=(0, 1)) for each in grad_v)
    own_part = jnp.concatenate(
        [
            dot(grad_q[i], t_qkv[:width])
            + dot(grad_k[i][:, :rows], t_qkv[width : 2 * width])
            + dot(grad_v[i][:, :rows], t_qkv[2 * width :])
            for i in range(count)
        ],
        axis=0,
    )
    sent = chain.advance(own_part)
    far_sum = jnp.stack([steps_of.finish() for steps_of in far_parts])
    grad_attn_in = tie(own_part, *sent) + far_sum
    normed_one, inverse_one = jnp.stack(normed_all), jnp.stack(inverse_all)
    grad_shift_one = jnp.sum(grad_attn_in, axis=1)
    grad_scale_one = jnp.sum(grad_attn_in * normed_one, axis=1)
    grad_inputs = grad_mixed + norm_back(normed_one, inverse_one, grad_attn_in * (1.0 + scale_one))
    grad_inputs = grad_inputs.astype(BF).reshape(tokens.shape)

    grad_mod_local = jnp.concatenate(
        [grad_shift_one, grad_scale_one, grad_gate_one, grad_shift_two, grad_scale_two, grad_gate_two], axis=-1
    )
    bias_ada = jnp.sum(grad_mod_local, axis=0)
    sent = jnp.transpose(grad_mod_local.reshape(count, dp, 1, ada_cols), (1, 2, 0, 3))
    sent = jnp.broadcast_to(sent, (dp, seq, count, ada_cols))
    mod_parts = net.to_all(sent)
    anchor = grad_mod_local
    while not chain.done:
        anchor = (chain.advance(anchor) or [None])[0]
        if anchor is not None:
            mod_parts = tie(mod_parts, anchor)
    halves = Staged(net.halves_steps(tie(sum_qkv, mod_parts)))
    halves.advance()
    mod_cols = jnp.sum(mod_parts, axis=1).astype(BF).reshape(dp * count, ada_cols)
    shard_ada = jnp.einsum("sr,sc->cr", cond_all, mod_cols, preferred_element_type=F32)

    last = Staged(
        net.muon_steps(
            [
                (halves.finish(), [turned[0]]),
                (shard_ada, [turned[4]]),
            ],
            [w_qkv.T, w_ada.T],
            [math.sqrt(3.0), math.sqrt(6.0)],
        )
    )
    sent = last.advance()

    cond_part = jnp.einsum("sc,rc->sr", mod_cols, low_ada, preferred_element_type=F32)
    cond_part = jnp.broadcast_to(cond_part.reshape(dp, 1, -1), (dp, seq, count * ada_rows))
    term_bias = jnp.concatenate([bias_ada, bias_q, bias_v, bias_proj, bias_fc1, bias_fc2])
    parcel = jnp.concatenate([term_bias.reshape(dp, seq, -1), cond_part], axis=-1)
    parcel = net.to_all(tie(parcel, *sent))
    while not last.done:
        anchor = sent[0] if sent else None
        sent = last.advance(anchor)
    (next_qkv, next_ada), (new_qkv, new_ada) = last.result
    (next_proj, next_fc1, next_fc2), (new_proj, new_fc1, new_fc2) = chain.result

    size = biases.shape[0]
    grad_bias = jnp.sum(parcel[..., :size], axis=(0, 1))
    cond_part = jnp.sum(parcel[..., size:], axis=0).reshape(seq, count, ada_rows)
    grad_cond = silu_back(jnp.transpose(cond_part, (1, 0, 2)).reshape(count, width))[0]
    next_first = BETA_FIRST * bias_first + (1.0 - BETA_FIRST) * grad_bias
    next_second = BETA_SECOND * bias_second + (1.0 - BETA_SECOND) * grad_bias * grad_bias
    first_hat = next_first / (1.0 - BETA_FIRST**STEP_COUNT)
    second_hat = next_second / (1.0 - BETA_SECOND**STEP_COUNT)
    new_biases = biases * (1.0 - ADAM_RATE * ADAM_DECAY) - ADAM_RATE * first_hat / (
        jnp.sqrt(second_hat) + ADAM_EPS
    )
    return (
        result.reshape(tokens.shape),
        grad_inputs,
        grad_cond.reshape(conditioning.shape),
        new_qkv.T, new_proj.T, new_fc1.T, new_fc2.T, new_ada.T,
        next_qkv.T, next_proj.T, next_fc1.T, next_fc2.T, next_ada.T,
        new_biases,
        next_first,
        next_second,
    )


def solution(mesh):
    rows = P(None, "dp", "seq", None)
    matrix = P("seq", "dp")
    flat = P(("dp", "seq"))
    in_specs = (rows, P(None, "dp", None), P(None, "dp"), P(None, "dp"), rows) + (matrix,) * 10 + (flat,) * 3
    out_specs = (rows, rows, P(None, "dp", None)) + (matrix,) * 10 + (flat,) * 3
    return jax.shard_map(
        functools.partial(body, Net(mesh)), mesh=mesh, in_specs=in_specs, out_specs=out_specs, check_vma=False
    )
```

```python
import functools
import math

import jax
import jax.numpy as jnp
from jax import lax
from jax.experimental import pallas as pl
from jax.experimental.pallas import tpu as pltpu
from jax.sharding import PartitionSpec as P

HEADS = 16
ROW_BLOCK = 144
NS_STEPS = 5
STEP_COUNT = 10

PRECISE = lax.Precision.HIGHEST
LN_EPS = 1e-06
MASKED = -1e30
NS_A = 3.4445
NS_B = -4.775
NS_C = 2.0315
MUON_DECAY = 0.5
WEIGHT_SHRINK = 0.0001
NORM_EPS = 1e-07
BETA_FIRST = 0.9
BETA_SECOND = 0.999
ADAM_RATE = 0.1
ADAM_DECAY = 0.01
ADAM_EPS = 1e-08
BF = jnp.bfloat16
F32 = jnp.float32
VMEM_LIMIT = 60 * 2**20


class Ring:
    def __init__(self, name, total, stride, size):
        self.name, self.total, self.stride, self.size = name, total, stride, size

    def digit(self):
        return (lax.axis_index(self.name) // self.stride) % self.size

    def send(self, value, shift):
        pairs = []
        for i in range(self.total):
            d = (i // self.stride) % self.size
            pairs.append((i, i + ((d + shift) % self.size - d) * self.stride))
        return lax.ppermute(value, self.name, pairs)

    def gather(self, value, far=1):
        n = self.size
        blocks = [value] + [None] * (n - 1)
        if n == 2:
            blocks[1] = self.send(value, 1)
        elif n > 2:
            low = high = value
            for t in range(1, n // 2):
                low, high = self.send(low, 1), self.send(high, -1)
                blocks[n - t], blocks[t] = low, high
            blocks[n // 2] = self.send(low, 1) if far == 1 else self.send(high, -1)
        return blocks

    def gather_steps(self, value, far=1):
        n = self.size
        blocks = [value] + [None] * (n - 1)
        if n == 2:
            blocks[1] = self.send(value, 1)
            anchor = yield [value]
            blocks[1] = tie(blocks[1], anchor)
            return blocks
        low = high = value
        for t in range(1, n // 2):
            sent = [low, high]
            low, high = self.send(low, 1), self.send(high, -1)
            anchor = yield sent
            low, high = tie(low, anchor), tie(high, anchor)
            blocks[n - t], blocks[t] = low, high
        sent = [low if far == 1 else high]
        last = self.send(sent[0], far)
        anchor = yield sent
        blocks[n // 2] = tie(last, anchor)
        return blocks

    def scatter_steps(self, block_of, far=1):
        n = self.size
        if n == 1:
            return block_of(0).astype(F32)
        if n == 2:
            sent = block_of(1)
            got = self.send(sent, 1)
            anchor = yield [sent]
            return block_of(0).astype(F32) + tie(got, anchor).astype(F32)
        sent = block_of(n // 2)
        got = self.send(sent, far)
        anchor = yield [sent]
        low, high = (tie(got, anchor), None) if far == 1 else (None, tie(got, anchor))
        for t in range(n // 2 - 1, 0, -1):
            up, down = block_of(t), block_of(n - t)
            if low is not None:
                up = (up.astype(F32) + low.astype(F32)).astype(up.dtype)
            if high is not None:
                down = (down.astype(F32) + high.astype(F32)).astype(down.dtype)
            low, high = self.send(up, 1), self.send(down, -1)
            anchor = yield [up, down]
            low, high = tie(low, anchor), tie(high, anchor)
        return block_of(0).astype(F32) + low.astype(F32) + high.astype(F32)


def tie(value, *earlier):
    earlier = [array for array in earlier if array is not None]
    if not earlier:
        return value
    anywhere = pl.BlockSpec(memory_space=pl.ANY)
    return pl.pallas_call(
        lambda *refs: None,
        out_shape=jax.ShapeDtypeStruct(value.shape, value.dtype),
        in_specs=[anywhere] * (1 + len(earlier)),
        out_specs=anywhere,
        input_output_aliases={0: 0},
        name="tie",
    )(value, *earlier)


def lockstep(*steps):
    results = [None] * len(steps)
    alive = dict(enumerate(steps))
    anchor = None
    while alive:
        sent = []
        for n, step in list(alive.items()):
            try:
                sent += step.send(anchor)
            except StopIteration as stop:
                results[n] = stop.value
                del alive[n]
        if alive:
            anchor = yield sent
    return results


class Staged:
    def __init__(self, steps):
        self.steps, self.result, self.started, self.done = steps, None, False, False

    def advance(self, anchor=None):
        if self.done:
            return []
        try:
            sent = self.steps.send(anchor if self.started else None)
            self.started = True
            return sent
        except StopIteration as stop:
            self.result, self.done = stop.value, True
            return []

    def finish(self, anchor=None):
        while not self.done:
            self.advance(anchor)
        return self.result


def place_kernel(zs, ga, parts, count, outs, *refs):
    spots, sources = refs[0], refs[1 : 1 + count]
    outputs, (full, in_sems, out_sems) = refs[1 + count : 1 + count + outs], refs[1 + count + outs :]
    g = full.shape[3]
    half = count // 2
    shards = []
    for sc in range(2):
        for sx in range(2):
            for sz in range(zs):
                where = (lax.rem(spots[0] + sz, zs), lax.rem(spots[1] + sx, 2), lax.rem(spots[2] + sc, 2))
                n = 2 * len(shards)
                line, pair = sources[sc * half + sx].at[sz], sources[sc * half + 2 + sz].at[sx]
                copies = [
                    pltpu.make_async_copy(line, full.at[(*where, pl.ds(0, ga))], in_sems.at[n]),
                    pltpu.make_async_copy(pair, full.at[(*where, pl.ds(ga, g - ga))], in_sems.at[n + 1]),
                ]
                for copy in copies:
                    copy.start()
                shards.append((where, copies))
    exits = []
    for where, copies in shards:
        for copy in copies:
            copy.wait()
        for output, start, size, column, depth in parts:
            target = outputs[output].at[(*where, slice(None), slice(None), pl.ds(column, depth))]
            copy = pltpu.make_async_copy(
                full.at[(*where, pl.ds(start, size))], target, out_sems.at[len(exits)]
            )
            copy.start()
            exits.append(copy)
    for copy in exits:
        copy.wait()


def place(spots, sources, shape, ga, parts, shapes):
    zs = shape[0]
    moved = math.prod(shape) * 2
    return pl.pallas_call(
        functools.partial(place_kernel, zs, ga, parts, len(sources), len(shapes)),
        out_shape=[jax.ShapeDtypeStruct(each, BF) for each in shapes],
        in_specs=[pl.BlockSpec(memory_space=pltpu.SMEM)]
        + [pl.BlockSpec(memory_space=pl.ANY)] * len(sources),
        out_specs=[pl.BlockSpec(memory_space=pl.ANY)] * len(shapes),
        scratch_shapes=[
            pltpu.VMEM(shape, BF),
            pltpu.SemaphoreType.DMA((8 * zs,)),
            pltpu.SemaphoreType.DMA((4 * zs * len(parts),)),
        ],
        compiler_params=pltpu.CompilerParams(vmem_limit_bytes=VMEM_LIMIT),
        cost_estimate=pl.CostEstimate(flops=0, bytes_accessed=2 * moved, transcendentals=0),
        name="place",
    )(spots, *sources)


class Net:
    def __init__(self, mesh):
        dp, seq = mesh.shape["dp"], mesh.shape["seq"]
        self.dp, self.seq = dp, seq
        self.core = Ring("dp", dp, 1, 2)
        self.x = Ring("dp", dp, 2, 2)
        self.z = Ring("dp", dp, 4, dp // 4)
        self.y = Ring("seq", seq, 1, seq)

    def spots(self):
        return jnp.stack([self.z.digit(), self.x.digit(), self.core.digit()]).astype(jnp.int32)


    def wire(self, shards):
        turned = [shard.astype(BF).T for shard in shards]
        return turned[0] if len(turned) == 1 else jnp.concatenate(turned, axis=0)

    def rows(self, wires):
        if self.seq == 2:
            own, other = wires
            return jnp.where(
                self.y.digit() == 0,
                jnp.concatenate([own, other], axis=1),
                jnp.concatenate([other, own], axis=1),
            )
        order = (jnp.arange(self.seq) - self.y.digit()) % self.seq
        full = jnp.take(jnp.stack(wires), order, axis=0)
        return jnp.transpose(full, (1, 0, 2)).reshape(full.shape[1], -1)

    def joined(self, wires, unit, depth):
        full = self.rows(wires)
        return full.reshape(full.shape[0] // unit, unit, depth)

    def scatter(self, term):
        return lax.psum_scatter(term, "dp", scatter_dimension=0, tiled=True)

    def halves_steps(self, term):
        y = self.y.digit()
        blocks = term.reshape(term.shape[0], self.seq, -1)
        return (
            yield from self.y.scatter_steps(
                lambda s: lax.dynamic_index_in_dim(blocks, (y + s) % self.seq, 1, keepdims=False)
            )
        )

    def gather_steps(self, units, layout, part):
        g, unit, depth = units.shape
        zs = self.z.size
        ga = max(1, int(part * g))
        first, second = units[:ga], units[ga:]

        def line_steps():
            blocks = yield from self.z.gather_steps(first, 1)
            line = jnp.stack(blocks)
            return (yield from self.x.gather_steps(line))

        def pair_steps():
            blocks = yield from self.x.gather_steps(second)
            return (yield from self.z.gather_steps(jnp.stack(blocks), -1))

        lines, pairs = yield from lockstep(line_steps(), pair_steps())
        pieces = lines + pairs
        others = [self.core.send(piece, 1) for piece in pieces]
        anchor = yield pieces
        sources = pieces + [tie(other, anchor) for other in others]
        parts, shapes, start = [], [], 0
        for n, (rows, blocks) in enumerate(layout):
            size = rows // unit
            shapes.append((zs, 2, 2, size, unit, blocks * depth))
            for j in range(blocks):
                parts.append((n, start, size, j * depth, depth))
                start += size
        full = place(self.spots(), sources, (zs, 2, 2, g, unit, depth), ga, parts, shapes)
        return [f.reshape(-1, f.shape[-1]) for f in full], lines[1:] + pairs[1:]

    def scatter_steps(self, own, other, layout, part):
        zs, _, g, unit, depth = own.shape
        ga = max(1, int(part * g))
        x, z = self.x.digit(), self.z.digit()
        got = self.core.send(other, 1)
        anchor = yield [other]
        half = (own.astype(F32) + tie(got, anchor).astype(F32)).astype(BF)

        def line_steps():
            line = yield from self.x.scatter_steps(
                lambda s: lax.dynamic_index_in_dim(half[:, :, :ga], (x + s) % 2, 1, keepdims=False)
            )
            line = line.astype(BF)
            return (
                yield from self.z.scatter_steps(
                    lambda s: lax.dynamic_index_in_dim(line, (z + s) % zs, 0, keepdims=False), 1
                )
            )

        def pair_steps():
            pair = yield from self.z.scatter_steps(
                lambda s: lax.dynamic_index_in_dim(half[:, :, ga:], (z + s) % zs, 0, keepdims=False), -1
            )
            pair = pair.astype(BF)
            return (
                yield from self.x.scatter_steps(
                    lambda s: lax.dynamic_index_in_dim(pair, (x + s) % 2, 0, keepdims=False)
                )
            )

        line, pair = yield from lockstep(line_steps(), pair_steps())
        joined = jnp.concatenate([line, pair], axis=0).astype(BF)
        count = layout[0][1]
        if count > 1:
            joined = jnp.transpose(joined.reshape(count, -1, unit, depth), (1, 2, 0, 3))
        joined = joined.reshape(-1, self.seq, count * depth // self.seq)
        y = self.y.digit()
        return (
            yield from self.y.scatter_steps(
                lambda s: lax.dynamic_index_in_dim(joined, (y + s) % self.seq, 1, keepdims=False)
            )
        )


    def muon_steps(self, groups, masters, rates):
        momenta, own, other = muon_gram(self.spots(), self.z.size, groups)
        got = self.core.send(other, 1)
        anchor = yield [other]
        half = own + tie(got, anchor)
        sent = half[1]
        got = self.x.send(sent, 1)
        anchor = yield [sent]
        kept = half[0] + tie(got, anchor)
        blocks = [kept[shift] for shift in range(self.z.size)]
        got = [self.z.send(blocks[shift], shift) for shift in range(1, self.z.size)]
        anchor = yield blocks[1:]
        factor = polynomial([blocks[0]] + [tie(each, anchor) for each in got])
        got = [self.z.send(factor, -shift) for shift in range(1, self.z.size)]
        anchor = yield [factor]
        line = jnp.stack([factor] + [tie(each, anchor) for each in got])
        got = self.x.send(line, 1)
        anchor = yield [line]
        pair = [line, tie(got, anchor)]
        others = [self.core.send(each, 1) for each in pair]
        anchor = yield pair
        factors = pair + [tie(each, anchor) for each in others]
        return momenta, muon_apply(self.spots(), factors, momenta, masters, rates)


    def to_all(self, value):
        flat = value.reshape((self.dp * self.seq,) + value.shape[2:])
        return lax.all_to_all(flat, ("dp", "seq"), 0, 0, tiled=True).reshape(value.shape)

    def to_dp(self, value):
        return lax.all_to_all(value, "dp", 0, 0, tiled=True)


def layer_norm(values):
    centered = values - jnp.mean(values, axis=-1, keepdims=True)
    inverse = lax.rsqrt(jnp.mean(centered * centered, axis=-1, keepdims=True) + LN_EPS)
    return (centered * inverse, inverse)


def norm_back(normed, inverse, grad):
    mean_grad = jnp.mean(grad, axis=-1, keepdims=True)
    mean_cross = jnp.mean(grad * normed, axis=-1, keepdims=True)
    return inverse * (grad - mean_grad - normed * mean_cross)


def sigmoid_linear(values):
    return values * jax.nn.sigmoid(values)


def gelu_tanh(values):
    return jax.nn.gelu(values, approximate=True)


def dot_t(left, right):
    return jnp.einsum("srk,nk->srn", left, right, preferred_element_type=F32)


def dot(left, right):
    return jnp.einsum("srn,nk->srk", left, right, preferred_element_type=F32)


def outer(left, right):
    return jnp.einsum("srn,srk->nk", left, right, preferred_element_type=F32).astype(BF)


def shard_outer_kernel(plan, counts, tile, split, spots_ref, *refs):
    outs = 2 if split else 1
    inputs, where = refs[: counts[0]], refs[counts[1] : counts[1] + outs]
    buffers = refs[counts[1] + outs : counts[1] + outs + len(plan["loads"])]
    acc, in_sems, out_sems = refs[counts[1] + outs + len(plan["loads"]) :]
    loads = []
    for n, (sources, start, size) in enumerate(plan["loads"]):
        row, copies = 0, []
        for m, source in enumerate(sources):
            rows = inputs[source].shape[0]
            window = inputs[source].at[:, pl.ds(start, size)]
            copies.append(pltpu.make_async_copy(window, buffers[n].at[pl.ds(row, rows)], in_sems.at[n, m]))
            copies[-1].start()
            row += rows
        loads.append(copies)
    ready = set()
    shipped = []
    unit = acc.shape[1]
    for left, right, base, ships in plan["parts"]:
        for n in (left, right):
            if n not in ready:
                for copy in loads[n]:
                    copy.wait()
                ready.add(n)
        width = buffers[left].shape[1]
        step = tile if width % tile == 0 else width

        @pl.loop(0, width // step)
        def _(t):
            block = buffers[left][:, pl.ds(pl.multiple_of(t * step, step), step)]
            product = lax.dot_general(
                block, buffers[right][...], (((0,), (0,)), ((), ())), preferred_element_type=F32
            )
            product = product.reshape(step // unit, unit, product.shape[1]).astype(BF)
            acc[pl.ds(base + t * (step // unit), step // unit)] = product

        for core, z, x, row, target, size in ships:
            spot = (z, x) if split else (z, x, core)
            places = [ref.at[(*spot, pl.ds(target, size))] for ref in where]
            copies = [
                pltpu.make_async_copy(acc.at[pl.ds(row, size)], each, out_sems.at[len(shipped)]) for each in places
            ]
            shipped.append((core, copies))
            on_own_core(split, spots_ref, core, [copy.start for copy in copies])
    for core, copies in shipped:
        on_own_core(split, spots_ref, core, [copy.wait for copy in copies])


def on_own_core(split, spots_ref, core, actions):
    if not split:
        actions[0]()
        return

    @pl.when(spots_ref[2] == core)
    def _():
        actions[0]()

    @pl.when(spots_ref[2] != core)
    def _():
        actions[1]()


def shard_outer(spots, inputs, loads, parts, zs, depth, unit, shard_units, deps=(), tile=384, split=True):
    dp = zs * 4
    plan_parts, base, row, placed = [], 0, 0, {}
    begun = {}
    for left, right, rows, first in parts:
        if first not in begun:
            begun[first] = (base, 0)
        start, shipped = begun[first]
        width = loads[left][2]
        size = rows // unit
        end = base + width // unit
        ships = []
        while shipped < dp and start + (shipped + 1) * size <= end:
            core, x, z = shipped % 2, shipped // 2 % 2, shipped // 4
            ships.append((core, z, x, start + shipped * size, first, size))
            shipped += 1
        begun[first] = (start, shipped)
        plan_parts.append((left, right, base, ships))
        base = end
    total = sum(len(part[3]) for part in plan_parts)
    shape = (zs, 2, shard_units, unit, depth) if split else (zs, 2, 2, shard_units, unit, depth)
    outs = [jax.ShapeDtypeStruct(shape, BF)] * (2 if split else 1)
    anywhere = pl.BlockSpec(memory_space=pl.ANY)
    heights = [sum(inputs[source].shape[0] for source in sources) for sources, _, _ in loads]
    flops = sum(2 * heights[p[0]] * loads[p[0]][2] * loads[p[1]][2] for p in parts)
    return pl.pallas_call(
        functools.partial(
            shard_outer_kernel, {"loads": loads, "parts": plan_parts}, (len(inputs), len(inputs) + len(deps)), tile, split
        ),
        out_shape=outs,
        in_specs=[pl.BlockSpec(memory_space=pltpu.SMEM)] + [anywhere] * (len(inputs) + len(deps)),
        out_specs=[anywhere] * len(outs),
        scratch_shapes=[pltpu.VMEM((height, load[2]), BF) for height, load in zip(heights, loads)]
        + [
            pltpu.VMEM((base, unit, depth), BF),
            pltpu.SemaphoreType.DMA((len(loads), max(len(load[0]) for load in loads))),
            pltpu.SemaphoreType.DMA((total,)),
        ],
        compiler_params=pltpu.CompilerParams(vmem_limit_bytes=VMEM_LIMIT),
        cost_estimate=pl.CostEstimate(flops=flops, bytes_accessed=2 * base * unit * depth, transcendentals=0),
        name="shard_outer",
    )(spots, *inputs, *deps)


LANES = 128
LOG2E = math.log2(math.e)


def padded(block, column=None):
    rows, depth = block.shape
    if column is None:
        return jnp.concatenate([block, jnp.zeros((rows, LANES - depth), block.dtype)], axis=1)
    rest = jnp.zeros((rows, LANES - depth - 1), block.dtype)
    return jnp.concatenate([block, column.astype(block.dtype), rest], axis=1)


def mask_column(lengths_ref, offsets_ref, sample, total, rows):
    place = lax.broadcasted_iota(jnp.int32, (total, 1), 0)
    position = place
    for s in range(total // rows):
        position = jnp.where(place // rows == s, place - s * rows + offsets_ref[s], position)
    return jnp.where(position < lengths_ref[sample], 0.0, MASKED)


def nt(left, right):
    return lax.dot_general(left, right, (((1,), (1,)), ((), ())), preferred_element_type=F32)


def nn(left, right):
    return jnp.dot(left, right, preferred_element_type=F32)


def without(kernel, start, count, *fixed):
    def run(*refs):
        kernel(*fixed, *refs[:start], *refs[start + count :])

    return run


def attend_kernel(heads, chunk, lengths_ref, offsets_ref, q_ref, k_ref, v_ref, o_ref, lse_ref, q_s, k_s, vt_s, o_s):
    rows, width = q_ref.shape[1:]
    total = k_ref.shape[1]
    depth = width // heads
    factor = depth**-0.5 * LOG2E
    mask = mask_column(lengths_ref, offsets_ref, pl.program_id(0), total, rows)
    ones = jnp.ones((rows, 1), F32)
    for h in range(heads):
        span = slice(h * depth, (h + 1) * depth)
        q_s[h] = padded(q_ref[0, :, span], ones)
        k_s[h] = padded(k_ref[0, :, span], mask)
        vt_s[h] = jnp.transpose(v_ref[0, :, span])

    def one_head(h, carry):
        peak = jnp.full((1, rows), MASKED, F32)
        sums = jnp.zeros((1, rows), F32)
        mixed = jnp.zeros((depth, rows), F32)
        for c in range(total // chunk):
            part = slice(c * chunk, (c + 1) * chunk)
            scores = nt(k_s[h, part], q_s[h])
            higher = jnp.maximum(peak, jnp.max(scores, axis=0, keepdims=True))
            weights = jnp.exp2((scores - higher) * factor)
            if c == 0:
                sums = jnp.sum(weights, axis=0, keepdims=True)
                mixed = nn(vt_s[h, :, part], weights.astype(BF))
            else:
                shrink = jnp.exp2((peak - higher) * factor)
                sums = sums * shrink + jnp.sum(weights, axis=0, keepdims=True)
                mixed = mixed * shrink + nn(vt_s[h, :, part], weights.astype(BF))
            peak = higher
        o_s[h] = jnp.transpose(mixed / sums)
        lse_ref[0, h] = peak * factor + jnp.log2(sums)
        return carry

    lax.fori_loop(0, heads, one_head, 0)
    for h in range(heads):
        o_ref[0, :, h * depth : (h + 1) * depth] = o_s[h].astype(BF)


def attend(lengths, offsets, queries, keys, values, heads, tile, deps=()):
    count, rows, width = queries.shape
    total = keys.shape[1]
    depth = width // heads
    tile = min(tile, total)
    pick = lambda i, *_: (i, 0, 0)
    return pl.pallas_call(
        without(attend_kernel, 5, len(deps), heads, tile),
        grid_spec=pltpu.PrefetchScalarGridSpec(
            num_scalar_prefetch=2,
            grid=(count,),
            in_specs=[
                pl.BlockSpec((1, rows, width), pick),
                pl.BlockSpec((1, total, width), pick),
                pl.BlockSpec((1, total, width), pick),
            ]
            + [pl.BlockSpec(memory_space=pl.ANY)] * len(deps),
            out_specs=[
                pl.BlockSpec((1, rows, width), pick),
                pl.BlockSpec((1, heads, 1, rows), lambda i, *_: (i, 0, 0, 0)),
            ],
            scratch_shapes=[
                pltpu.VMEM((heads, rows, LANES), BF),
                pltpu.VMEM((heads, total, LANES), BF),
                pltpu.VMEM((heads, depth, total), BF),
                pltpu.VMEM((heads, rows, depth), F32),
            ],
        ),
        out_shape=[
            jax.ShapeDtypeStruct((count, rows, width), BF),
            jax.ShapeDtypeStruct((count, heads, 1, rows), F32),
        ],
        compiler_params=pltpu.CompilerParams(vmem_limit_bytes=VMEM_LIMIT),
        cost_estimate=pl.CostEstimate(
            flops=4 * count * heads * rows * total * LANES,
            bytes_accessed=2 * count * width * (2 * rows + 2 * total),
            transcendentals=count * heads * rows * total,
        ),
        name="attend",
    )(lengths, offsets, queries, keys, values, *deps)


def attend_back_kernel(
    heads, chunk, lengths_ref, offsets_ref, q_ref, k_ref, v_ref, o_ref, g_ref, lse_ref,
    dq_ref, dk_ref, dv_ref, q_s, k_s, kt_s, v_s, g_s, delta_s, dq_s, dk_s, dv_s
):
    rows, width = q_ref.shape[1:]
    total = k_ref.shape[1]
    depth = width // heads
    scale = depth**-0.5
    factor = scale * LOG2E
    mask = mask_column(lengths_ref, offsets_ref, pl.program_id(0), total, rows)
    ones = jnp.ones((rows, 1), F32)
    cross = jnp.transpose(g_ref[0].astype(F32) * o_ref[0].astype(F32))
    for h in range(heads):
        span = slice(h * depth, (h + 1) * depth)
        delta_s[h] = jnp.sum(cross[span], axis=0, keepdims=True)
        q_s[h] = padded(q_ref[0, :, span], ones)
        k_s[h] = padded(k_ref[0, :, span], mask)
        kt_s[h] = jnp.transpose(k_ref[0, :, span])
        g_s[h] = padded(g_ref[0, :, span])
        v_s[h] = padded(v_ref[0, :, span])

    def one_head(h, carry):
        dq = jnp.zeros((depth, rows), F32)
        for c in range(total // chunk):
            part = slice(c * chunk, (c + 1) * chunk)
            probs = jnp.exp2(nt(k_s[h, part], q_s[h]) * factor - lse_ref[0, h])
            slopes = (probs * (nt(v_s[h, part], g_s[h]) - delta_s[h])).astype(BF)
            dv_s[h, part] = nn(probs.astype(BF), g_s[h]).astype(BF)
            dk_s[h, part] = (nn(slopes, q_s[h]) * scale).astype(BF)
            dq = dq + nn(kt_s[h, :, part], slopes)
        dq_s[h] = jnp.transpose(dq * scale)
        return carry

    lax.fori_loop(0, heads, one_head, 0)
    for h in range(heads):
        span = slice(h * depth, (h + 1) * depth)
        dq_ref[0, :, span] = dq_s[h].astype(BF)
        dk_ref[0, :, span] = dk_s[h][:, :depth]
        dv_ref[0, :, span] = dv_s[h][:, :depth]


def attend_back(lengths, offsets, queries, keys, values, mixed, grads, lse, heads, tile, deps=()):
    count, rows, width = queries.shape
    total = keys.shape[1]
    depth = width // heads
    tile = min(tile, total)
    pick = lambda i, *_: (i, 0, 0)
    near = pl.BlockSpec((1, rows, width), pick)
    far = pl.BlockSpec((1, total, width), pick)
    return pl.pallas_call(
        without(attend_back_kernel, 8, len(deps), heads, tile),
        grid_spec=pltpu.PrefetchScalarGridSpec(
            num_scalar_prefetch=2,
            grid=(count,),
            in_specs=[near, far, far, near, near, pl.BlockSpec((1, heads, 1, rows), lambda i, *_: (i, 0, 0, 0))]
            + [pl.BlockSpec(memory_space=pl.ANY)] * len(deps),
            out_specs=[near, far, far],
            scratch_shapes=[
                pltpu.VMEM((heads, rows, LANES), BF),
                pltpu.VMEM((heads, total, LANES), BF),
                pltpu.VMEM((heads, depth, total), BF),
                pltpu.VMEM((heads, total, LANES), BF),
                pltpu.VMEM((heads, rows, LANES), BF),
                pltpu.VMEM((heads, 1, rows), F32),
                pltpu.VMEM((heads, rows, depth), F32),
                pltpu.VMEM((heads, total, LANES), BF),
                pltpu.VMEM((heads, total, LANES), BF),
            ],
        ),
        out_shape=[
            jax.ShapeDtypeStruct((count, rows, width), BF),
            jax.ShapeDtypeStruct((count, total, width), BF),
            jax.ShapeDtypeStruct((count, total, width), BF),
        ],
        compiler_params=pltpu.CompilerParams(vmem_limit_bytes=VMEM_LIMIT),
        cost_estimate=pl.CostEstimate(
            flops=10 * count * heads * rows * total * LANES,
            bytes_accessed=2 * count * width * (4 * rows + 4 * total),
            transcendentals=count * heads * rows * total,
        ),
        name="attend_back",
    )(lengths, offsets, queries, keys, values, mixed, grads, lse, *deps)


def block_spots(counts, zs):
    per = -(-sum(counts) // (4 * zs))
    spots = []
    for matrix, count in enumerate(counts):
        for block in range(count):
            device, place_in = divmod(len(spots), per)
            spots.append((matrix, block, device // 4, device // 2 % 2, device % 2, place_in))
    return spots, per


def precise(left, right, dims):
    return lax.dot_general(left, right, (dims, ((), ())), precision=PRECISE, preferred_element_type=F32)


def muon_gram_kernel(groups, spots_ref, *refs):
    count = sum(groups)
    sums, momenta = refs[: len(groups)], refs[len(groups) : len(groups) + count]
    outs = refs[len(groups) + count : len(groups) + 2 * count]
    own_ref, other_ref = refs[len(groups) + 2 * count :]
    n = 0
    for matrices, sum_ref in zip(groups, sums):
        start = 0
        for _ in range(matrices):
            size = momenta[n].shape[0]
            outs[n][...] = MUON_DECAY * momenta[n][...] + sum_ref[start : start + size]
            start += size
            n += 1
    zs = own_ref.shape[1]
    spots, per = block_spots([out.shape[1] // ROW_BLOCK for out in outs], zs)
    if len(spots) < 4 * zs * per:
        own_ref[...] = jnp.zeros_like(own_ref)
        other_ref[...] = jnp.zeros_like(other_ref)
    for matrix, block, z, x, core, place_in in spots:
        turned = outs[matrix][:, block * ROW_BLOCK : (block + 1) * ROW_BLOCK]
        gram = precise(turned, turned, ((0,), (0,)))
        away = (lax.rem(spots_ref[1] + x, 2), lax.rem(zs + z - spots_ref[0], zs), place_in)

        @pl.when(spots_ref[2] == core)
        def _():
            own_ref[away] = gram

        @pl.when(spots_ref[2] != core)
        def _():
            other_ref[away] = gram


def muon_gram(spots, zs, groups):
    momenta = [momentum for _, each in groups for momentum in each]
    _, per = block_spots([momentum.shape[1] // ROW_BLOCK for momentum in momenta], zs)
    grams = jax.ShapeDtypeStruct((2, zs, per, ROW_BLOCK, ROW_BLOCK), F32)
    vmem = pl.BlockSpec(memory_space=pltpu.VMEM)
    outs = pl.pallas_call(
        functools.partial(muon_gram_kernel, [len(each) for _, each in groups]),
        out_shape=[jax.ShapeDtypeStruct(momentum.shape, F32) for momentum in momenta] + [grams, grams],
        in_specs=[pl.BlockSpec(memory_space=pltpu.SMEM)] + [vmem] * (len(groups) + len(momenta)),
        out_specs=[vmem] * (len(momenta) + 2),
        compiler_params=pltpu.CompilerParams(vmem_limit_bytes=VMEM_LIMIT),
        name="muon_gram",
    )(spots, *[group[0] for group in groups], *momenta)
    return outs[:-2], outs[-2], outs[-1]


def polynomial_kernel(count, *refs):
    out = refs[count]
    shape = (ROW_BLOCK, ROW_BLOCK)
    eye = (lax.broadcasted_iota(jnp.int32, shape, 0) == lax.broadcasted_iota(jnp.int32, shape, 1)).astype(F32)
    mul = lambda left, right: precise(left, right, ((1,), (0,)))
    blocks = range(out.shape[0])
    currents, scales, totals = [], [], []
    for n in blocks:
        gram = refs[0][n]
        for ref in refs[1:count]:
            gram = gram + ref[n]
        square = jnp.sum(jnp.sum(gram * eye, axis=1, keepdims=True), axis=0, keepdims=True)
        scale = 1.0 / (jnp.sqrt(square) + NORM_EPS)
        scales.append(scale)
        currents.append(gram * (scale * scale))
    for step in range(NS_STEPS):
        factors = [NS_A * eye + NS_B * a + NS_C * mul(a, a) for a in currents]
        totals = factors if step == 0 else [mul(f, t) for f, t in zip(factors, totals)]
        if step + 1 < NS_STEPS:
            currents = [mul(f, a) for f, a in zip(factors, currents)]
            currents = [mul(a, f) for f, a in zip(factors, currents)]
    for n in blocks:
        out[n] = totals[n] * scales[n]


def polynomial(parts):
    vmem = pl.BlockSpec(memory_space=pltpu.VMEM)
    return pl.pallas_call(
        functools.partial(polynomial_kernel, len(parts)),
        out_shape=jax.ShapeDtypeStruct(parts[0].shape, F32),
        in_specs=[vmem] * len(parts),
        out_specs=vmem,
        compiler_params=pltpu.CompilerParams(vmem_limit_bytes=VMEM_LIMIT),
        name="polynomial",
    )(*parts)


def muon_apply_kernel(rates, spots_ref, *refs):
    count = len(rates)
    parts, momenta, masters = refs[:4], refs[4 : 4 + count], refs[4 + count : 4 + 2 * count]
    outs, factors = refs[4 + 2 * count : 4 + 3 * count], refs[4 + 3 * count]
    for n in range(4):
        factors[n] = parts[n][...]
    zs = factors.shape[1]
    spots, _ = block_spots([momentum.shape[1] // ROW_BLOCK for momentum in momenta], zs)
    for matrix, block, z, x, core, place_in in spots:
        part = slice(block * ROW_BLOCK, (block + 1) * ROW_BLOCK)
        away = 2 * lax.rem(spots_ref[2] + core, 2) + lax.rem(spots_ref[1] + x, 2)
        factor = factors[away, lax.rem(zs + z - spots_ref[0], zs), place_in]
        direction = precise(momenta[matrix][:, part], factor, ((1,), (1,)))
        outs[matrix][:, part] = masters[matrix][:, part] * (1.0 - WEIGHT_SHRINK) - rates[matrix] * direction


def muon_apply(spots, factors, momenta, masters, rates):
    vmem = pl.BlockSpec(memory_space=pltpu.VMEM)
    return pl.pallas_call(
        functools.partial(muon_apply_kernel, rates),
        out_shape=[jax.ShapeDtypeStruct(master.shape, F32) for master in masters],
        in_specs=[pl.BlockSpec(memory_space=pltpu.SMEM)] + [vmem] * (4 + 2 * len(masters)),
        out_specs=[vmem] * len(masters),
        scratch_shapes=[pltpu.VMEM((4,) + factors[0].shape, F32)],
        compiler_params=pltpu.CompilerParams(vmem_limit_bytes=VMEM_LIMIT),
        name="muon_apply",
    )(spots, *factors, *momenta, *masters)


def body(net, tokens, conditioning, heights, widths, upstream, *state):
    masters, momenta = state[0:5], state[5:10]
    biases, bias_first, bias_second = state[10:13]
    w_qkv, w_proj, w_fc1, w_fc2, w_ada = masters
    micro, local, rows, width = tokens.shape
    count = micro * local
    head_dim = width // HEADS
    hidden = w_fc1.shape[1] * net.dp
    seq, dp = net.seq, net.dp
    y = net.y.digit()

    bounds = [0, 6 * width, 7 * width, 8 * width, 9 * width, 9 * width + hidden, 10 * width + hidden]

    n_qkv, n_proj, n_fc1, n_fc2 = [w.shape[1] for w in (w_qkv, w_proj, w_fc1, w_fc2)]
    unit = math.gcd(math.gcd(n_qkv, n_proj), 8)
    unit_qkv, layout_qkv = math.gcd(n_qkv, 8), [(n_qkv, 1)]
    own_tokens = tokens.reshape(count, rows, width)
    wires = net.y.gather(net.wire([w_qkv, w_proj]))
    first = Staged(net.gather_steps(net.joined(wires, unit, width), [(n_qkv, 1), (n_proj, 1)], 0.45))
    sent = [first.advance(), first.advance(), first.advance()]
    token_pieces = [net.y.gather(tie(own_tokens[0], wires[-1]))]
    wires = net.y.gather(tie(net.wire([w_fc1]), token_pieces[0][-1], *sent[2]))
    t_fc1 = lax.all_gather(net.rows(wires), "dp", axis=0, tiled=True)
    for i in range(1, count):
        token_pieces.append(net.y.gather(tie(own_tokens[i], wires[-1])))
    t_qkv, t_proj = first.finish()[0]

    ada_rows, ada_cols = w_ada.shape
    cond = conditioning.astype(F32).reshape(count, width)
    cond_act, silu_back = jax.vjp(sigmoid_linear, cond)
    cond_low = cond_act.astype(BF).astype(F32)
    cond_parts = jnp.transpose(cond_low.reshape(count, seq, ada_rows), (1, 0, 2)).reshape(seq, -1)
    parcel = jnp.concatenate([jnp.broadcast_to(biases, (seq,) + biases.shape), cond_parts], axis=1)
    parcel = net.to_all(jnp.broadcast_to(parcel[None], (dp,) + parcel.shape))
    bias_full = parcel[:, :, : biases.shape[0]].reshape(-1)
    cond_all = parcel[:, 0, biases.shape[0] :].reshape(dp * count, ada_rows).astype(BF)
    b_ada, b_q, b_v, b_proj, b_fc1, b_fc2 = [bias_full[bounds[i] : bounds[i + 1]] for i in range(6)]

    low_ada = w_ada.astype(BF)
    partial = jnp.dot(cond_all, low_ada, preferred_element_type=F32).reshape(dp, 1, count, ada_cols)
    received = jnp.sum(net.to_all(jnp.broadcast_to(partial, (dp, seq, count, ada_cols))), axis=1)
    modulation = jnp.transpose(received, (1, 0, 2)).reshape(count, dp * ada_cols) + b_ada
    shift_one, scale_one, gate_one, shift_two, scale_two, gate_two = jnp.split(
        modulation[:, None, :], 6, axis=-1
    )

    lengths = (heights * widths).reshape(count).astype(jnp.int32)
    offsets = jnp.stack([((y + s) % seq) * rows for s in range(seq)]).astype(jnp.int32)
    normed_all, inverse_all, attn_all, queries, keys, values, attended_low, log_total = [[] for _ in range(8)]
    for i in range(count):
        normed, inverse = layer_norm(jnp.concatenate(token_pieces[i], axis=0).astype(F32))
        attn = (normed * (1.0 + scale_one[i]) + shift_one[i]).astype(BF)
        queries.append((dot_t(attn[None, :rows], t_qkv[:width]) + b_q).astype(BF))
        keys.append(dot_t(attn[None], t_qkv[width : 2 * width]).astype(BF))
        values.append((dot_t(attn[None], t_qkv[2 * width :]) + b_v).astype(BF))
        mixed, lse = attend(lengths[i : i + 1], offsets, queries[i], keys[i], values[i], HEADS, 512)
        if i == 0:
            token_pieces[1:] = [each[:1] + [tie(a, mixed) for a in each[1:]] for each in token_pieces[1:]]
            last_piece = token_pieces[-1][-1] if count > 1 else mixed
            wires = net.y.gather(tie(net.wire([w_fc2]), last_piece))
            t_fc2 = lax.all_gather(net.rows(wires), "dp", axis=0, tiled=True)
        normed_all.append(normed[:rows])
        inverse_all.append(inverse[:rows])
        attn_all.append(attn)
        attended_low.append(mixed[0])
        log_total.append(lse)
    attended_low = jnp.stack(attended_low)

    inputs = own_tokens.astype(F32)
    branch_one = dot_t(attended_low, t_proj) + b_proj
    mixed_one = inputs + gate_one * branch_one
    normed_two, inverse_two = layer_norm(mixed_one)
    ffn_in = (normed_two * (1.0 + scale_two) + shift_two).astype(BF)
    pre_act = dot_t(ffn_in, t_fc1) + b_fc1
    activated, gelu_back = jax.vjp(gelu_tanh, pre_act)
    activated_low = activated.astype(BF)
    grad_out = upstream.reshape(count, rows, width).astype(F32)
    grad_branch_two = (gate_two * grad_out).astype(BF)
    flat = lambda array: array.reshape(-1, array.shape[-1])
    term_fc2 = outer(grad_branch_two, activated_low)
    sum_fc2 = net.scatter(term_fc2)
    branch_two = dot_t(tie(activated_low, term_fc2), t_fc2) + b_fc2
    grad_branch_two = tie(grad_branch_two, term_fc2)
    result = (mixed_one + gate_two * branch_two).astype(BF)

    grad_gate_two = jnp.sum(branch_two * grad_out, axis=1)
    bias_fc2 = jnp.sum(grad_branch_two.astype(F32), axis=(0, 1))
    grad_pre = gelu_back(dot(grad_branch_two, t_fc2))[0].astype(BF)
    bias_fc1 = jnp.sum(grad_pre.astype(F32), axis=(0, 1))
    grad_ffn_in = dot(grad_pre, t_fc1)
    grad_shift_two = jnp.sum(grad_ffn_in, axis=1)
    grad_scale_two = jnp.sum(grad_ffn_in * normed_two, axis=1)
    grad_mixed = grad_out + norm_back(normed_two, inverse_two, grad_ffn_in * (1.0 + scale_two))
    grad_gate_one = jnp.sum(branch_one * grad_mixed, axis=1)
    grad_branch_one = (gate_one * grad_mixed).astype(BF)
    unit_mid = math.gcd(math.gcd(n_proj, n_fc1), 8)
    (term_mid,) = shard_outer(
        net.spots(),
        [flat(grad_pre), flat(ffn_in), flat(grad_branch_one), flat(attended_low)],
        [([2], 0, width), ([3], 0, width), ([1], 0, width)] + [([0], j * width, width) for j in range(hidden // width)],
        [(0, 1, n_proj, 0)] + [(3 + j, 2, n_fc1, n_proj // unit_mid) for j in range(hidden // width)],
        net.z.size, width, unit_mid, (n_proj + n_fc1) // unit_mid, split=False,
    )
    term_mid = tie(term_mid, sum_fc2)
    sum_mid = net.scatter(term_mid.reshape(dp * (n_proj + n_fc1), width))
    grad_branch_one = tie(grad_branch_one, term_mid)
    bias_proj = jnp.sum(grad_branch_one.astype(F32), axis=(0, 1))
    grad_attended = dot(grad_branch_one, t_proj).astype(BF)

    grad_q, grad_k, grad_v, far_parts = [], [], [], []
    turned = [momentum.T for momentum in momenta]
    sent = []
    for i in range(count):
        dq, dk, dv = attend_back(
            lengths[i : i + 1], offsets, queries[i], keys[i], values[i], attended_low[i : i + 1],
            grad_attended[i : i + 1], log_total[i], HEADS, 512, sent,
        )
        sent = []
        grad_q.append(dq)
        grad_k.append(dk)
        grad_v.append(dv)
        far_part = (
            dot(dk[:, rows:], t_qkv[width : 2 * width]) + dot(dv[:, rows:], t_qkv[2 * width :])
        ).astype(BF)[0]
        far_steps = Staged(
            net.y.scatter_steps(
                lambda s, p=far_part: (
                    jnp.zeros((rows, width), BF) if s == 0 else p[(s - 1) * rows : s * rows]
                )
            )
        )
        sent = sent + far_steps.advance()
        far_parts.append(far_steps)
    own, other = shard_outer(
        net.spots(),
        [flat(each) for each in grad_q + grad_k + grad_v] + [attn[:rows] for attn in attn_all] + attn_all,
        [([n * count + i for i in range(count)], 0, width) for n in range(5)],
        [(0, 3, n_qkv, 0), (1, 4, n_qkv, 0), (2, 4, n_qkv, 0)],
        net.z.size, width, unit_qkv, n_qkv // unit_qkv, sent,
    )
    back_qkv = Staged(net.scatter_steps(own, other, layout_qkv, 0.45))
    sent = back_qkv.advance()
    grad_q[0] = tie(grad_q[0], *sent)
    bias_q = sum(jnp.sum(each.astype(F32), axis=(0, 1)) for each in grad_q)
    bias_v = sum(jnp.sum(each.astype(F32), axis=(0, 1)) for each in grad_v)
    own_part = jnp.concatenate(
        [
            dot(grad_q[i], t_qkv[:width])
            + dot(grad_k[i][:, :rows], t_qkv[width : 2 * width])
            + dot(grad_v[i][:, :rows], t_qkv[2 * width :])
            for i in range(count)
        ],
        axis=0,
    )
    sent = back_qkv.advance(own_part)
    early = Staged(
        lockstep(*[net.halves_steps(tie(each, *sent)) for each in (sum_fc2, sum_mid)])
    )
    sent = early.advance()
    far_sum = jnp.stack([steps_of.finish() for steps_of in far_parts])
    grad_attn_in = tie(own_part, *sent) + far_sum
    normed_one, inverse_one = jnp.stack(normed_all), jnp.stack(inverse_all)
    grad_shift_one = jnp.sum(grad_attn_in, axis=1)
    grad_scale_one = jnp.sum(grad_attn_in * normed_one, axis=1)
    grad_inputs = grad_mixed + norm_back(normed_one, inverse_one, grad_attn_in * (1.0 + scale_one))
    grad_inputs = grad_inputs.astype(BF).reshape(tokens.shape)

    grad_mod_local = jnp.concatenate(
        [grad_shift_one, grad_scale_one, grad_gate_one, grad_shift_two, grad_scale_two, grad_gate_two], axis=-1
    )
    bias_ada = jnp.sum(grad_mod_local, axis=0)
    sent = jnp.transpose(grad_mod_local.reshape(count, dp, 1, ada_cols), (1, 2, 0, 3))
    sent = jnp.broadcast_to(sent, (dp, seq, count, ada_cols))
    mod_parts = net.to_all(sent)
    sent = back_qkv.advance(sent)
    sums = early.finish(sent[0])
    chain = Staged(
        net.muon_steps(
            [(sums[1], [turned[1], turned[2]]), (sums[0], [turned[3]])],
            [w_proj.T, w_fc1.T, w_fc2.T],
            [1.0, math.sqrt(hidden / width), math.sqrt(width / hidden)],
        )
    )
    anchor = chain.advance()[0]
    while not back_qkv.done:
        sent = back_qkv.advance(anchor)
        if sent:
            mod_parts = tie(mod_parts, *sent)
            anchor = (chain.advance(sent[0]) or sent)[0]
    mod_cols = jnp.sum(mod_parts, axis=1).astype(BF).reshape(dp * count, ada_cols)
    shard_ada = jnp.einsum("sr,sc->cr", cond_all, mod_cols, preferred_element_type=F32)

    last = Staged(
        net.muon_steps(
            [
                (back_qkv.result, [turned[0]]),
                (shard_ada, [turned[4]]),
            ],
            [w_qkv.T, w_ada.T],
            [math.sqrt(3.0), math.sqrt(6.0)],
        )
    )
    sent = last.advance()

    cond_part = jnp.einsum("sc,rc->sr", mod_cols, low_ada, preferred_element_type=F32)
    cond_part = jnp.broadcast_to(cond_part.reshape(dp, 1, -1), (dp, seq, count * ada_rows))
    term_bias = jnp.concatenate([bias_ada, bias_q, bias_v, bias_proj, bias_fc1, bias_fc2])
    parcel = jnp.concatenate([term_bias.reshape(dp, seq, -1), cond_part], axis=-1)
    parcel = net.to_all(tie(parcel, *sent))
    while not last.done:
        anchor = sent[0] if sent else None
        sent = last.advance(anchor)
        sent = sent + chain.advance(sent[0] if sent else None)
    chain.finish()
    (next_qkv, next_ada), (new_qkv, new_ada) = last.result
    (next_proj, next_fc1, next_fc2), (new_proj, new_fc1, new_fc2) = chain.result

    size = biases.shape[0]
    grad_bias = jnp.sum(parcel[..., :size], axis=(0, 1))
    cond_part = jnp.sum(parcel[..., size:], axis=0).reshape(seq, count, ada_rows)
    grad_cond = silu_back(jnp.transpose(cond_part, (1, 0, 2)).reshape(count, width))[0]
    next_first = BETA_FIRST * bias_first + (1.0 - BETA_FIRST) * grad_bias
    next_second = BETA_SECOND * bias_second + (1.0 - BETA_SECOND) * grad_bias * grad_bias
    first_hat = next_first / (1.0 - BETA_FIRST**STEP_COUNT)
    second_hat = next_second / (1.0 - BETA_SECOND**STEP_COUNT)
    new_biases = biases * (1.0 - ADAM_RATE * ADAM_DECAY) - ADAM_RATE * first_hat / (
        jnp.sqrt(second_hat) + ADAM_EPS
    )
    return (
        result.reshape(tokens.shape),
        grad_inputs,
        grad_cond.reshape(conditioning.shape),
        new_qkv.T, new_proj.T, new_fc1.T, new_fc2.T, new_ada.T,
        next_qkv.T, next_proj.T, next_fc1.T, next_fc2.T, next_ada.T,
        new_biases,
        next_first,
        next_second,
    )


def solution(mesh):
    rows = P(None, "dp", "seq", None)
    matrix = P("seq", "dp")
    flat = P(("dp", "seq"))
    in_specs = (rows, P(None, "dp", None), P(None, "dp"), P(None, "dp"), rows) + (matrix,) * 10 + (flat,) * 3
    out_specs = (rows, rows, P(None, "dp", None)) + (matrix,) * 10 + (flat,) * 3
    return jax.shard_map(
        functools.partial(body, Net(mesh)), mesh=mesh, in_specs=in_specs, out_specs=out_specs, check_vma=False
    )
```

```python
import functools
import math

import jax
import jax.numpy as jnp
from jax import lax
from jax.experimental import pallas as pl
from jax.experimental.pallas import tpu as pltpu
from jax.sharding import PartitionSpec as P

HEADS = 16
ROW_BLOCK = 144
NS_STEPS = 5
STEP_COUNT = 10

PRECISE = lax.Precision.HIGHEST
LN_EPS = 1e-06
MASKED = -1e30
NS_A = 3.4445
NS_B = -4.775
NS_C = 2.0315
MUON_DECAY = 0.5
WEIGHT_SHRINK = 0.0001
NORM_EPS = 1e-07
BETA_FIRST = 0.9
BETA_SECOND = 0.999
ADAM_RATE = 0.1
ADAM_DECAY = 0.01
ADAM_EPS = 1e-08
BF = jnp.bfloat16
F32 = jnp.float32
VMEM_LIMIT = 60 * 2**20


class Ring:
    def __init__(self, name, total, stride, size):
        self.name, self.total, self.stride, self.size = name, total, stride, size

    def digit(self):
        return (lax.axis_index(self.name) // self.stride) % self.size

    def send(self, value, shift):
        pairs = []
        for i in range(self.total):
            d = (i // self.stride) % self.size
            pairs.append((i, i + ((d + shift) % self.size - d) * self.stride))
        return lax.ppermute(value, self.name, pairs)

    def gather(self, value, far=1):
        n = self.size
        blocks = [value] + [None] * (n - 1)
        if n == 2:
            blocks[1] = self.send(value, 1)
        elif n > 2:
            low = high = value
            for t in range(1, n // 2):
                low, high = self.send(low, 1), self.send(high, -1)
                blocks[n - t], blocks[t] = low, high
            blocks[n // 2] = self.send(low, 1) if far == 1 else self.send(high, -1)
        return blocks

    def gather_steps(self, value, far=1):
        n = self.size
        blocks = [value] + [None] * (n - 1)
        if n == 2:
            blocks[1] = self.send(value, 1)
            anchor = yield [value]
            blocks[1] = tie(blocks[1], anchor)
            return blocks
        low = high = value
        for t in range(1, n // 2):
            sent = [low, high]
            low, high = self.send(low, 1), self.send(high, -1)
            anchor = yield sent
            low, high = tie(low, anchor), tie(high, anchor)
            blocks[n - t], blocks[t] = low, high
        sent = [low if far == 1 else high]
        last = self.send(sent[0], far)
        anchor = yield sent
        blocks[n // 2] = tie(last, anchor)
        return blocks

    def scatter_steps(self, block_of, far=1):
        n = self.size
        if n == 1:
            return block_of(0).astype(F32)
        if n == 2:
            sent = block_of(1)
            got = self.send(sent, 1)
            anchor = yield [sent]
            return block_of(0).astype(F32) + tie(got, anchor).astype(F32)
        sent = block_of(n // 2)
        got = self.send(sent, far)
        anchor = yield [sent]
        low, high = (tie(got, anchor), None) if far == 1 else (None, tie(got, anchor))
        for t in range(n // 2 - 1, 0, -1):
            up, down = block_of(t), block_of(n - t)
            if low is not None:
                up = (up.astype(F32) + low.astype(F32)).astype(up.dtype)
            if high is not None:
                down = (down.astype(F32) + high.astype(F32)).astype(down.dtype)
            low, high = self.send(up, 1), self.send(down, -1)
            anchor = yield [up, down]
            low, high = tie(low, anchor), tie(high, anchor)
        return block_of(0).astype(F32) + low.astype(F32) + high.astype(F32)


def tie(value, *earlier):
    earlier = [array for array in earlier if array is not None]
    if not earlier:
        return value
    anywhere = pl.BlockSpec(memory_space=pl.ANY)
    return pl.pallas_call(
        lambda *refs: None,
        out_shape=jax.ShapeDtypeStruct(value.shape, value.dtype),
        in_specs=[anywhere] * (1 + len(earlier)),
        out_specs=anywhere,
        input_output_aliases={0: 0},
        name="tie",
    )(value, *earlier)


def lockstep(*steps):
    results = [None] * len(steps)
    alive = dict(enumerate(steps))
    anchor = None
    while alive:
        sent = []
        for n, step in list(alive.items()):
            try:
                sent += step.send(anchor)
            except StopIteration as stop:
                results[n] = stop.value
                del alive[n]
        if alive:
            anchor = yield sent
    return results


class Staged:
    def __init__(self, steps):
        self.steps, self.result, self.started, self.done = steps, None, False, False

    def advance(self, anchor=None):
        if self.done:
            return []
        try:
            sent = self.steps.send(anchor if self.started else None)
            self.started = True
            return sent
        except StopIteration as stop:
            self.result, self.done = stop.value, True
            return []

    def finish(self, anchor=None):
        while not self.done:
            self.advance(anchor)
        return self.result


def place_kernel(zs, ga, parts, count, outs, *refs):
    spots, sources = refs[0], refs[1 : 1 + count]
    outputs, (full, in_sems, out_sems) = refs[1 + count : 1 + count + outs], refs[1 + count + outs :]
    g = full.shape[3]
    half = count // 2
    shards = []
    for sc in range(2):
        for sx in range(2):
            for sz in range(zs):
                where = (lax.rem(spots[0] + sz, zs), lax.rem(spots[1] + sx, 2), lax.rem(spots[2] + sc, 2))
                n = 2 * len(shards)
                line, pair = sources[sc * half + sx].at[sz], sources[sc * half + 2 + sz].at[sx]
                copies = [
                    pltpu.make_async_copy(line, full.at[(*where, pl.ds(0, ga))], in_sems.at[n]),
                    pltpu.make_async_copy(pair, full.at[(*where, pl.ds(ga, g - ga))], in_sems.at[n + 1]),
                ]
                for copy in copies:
                    copy.start()
                shards.append((where, copies))
    exits = []
    for where, copies in shards:
        for copy in copies:
            copy.wait()
        for output, start, size, column, depth in parts:
            target = outputs[output].at[(*where, slice(None), slice(None), pl.ds(column, depth))]
            copy = pltpu.make_async_copy(
                full.at[(*where, pl.ds(start, size))], target, out_sems.at[len(exits)]
            )
            copy.start()
            exits.append(copy)
    for copy in exits:
        copy.wait()


def place(spots, sources, shape, ga, parts, shapes):
    zs = shape[0]
    moved = math.prod(shape) * 2
    return pl.pallas_call(
        functools.partial(place_kernel, zs, ga, parts, len(sources), len(shapes)),
        out_shape=[jax.ShapeDtypeStruct(each, BF) for each in shapes],
        in_specs=[pl.BlockSpec(memory_space=pltpu.SMEM)]
        + [pl.BlockSpec(memory_space=pl.ANY)] * len(sources),
        out_specs=[pl.BlockSpec(memory_space=pl.ANY)] * len(shapes),
        scratch_shapes=[
            pltpu.VMEM(shape, BF),
            pltpu.SemaphoreType.DMA((8 * zs,)),
            pltpu.SemaphoreType.DMA((4 * zs * len(parts),)),
        ],
        compiler_params=pltpu.CompilerParams(vmem_limit_bytes=VMEM_LIMIT),
        cost_estimate=pl.CostEstimate(flops=0, bytes_accessed=2 * moved, transcendentals=0),
        name="place",
    )(spots, *sources)


class Net:
    def __init__(self, mesh):
        dp, seq = mesh.shape["dp"], mesh.shape["seq"]
        self.dp, self.seq = dp, seq
        self.core = Ring("dp", dp, 1, 2)
        self.x = Ring("dp", dp, 2, 2)
        self.z = Ring("dp", dp, 4, dp // 4)
        self.y = Ring("seq", seq, 1, seq)

    def spots(self):
        return jnp.stack([self.z.digit(), self.x.digit(), self.core.digit()]).astype(jnp.int32)


    def wire(self, shards):
        turned = [shard.astype(BF).T for shard in shards]
        return turned[0] if len(turned) == 1 else jnp.concatenate(turned, axis=0)

    def rows(self, wires):
        if self.seq == 2:
            own, other = wires
            return jnp.where(
                self.y.digit() == 0,
                jnp.concatenate([own, other], axis=1),
                jnp.concatenate([other, own], axis=1),
            )
        order = (jnp.arange(self.seq) - self.y.digit()) % self.seq
        full = jnp.take(jnp.stack(wires), order, axis=0)
        return jnp.transpose(full, (1, 0, 2)).reshape(full.shape[1], -1)

    def joined(self, wires, unit, depth):
        full = self.rows(wires)
        return full.reshape(full.shape[0] // unit, unit, depth)

    def scatter(self, term):
        return lax.psum_scatter(term, "dp", scatter_dimension=0, tiled=True)

    def halves_steps(self, term):
        y = self.y.digit()
        blocks = term.reshape(term.shape[0], self.seq, -1)
        return (
            yield from self.y.scatter_steps(
                lambda s: lax.dynamic_index_in_dim(blocks, (y + s) % self.seq, 1, keepdims=False)
            )
        )

    def gather_steps(self, units, layout, part):
        g, unit, depth = units.shape
        zs = self.z.size
        ga = max(1, int(part * g))
        first, second = units[:ga], units[ga:]

        def line_steps():
            blocks = yield from self.z.gather_steps(first, 1)
            line = jnp.stack(blocks)
            return (yield from self.x.gather_steps(line))

        def pair_steps():
            blocks = yield from self.x.gather_steps(second)
            return (yield from self.z.gather_steps(jnp.stack(blocks), -1))

        lines, pairs = yield from lockstep(line_steps(), pair_steps())
        pieces = lines + pairs
        others = [self.core.send(piece, 1) for piece in pieces]
        anchor = yield pieces
        sources = pieces + [tie(other, anchor) for other in others]
        parts, shapes, start = [], [], 0
        for n, (rows, blocks) in enumerate(layout):
            size = rows // unit
            shapes.append((zs, 2, 2, size, unit, blocks * depth))
            for j in range(blocks):
                parts.append((n, start, size, j * depth, depth))
                start += size
        full = place(self.spots(), sources, (zs, 2, 2, g, unit, depth), ga, parts, shapes)
        return [f.reshape(-1, f.shape[-1]) for f in full], lines[1:] + pairs[1:]


    def muon_scatter_steps(self, groups, spread):
        momenta, own, other = muon_gram(self.spots(), self.z.size, groups, spread)
        got = self.core.send(other, 1)
        anchor = yield [other]
        half = own + tie(got, anchor)
        sent = half[1]
        got = self.x.send(sent, 1)
        anchor = yield [sent]
        kept = half[0] + tie(got, anchor)
        blocks = [kept[shift] for shift in range(self.z.size)]
        got = [self.z.send(blocks[shift], shift) for shift in range(1, self.z.size)]
        anchor = yield blocks[1:]
        return momenta, [blocks[0]] + [tie(each, anchor) for each in got]

    def muon_gather_steps(self, parts):
        factor = polynomial(parts)
        got = [self.z.send(factor, -shift) for shift in range(1, self.z.size)]
        anchor = yield [factor]
        line = jnp.stack([factor] + [tie(each, anchor) for each in got])
        got = self.x.send(line, 1)
        anchor = yield [line]
        pair = [line, tie(got, anchor)]
        others = [self.core.send(each, 1) for each in pair]
        anchor = yield pair
        return pair + [tie(each, anchor) for each in others]


    def to_all(self, value):
        flat = value.reshape((self.dp * self.seq,) + value.shape[2:])
        return lax.all_to_all(flat, ("dp", "seq"), 0, 0, tiled=True).reshape(value.shape)

    def to_dp(self, value):
        return lax.all_to_all(value, "dp", 0, 0, tiled=True)


def layer_norm(values):
    centered = values - jnp.mean(values, axis=-1, keepdims=True)
    inverse = lax.rsqrt(jnp.mean(centered * centered, axis=-1, keepdims=True) + LN_EPS)
    return (centered * inverse, inverse)


def norm_back(normed, inverse, grad):
    mean_grad = jnp.mean(grad, axis=-1, keepdims=True)
    mean_cross = jnp.mean(grad * normed, axis=-1, keepdims=True)
    return inverse * (grad - mean_grad - normed * mean_cross)


def sigmoid_linear(values):
    return values * jax.nn.sigmoid(values)


def gelu_tanh(values):
    return jax.nn.gelu(values, approximate=True)


def dot_t(left, right):
    return jnp.einsum("srk,nk->srn", left, right, preferred_element_type=F32)


def dot(left, right):
    return jnp.einsum("srn,nk->srk", left, right, preferred_element_type=F32)


def outer(left, right):
    return jnp.einsum("srn,srk->nk", left, right, preferred_element_type=F32).astype(BF)


def shard_outer_kernel(plan, counts, tile, split, spots_ref, *refs):
    outs = 2 if split else 1
    inputs, where = refs[: counts[0]], refs[counts[1] : counts[1] + outs]
    buffers = refs[counts[1] + outs : counts[1] + outs + len(plan["loads"])]
    acc, in_sems, out_sems = refs[counts[1] + outs + len(plan["loads"]) :]
    loads = []
    for n, (sources, start, size) in enumerate(plan["loads"]):
        row, copies = 0, []
        for m, source in enumerate(sources):
            rows = inputs[source].shape[0]
            window = inputs[source].at[:, pl.ds(start, size)]
            copies.append(pltpu.make_async_copy(window, buffers[n].at[pl.ds(row, rows)], in_sems.at[n, m]))
            copies[-1].start()
            row += rows
        loads.append(copies)
    ready = set()
    shipped = []
    unit = acc.shape[1]
    for left, right, base, ships in plan["parts"]:
        for n in (left, right):
            if n not in ready:
                for copy in loads[n]:
                    copy.wait()
                ready.add(n)
        width = buffers[left].shape[1]
        step = tile if width % tile == 0 else width

        @pl.loop(0, width // step)
        def _(t):
            block = buffers[left][:, pl.ds(pl.multiple_of(t * step, step), step)]
            product = lax.dot_general(
                block, buffers[right][...], (((0,), (0,)), ((), ())), preferred_element_type=F32
            )
            product = product.reshape(step // unit, unit, product.shape[1]).astype(BF)
            acc[pl.ds(base + t * (step // unit), step // unit)] = product

        for core, z, x, row, target, size in ships:
            spot = (z, x) if split else (z, x, core)
            places = [ref.at[(*spot, pl.ds(target, size))] for ref in where]
            copies = [
                pltpu.make_async_copy(acc.at[pl.ds(row, size)], each, out_sems.at[len(shipped)]) for each in places
            ]
            shipped.append((core, copies))
            on_own_core(split, spots_ref, core, [copy.start for copy in copies])
    for core, copies in shipped:
        on_own_core(split, spots_ref, core, [copy.wait for copy in copies])


def on_own_core(split, spots_ref, core, actions):
    if not split:
        actions[0]()
        return

    @pl.when(spots_ref[2] == core)
    def _():
        actions[0]()

    @pl.when(spots_ref[2] != core)
    def _():
        actions[1]()


def shard_outer(spots, inputs, loads, parts, zs, depth, unit, shard_units, deps=(), tile=384, split=True):
    dp = zs * 4
    plan_parts, base, row, placed = [], 0, 0, {}
    begun = {}
    for left, right, rows, first in parts:
        if first not in begun:
            begun[first] = (base, 0)
        start, shipped = begun[first]
        width = loads[left][2]
        size = rows // unit
        end = base + width // unit
        ships = []
        while shipped < dp and start + (shipped + 1) * size <= end:
            core, x, z = shipped % 2, shipped // 2 % 2, shipped // 4
            ships.append((core, z, x, start + shipped * size, first, size))
            shipped += 1
        begun[first] = (start, shipped)
        plan_parts.append((left, right, base, ships))
        base = end
    total = sum(len(part[3]) for part in plan_parts)
    shape = (zs, 2, shard_units, unit, depth) if split else (zs, 2, 2, shard_units, unit, depth)
    outs = [jax.ShapeDtypeStruct(shape, BF)] * (2 if split else 1)
    anywhere = pl.BlockSpec(memory_space=pl.ANY)
    heights = [sum(inputs[source].shape[0] for source in sources) for sources, _, _ in loads]
    flops = sum(2 * heights[p[0]] * loads[p[0]][2] * loads[p[1]][2] for p in parts)
    return pl.pallas_call(
        functools.partial(
            shard_outer_kernel, {"loads": loads, "parts": plan_parts}, (len(inputs), len(inputs) + len(deps)), tile, split
        ),
        out_shape=outs,
        in_specs=[pl.BlockSpec(memory_space=pltpu.SMEM)] + [anywhere] * (len(inputs) + len(deps)),
        out_specs=[anywhere] * len(outs),
        scratch_shapes=[pltpu.VMEM((height, load[2]), BF) for height, load in zip(heights, loads)]
        + [
            pltpu.VMEM((base, unit, depth), BF),
            pltpu.SemaphoreType.DMA((len(loads), max(len(load[0]) for load in loads))),
            pltpu.SemaphoreType.DMA((total,)),
        ],
        compiler_params=pltpu.CompilerParams(vmem_limit_bytes=VMEM_LIMIT),
        cost_estimate=pl.CostEstimate(flops=flops, bytes_accessed=2 * base * unit * depth, transcendentals=0),
        name="shard_outer",
    )(spots, *inputs, *deps)


LANES = 128
LOG2E = math.log2(math.e)


def padded(block, column=None):
    rows, depth = block.shape
    if column is None:
        return jnp.concatenate([block, jnp.zeros((rows, LANES - depth), block.dtype)], axis=1)
    rest = jnp.zeros((rows, LANES - depth - 1), block.dtype)
    return jnp.concatenate([block, column.astype(block.dtype), rest], axis=1)


def mask_column(lengths_ref, offsets_ref, sample, total, rows):
    place = lax.broadcasted_iota(jnp.int32, (total, 1), 0)
    position = place
    for s in range(total // rows):
        position = jnp.where(place // rows == s, place - s * rows + offsets_ref[s], position)
    return jnp.where(position < lengths_ref[sample], 0.0, MASKED)


def nt(left, right):
    return lax.dot_general(left, right, (((1,), (1,)), ((), ())), preferred_element_type=F32)


def nn(left, right):
    return jnp.dot(left, right, preferred_element_type=F32)


def without(kernel, start, count, *fixed):
    def run(*refs):
        kernel(*fixed, *refs[:start], *refs[start + count :])

    return run


def attend_kernel(heads, chunk, lengths_ref, offsets_ref, q_ref, k_ref, v_ref, o_ref, lse_ref, q_s, k_s, vt_s, o_s):
    rows, width = q_ref.shape[1:]
    total = k_ref.shape[1]
    depth = width // heads
    factor = depth**-0.5 * LOG2E
    mask = mask_column(lengths_ref, offsets_ref, pl.program_id(0), total, rows)
    ones = jnp.ones((rows, 1), F32)
    for h in range(heads):
        span = slice(h * depth, (h + 1) * depth)
        q_s[h] = padded(q_ref[0, :, span], ones)
        k_s[h] = padded(k_ref[0, :, span], mask)
        vt_s[h] = jnp.transpose(v_ref[0, :, span])

    def one_head(h, carry):
        peak = jnp.full((1, rows), MASKED, F32)
        sums = jnp.zeros((1, rows), F32)
        mixed = jnp.zeros((depth, rows), F32)
        for c in range(total // chunk):
            part = slice(c * chunk, (c + 1) * chunk)
            scores = nt(k_s[h, part], q_s[h])
            higher = jnp.maximum(peak, jnp.max(scores, axis=0, keepdims=True))
            weights = jnp.exp2((scores - higher) * factor)
            if c == 0:
                sums = jnp.sum(weights, axis=0, keepdims=True)
                mixed = nn(vt_s[h, :, part], weights.astype(BF))
            else:
                shrink = jnp.exp2((peak - higher) * factor)
                sums = sums * shrink + jnp.sum(weights, axis=0, keepdims=True)
                mixed = mixed * shrink + nn(vt_s[h, :, part], weights.astype(BF))
            peak = higher
        o_s[h] = jnp.transpose(mixed / sums)
        lse_ref[0, h] = peak * factor + jnp.log2(sums)
        return carry

    lax.fori_loop(0, heads, one_head, 0)
    for h in range(heads):
        o_ref[0, :, h * depth : (h + 1) * depth] = o_s[h].astype(BF)


def attend(lengths, offsets, queries, keys, values, heads, tile, deps=()):
    count, rows, width = queries.shape
    total = keys.shape[1]
    depth = width // heads
    tile = min(tile, total)
    pick = lambda i, *_: (i, 0, 0)
    return pl.pallas_call(
        without(attend_kernel, 5, len(deps), heads, tile),
        grid_spec=pltpu.PrefetchScalarGridSpec(
            num_scalar_prefetch=2,
            grid=(count,),
            in_specs=[
                pl.BlockSpec((1, rows, width), pick),
                pl.BlockSpec((1, total, width), pick),
                pl.BlockSpec((1, total, width), pick),
            ]
            + [pl.BlockSpec(memory_space=pl.ANY)] * len(deps),
            out_specs=[
                pl.BlockSpec((1, rows, width), pick),
                pl.BlockSpec((1, heads, 1, rows), lambda i, *_: (i, 0, 0, 0)),
            ],
            scratch_shapes=[
                pltpu.VMEM((heads, rows, LANES), BF),
                pltpu.VMEM((heads, total, LANES), BF),
                pltpu.VMEM((heads, depth, total), BF),
                pltpu.VMEM((heads, rows, depth), F32),
            ],
        ),
        out_shape=[
            jax.ShapeDtypeStruct((count, rows, width), BF),
            jax.ShapeDtypeStruct((count, heads, 1, rows), F32),
        ],
        compiler_params=pltpu.CompilerParams(vmem_limit_bytes=VMEM_LIMIT),
        cost_estimate=pl.CostEstimate(
            flops=4 * count * heads * rows * total * LANES,
            bytes_accessed=2 * count * width * (2 * rows + 2 * total),
            transcendentals=count * heads * rows * total,
        ),
        name="attend",
    )(lengths, offsets, queries, keys, values, *deps)


def attend_back_kernel(
    heads, chunk, lengths_ref, offsets_ref, q_ref, k_ref, v_ref, o_ref, g_ref, lse_ref,
    dq_ref, dk_ref, dv_ref, q_s, k_s, kt_s, v_s, g_s, delta_s, dq_s, dk_s, dv_s
):
    rows, width = q_ref.shape[1:]
    total = k_ref.shape[1]
    depth = width // heads
    scale = depth**-0.5
    factor = scale * LOG2E
    mask = mask_column(lengths_ref, offsets_ref, pl.program_id(0), total, rows)
    ones = jnp.ones((rows, 1), F32)
    cross = jnp.transpose(g_ref[0].astype(F32) * o_ref[0].astype(F32))
    for h in range(heads):
        span = slice(h * depth, (h + 1) * depth)
        delta_s[h] = jnp.sum(cross[span], axis=0, keepdims=True)
        q_s[h] = padded(q_ref[0, :, span], ones)
        k_s[h] = padded(k_ref[0, :, span], mask)
        kt_s[h] = jnp.transpose(k_ref[0, :, span])
        g_s[h] = padded(g_ref[0, :, span])
        v_s[h] = padded(v_ref[0, :, span])

    def one_head(h, carry):
        dq = jnp.zeros((depth, rows), F32)
        for c in range(total // chunk):
            part = slice(c * chunk, (c + 1) * chunk)
            probs = jnp.exp2(nt(k_s[h, part], q_s[h]) * factor - lse_ref[0, h])
            slopes = (probs * (nt(v_s[h, part], g_s[h]) - delta_s[h])).astype(BF)
            dv_s[h, part] = nn(probs.astype(BF), g_s[h]).astype(BF)
            dk_s[h, part] = (nn(slopes, q_s[h]) * scale).astype(BF)
            dq = dq + nn(kt_s[h, :, part], slopes)
        dq_s[h] = jnp.transpose(dq * scale)
        return carry

    lax.fori_loop(0, heads, one_head, 0)
    for h in range(heads):
        span = slice(h * depth, (h + 1) * depth)
        dq_ref[0, :, span] = dq_s[h].astype(BF)
        dk_ref[0, :, span] = dk_s[h][:, :depth]
        dv_ref[0, :, span] = dv_s[h][:, :depth]


def attend_back(lengths, offsets, queries, keys, values, mixed, grads, lse, heads, tile, deps=()):
    count, rows, width = queries.shape
    total = keys.shape[1]
    depth = width // heads
    tile = min(tile, total)
    pick = lambda i, *_: (i, 0, 0)
    near = pl.BlockSpec((1, rows, width), pick)
    far = pl.BlockSpec((1, total, width), pick)
    return pl.pallas_call(
        without(attend_back_kernel, 8, len(deps), heads, tile),
        grid_spec=pltpu.PrefetchScalarGridSpec(
            num_scalar_prefetch=2,
            grid=(count,),
            in_specs=[near, far, far, near, near, pl.BlockSpec((1, heads, 1, rows), lambda i, *_: (i, 0, 0, 0))]
            + [pl.BlockSpec(memory_space=pl.ANY)] * len(deps),
            out_specs=[near, far, far],
            scratch_shapes=[
                pltpu.VMEM((heads, rows, LANES), BF),
                pltpu.VMEM((heads, total, LANES), BF),
                pltpu.VMEM((heads, depth, total), BF),
                pltpu.VMEM((heads, total, LANES), BF),
                pltpu.VMEM((heads, rows, LANES), BF),
                pltpu.VMEM((heads, 1, rows), F32),
                pltpu.VMEM((heads, rows, depth), F32),
                pltpu.VMEM((heads, total, LANES), BF),
                pltpu.VMEM((heads, total, LANES), BF),
            ],
        ),
        out_shape=[
            jax.ShapeDtypeStruct((count, rows, width), BF),
            jax.ShapeDtypeStruct((count, total, width), BF),
            jax.ShapeDtypeStruct((count, total, width), BF),
        ],
        compiler_params=pltpu.CompilerParams(vmem_limit_bytes=VMEM_LIMIT),
        cost_estimate=pl.CostEstimate(
            flops=10 * count * heads * rows * total * LANES,
            bytes_accessed=2 * count * width * (4 * rows + 4 * total),
            transcendentals=count * heads * rows * total,
        ),
        name="attend_back",
    )(lengths, offsets, queries, keys, values, mixed, grads, lse, *deps)


def block_spots(counts, spread):
    per, first = spread
    spots = []
    for matrix, count in enumerate(counts):
        for block in range(count):
            device, place_in = divmod(len(spots), per)
            device += first
            spots.append((matrix, block, device // 4, device // 2 % 2, device % 2, place_in))
    return spots


def precise(left, right, dims):
    return lax.dot_general(left, right, (dims, ((), ())), precision=PRECISE, preferred_element_type=F32)


def muon_gram_kernel(groups, spread, spots_ref, *refs):
    count = sum(groups)
    sums, momenta = refs[: len(groups)], refs[len(groups) : len(groups) + count]
    outs = refs[len(groups) + count : len(groups) + 2 * count]
    own_ref, other_ref = refs[len(groups) + 2 * count :]
    n = 0
    for matrices, sum_ref in zip(groups, sums):
        start = 0
        for _ in range(matrices):
            size = momenta[n].shape[0]
            outs[n][...] = MUON_DECAY * momenta[n][...] + sum_ref[start : start + size]
            start += size
            n += 1
    zs = own_ref.shape[1]
    spots = block_spots([out.shape[1] // ROW_BLOCK for out in outs], spread)
    own_ref[...] = jnp.zeros_like(own_ref)
    other_ref[...] = jnp.zeros_like(other_ref)
    for matrix, block, z, x, core, place_in in spots:
        turned = outs[matrix][:, block * ROW_BLOCK : (block + 1) * ROW_BLOCK]
        gram = precise(turned, turned, ((0,), (0,)))
        away = (lax.rem(spots_ref[1] + x, 2), lax.rem(zs + z - spots_ref[0], zs), place_in)

        @pl.when(spots_ref[2] == core)
        def _():
            own_ref[away] = gram

        @pl.when(spots_ref[2] != core)
        def _():
            other_ref[away] = gram


def muon_gram(spots, zs, groups, spread):
    momenta = [momentum for _, each in groups for momentum in each]
    grams = jax.ShapeDtypeStruct((2, zs, spread[0], ROW_BLOCK, ROW_BLOCK), F32)
    vmem = pl.BlockSpec(memory_space=pltpu.VMEM)
    outs = pl.pallas_call(
        functools.partial(muon_gram_kernel, [len(each) for _, each in groups], spread),
        out_shape=[jax.ShapeDtypeStruct(momentum.shape, F32) for momentum in momenta] + [grams, grams],
        in_specs=[pl.BlockSpec(memory_space=pltpu.SMEM)] + [vmem] * (len(groups) + len(momenta)),
        out_specs=[vmem] * (len(momenta) + 2),
        compiler_params=pltpu.CompilerParams(vmem_limit_bytes=VMEM_LIMIT),
        name="muon_gram",
    )(spots, *[group[0] for group in groups], *momenta)
    return outs[:-2], outs[-2], outs[-1]


def polynomial_kernel(count, *refs):
    out = refs[count]
    shape = (ROW_BLOCK, ROW_BLOCK)
    eye = (lax.broadcasted_iota(jnp.int32, shape, 0) == lax.broadcasted_iota(jnp.int32, shape, 1)).astype(F32)
    mul = lambda left, right: precise(left, right, ((1,), (0,)))
    blocks = range(out.shape[0])
    currents, scales, totals = [], [], []
    for n in blocks:
        gram = refs[0][n]
        for ref in refs[1:count]:
            gram = gram + ref[n]
        square = jnp.sum(jnp.sum(gram * eye, axis=1, keepdims=True), axis=0, keepdims=True)
        scale = 1.0 / (jnp.sqrt(square) + NORM_EPS)
        scales.append(scale)
        currents.append(gram * (scale * scale))
    for step in range(NS_STEPS):
        factors = [NS_A * eye + NS_B * a + NS_C * mul(a, a) for a in currents]
        totals = factors if step == 0 else [mul(f, t) for f, t in zip(factors, totals)]
        if step + 1 < NS_STEPS:
            currents = [mul(f, a) for f, a in zip(factors, currents)]
            currents = [mul(a, f) for f, a in zip(factors, currents)]
    for n in blocks:
        out[n] = totals[n] * scales[n]


def polynomial(parts):
    vmem = pl.BlockSpec(memory_space=pltpu.VMEM)
    return pl.pallas_call(
        functools.partial(polynomial_kernel, len(parts)),
        out_shape=jax.ShapeDtypeStruct(parts[0].shape, F32),
        in_specs=[vmem] * len(parts),
        out_specs=vmem,
        compiler_params=pltpu.CompilerParams(vmem_limit_bytes=VMEM_LIMIT),
        name="polynomial",
    )(*parts)


def muon_apply_kernel(rates, spread, spots_ref, *refs):
    count = len(rates)
    parts, momenta, masters = refs[:4], refs[4 : 4 + count], refs[4 + count : 4 + 2 * count]
    outs, factors = refs[4 + 2 * count : 4 + 3 * count], refs[4 + 3 * count]
    for n in range(4):
        factors[n] = parts[n][...]
    zs = factors.shape[1]
    spots = block_spots([momentum.shape[1] // ROW_BLOCK for momentum in momenta], spread)
    for matrix, block, z, x, core, place_in in spots:
        part = slice(block * ROW_BLOCK, (block + 1) * ROW_BLOCK)
        away = 2 * lax.rem(spots_ref[2] + core, 2) + lax.rem(spots_ref[1] + x, 2)
        factor = factors[away, lax.rem(zs + z - spots_ref[0], zs), place_in]
        direction = precise(momenta[matrix][:, part], factor, ((1,), (1,)))
        outs[matrix][:, part] = masters[matrix][:, part] * (1.0 - WEIGHT_SHRINK) - rates[matrix] * direction


def muon_apply(spots, factors, momenta, masters, rates, spread):
    vmem = pl.BlockSpec(memory_space=pltpu.VMEM)
    return pl.pallas_call(
        functools.partial(muon_apply_kernel, rates, spread),
        out_shape=[jax.ShapeDtypeStruct(master.shape, F32) for master in masters],
        in_specs=[pl.BlockSpec(memory_space=pltpu.SMEM)] + [vmem] * (4 + 2 * len(masters)),
        out_specs=[vmem] * len(masters),
        scratch_shapes=[pltpu.VMEM((4,) + factors[0].shape, F32)],
        compiler_params=pltpu.CompilerParams(vmem_limit_bytes=VMEM_LIMIT),
        name="muon_apply",
    )(spots, *factors, *momenta, *masters)


def body(net, tokens, conditioning, heights, widths, upstream, *state):
    masters, momenta = state[0:5], state[5:10]
    biases, bias_first, bias_second = state[10:13]
    w_qkv, w_proj, w_fc1, w_fc2, w_ada = masters
    micro, local, rows, width = tokens.shape
    count = micro * local
    head_dim = width // HEADS
    hidden = w_fc1.shape[1] * net.dp
    seq, dp = net.seq, net.dp
    y = net.y.digit()

    bounds = [0, 6 * width, 7 * width, 8 * width, 9 * width, 9 * width + hidden, 10 * width + hidden]

    n_qkv, n_proj, n_fc1, n_fc2 = [w.shape[1] for w in (w_qkv, w_proj, w_fc1, w_fc2)]
    unit = math.gcd(math.gcd(n_qkv, n_proj), 8)
    unit_qkv, layout_qkv = math.gcd(n_qkv, 8), [(n_qkv, 1)]
    own_tokens = tokens.reshape(count, rows, width)
    wires = net.y.gather(net.wire([w_qkv, w_proj]))

    ada_rows, ada_cols = w_ada.shape
    cond = conditioning.astype(F32).reshape(count, width)
    cond_act, silu_back = jax.vjp(sigmoid_linear, cond)
    cond_low = cond_act.astype(BF).astype(F32)
    cond_parts = jnp.transpose(cond_low.reshape(count, seq, ada_rows), (1, 0, 2)).reshape(seq, -1)
    parcel = jnp.concatenate([jnp.broadcast_to(biases, (seq,) + biases.shape), cond_parts], axis=1)
    parcel = net.to_all(tie(jnp.broadcast_to(parcel[None], (dp,) + parcel.shape), wires[0]))
    cond_all = parcel[:, 0, biases.shape[0] :].reshape(dp * count, ada_rows).astype(BF)
    first = Staged(net.gather_steps(net.joined(wires, unit, width), [(n_qkv, 1), (n_proj, 1)], 0.45))
    sent = first.advance()
    token_pieces = [net.y.gather(tie(own_tokens[0], *sent))]

    low_ada = w_ada.astype(BF)
    partial = jnp.dot(tie(cond_all, *sent), low_ada, preferred_element_type=F32).reshape(dp, 1, count, ada_cols)
    partial = jnp.broadcast_to(partial, (dp, seq, count, ada_cols))
    received = net.to_all(partial)
    sent = first.advance(partial)
    sent = first.advance()
    received, parcel = tie(received, *sent), tie(parcel, *sent)
    received = jnp.sum(received, axis=1)
    bias_full = parcel[:, :, : biases.shape[0]].reshape(-1)
    b_ada, b_q, b_v, b_proj, b_fc1, b_fc2 = [bias_full[bounds[i] : bounds[i + 1]] for i in range(6)]
    modulation = jnp.transpose(received, (1, 0, 2)).reshape(count, dp * ada_cols) + b_ada
    shift_one, scale_one, gate_one, shift_two, scale_two, gate_two = jnp.split(
        modulation[:, None, :], 6, axis=-1
    )
    (t_qkv, t_proj), arrived = first.finish(modulation)
    wires = net.y.gather(tie(net.wire([w_fc1]), token_pieces[0][-1], *arrived))
    t_fc1 = lax.all_gather(net.rows(wires), "dp", axis=0, tiled=True)
    for i in range(1, count):
        token_pieces.append(net.y.gather(tie(own_tokens[i], wires[-1])))

    lengths = (heights * widths).reshape(count).astype(jnp.int32)
    offsets = jnp.stack([((y + s) % seq) * rows for s in range(seq)]).astype(jnp.int32)
    normed_all, inverse_all, attn_all, queries, keys, values, attended_low, log_total = [[] for _ in range(8)]
    for i in range(count):
        normed, inverse = layer_norm(jnp.concatenate(token_pieces[i], axis=0).astype(F32))
        attn = (normed * (1.0 + scale_one[i]) + shift_one[i]).astype(BF)
        queries.append((dot_t(attn[None, :rows], t_qkv[:width]) + b_q).astype(BF))
        keys.append(dot_t(attn[None], t_qkv[width : 2 * width]).astype(BF))
        values.append((dot_t(attn[None], t_qkv[2 * width :]) + b_v).astype(BF))
        mixed, lse = attend(lengths[i : i + 1], offsets, queries[i], keys[i], values[i], HEADS, 512)
        if i == 0:
            token_pieces[1:] = [each[:1] + [tie(a, mixed) for a in each[1:]] for each in token_pieces[1:]]
            last_piece = token_pieces[-1][-1] if count > 1 else mixed
            wires = net.y.gather(tie(net.wire([w_fc2]), last_piece))
            t_fc2 = lax.all_gather(net.rows(wires), "dp", axis=0, tiled=True)
        normed_all.append(normed[:rows])
        inverse_all.append(inverse[:rows])
        attn_all.append(attn)
        attended_low.append(mixed[0])
        log_total.append(lse)
    attended_low = jnp.stack(attended_low)

    inputs = own_tokens.astype(F32)
    branch_one = dot_t(attended_low, t_proj) + b_proj
    mixed_one = inputs + gate_one * branch_one
    normed_two, inverse_two = layer_norm(mixed_one)
    ffn_in = (normed_two * (1.0 + scale_two) + shift_two).astype(BF)
    pre_act = dot_t(ffn_in, t_fc1) + b_fc1
    activated, gelu_back = jax.vjp(gelu_tanh, pre_act)
    activated_low = activated.astype(BF)
    grad_out = upstream.reshape(count, rows, width).astype(F32)
    grad_branch_two = (gate_two * grad_out).astype(BF)
    flat = lambda array: array.reshape(-1, array.shape[-1])
    term_fc2 = outer(grad_branch_two, activated_low)
    sum_fc2 = net.scatter(term_fc2)
    branch_two = dot_t(tie(activated_low, term_fc2), t_fc2) + b_fc2
    grad_branch_two = tie(grad_branch_two, term_fc2)
    result = (mixed_one + gate_two * branch_two).astype(BF)

    grad_gate_two = jnp.sum(branch_two * grad_out, axis=1)
    bias_fc2 = jnp.sum(grad_branch_two.astype(F32), axis=(0, 1))
    grad_pre = gelu_back(dot(grad_branch_two, t_fc2))[0].astype(BF)
    term_fc1 = outer(grad_pre, ffn_in)
    grad_pre = tie(grad_pre, term_fc1)
    bias_fc1 = jnp.sum(grad_pre.astype(F32), axis=(0, 1))
    grad_ffn_in = dot(grad_pre, t_fc1)
    grad_shift_two = jnp.sum(grad_ffn_in, axis=1)
    grad_scale_two = jnp.sum(grad_ffn_in * normed_two, axis=1)
    grad_mixed = grad_out + norm_back(normed_two, inverse_two, grad_ffn_in * (1.0 + scale_two))
    grad_gate_one = jnp.sum(branch_one * grad_mixed, axis=1)
    grad_branch_one = (gate_one * grad_mixed).astype(BF)
    bias_proj = jnp.sum(grad_branch_one.astype(F32), axis=(0, 1))
    grad_attended = dot(grad_branch_one, t_proj).astype(BF)
    term_fc1 = tie(term_fc1, sum_fc2, grad_attended)
    sum_fc1 = net.scatter(term_fc1)
    grad_attended = tie(grad_attended, term_fc1)

    grad_q, grad_k, grad_v, far_parts = [], [], [], []
    turned = [momentum.T for momentum in momenta]
    sent = []
    for i in range(count):
        dq, dk, dv = attend_back(
            lengths[i : i + 1], offsets, queries[i], keys[i], values[i], attended_low[i : i + 1],
            grad_attended[i : i + 1], log_total[i], HEADS, 512, sent,
        )
        sent = []
        grad_q.append(dq)
        grad_k.append(dk)
        grad_v.append(dv)
        far_part = (
            dot(dk[:, rows:], t_qkv[width : 2 * width]) + dot(dv[:, rows:], t_qkv[2 * width :])
        ).astype(BF)[0]
        far_steps = Staged(
            net.y.scatter_steps(
                lambda s, p=far_part: (
                    jnp.zeros((rows, width), BF) if s == 0 else p[(s - 1) * rows : s * rows]
                )
            )
        )
        sent = sent + far_steps.advance()
        far_parts.append(far_steps)
    unit_last = math.gcd(math.gcd(n_qkv, n_proj), 8)
    (term_last,) = shard_outer(
        net.spots(),
        [flat(each) for each in grad_q + grad_k + grad_v]
        + [attn[:rows] for attn in attn_all]
        + attn_all
        + [flat(grad_branch_one), flat(attended_low)],
        [([n * count + i for i in range(count)], 0, width) for n in range(5)]
        + [([5 * count], 0, width), ([5 * count + 1], 0, width)],
        [(0, 3, n_qkv, 0), (1, 4, n_qkv, 0), (2, 4, n_qkv, 0), (5, 6, n_proj, n_qkv // unit_last)],
        net.z.size, width, unit_last, (n_qkv + n_proj) // unit_last, sent, split=False,
    )
    sum_last = net.scatter(term_last.reshape(dp * (n_qkv + n_proj), width))
    halves = Staged(lockstep(*[net.halves_steps(tie(each, term_last)) for each in (sum_fc2, sum_fc1)]))
    sent = halves.advance()
    grad_q[0] = tie(grad_q[0], *sent)
    bias_q = sum(jnp.sum(each.astype(F32), axis=(0, 1)) for each in grad_q)
    bias_v = sum(jnp.sum(each.astype(F32), axis=(0, 1)) for each in grad_v)
    own_part = jnp.concatenate(
        [
            dot(grad_q[i], t_qkv[:width])
            + dot(grad_k[i][:, :rows], t_qkv[width : 2 * width])
            + dot(grad_v[i][:, :rows], t_qkv[2 * width :])
            for i in range(count)
        ],
        axis=0,
    )
    matrices = (w_qkv, w_proj, w_fc1, w_fc2, w_ada)
    per = -(-sum(matrix.shape[0] // ROW_BLOCK for matrix in matrices) // dp)
    spread_early = (per, 0)
    early_blocks = (w_fc2.shape[0] + w_fc1.shape[0]) // ROW_BLOCK
    spread_last = (per, -(-early_blocks // per))
    sums = halves.finish(own_part)
    early = Staged(
        net.muon_scatter_steps([(sums[0], [turned[3]]), (sums[1], [turned[2]])], spread_early)
    )
    sent = early.advance()
    far_sum = jnp.stack([steps_of.finish() for steps_of in far_parts])
    grad_attn_in = tie(own_part, *sent) + far_sum
    normed_one, inverse_one = jnp.stack(normed_all), jnp.stack(inverse_all)
    grad_shift_one = jnp.sum(grad_attn_in, axis=1)
    grad_scale_one = jnp.sum(grad_attn_in * normed_one, axis=1)
    grad_inputs = grad_mixed + norm_back(normed_one, inverse_one, grad_attn_in * (1.0 + scale_one))
    grad_inputs = grad_inputs.astype(BF).reshape(tokens.shape)

    grad_mod_local = jnp.concatenate(
        [grad_shift_one, grad_scale_one, grad_gate_one, grad_shift_two, grad_scale_two, grad_gate_two], axis=-1
    )
    bias_ada = jnp.sum(grad_mod_local, axis=0)
    sent = jnp.transpose(grad_mod_local.reshape(count, dp, 1, ada_cols), (1, 2, 0, 3))
    sent = jnp.broadcast_to(sent, (dp, seq, count, ada_cols))
    mod_parts = net.to_all(sent)
    while not early.done:
        sent = early.advance(sent if not isinstance(sent, list) else sent[0])
    halves = Staged(net.halves_steps(tie(sum_last, *early.result[1])))
    halves.advance()
    mod_cols = jnp.sum(mod_parts, axis=1).astype(BF).reshape(dp * count, ada_cols)
    shard_ada = jnp.einsum("sr,sc->cr", cond_all, mod_cols, preferred_element_type=F32)

    total = halves.finish(shard_ada)
    last = Staged(
        net.muon_scatter_steps([(total, [turned[0], turned[1]]), (shard_ada, [turned[4]])], spread_last)
    )
    sent = last.advance()

    cond_part = jnp.einsum("sc,rc->sr", mod_cols, low_ada, preferred_element_type=F32)
    cond_part = jnp.broadcast_to(cond_part.reshape(dp, 1, -1), (dp, seq, count * ada_rows))
    term_bias = jnp.concatenate([bias_ada, bias_q, bias_v, bias_proj, bias_fc1, bias_fc2])
    parcel = jnp.concatenate([term_bias.reshape(dp, seq, -1), cond_part], axis=-1)
    parcel = net.to_all(tie(parcel, *sent))
    while not last.done:
        sent = last.advance(sent[0])
    gathered = Staged(net.muon_gather_steps(early.result[1] + last.result[1]))
    sent = gathered.advance()
    while not gathered.done:
        sent = gathered.advance(sent[0])
    next_fc2, next_fc1 = early.result[0]
    next_qkv, next_proj, next_ada = last.result[0]
    new_fc2, new_fc1 = muon_apply(
        net.spots(), gathered.result, [next_fc2, next_fc1], [w_fc2.T, w_fc1.T],
        [math.sqrt(width / hidden), math.sqrt(hidden / width)], spread_early,
    )
    new_qkv, new_proj, new_ada = muon_apply(
        net.spots(), gathered.result, [next_qkv, next_proj, next_ada], [w_qkv.T, w_proj.T, w_ada.T],
        [math.sqrt(3.0), 1.0, math.sqrt(6.0)], spread_last,
    )

    size = biases.shape[0]
    grad_bias = jnp.sum(parcel[..., :size], axis=(0, 1))
    cond_part = jnp.sum(parcel[..., size:], axis=0).reshape(seq, count, ada_rows)
    grad_cond = silu_back(jnp.transpose(cond_part, (1, 0, 2)).reshape(count, width))[0]
    next_first = BETA_FIRST * bias_first + (1.0 - BETA_FIRST) * grad_bias
    next_second = BETA_SECOND * bias_second + (1.0 - BETA_SECOND) * grad_bias * grad_bias
    first_hat = next_first / (1.0 - BETA_FIRST**STEP_COUNT)
    second_hat = next_second / (1.0 - BETA_SECOND**STEP_COUNT)
    new_biases = biases * (1.0 - ADAM_RATE * ADAM_DECAY) - ADAM_RATE * first_hat / (
        jnp.sqrt(second_hat) + ADAM_EPS
    )
    return (
        result.reshape(tokens.shape),
        grad_inputs,
        grad_cond.reshape(conditioning.shape),
        new_qkv.T, new_proj.T, new_fc1.T, new_fc2.T, new_ada.T,
        next_qkv.T, next_proj.T, next_fc1.T, next_fc2.T, next_ada.T,
        new_biases,
        next_first,
        next_second,
    )


def solution(mesh):
    rows = P(None, "dp", "seq", None)
    matrix = P("seq", "dp")
    flat = P(("dp", "seq"))
    in_specs = (rows, P(None, "dp", None), P(None, "dp"), P(None, "dp"), rows) + (matrix,) * 10 + (flat,) * 3
    out_specs = (rows, rows, P(None, "dp", None)) + (matrix,) * 10 + (flat,) * 3
    return jax.shard_map(
        functools.partial(body, Net(mesh)), mesh=mesh, in_specs=in_specs, out_specs=out_specs, check_vma=False
    )
```

```python
import functools
import math

import jax
import jax.numpy as jnp
from jax import lax
from jax.experimental import pallas as pl
from jax.experimental.pallas import tpu as pltpu
from jax.sharding import PartitionSpec as P

HEADS = 16
ROW_BLOCK = 144
NS_STEPS = 5
STEP_COUNT = 10

PRECISE = lax.Precision.HIGHEST
LN_EPS = 1e-06
MASKED = -1e30
NS_A = 3.4445
NS_B = -4.775
NS_C = 2.0315
MUON_DECAY = 0.5
WEIGHT_SHRINK = 0.0001
NORM_EPS = 1e-07
BETA_FIRST = 0.9
BETA_SECOND = 0.999
ADAM_RATE = 0.1
ADAM_DECAY = 0.01
ADAM_EPS = 1e-08
BF = jnp.bfloat16
F32 = jnp.float32
VMEM_LIMIT = 60 * 2**20


class Ring:
    def __init__(self, name, total, stride, size):
        self.name, self.total, self.stride, self.size = name, total, stride, size

    def digit(self):
        return (lax.axis_index(self.name) // self.stride) % self.size

    def send(self, value, shift):
        pairs = []
        for i in range(self.total):
            d = (i // self.stride) % self.size
            pairs.append((i, i + ((d + shift) % self.size - d) * self.stride))
        return lax.ppermute(value, self.name, pairs)

    def gather(self, value, far=1):
        n = self.size
        blocks = [value] + [None] * (n - 1)
        if n == 2:
            blocks[1] = self.send(value, 1)
        elif n > 2:
            low = high = value
            for t in range(1, n // 2):
                low, high = self.send(low, 1), self.send(high, -1)
                blocks[n - t], blocks[t] = low, high
            blocks[n // 2] = self.send(low, 1) if far == 1 else self.send(high, -1)
        return blocks

    def gather_steps(self, value, far=1):
        n = self.size
        blocks = [value] + [None] * (n - 1)
        if n == 2:
            blocks[1] = self.send(value, 1)
            anchor = yield [value]
            blocks[1] = tie(blocks[1], anchor)
            return blocks
        low = high = value
        for t in range(1, n // 2):
            sent = [low, high]
            low, high = self.send(low, 1), self.send(high, -1)
            anchor = yield sent
            low, high = tie(low, anchor), tie(high, anchor)
            blocks[n - t], blocks[t] = low, high
        sent = [low if far == 1 else high]
        last = self.send(sent[0], far)
        anchor = yield sent
        blocks[n // 2] = tie(last, anchor)
        return blocks

    def scatter_steps(self, block_of, far=1):
        n = self.size
        if n == 1:
            return block_of(0).astype(F32)
        if n == 2:
            sent = block_of(1)
            got = self.send(sent, 1)
            anchor = yield [sent]
            return block_of(0).astype(F32) + tie(got, anchor).astype(F32)
        sent = block_of(n // 2)
        got = self.send(sent, far)
        anchor = yield [sent]
        low, high = (tie(got, anchor), None) if far == 1 else (None, tie(got, anchor))
        for t in range(n // 2 - 1, 0, -1):
            up, down = block_of(t), block_of(n - t)
            if low is not None:
                up = (up.astype(F32) + low.astype(F32)).astype(up.dtype)
            if high is not None:
                down = (down.astype(F32) + high.astype(F32)).astype(down.dtype)
            low, high = self.send(up, 1), self.send(down, -1)
            anchor = yield [up, down]
            low, high = tie(low, anchor), tie(high, anchor)
        return block_of(0).astype(F32) + low.astype(F32) + high.astype(F32)


def tie(value, *earlier):
    earlier = [array for array in earlier if array is not None]
    if not earlier:
        return value
    anywhere = pl.BlockSpec(memory_space=pl.ANY)
    return pl.pallas_call(
        lambda *refs: None,
        out_shape=jax.ShapeDtypeStruct(value.shape, value.dtype),
        in_specs=[anywhere] * (1 + len(earlier)),
        out_specs=anywhere,
        input_output_aliases={0: 0},
        name="tie",
    )(value, *earlier)


def lockstep(*steps):
    results = [None] * len(steps)
    alive = dict(enumerate(steps))
    anchor = None
    while alive:
        sent = []
        for n, step in list(alive.items()):
            try:
                sent += step.send(anchor)
            except StopIteration as stop:
                results[n] = stop.value
                del alive[n]
        if alive:
            anchor = yield sent
    return results


class Staged:
    def __init__(self, steps):
        self.steps, self.result, self.started, self.done = steps, None, False, False

    def advance(self, anchor=None):
        if self.done:
            return []
        try:
            sent = self.steps.send(anchor if self.started else None)
            self.started = True
            return sent
        except StopIteration as stop:
            self.result, self.done = stop.value, True
            return []

    def finish(self, anchor=None):
        while not self.done:
            self.advance(anchor)
        return self.result


def place_kernel(zs, ga, parts, count, outs, *refs):
    spots, sources = refs[0], refs[1 : 1 + count]
    outputs, (full, in_sems, out_sems) = refs[1 + count : 1 + count + outs], refs[1 + count + outs :]
    g = full.shape[3]
    half = count // 2
    shards = []
    for sc in range(2):
        for sx in range(2):
            for sz in range(zs):
                where = (lax.rem(spots[0] + sz, zs), lax.rem(spots[1] + sx, 2), lax.rem(spots[2] + sc, 2))
                n = 2 * len(shards)
                line, pair = sources[sc * half + sx].at[sz], sources[sc * half + 2 + sz].at[sx]
                copies = [
                    pltpu.make_async_copy(line, full.at[(*where, pl.ds(0, ga))], in_sems.at[n]),
                    pltpu.make_async_copy(pair, full.at[(*where, pl.ds(ga, g - ga))], in_sems.at[n + 1]),
                ]
                for copy in copies:
                    copy.start()
                shards.append((where, copies))
    exits = []
    for where, copies in shards:
        for copy in copies:
            copy.wait()
        for output, start, size, column, depth in parts:
            target = outputs[output].at[(*where, slice(None), slice(None), pl.ds(column, depth))]
            copy = pltpu.make_async_copy(
                full.at[(*where, pl.ds(start, size))], target, out_sems.at[len(exits)]
            )
            copy.start()
            exits.append(copy)
    for copy in exits:
        copy.wait()


def place(spots, sources, shape, ga, parts, shapes):
    zs = shape[0]
    moved = math.prod(shape) * 2
    return pl.pallas_call(
        functools.partial(place_kernel, zs, ga, parts, len(sources), len(shapes)),
        out_shape=[jax.ShapeDtypeStruct(each, BF) for each in shapes],
        in_specs=[pl.BlockSpec(memory_space=pltpu.SMEM)]
        + [pl.BlockSpec(memory_space=pl.ANY)] * len(sources),
        out_specs=[pl.BlockSpec(memory_space=pl.ANY)] * len(shapes),
        scratch_shapes=[
            pltpu.VMEM(shape, BF),
            pltpu.SemaphoreType.DMA((8 * zs,)),
            pltpu.SemaphoreType.DMA((4 * zs * len(parts),)),
        ],
        compiler_params=pltpu.CompilerParams(vmem_limit_bytes=VMEM_LIMIT),
        cost_estimate=pl.CostEstimate(flops=0, bytes_accessed=2 * moved, transcendentals=0),
        name="place",
    )(spots, *sources)


class Net:
    def __init__(self, mesh):
        dp, seq = mesh.shape["dp"], mesh.shape["seq"]
        self.dp, self.seq = dp, seq
        self.core = Ring("dp", dp, 1, 2)
        self.x = Ring("dp", dp, 2, 2)
        self.z = Ring("dp", dp, 4, dp // 4)
        self.y = Ring("seq", seq, 1, seq)

    def spots(self):
        return jnp.stack([self.z.digit(), self.x.digit(), self.core.digit()]).astype(jnp.int32)


    def wire(self, shards):
        turned = [shard.astype(BF).T for shard in shards]
        return turned[0] if len(turned) == 1 else jnp.concatenate(turned, axis=0)

    def rows(self, wires):
        if self.seq == 2:
            own, other = wires
            return jnp.where(
                self.y.digit() == 0,
                jnp.concatenate([own, other], axis=1),
                jnp.concatenate([other, own], axis=1),
            )
        order = (jnp.arange(self.seq) - self.y.digit()) % self.seq
        full = jnp.take(jnp.stack(wires), order, axis=0)
        return jnp.transpose(full, (1, 0, 2)).reshape(full.shape[1], -1)

    def joined(self, wires, unit, depth):
        full = self.rows(wires)
        return full.reshape(full.shape[0] // unit, unit, depth)

    def scatter(self, term):
        return lax.psum_scatter(term, "dp", scatter_dimension=0, tiled=True)

    def halves_steps(self, term):
        y = self.y.digit()
        blocks = term.reshape(term.shape[0], self.seq, -1)
        return (
            yield from self.y.scatter_steps(
                lambda s: lax.dynamic_index_in_dim(blocks, (y + s) % self.seq, 1, keepdims=False)
            )
        )

    def gather_steps(self, units, layout, part):
        g, unit, depth = units.shape
        zs = self.z.size
        ga = max(1, int(part * g))
        first, second = units[:ga], units[ga:]

        def line_steps():
            blocks = yield from self.z.gather_steps(first, 1)
            line = jnp.stack(blocks)
            return (yield from self.x.gather_steps(line))

        def pair_steps():
            blocks = yield from self.x.gather_steps(second)
            return (yield from self.z.gather_steps(jnp.stack(blocks), -1))

        lines, pairs = yield from lockstep(line_steps(), pair_steps())
        pieces = lines + pairs
        others = [self.core.send(piece, 1) for piece in pieces]
        anchor = yield pieces
        sources = pieces + [tie(other, anchor) for other in others]
        parts, shapes, start = [], [], 0
        for n, (rows, blocks) in enumerate(layout):
            size = rows // unit
            shapes.append((zs, 2, 2, size, unit, blocks * depth))
            for j in range(blocks):
                parts.append((n, start, size, j * depth, depth))
                start += size
        full = place(self.spots(), sources, (zs, 2, 2, g, unit, depth), ga, parts, shapes)
        return [f.reshape(-1, f.shape[-1]) for f in full], lines[1:] + pairs[1:]


    def gram_steps(self, own, other):
        got = self.core.send(other, 1)
        anchor = yield [other]
        half = own + tie(got, anchor)
        sent = half[1].astype(BF)
        got = self.x.send(sent, 1)
        anchor = yield [sent]
        kept = half[0] + tie(got, anchor).astype(F32)
        sent = [kept[shift].astype(BF) for shift in range(1, self.z.size)]
        got = [self.z.send(each, shift) for shift, each in enumerate(sent, 1)]
        anchor = yield sent
        return [kept[0]] + [tie(each, anchor) for each in got]

    def muon_gather_steps(self, parts):
        factor = polynomial(parts)
        got = [self.z.send(factor, -shift) for shift in range(1, self.z.size)]
        anchor = yield [factor]
        line = jnp.stack([factor] + [tie(each, anchor) for each in got])
        got = self.x.send(line, 1)
        anchor = yield [line]
        pair = [line, tie(got, anchor)]
        others = [self.core.send(each, 1) for each in pair]
        anchor = yield pair
        return pair + [tie(each, anchor) for each in others]


    def to_all(self, value):
        flat = value.reshape((self.dp * self.seq,) + value.shape[2:])
        return lax.all_to_all(flat, ("dp", "seq"), 0, 0, tiled=True).reshape(value.shape)

    def to_dp(self, value):
        return lax.all_to_all(value, "dp", 0, 0, tiled=True)


def layer_norm(values):
    centered = values - jnp.mean(values, axis=-1, keepdims=True)
    inverse = lax.rsqrt(jnp.mean(centered * centered, axis=-1, keepdims=True) + LN_EPS)
    return (centered * inverse, inverse)


def norm_back(normed, inverse, grad):
    mean_grad = jnp.mean(grad, axis=-1, keepdims=True)
    mean_cross = jnp.mean(grad * normed, axis=-1, keepdims=True)
    return inverse * (grad - mean_grad - normed * mean_cross)


def sigmoid_linear(values):
    return values * jax.nn.sigmoid(values)


def gelu_tanh(values):
    return jax.nn.gelu(values, approximate=True)


def dot_t(left, right):
    return jnp.einsum("srk,nk->srn", left, right, preferred_element_type=F32)


def dot(left, right):
    return jnp.einsum("srn,nk->srk", left, right, preferred_element_type=F32)


def outer(left, right):
    return jnp.einsum("srn,srk->nk", left, right, preferred_element_type=F32).astype(BF)


def shard_outer_kernel(plan, counts, tile, split, spots_ref, *refs):
    outs = 2 if split else 1
    inputs, where = refs[: counts[0]], refs[counts[1] : counts[1] + outs]
    buffers = refs[counts[1] + outs : counts[1] + outs + len(plan["loads"])]
    acc, in_sems, out_sems = refs[counts[1] + outs + len(plan["loads"]) :]
    loads = []
    for n, (sources, start, size) in enumerate(plan["loads"]):
        row, copies = 0, []
        for m, source in enumerate(sources):
            rows = inputs[source].shape[0]
            window = inputs[source].at[:, pl.ds(start, size)]
            copies.append(pltpu.make_async_copy(window, buffers[n].at[pl.ds(row, rows)], in_sems.at[n, m]))
            copies[-1].start()
            row += rows
        loads.append(copies)
    ready = set()
    shipped = []
    unit = acc.shape[1]
    for left, right, base, ships in plan["parts"]:
        for n in (left, right):
            if n not in ready:
                for copy in loads[n]:
                    copy.wait()
                ready.add(n)
        width = buffers[left].shape[1]
        step = tile if width % tile == 0 else width

        @pl.loop(0, width // step)
        def _(t):
            block = buffers[left][:, pl.ds(pl.multiple_of(t * step, step), step)]
            product = lax.dot_general(
                block, buffers[right][...], (((0,), (0,)), ((), ())), preferred_element_type=F32
            )
            product = product.reshape(step // unit, unit, product.shape[1]).astype(BF)
            acc[pl.ds(base + t * (step // unit), step // unit)] = product

        for core, z, x, row, target, size in ships:
            spot = (z, x) if split else (z, x, core)
            places = [ref.at[(*spot, pl.ds(target, size))] for ref in where]
            copies = [
                pltpu.make_async_copy(acc.at[pl.ds(row, size)], each, out_sems.at[len(shipped)]) for each in places
            ]
            shipped.append((core, copies))
            on_own_core(split, spots_ref, core, [copy.start for copy in copies])
    for core, copies in shipped:
        on_own_core(split, spots_ref, core, [copy.wait for copy in copies])


def on_own_core(split, spots_ref, core, actions):
    if not split:
        actions[0]()
        return

    @pl.when(spots_ref[2] == core)
    def _():
        actions[0]()

    @pl.when(spots_ref[2] != core)
    def _():
        actions[1]()


def shard_outer(spots, inputs, loads, parts, zs, depth, unit, shard_units, deps=(), tile=384, split=True):
    dp = zs * 4
    plan_parts, base, row, placed = [], 0, 0, {}
    begun = {}
    for left, right, rows, first in parts:
        if first not in begun:
            begun[first] = (base, 0)
        start, shipped = begun[first]
        width = loads[left][2]
        size = rows // unit
        end = base + width // unit
        ships = []
        while shipped < dp and start + (shipped + 1) * size <= end:
            core, x, z = shipped % 2, shipped // 2 % 2, shipped // 4
            ships.append((core, z, x, start + shipped * size, first, size))
            shipped += 1
        begun[first] = (start, shipped)
        plan_parts.append((left, right, base, ships))
        base = end
    total = sum(len(part[3]) for part in plan_parts)
    shape = (zs, 2, shard_units, unit, depth) if split else (zs, 2, 2, shard_units, unit, depth)
    outs = [jax.ShapeDtypeStruct(shape, BF)] * (2 if split else 1)
    anywhere = pl.BlockSpec(memory_space=pl.ANY)
    heights = [sum(inputs[source].shape[0] for source in sources) for sources, _, _ in loads]
    flops = sum(2 * heights[p[0]] * loads[p[0]][2] * loads[p[1]][2] for p in parts)
    return pl.pallas_call(
        functools.partial(
            shard_outer_kernel, {"loads": loads, "parts": plan_parts}, (len(inputs), len(inputs) + len(deps)), tile, split
        ),
        out_shape=outs,
        in_specs=[pl.BlockSpec(memory_space=pltpu.SMEM)] + [anywhere] * (len(inputs) + len(deps)),
        out_specs=[anywhere] * len(outs),
        scratch_shapes=[pltpu.VMEM((height, load[2]), BF) for height, load in zip(heights, loads)]
        + [
            pltpu.VMEM((base, unit, depth), BF),
            pltpu.SemaphoreType.DMA((len(loads), max(len(load[0]) for load in loads))),
            pltpu.SemaphoreType.DMA((total,)),
        ],
        compiler_params=pltpu.CompilerParams(vmem_limit_bytes=VMEM_LIMIT),
        cost_estimate=pl.CostEstimate(flops=flops, bytes_accessed=2 * base * unit * depth, transcendentals=0),
        name="shard_outer",
    )(spots, *inputs, *deps)


LANES = 128
LOG2E = math.log2(math.e)


def padded(block, column=None):
    rows, depth = block.shape
    if column is None:
        return jnp.concatenate([block, jnp.zeros((rows, LANES - depth), block.dtype)], axis=1)
    rest = jnp.zeros((rows, LANES - depth - 1), block.dtype)
    return jnp.concatenate([block, column.astype(block.dtype), rest], axis=1)


def mask_column(lengths_ref, offsets_ref, sample, total, rows):
    place = lax.broadcasted_iota(jnp.int32, (total, 1), 0)
    position = place
    for s in range(total // rows):
        position = jnp.where(place // rows == s, place - s * rows + offsets_ref[s], position)
    return jnp.where(position < lengths_ref[sample], 0.0, MASKED)


def nt(left, right):
    return lax.dot_general(left, right, (((1,), (1,)), ((), ())), preferred_element_type=F32)


def nn(left, right):
    return jnp.dot(left, right, preferred_element_type=F32)


def without(kernel, start, count, *fixed):
    def run(*refs):
        kernel(*fixed, *refs[:start], *refs[start + count :])

    return run


def attend_kernel(heads, chunk, lengths_ref, offsets_ref, q_ref, k_ref, v_ref, o_ref, lse_ref, q_s, k_s, vt_s, o_s):
    rows, width = q_ref.shape[1:]
    total = k_ref.shape[1]
    depth = width // heads
    factor = depth**-0.5 * LOG2E
    mask = mask_column(lengths_ref, offsets_ref, pl.program_id(0), total, rows)
    ones = jnp.ones((rows, 1), F32)
    for h in range(heads):
        span = slice(h * depth, (h + 1) * depth)
        q_s[h] = padded(q_ref[0, :, span], ones)
        k_s[h] = padded(k_ref[0, :, span], mask)
        vt_s[h] = jnp.transpose(v_ref[0, :, span])

    def one_head(h, carry):
        peak = jnp.full((1, rows), MASKED, F32)
        sums = jnp.zeros((1, rows), F32)
        mixed = jnp.zeros((depth, rows), F32)
        for c in range(total // chunk):
            part = slice(c * chunk, (c + 1) * chunk)
            scores = nt(k_s[h, part], q_s[h])
            higher = jnp.maximum(peak, jnp.max(scores, axis=0, keepdims=True))
            weights = jnp.exp2((scores - higher) * factor)
            if c == 0:
                sums = jnp.sum(weights, axis=0, keepdims=True)
                mixed = nn(vt_s[h, :, part], weights.astype(BF))
            else:
                shrink = jnp.exp2((peak - higher) * factor)
                sums = sums * shrink + jnp.sum(weights, axis=0, keepdims=True)
                mixed = mixed * shrink + nn(vt_s[h, :, part], weights.astype(BF))
            peak = higher
        o_s[h] = jnp.transpose(mixed / sums)
        lse_ref[0, h] = peak * factor + jnp.log2(sums)
        return carry

    lax.fori_loop(0, heads, one_head, 0)
    for h in range(heads):
        o_ref[0, :, h * depth : (h + 1) * depth] = o_s[h].astype(BF)


def attend(lengths, offsets, queries, keys, values, heads, tile, deps=()):
    count, rows, width = queries.shape
    total = keys.shape[1]
    depth = width // heads
    tile = min(tile, total)
    pick = lambda i, *_: (i, 0, 0)
    return pl.pallas_call(
        without(attend_kernel, 5, len(deps), heads, tile),
        grid_spec=pltpu.PrefetchScalarGridSpec(
            num_scalar_prefetch=2,
            grid=(count,),
            in_specs=[
                pl.BlockSpec((1, rows, width), pick),
                pl.BlockSpec((1, total, width), pick),
                pl.BlockSpec((1, total, width), pick),
            ]
            + [pl.BlockSpec(memory_space=pl.ANY)] * len(deps),
            out_specs=[
                pl.BlockSpec((1, rows, width), pick),
                pl.BlockSpec((1, heads, 1, rows), lambda i, *_: (i, 0, 0, 0)),
            ],
            scratch_shapes=[
                pltpu.VMEM((heads, rows, LANES), BF),
                pltpu.VMEM((heads, total, LANES), BF),
                pltpu.VMEM((heads, depth, total), BF),
                pltpu.VMEM((heads, rows, depth), F32),
            ],
        ),
        out_shape=[
            jax.ShapeDtypeStruct((count, rows, width), BF),
            jax.ShapeDtypeStruct((count, heads, 1, rows), F32),
        ],
        compiler_params=pltpu.CompilerParams(vmem_limit_bytes=VMEM_LIMIT),
        cost_estimate=pl.CostEstimate(
            flops=4 * count * heads * rows * total * LANES,
            bytes_accessed=2 * count * width * (2 * rows + 2 * total),
            transcendentals=count * heads * rows * total,
        ),
        name="attend",
    )(lengths, offsets, queries, keys, values, *deps)


def attend_back_kernel(
    heads, chunk, lengths_ref, offsets_ref, q_ref, k_ref, v_ref, o_ref, g_ref, lse_ref,
    dq_ref, dk_ref, dv_ref, q_s, k_s, kt_s, v_s, g_s, delta_s, dq_s, dk_s, dv_s
):
    rows, width = q_ref.shape[1:]
    total = k_ref.shape[1]
    depth = width // heads
    scale = depth**-0.5
    factor = scale * LOG2E
    mask = mask_column(lengths_ref, offsets_ref, pl.program_id(0), total, rows)
    ones = jnp.ones((rows, 1), F32)
    cross = jnp.transpose(g_ref[0].astype(F32) * o_ref[0].astype(F32))
    for h in range(heads):
        span = slice(h * depth, (h + 1) * depth)
        delta_s[h] = jnp.sum(cross[span], axis=0, keepdims=True)
        q_s[h] = padded(q_ref[0, :, span], ones)
        k_s[h] = padded(k_ref[0, :, span], mask)
        kt_s[h] = jnp.transpose(k_ref[0, :, span])
        g_s[h] = padded(g_ref[0, :, span])
        v_s[h] = padded(v_ref[0, :, span])

    def one_head(h, carry):
        dq = jnp.zeros((depth, rows), F32)
        for c in range(total // chunk):
            part = slice(c * chunk, (c + 1) * chunk)
            probs = jnp.exp2(nt(k_s[h, part], q_s[h]) * factor - lse_ref[0, h])
            slopes = (probs * (nt(v_s[h, part], g_s[h]) - delta_s[h])).astype(BF)
            dv_s[h, part] = nn(probs.astype(BF), g_s[h]).astype(BF)
            dk_s[h, part] = (nn(slopes, q_s[h]) * scale).astype(BF)
            dq = dq + nn(kt_s[h, :, part], slopes)
        dq_s[h] = jnp.transpose(dq * scale)
        return carry

    lax.fori_loop(0, heads, one_head, 0)
    for h in range(heads):
        span = slice(h * depth, (h + 1) * depth)
        dq_ref[0, :, span] = dq_s[h].astype(BF)
        dk_ref[0, :, span] = dk_s[h][:, :depth]
        dv_ref[0, :, span] = dv_s[h][:, :depth]


def attend_back(lengths, offsets, queries, keys, values, mixed, grads, lse, heads, tile, deps=()):
    count, rows, width = queries.shape
    total = keys.shape[1]
    depth = width // heads
    tile = min(tile, total)
    pick = lambda i, *_: (i, 0, 0)
    near = pl.BlockSpec((1, rows, width), pick)
    far = pl.BlockSpec((1, total, width), pick)
    return pl.pallas_call(
        without(attend_back_kernel, 8, len(deps), heads, tile),
        grid_spec=pltpu.PrefetchScalarGridSpec(
            num_scalar_prefetch=2,
            grid=(count,),
            in_specs=[near, far, far, near, near, pl.BlockSpec((1, heads, 1, rows), lambda i, *_: (i, 0, 0, 0))]
            + [pl.BlockSpec(memory_space=pl.ANY)] * len(deps),
            out_specs=[near, far, far],
            scratch_shapes=[
                pltpu.VMEM((heads, rows, LANES), BF),
                pltpu.VMEM((heads, total, LANES), BF),
                pltpu.VMEM((heads, depth, total), BF),
                pltpu.VMEM((heads, total, LANES), BF),
                pltpu.VMEM((heads, rows, LANES), BF),
                pltpu.VMEM((heads, 1, rows), F32),
                pltpu.VMEM((heads, rows, depth), F32),
                pltpu.VMEM((heads, total, LANES), BF),
                pltpu.VMEM((heads, total, LANES), BF),
            ],
        ),
        out_shape=[
            jax.ShapeDtypeStruct((count, rows, width), BF),
            jax.ShapeDtypeStruct((count, total, width), BF),
            jax.ShapeDtypeStruct((count, total, width), BF),
        ],
        compiler_params=pltpu.CompilerParams(vmem_limit_bytes=VMEM_LIMIT),
        cost_estimate=pl.CostEstimate(
            flops=10 * count * heads * rows * total * LANES,
            bytes_accessed=2 * count * width * (4 * rows + 4 * total),
            transcendentals=count * heads * rows * total,
        ),
        name="attend_back",
    )(lengths, offsets, queries, keys, values, mixed, grads, lse, *deps)


def block_spots(counts, spread):
    per, first = spread
    spots = []
    for matrix, count in enumerate(counts):
        for block in range(count):
            device, place_in = divmod(len(spots), per)
            device += first
            spots.append((matrix, block, device // 4, device // 2 % 2, device % 2, place_in))
    return spots


def precise(left, right, dims):
    return lax.dot_general(left, right, (dims, ((), ())), precision=PRECISE, preferred_element_type=F32)


def muon_gram_kernel(groups, spread, spots_ref, base_own, base_other, *refs):
    count = sum(groups)
    sums, momenta = refs[: len(groups)], refs[len(groups) : len(groups) + count]
    outs = refs[len(groups) + count : len(groups) + 2 * count]
    own_ref, other_ref = refs[len(groups) + 2 * count :]
    n = 0
    for matrices, sum_ref in zip(groups, sums):
        start = 0
        for _ in range(matrices):
            size = momenta[n].shape[0]
            outs[n][...] = MUON_DECAY * momenta[n][...] + sum_ref[start : start + size]
            start += size
            n += 1
    zs = own_ref.shape[1]
    spots = block_spots([out.shape[1] // ROW_BLOCK for out in outs], spread)
    own_ref[...] = base_own[...]
    other_ref[...] = base_other[...]
    for matrix, block, z, x, core, place_in in spots:
        turned = outs[matrix][:, block * ROW_BLOCK : (block + 1) * ROW_BLOCK]
        gram = precise(turned, turned, ((0,), (0,)))
        away = (lax.rem(spots_ref[1] + x, 2), lax.rem(zs + z - spots_ref[0], zs), place_in)

        @pl.when(spots_ref[2] == core)
        def _():
            own_ref[away] = gram

        @pl.when(spots_ref[2] != core)
        def _():
            other_ref[away] = gram


def muon_gram(spots, groups, spread, base):
    momenta = [momentum for _, each in groups for momentum in each]
    grams = jax.ShapeDtypeStruct(base[0].shape, F32)
    vmem = pl.BlockSpec(memory_space=pltpu.VMEM)
    outs = pl.pallas_call(
        functools.partial(muon_gram_kernel, [len(each) for _, each in groups], spread),
        out_shape=[jax.ShapeDtypeStruct(momentum.shape, F32) for momentum in momenta] + [grams, grams],
        in_specs=[pl.BlockSpec(memory_space=pltpu.SMEM)] + [vmem] * (2 + len(groups) + len(momenta)),
        out_specs=[vmem] * (len(momenta) + 2),
        compiler_params=pltpu.CompilerParams(vmem_limit_bytes=VMEM_LIMIT),
        name="muon_gram",
    )(spots, *base, *[group[0] for group in groups], *momenta)
    return outs[:-2], outs[-2], outs[-1]


def polynomial_kernel(count, *refs):
    out = refs[count]
    shape = (ROW_BLOCK, ROW_BLOCK)
    eye = (lax.broadcasted_iota(jnp.int32, shape, 0) == lax.broadcasted_iota(jnp.int32, shape, 1)).astype(F32)
    mul = lambda left, right: precise(left, right, ((1,), (0,)))
    blocks = range(out.shape[0])
    currents, scales, totals = [], [], []
    for n in blocks:
        gram = refs[0][n]
        for ref in refs[1:count]:
            gram = gram + ref[n].astype(F32)
        square = jnp.sum(jnp.sum(gram * eye, axis=1, keepdims=True), axis=0, keepdims=True)
        scale = 1.0 / (jnp.sqrt(square) + NORM_EPS)
        scales.append(scale)
        currents.append(gram * (scale * scale))
    for step in range(NS_STEPS):
        factors = [NS_A * eye + NS_B * a + NS_C * mul(a, a) for a in currents]
        totals = factors if step == 0 else [mul(f, t) for f, t in zip(factors, totals)]
        if step + 1 < NS_STEPS:
            currents = [mul(f, a) for f, a in zip(factors, currents)]
            currents = [mul(a, f) for f, a in zip(factors, currents)]
    for n in blocks:
        out[n] = totals[n] * scales[n]


def polynomial(parts):
    vmem = pl.BlockSpec(memory_space=pltpu.VMEM)
    return pl.pallas_call(
        functools.partial(polynomial_kernel, len(parts)),
        out_shape=jax.ShapeDtypeStruct(parts[0].shape, F32),
        in_specs=[vmem] * len(parts),
        out_specs=vmem,
        compiler_params=pltpu.CompilerParams(vmem_limit_bytes=VMEM_LIMIT),
        name="polynomial",
    )(*parts)


def muon_apply_kernel(rates, spread, spots_ref, *refs):
    count = len(rates)
    parts, momenta, masters = refs[:4], refs[4 : 4 + count], refs[4 + count : 4 + 2 * count]
    outs, factors = refs[4 + 2 * count : 4 + 3 * count], refs[4 + 3 * count]
    for n in range(4):
        factors[n] = parts[n][...]
    zs = factors.shape[1]
    spots = block_spots([momentum.shape[1] // ROW_BLOCK for momentum in momenta], spread)
    for matrix, block, z, x, core, place_in in spots:
        part = slice(block * ROW_BLOCK, (block + 1) * ROW_BLOCK)
        away = 2 * lax.rem(spots_ref[2] + core, 2) + lax.rem(spots_ref[1] + x, 2)
        factor = factors[away, lax.rem(zs + z - spots_ref[0], zs), place_in]
        direction = precise(momenta[matrix][:, part], factor, ((1,), (1,)))
        outs[matrix][:, part] = masters[matrix][:, part] * (1.0 - WEIGHT_SHRINK) - rates[matrix] * direction


def muon_apply(spots, factors, momenta, masters, rates, spread):
    vmem = pl.BlockSpec(memory_space=pltpu.VMEM)
    return pl.pallas_call(
        functools.partial(muon_apply_kernel, rates, spread),
        out_shape=[jax.ShapeDtypeStruct(master.shape, F32) for master in masters],
        in_specs=[pl.BlockSpec(memory_space=pltpu.SMEM)] + [vmem] * (4 + 2 * len(masters)),
        out_specs=[vmem] * len(masters),
        scratch_shapes=[pltpu.VMEM((4,) + factors[0].shape, F32)],
        compiler_params=pltpu.CompilerParams(vmem_limit_bytes=VMEM_LIMIT),
        name="muon_apply",
    )(spots, *factors, *momenta, *masters)


def body(net, tokens, conditioning, heights, widths, upstream, *state):
    masters, momenta = state[0:5], state[5:10]
    biases, bias_first, bias_second = state[10:13]
    w_qkv, w_proj, w_fc1, w_fc2, w_ada = masters
    micro, local, rows, width = tokens.shape
    count = micro * local
    head_dim = width // HEADS
    hidden = w_fc1.shape[1] * net.dp
    seq, dp = net.seq, net.dp
    y = net.y.digit()

    bounds = [0, 6 * width, 7 * width, 8 * width, 9 * width, 9 * width + hidden, 10 * width + hidden]

    n_qkv, n_proj, n_fc1, n_fc2 = [w.shape[1] for w in (w_qkv, w_proj, w_fc1, w_fc2)]
    unit = math.gcd(math.gcd(n_qkv, n_proj), 8)
    unit_qkv, layout_qkv = math.gcd(n_qkv, 8), [(n_qkv, 1)]
    own_tokens = tokens.reshape(count, rows, width)
    wires = net.y.gather(net.wire([w_qkv, w_proj]))

    ada_rows, ada_cols = w_ada.shape
    cond = conditioning.astype(F32).reshape(count, width)
    cond_act, silu_back = jax.vjp(sigmoid_linear, cond)
    cond_low = cond_act.astype(BF).astype(F32)
    cond_parts = jnp.transpose(cond_low.reshape(count, seq, ada_rows), (1, 0, 2)).reshape(seq, -1)
    parcel = jnp.concatenate([jnp.broadcast_to(biases, (seq,) + biases.shape), cond_parts], axis=1)
    parcel = net.to_all(tie(jnp.broadcast_to(parcel[None], (dp,) + parcel.shape), wires[0]))
    cond_all = parcel[:, 0, biases.shape[0] :].reshape(dp * count, ada_rows).astype(BF)
    first = Staged(net.gather_steps(net.joined(wires, unit, width), [(n_qkv, 1), (n_proj, 1)], 0.45))
    sent = first.advance()
    token_pieces = [net.y.gather(tie(own_tokens[0], *sent))]

    low_ada = w_ada.astype(BF)
    partial = jnp.dot(tie(cond_all, *sent), low_ada, preferred_element_type=F32).reshape(dp, 1, count, ada_cols)
    partial = jnp.broadcast_to(partial, (dp, seq, count, ada_cols))
    received = net.to_all(partial)
    sent = first.advance(partial)
    sent = first.advance()
    sent = first.advance()
    arrived = sent[-1]
    received, parcel = tie(received, arrived), tie(parcel, arrived)
    received = jnp.sum(received, axis=1)
    bias_full = parcel[:, :, : biases.shape[0]].reshape(-1)
    b_ada, b_q, b_v, b_proj, b_fc1, b_fc2 = [bias_full[bounds[i] : bounds[i + 1]] for i in range(6)]
    modulation = jnp.transpose(received, (1, 0, 2)).reshape(count, dp * ada_cols) + b_ada
    shift_one, scale_one, gate_one, shift_two, scale_two, gate_two = jnp.split(
        modulation[:, None, :], 6, axis=-1
    )
    t_qkv, t_proj = first.finish(modulation)[0]
    wires = net.y.gather(tie(net.wire([w_fc1]), token_pieces[0][-1], arrived))
    wires = wires[:1] + [tie(wire, t_qkv) for wire in wires[1:]]
    t_fc1 = lax.all_gather(net.rows(wires), "dp", axis=0, tiled=True)
    for i in range(1, count):
        token_pieces.append(net.y.gather(tie(own_tokens[i], wires[-1])))

    lengths = (heights * widths).reshape(count).astype(jnp.int32)
    offsets = jnp.stack([((y + s) % seq) * rows for s in range(seq)]).astype(jnp.int32)
    normed_all, inverse_all, attn_all, queries, keys, values, attended_low, log_total = [[] for _ in range(8)]
    for i in range(count):
        normed, inverse = layer_norm(jnp.concatenate(token_pieces[i], axis=0).astype(F32))
        attn = (normed * (1.0 + scale_one[i]) + shift_one[i]).astype(BF)
        queries.append((dot_t(attn[None, :rows], t_qkv[:width]) + b_q).astype(BF))
        keys.append(dot_t(attn[None], t_qkv[width : 2 * width]).astype(BF))
        values.append((dot_t(attn[None], t_qkv[2 * width :]) + b_v).astype(BF))
        mixed, lse = attend(lengths[i : i + 1], offsets, queries[i], keys[i], values[i], HEADS, 512)
        if i == 0:
            token_pieces[1:] = [each[:1] + [tie(a, mixed) for a in each[1:]] for each in token_pieces[1:]]
            last_piece = token_pieces[-1][-1] if count > 1 else mixed
            wires = net.y.gather(tie(net.wire([w_fc2]), last_piece))
            t_fc2 = lax.all_gather(net.rows(wires), "dp", axis=0, tiled=True)
        normed_all.append(normed[:rows])
        inverse_all.append(inverse[:rows])
        attn_all.append(attn)
        attended_low.append(mixed[0])
        log_total.append(lse)
    attended_low = jnp.stack(attended_low)

    inputs = own_tokens.astype(F32)
    branch_one = dot_t(attended_low, t_proj) + b_proj
    mixed_one = inputs + gate_one * branch_one
    normed_two, inverse_two = layer_norm(mixed_one)
    ffn_in = (normed_two * (1.0 + scale_two) + shift_two).astype(BF)
    pre_act = dot_t(ffn_in, t_fc1) + b_fc1
    activated, gelu_back = jax.vjp(gelu_tanh, pre_act)
    activated_low = activated.astype(BF)
    grad_out = upstream.reshape(count, rows, width).astype(F32)
    grad_branch_two = (gate_two * grad_out).astype(BF)
    flat = lambda array: array.reshape(-1, array.shape[-1])
    term_fc2 = outer(grad_branch_two, activated_low)
    sum_fc2 = net.scatter(term_fc2)
    branch_two = dot_t(tie(activated_low, term_fc2), t_fc2) + b_fc2
    grad_branch_two = tie(grad_branch_two, term_fc2)
    result = (mixed_one + gate_two * branch_two).astype(BF)

    grad_gate_two = jnp.sum(branch_two * grad_out, axis=1)
    bias_fc2 = jnp.sum(grad_branch_two.astype(F32), axis=(0, 1))
    grad_pre = gelu_back(dot(grad_branch_two, t_fc2))[0].astype(BF)
    term_fc1 = outer(grad_pre, ffn_in)
    grad_pre = tie(grad_pre, term_fc1)
    bias_fc1 = jnp.sum(grad_pre.astype(F32), axis=(0, 1))
    grad_ffn_in = dot(grad_pre, t_fc1)
    grad_shift_two = jnp.sum(grad_ffn_in, axis=1)
    grad_scale_two = jnp.sum(grad_ffn_in * normed_two, axis=1)
    grad_mixed = grad_out + norm_back(normed_two, inverse_two, grad_ffn_in * (1.0 + scale_two))
    grad_gate_one = jnp.sum(branch_one * grad_mixed, axis=1)
    grad_branch_one = (gate_one * grad_mixed).astype(BF)
    bias_proj = jnp.sum(grad_branch_one.astype(F32), axis=(0, 1))
    grad_attended = dot(grad_branch_one, t_proj).astype(BF)
    term_fc1 = tie(term_fc1, sum_fc2, grad_attended)
    sum_fc1 = net.scatter(term_fc1)
    grad_attended = tie(grad_attended, term_fc1)

    grad_q, grad_k, grad_v, far_parts = [], [], [], []
    turned = [momentum.T for momentum in momenta]
    sent = []
    for i in range(count):
        dq, dk, dv = attend_back(
            lengths[i : i + 1], offsets, queries[i], keys[i], values[i], attended_low[i : i + 1],
            grad_attended[i : i + 1], log_total[i], HEADS, 512, sent,
        )
        sent = []
        grad_q.append(dq)
        grad_k.append(dk)
        grad_v.append(dv)
        far_part = (
            dot(dk[:, rows:], t_qkv[width : 2 * width]) + dot(dv[:, rows:], t_qkv[2 * width :])
        ).astype(BF)[0]
        far_steps = Staged(
            net.y.scatter_steps(
                lambda s, p=far_part: (
                    jnp.zeros((rows, width), BF) if s == 0 else p[(s - 1) * rows : s * rows]
                )
            )
        )
        sent = sent + far_steps.advance()
        far_parts.append(far_steps)
    unit_last = math.gcd(math.gcd(n_qkv, n_proj), 8)
    (term_last,) = shard_outer(
        net.spots(),
        [flat(each) for each in grad_q + grad_k + grad_v]
        + [attn[:rows] for attn in attn_all]
        + attn_all
        + [flat(grad_branch_one), flat(attended_low)],
        [([n * count + i for i in range(count)], 0, width) for n in range(5)]
        + [([5 * count], 0, width), ([5 * count + 1], 0, width)],
        [(0, 3, n_qkv, 0), (1, 4, n_qkv, 0), (2, 4, n_qkv, 0), (5, 6, n_proj, n_qkv // unit_last)],
        net.z.size, width, unit_last, (n_qkv + n_proj) // unit_last, sent, split=False,
    )
    sum_last = net.scatter(term_last.reshape(dp * (n_qkv + n_proj), width))
    halves = Staged(lockstep(*[net.halves_steps(tie(each, term_last)) for each in (sum_fc2, sum_fc1)]))
    sent = halves.advance()
    grad_q[0] = tie(grad_q[0], *sent)
    bias_q = sum(jnp.sum(each.astype(F32), axis=(0, 1)) for each in grad_q)
    bias_v = sum(jnp.sum(each.astype(F32), axis=(0, 1)) for each in grad_v)
    own_part = jnp.concatenate(
        [
            dot(grad_q[i], t_qkv[:width])
            + dot(grad_k[i][:, :rows], t_qkv[width : 2 * width])
            + dot(grad_v[i][:, :rows], t_qkv[2 * width :])
            for i in range(count)
        ],
        axis=0,
    )
    matrices = (w_qkv, w_proj, w_fc1, w_fc2, w_ada)
    per = -(-sum(matrix.shape[0] // ROW_BLOCK for matrix in matrices) // dp)
    spread_early = (per, 0)
    early_blocks = (w_fc2.shape[0] + w_fc1.shape[0]) // ROW_BLOCK
    spread_last = (per, -(-early_blocks // per))
    far_sum = jnp.stack([steps_of.finish() for steps_of in far_parts])
    grad_attn_in = own_part + far_sum
    normed_one, inverse_one = jnp.stack(normed_all), jnp.stack(inverse_all)
    grad_shift_one = jnp.sum(grad_attn_in, axis=1)
    grad_scale_one = jnp.sum(grad_attn_in * normed_one, axis=1)
    grad_inputs = grad_mixed + norm_back(normed_one, inverse_one, grad_attn_in * (1.0 + scale_one))
    grad_inputs = grad_inputs.astype(BF).reshape(tokens.shape)

    grad_mod_local = jnp.concatenate(
        [grad_shift_one, grad_scale_one, grad_gate_one, grad_shift_two, grad_scale_two, grad_gate_two], axis=-1
    )
    bias_ada = jnp.sum(grad_mod_local, axis=0)
    sent = jnp.transpose(grad_mod_local.reshape(count, dp, 1, ada_cols), (1, 2, 0, 3))
    sent = jnp.broadcast_to(sent, (dp, seq, count, ada_cols))
    mod_parts = net.to_all(sent)
    sums = halves.finish(sent)
    blank = jnp.zeros((2, net.z.size, per, ROW_BLOCK, ROW_BLOCK), F32)
    (next_fc2, next_fc1), *early = muon_gram(
        net.spots(), [(sums[0], [turned[3]]), (sums[1], [turned[2]])], spread_early, (blank, blank)
    )
    mod_parts = tie(mod_parts, early[0])
    mod_cols = jnp.sum(mod_parts, axis=1).astype(BF).reshape(dp * count, ada_cols)
    shard_ada = jnp.einsum("sr,sc->cr", cond_all, mod_cols, preferred_element_type=F32)

    cond_part = jnp.einsum("sc,rc->sr", mod_cols, low_ada, preferred_element_type=F32)
    cond_part = jnp.broadcast_to(cond_part.reshape(dp, 1, -1), (dp, seq, count * ada_rows))
    term_bias = jnp.concatenate([bias_ada, bias_q, bias_v, bias_proj, bias_fc1, bias_fc2])
    parcel = jnp.concatenate([term_bias.reshape(dp, seq, -1), cond_part], axis=-1)
    got_parcel = net.to_all(parcel)

    halves = Staged(net.halves_steps(tie(sum_last, parcel)))
    sent = halves.advance()
    total = halves.finish(shard_ada)
    (next_qkv, next_proj, next_ada), *grams = muon_gram(
        net.spots(), [(total, [turned[0], turned[1]]), (shard_ada, [turned[4]])], spread_last, early
    )
    grams = Staged(net.gram_steps(*grams))
    sent = grams.advance()
    parcel = tie(got_parcel, *sent)
    while not grams.done:
        sent = grams.advance(sent[0])
    gathered = Staged(net.muon_gather_steps(grams.result))
    sent = gathered.advance()
    while not gathered.done:
        sent = gathered.advance(sent[0])
    new_fc2, new_fc1 = muon_apply(
        net.spots(), gathered.result, [next_fc2, next_fc1], [w_fc2.T, w_fc1.T],
        [math.sqrt(width / hidden), math.sqrt(hidden / width)], spread_early,
    )
    new_qkv, new_proj, new_ada = muon_apply(
        net.spots(), gathered.result, [next_qkv, next_proj, next_ada], [w_qkv.T, w_proj.T, w_ada.T],
        [math.sqrt(3.0), 1.0, math.sqrt(6.0)], spread_last,
    )

    size = biases.shape[0]
    grad_bias = jnp.sum(parcel[..., :size], axis=(0, 1))
    cond_part = jnp.sum(parcel[..., size:], axis=0).reshape(seq, count, ada_rows)
    grad_cond = silu_back(jnp.transpose(cond_part, (1, 0, 2)).reshape(count, width))[0]
    next_first = BETA_FIRST * bias_first + (1.0 - BETA_FIRST) * grad_bias
    next_second = BETA_SECOND * bias_second + (1.0 - BETA_SECOND) * grad_bias * grad_bias
    first_hat = next_first / (1.0 - BETA_FIRST**STEP_COUNT)
    second_hat = next_second / (1.0 - BETA_SECOND**STEP_COUNT)
    new_biases = biases * (1.0 - ADAM_RATE * ADAM_DECAY) - ADAM_RATE * first_hat / (
        jnp.sqrt(second_hat) + ADAM_EPS
    )
    return (
        result.reshape(tokens.shape),
        grad_inputs,
        grad_cond.reshape(conditioning.shape),
        new_qkv.T, new_proj.T, new_fc1.T, new_fc2.T, new_ada.T,
        next_qkv.T, next_proj.T, next_fc1.T, next_fc2.T, next_ada.T,
        new_biases,
        next_first,
        next_second,
    )


def solution(mesh):
    rows = P(None, "dp", "seq", None)
    matrix = P("seq", "dp")
    flat = P(("dp", "seq"))
    in_specs = (rows, P(None, "dp", None), P(None, "dp"), P(None, "dp"), rows) + (matrix,) * 10 + (flat,) * 3
    out_specs = (rows, rows, P(None, "dp", None)) + (matrix,) * 10 + (flat,) * 3
    return jax.shard_map(
        functools.partial(body, Net(mesh)), mesh=mesh, in_specs=in_specs, out_specs=out_specs, check_vma=False
    )
```

```python
import functools
import math

import jax
import jax.numpy as jnp
from jax import lax
from jax.experimental import pallas as pl
from jax.experimental.pallas import tpu as pltpu
from jax.sharding import PartitionSpec as P

HEADS = 16
ROW_BLOCK = 144
NS_STEPS = 5
STEP_COUNT = 10

PRECISE = lax.Precision.HIGHEST
LN_EPS = 1e-06
MASKED = -1e30
NS_A = 3.4445
NS_B = -4.775
NS_C = 2.0315
MUON_DECAY = 0.5
WEIGHT_SHRINK = 0.0001
NORM_EPS = 1e-07
BETA_FIRST = 0.9
BETA_SECOND = 0.999
ADAM_RATE = 0.1
ADAM_DECAY = 0.01
ADAM_EPS = 1e-08
BF = jnp.bfloat16
F32 = jnp.float32
VMEM_LIMIT = 60 * 2**20


class Ring:
    def __init__(self, name, total, stride, size):
        self.name, self.total, self.stride, self.size = name, total, stride, size

    def digit(self):
        return (lax.axis_index(self.name) // self.stride) % self.size

    def send(self, value, shift):
        pairs = []
        for i in range(self.total):
            d = (i // self.stride) % self.size
            pairs.append((i, i + ((d + shift) % self.size - d) * self.stride))
        return lax.ppermute(value, self.name, pairs)

    def gather(self, value, far=1):
        n = self.size
        blocks = [value] + [None] * (n - 1)
        if n == 2:
            blocks[1] = self.send(value, 1)
        elif n > 2:
            low = high = value
            for t in range(1, n // 2):
                low, high = self.send(low, 1), self.send(high, -1)
                blocks[n - t], blocks[t] = low, high
            blocks[n // 2] = self.send(low, 1) if far == 1 else self.send(high, -1)
        return blocks

    def gather_steps(self, value, far=1):
        n = self.size
        blocks = [value] + [None] * (n - 1)
        if n == 2:
            blocks[1] = self.send(value, 1)
            anchor = yield [value]
            blocks[1] = tie(blocks[1], anchor)
            return blocks
        low = high = value
        for t in range(1, n // 2):
            sent = [low, high]
            low, high = self.send(low, 1), self.send(high, -1)
            anchor = yield sent
            low, high = tie(low, anchor), tie(high, anchor)
            blocks[n - t], blocks[t] = low, high
        sent = [low if far == 1 else high]
        last = self.send(sent[0], far)
        anchor = yield sent
        blocks[n // 2] = tie(last, anchor)
        return blocks

    def scatter_steps(self, block_of, far=1):
        n = self.size
        if n == 1:
            return block_of(0).astype(F32)
        if n == 2:
            sent = block_of(1)
            got = self.send(sent, 1)
            anchor = yield [sent]
            return block_of(0).astype(F32) + tie(got, anchor).astype(F32)
        sent = block_of(n // 2)
        got = self.send(sent, far)
        anchor = yield [sent]
        low, high = (tie(got, anchor), None) if far == 1 else (None, tie(got, anchor))
        for t in range(n // 2 - 1, 0, -1):
            up, down = block_of(t), block_of(n - t)
            if low is not None:
                up = (up.astype(F32) + low.astype(F32)).astype(up.dtype)
            if high is not None:
                down = (down.astype(F32) + high.astype(F32)).astype(down.dtype)
            low, high = self.send(up, 1), self.send(down, -1)
            anchor = yield [up, down]
            low, high = tie(low, anchor), tie(high, anchor)
        return block_of(0).astype(F32) + low.astype(F32) + high.astype(F32)


def tie(value, *earlier):
    earlier = [array for array in earlier if array is not None]
    if not earlier:
        return value
    anywhere = pl.BlockSpec(memory_space=pl.ANY)
    return pl.pallas_call(
        lambda *refs: None,
        out_shape=jax.ShapeDtypeStruct(value.shape, value.dtype),
        in_specs=[anywhere] * (1 + len(earlier)),
        out_specs=anywhere,
        input_output_aliases={0: 0},
        name="tie",
    )(value, *earlier)


def lockstep(*steps):
    results = [None] * len(steps)
    alive = dict(enumerate(steps))
    anchor = None
    while alive:
        sent = []
        for n, step in list(alive.items()):
            try:
                sent += step.send(anchor)
            except StopIteration as stop:
                results[n] = stop.value
                del alive[n]
        if alive:
            anchor = yield sent
    return results


class Staged:
    def __init__(self, steps):
        self.steps, self.result, self.started, self.done = steps, None, False, False

    def advance(self, anchor=None):
        if self.done:
            return []
        try:
            sent = self.steps.send(anchor if self.started else None)
            self.started = True
            return sent
        except StopIteration as stop:
            self.result, self.done = stop.value, True
            return []

    def finish(self, anchor=None):
        while not self.done:
            self.advance(anchor)
        return self.result


def place_kernel(zs, ga, parts, count, outs, *refs):
    spots, sources = refs[0], refs[1 : 1 + count]
    outputs, (full, in_sems, out_sems) = refs[1 + count : 1 + count + outs], refs[1 + count + outs :]
    g = full.shape[3]
    half = count // 2
    shards = []
    for sc in range(2):
        for sx in range(2):
            for sz in range(zs):
                where = (lax.rem(spots[0] + sz, zs), lax.rem(spots[1] + sx, 2), lax.rem(spots[2] + sc, 2))
                n = 2 * len(shards)
                line, pair = sources[sc * half + sx].at[sz], sources[sc * half + 2 + sz].at[sx]
                copies = [
                    pltpu.make_async_copy(line, full.at[(*where, pl.ds(0, ga))], in_sems.at[n]),
                    pltpu.make_async_copy(pair, full.at[(*where, pl.ds(ga, g - ga))], in_sems.at[n + 1]),
                ]
                for copy in copies:
                    copy.start()
                shards.append((where, copies))
    exits = []
    for where, copies in shards:
        for copy in copies:
            copy.wait()
        for output, start, size, column, depth in parts:
            target = outputs[output].at[(*where, slice(None), slice(None), pl.ds(column, depth))]
            copy = pltpu.make_async_copy(
                full.at[(*where, pl.ds(start, size))], target, out_sems.at[len(exits)]
            )
            copy.start()
            exits.append(copy)
    for copy in exits:
        copy.wait()


def place(spots, sources, shape, ga, parts, shapes):
    zs = shape[0]
    moved = math.prod(shape) * 2
    return pl.pallas_call(
        functools.partial(place_kernel, zs, ga, parts, len(sources), len(shapes)),
        out_shape=[jax.ShapeDtypeStruct(each, BF) for each in shapes],
        in_specs=[pl.BlockSpec(memory_space=pltpu.SMEM)]
        + [pl.BlockSpec(memory_space=pl.ANY)] * len(sources),
        out_specs=[pl.BlockSpec(memory_space=pl.ANY)] * len(shapes),
        scratch_shapes=[
            pltpu.VMEM(shape, BF),
            pltpu.SemaphoreType.DMA((8 * zs,)),
            pltpu.SemaphoreType.DMA((4 * zs * len(parts),)),
        ],
        compiler_params=pltpu.CompilerParams(vmem_limit_bytes=VMEM_LIMIT),
        cost_estimate=pl.CostEstimate(flops=0, bytes_accessed=2 * moved, transcendentals=0),
        name="place",
    )(spots, *sources)


class Net:
    def __init__(self, mesh):
        dp, seq = mesh.shape["dp"], mesh.shape["seq"]
        self.dp, self.seq = dp, seq
        self.core = Ring("dp", dp, 1, 2)
        self.x = Ring("dp", dp, 2, 2)
        self.z = Ring("dp", dp, 4, dp // 4)
        self.y = Ring("seq", seq, 1, seq)

    def spots(self):
        return jnp.stack([self.z.digit(), self.x.digit(), self.core.digit()]).astype(jnp.int32)


    def wire(self, shards):
        turned = [shard.astype(BF).T for shard in shards]
        return turned[0] if len(turned) == 1 else jnp.concatenate(turned, axis=0)

    def rows(self, wires):
        if self.seq == 2:
            own, other = wires
            return jnp.where(
                self.y.digit() == 0,
                jnp.concatenate([own, other], axis=1),
                jnp.concatenate([other, own], axis=1),
            )
        order = (jnp.arange(self.seq) - self.y.digit()) % self.seq
        full = jnp.take(jnp.stack(wires), order, axis=0)
        return jnp.transpose(full, (1, 0, 2)).reshape(full.shape[1], -1)

    def joined(self, wires, unit, depth):
        full = self.rows(wires)
        return full.reshape(full.shape[0] // unit, unit, depth)

    def scatter(self, term):
        return lax.psum_scatter(term, "dp", scatter_dimension=0, tiled=True)

    def halves_steps(self, term):
        y = self.y.digit()
        blocks = term.reshape(term.shape[0], self.seq, -1)
        return (
            yield from self.y.scatter_steps(
                lambda s: lax.dynamic_index_in_dim(blocks, (y + s) % self.seq, 1, keepdims=False)
            )
        )

    def gather_steps(self, units, layout, part):
        g, unit, depth = units.shape
        zs = self.z.size
        ga = max(1, int(part * g))
        first, second = units[:ga], units[ga:]

        def line_steps():
            blocks = yield from self.z.gather_steps(first, 1)
            line = jnp.stack(blocks)
            return (yield from self.x.gather_steps(line))

        def pair_steps():
            blocks = yield from self.x.gather_steps(second)
            return (yield from self.z.gather_steps(jnp.stack(blocks), -1))

        lines, pairs = yield from lockstep(line_steps(), pair_steps())
        pieces = lines + pairs
        others = [self.core.send(piece, 1) for piece in pieces]
        anchor = yield pieces
        sources = pieces + [tie(other, anchor) for other in others]
        parts, shapes, start = [], [], 0
        for n, (rows, blocks) in enumerate(layout):
            size = rows // unit
            shapes.append((zs, 2, 2, size, unit, blocks * depth))
            for j in range(blocks):
                parts.append((n, start, size, j * depth, depth))
                start += size
        full = place(self.spots(), sources, (zs, 2, 2, g, unit, depth), ga, parts, shapes)
        return [f.reshape(-1, f.shape[-1]) for f in full], lines[1:] + pairs[1:]


    def gram_steps(self, own, other):
        got = self.core.send(other, 1)
        anchor = yield [other]
        half = own + tie(got, anchor)
        sent = half[1].astype(BF)
        got = self.x.send(sent, 1)
        anchor = yield [sent]
        kept = half[0] + tie(got, anchor).astype(F32)
        sent = [kept[shift].astype(BF) for shift in range(1, self.z.size)]
        got = [self.z.send(each, shift) for shift, each in enumerate(sent, 1)]
        anchor = yield sent
        return [kept[0]] + [tie(each, anchor) for each in got]

    def muon_gather_steps(self, parts):
        factor = polynomial(parts)
        got = [self.z.send(factor, -shift) for shift in range(1, self.z.size)]
        anchor = yield [factor]
        line = jnp.stack([factor] + [tie(each, anchor) for each in got])
        got = self.x.send(line, 1)
        anchor = yield [line]
        pair = [line, tie(got, anchor)]
        others = [self.core.send(each, 1) for each in pair]
        anchor = yield pair
        return pair + [tie(each, anchor) for each in others]


    def to_all(self, value):
        flat = value.reshape((self.dp * self.seq,) + value.shape[2:])
        return lax.all_to_all(flat, ("dp", "seq"), 0, 0, tiled=True).reshape(value.shape)

    def to_dp(self, value):
        return lax.all_to_all(value, "dp", 0, 0, tiled=True)


def layer_norm(values):
    centered = values - jnp.mean(values, axis=-1, keepdims=True)
    inverse = lax.rsqrt(jnp.mean(centered * centered, axis=-1, keepdims=True) + LN_EPS)
    return (centered * inverse, inverse)


def norm_back(normed, inverse, grad):
    mean_grad = jnp.mean(grad, axis=-1, keepdims=True)
    mean_cross = jnp.mean(grad * normed, axis=-1, keepdims=True)
    return inverse * (grad - mean_grad - normed * mean_cross)


def sigmoid_linear(values):
    return values * jax.nn.sigmoid(values)


def gelu_tanh(values):
    return jax.nn.gelu(values, approximate=True)


def dot_t(left, right):
    return jnp.einsum("srk,nk->srn", left, right, preferred_element_type=F32)


def dot(left, right):
    return jnp.einsum("srn,nk->srk", left, right, preferred_element_type=F32)


def outer(left, right):
    return jnp.einsum("srn,srk->nk", left, right, preferred_element_type=F32).astype(BF)


def shard_outer_kernel(plan, counts, tile, split, spots_ref, *refs):
    outs = 2 if split else 1
    inputs, where = refs[: counts[0]], refs[counts[1] : counts[1] + outs]
    buffers = refs[counts[1] + outs : counts[1] + outs + len(plan["loads"])]
    acc, in_sems, out_sems = refs[counts[1] + outs + len(plan["loads"]) :]
    loads = []
    for n, (sources, start, size) in enumerate(plan["loads"]):
        row, copies = 0, []
        for m, source in enumerate(sources):
            rows = inputs[source].shape[0]
            window = inputs[source].at[:, pl.ds(start, size)]
            copies.append(pltpu.make_async_copy(window, buffers[n].at[pl.ds(row, rows)], in_sems.at[n, m]))
            copies[-1].start()
            row += rows
        loads.append(copies)
    ready = set()
    shipped = []
    unit = acc.shape[1]
    for left, right, base, ships in plan["parts"]:
        for n in (left, right):
            if n not in ready:
                for copy in loads[n]:
                    copy.wait()
                ready.add(n)
        width = buffers[left].shape[1]
        step = tile if width % tile == 0 else width

        @pl.loop(0, width // step)
        def _(t):
            block = buffers[left][:, pl.ds(pl.multiple_of(t * step, step), step)]
            product = lax.dot_general(
                block, buffers[right][...], (((0,), (0,)), ((), ())), preferred_element_type=F32
            )
            product = product.reshape(step // unit, unit, product.shape[1]).astype(BF)
            acc[pl.ds(base + t * (step // unit), step // unit)] = product

        for core, z, x, row, target, size in ships:
            spot = (z, x) if split else (z, x, core)
            places = [ref.at[(*spot, pl.ds(target, size))] for ref in where]
            copies = [
                pltpu.make_async_copy(acc.at[pl.ds(row, size)], each, out_sems.at[len(shipped)]) for each in places
            ]
            shipped.append((core, copies))
            on_own_core(split, spots_ref, core, [copy.start for copy in copies])
    for core, copies in shipped:
        on_own_core(split, spots_ref, core, [copy.wait for copy in copies])


def on_own_core(split, spots_ref, core, actions):
    if not split:
        actions[0]()
        return

    @pl.when(spots_ref[2] == core)
    def _():
        actions[0]()

    @pl.when(spots_ref[2] != core)
    def _():
        actions[1]()


def shard_outer(spots, inputs, loads, parts, zs, depth, unit, shard_units, deps=(), tile=384, split=True):
    dp = zs * 4
    plan_parts, base, row, placed = [], 0, 0, {}
    begun = {}
    for left, right, rows, first in parts:
        if first not in begun:
            begun[first] = (base, 0)
        start, shipped = begun[first]
        width = loads[left][2]
        size = rows // unit
        end = base + width // unit
        ships = []
        while shipped < dp and start + (shipped + 1) * size <= end:
            core, x, z = shipped % 2, shipped // 2 % 2, shipped // 4
            ships.append((core, z, x, start + shipped * size, first, size))
            shipped += 1
        begun[first] = (start, shipped)
        plan_parts.append((left, right, base, ships))
        base = end
    total = sum(len(part[3]) for part in plan_parts)
    shape = (zs, 2, shard_units, unit, depth) if split else (zs, 2, 2, shard_units, unit, depth)
    outs = [jax.ShapeDtypeStruct(shape, BF)] * (2 if split else 1)
    anywhere = pl.BlockSpec(memory_space=pl.ANY)
    heights = [sum(inputs[source].shape[0] for source in sources) for sources, _, _ in loads]
    flops = sum(2 * heights[p[0]] * loads[p[0]][2] * loads[p[1]][2] for p in parts)
    return pl.pallas_call(
        functools.partial(
            shard_outer_kernel, {"loads": loads, "parts": plan_parts}, (len(inputs), len(inputs) + len(deps)), tile, split
        ),
        out_shape=outs,
        in_specs=[pl.BlockSpec(memory_space=pltpu.SMEM)] + [anywhere] * (len(inputs) + len(deps)),
        out_specs=[anywhere] * len(outs),
        scratch_shapes=[pltpu.VMEM((height, load[2]), BF) for height, load in zip(heights, loads)]
        + [
            pltpu.VMEM((base, unit, depth), BF),
            pltpu.SemaphoreType.DMA((len(loads), max(len(load[0]) for load in loads))),
            pltpu.SemaphoreType.DMA((total,)),
        ],
        compiler_params=pltpu.CompilerParams(vmem_limit_bytes=VMEM_LIMIT),
        cost_estimate=pl.CostEstimate(flops=flops, bytes_accessed=2 * base * unit * depth, transcendentals=0),
        name="shard_outer",
    )(spots, *inputs, *deps)


LANES = 128
LOG2E = math.log2(math.e)


def padded(block, column=None):
    rows, depth = block.shape
    if column is None:
        return jnp.concatenate([block, jnp.zeros((rows, LANES - depth), block.dtype)], axis=1)
    rest = jnp.zeros((rows, LANES - depth - 1), block.dtype)
    return jnp.concatenate([block, column.astype(block.dtype), rest], axis=1)


def mask_column(lengths_ref, offsets_ref, sample, total, rows):
    place = lax.broadcasted_iota(jnp.int32, (total, 1), 0)
    position = place
    for s in range(total // rows):
        position = jnp.where(place // rows == s, place - s * rows + offsets_ref[s], position)
    return jnp.where(position < lengths_ref[sample], 0.0, MASKED)


def nt(left, right):
    return lax.dot_general(left, right, (((1,), (1,)), ((), ())), preferred_element_type=F32)


def nn(left, right):
    return jnp.dot(left, right, preferred_element_type=F32)


def without(kernel, start, count, *fixed):
    def run(*refs):
        kernel(*fixed, *refs[:start], *refs[start + count :])

    return run


def attend_kernel(heads, chunk, lengths_ref, offsets_ref, q_ref, k_ref, v_ref, o_ref, lse_ref, q_s, k_s, vt_s, o_s):
    rows, width = q_ref.shape[1:]
    total = k_ref.shape[1]
    depth = width // heads
    factor = depth**-0.5 * LOG2E
    mask = mask_column(lengths_ref, offsets_ref, pl.program_id(0), total, rows)
    ones = jnp.ones((rows, 1), F32)
    for h in range(heads):
        span = slice(h * depth, (h + 1) * depth)
        q_s[h] = padded(q_ref[0, :, span], ones)
        k_s[h] = padded(k_ref[0, :, span], mask)
        vt_s[h] = jnp.transpose(v_ref[0, :, span])

    def one_head(h, carry):
        peak = jnp.full((1, rows), MASKED, F32)
        sums = jnp.zeros((1, rows), F32)
        mixed = jnp.zeros((depth, rows), F32)
        for c in range(total // chunk):
            part = slice(c * chunk, (c + 1) * chunk)
            scores = nt(k_s[h, part], q_s[h])
            higher = jnp.maximum(peak, jnp.max(scores, axis=0, keepdims=True))
            weights = jnp.exp2((scores - higher) * factor)
            if c == 0:
                sums = jnp.sum(weights, axis=0, keepdims=True)
                mixed = nn(vt_s[h, :, part], weights.astype(BF))
            else:
                shrink = jnp.exp2((peak - higher) * factor)
                sums = sums * shrink + jnp.sum(weights, axis=0, keepdims=True)
                mixed = mixed * shrink + nn(vt_s[h, :, part], weights.astype(BF))
            peak = higher
        o_s[h] = jnp.transpose(mixed / sums)
        lse_ref[0, h] = peak * factor + jnp.log2(sums)
        return carry

    lax.fori_loop(0, heads, one_head, 0)
    for h in range(heads):
        o_ref[0, :, h * depth : (h + 1) * depth] = o_s[h].astype(BF)


def attend(lengths, offsets, queries, keys, values, heads, tile, deps=()):
    count, rows, width = queries.shape
    total = keys.shape[1]
    depth = width // heads
    tile = min(tile, total)
    pick = lambda i, *_: (i, 0, 0)
    return pl.pallas_call(
        without(attend_kernel, 5, len(deps), heads, tile),
        grid_spec=pltpu.PrefetchScalarGridSpec(
            num_scalar_prefetch=2,
            grid=(count,),
            in_specs=[
                pl.BlockSpec((1, rows, width), pick),
                pl.BlockSpec((1, total, width), pick),
                pl.BlockSpec((1, total, width), pick),
            ]
            + [pl.BlockSpec(memory_space=pl.ANY)] * len(deps),
            out_specs=[
                pl.BlockSpec((1, rows, width), pick),
                pl.BlockSpec((1, heads, 1, rows), lambda i, *_: (i, 0, 0, 0)),
            ],
            scratch_shapes=[
                pltpu.VMEM((heads, rows, LANES), BF),
                pltpu.VMEM((heads, total, LANES), BF),
                pltpu.VMEM((heads, depth, total), BF),
                pltpu.VMEM((heads, rows, depth), F32),
            ],
        ),
        out_shape=[
            jax.ShapeDtypeStruct((count, rows, width), BF),
            jax.ShapeDtypeStruct((count, heads, 1, rows), F32),
        ],
        compiler_params=pltpu.CompilerParams(vmem_limit_bytes=VMEM_LIMIT),
        cost_estimate=pl.CostEstimate(
            flops=4 * count * heads * rows * total * LANES,
            bytes_accessed=2 * count * width * (2 * rows + 2 * total),
            transcendentals=count * heads * rows * total,
        ),
        name="attend",
    )(lengths, offsets, queries, keys, values, *deps)


def attend_back_kernel(
    heads, chunk, lengths_ref, offsets_ref, q_ref, k_ref, v_ref, o_ref, g_ref, lse_ref,
    dq_ref, dk_ref, dv_ref, q_s, k_s, kt_s, v_s, g_s, delta_s, dq_s, dk_s, dv_s
):
    rows, width = q_ref.shape[1:]
    total = k_ref.shape[1]
    depth = width // heads
    scale = depth**-0.5
    factor = scale * LOG2E
    mask = mask_column(lengths_ref, offsets_ref, pl.program_id(0), total, rows)
    ones = jnp.ones((rows, 1), F32)
    cross = jnp.transpose(g_ref[0].astype(F32) * o_ref[0].astype(F32))
    for h in range(heads):
        span = slice(h * depth, (h + 1) * depth)
        delta_s[h] = jnp.sum(cross[span], axis=0, keepdims=True)
        q_s[h] = padded(q_ref[0, :, span], ones)
        k_s[h] = padded(k_ref[0, :, span], mask)
        kt_s[h] = jnp.transpose(k_ref[0, :, span])
        g_s[h] = padded(g_ref[0, :, span])
        v_s[h] = padded(v_ref[0, :, span])

    def one_head(h, carry):
        dq = jnp.zeros((depth, rows), F32)
        for c in range(total // chunk):
            part = slice(c * chunk, (c + 1) * chunk)
            probs = jnp.exp2(nt(k_s[h, part], q_s[h]) * factor - lse_ref[0, h])
            slopes = (probs * (nt(v_s[h, part], g_s[h]) - delta_s[h])).astype(BF)
            dv_s[h, part] = nn(probs.astype(BF), g_s[h]).astype(BF)
            dk_s[h, part] = (nn(slopes, q_s[h]) * scale).astype(BF)
            dq = dq + nn(kt_s[h, :, part], slopes)
        dq_s[h] = jnp.transpose(dq * scale)
        return carry

    lax.fori_loop(0, heads, one_head, 0)
    for h in range(heads):
        span = slice(h * depth, (h + 1) * depth)
        dq_ref[0, :, span] = dq_s[h].astype(BF)
        dk_ref[0, :, span] = dk_s[h][:, :depth]
        dv_ref[0, :, span] = dv_s[h][:, :depth]


def attend_back(lengths, offsets, queries, keys, values, mixed, grads, lse, heads, tile, deps=()):
    count, rows, width = queries.shape
    total = keys.shape[1]
    depth = width // heads
    tile = min(tile, total)
    pick = lambda i, *_: (i, 0, 0)
    near = pl.BlockSpec((1, rows, width), pick)
    far = pl.BlockSpec((1, total, width), pick)
    return pl.pallas_call(
        without(attend_back_kernel, 8, len(deps), heads, tile),
        grid_spec=pltpu.PrefetchScalarGridSpec(
            num_scalar_prefetch=2,
            grid=(count,),
            in_specs=[near, far, far, near, near, pl.BlockSpec((1, heads, 1, rows), lambda i, *_: (i, 0, 0, 0))]
            + [pl.BlockSpec(memory_space=pl.ANY)] * len(deps),
            out_specs=[near, far, far],
            scratch_shapes=[
                pltpu.VMEM((heads, rows, LANES), BF),
                pltpu.VMEM((heads, total, LANES), BF),
                pltpu.VMEM((heads, depth, total), BF),
                pltpu.VMEM((heads, total, LANES), BF),
                pltpu.VMEM((heads, rows, LANES), BF),
                pltpu.VMEM((heads, 1, rows), F32),
                pltpu.VMEM((heads, rows, depth), F32),
                pltpu.VMEM((heads, total, LANES), BF),
                pltpu.VMEM((heads, total, LANES), BF),
            ],
        ),
        out_shape=[
            jax.ShapeDtypeStruct((count, rows, width), BF),
            jax.ShapeDtypeStruct((count, total, width), BF),
            jax.ShapeDtypeStruct((count, total, width), BF),
        ],
        compiler_params=pltpu.CompilerParams(vmem_limit_bytes=VMEM_LIMIT),
        cost_estimate=pl.CostEstimate(
            flops=10 * count * heads * rows * total * LANES,
            bytes_accessed=2 * count * width * (4 * rows + 4 * total),
            transcendentals=count * heads * rows * total,
        ),
        name="attend_back",
    )(lengths, offsets, queries, keys, values, mixed, grads, lse, *deps)


def block_spots(counts, spread):
    per, first = spread
    spots = []
    for matrix, count in enumerate(counts):
        for block in range(count):
            device, place_in = divmod(len(spots), per)
            device += first
            spots.append((matrix, block, device // 4, device // 2 % 2, device % 2, place_in))
    return spots


def precise(left, right, dims):
    return lax.dot_general(left, right, (dims, ((), ())), precision=PRECISE, preferred_element_type=F32)


def muon_gram_kernel(groups, spread, spots_ref, base_own, base_other, *refs):
    count = sum(groups)
    sums, momenta = refs[: len(groups)], refs[len(groups) : len(groups) + count]
    outs = refs[len(groups) + count : len(groups) + 2 * count]
    own_ref, other_ref, grams, sems = refs[len(groups) + 2 * count :]
    n = 0
    for matrices, sum_ref in zip(groups, sums):
        start = 0
        for _ in range(matrices):
            size = momenta[n].shape[0]
            outs[n][...] = MUON_DECAY * momenta[n][...] + sum_ref[start : start + size]
            start += size
            n += 1
    zs = own_ref.shape[1]
    spots = block_spots([out.shape[1] // ROW_BLOCK for out in outs], spread)
    copies = []
    for n, (matrix, block, z, x, core, place_in) in enumerate(spots):
        turned = outs[matrix][:, block * ROW_BLOCK : (block + 1) * ROW_BLOCK]
        grams[n] = precise(turned, turned, ((0,), (0,)))
        away = (lax.rem(spots_ref[1] + x, 2), lax.rem(zs + z - spots_ref[0], zs), place_in)
        pair = [pltpu.make_async_copy(grams.at[n], ref.at[away], sems.at[n]) for ref in (own_ref, other_ref)]
        on_own_core(True, spots_ref, core, [copy.start for copy in pair])
        copies.append((core, pair))
    for core, pair in copies:
        on_own_core(True, spots_ref, core, [copy.wait for copy in pair])


def muon_gram(spots, groups, spread, base):
    momenta = [momentum for _, each in groups for momentum in each]
    terms = jax.ShapeDtypeStruct(base[0].shape, F32)
    vmem, anywhere = pl.BlockSpec(memory_space=pltpu.VMEM), pl.BlockSpec(memory_space=pl.ANY)
    blocks = len(block_spots([momentum.shape[1] // ROW_BLOCK for momentum in momenta], spread))
    outs = pl.pallas_call(
        functools.partial(muon_gram_kernel, [len(each) for _, each in groups], spread),
        out_shape=[jax.ShapeDtypeStruct(momentum.shape, F32) for momentum in momenta] + [terms, terms],
        in_specs=[pl.BlockSpec(memory_space=pltpu.SMEM), anywhere, anywhere]
        + [vmem] * (len(groups) + len(momenta)),
        out_specs=[vmem] * len(momenta) + [anywhere, anywhere],
        input_output_aliases={1: len(momenta), 2: len(momenta) + 1},
        scratch_shapes=[
            pltpu.VMEM((blocks, ROW_BLOCK, ROW_BLOCK), F32),
            pltpu.SemaphoreType.DMA((blocks,)),
        ],
        compiler_params=pltpu.CompilerParams(vmem_limit_bytes=VMEM_LIMIT),
        name="muon_gram",
    )(spots, *base, *[group[0] for group in groups], *momenta)
    return outs[:-2], outs[-2], outs[-1]


def polynomial_kernel(count, *refs):
    out = refs[count]
    shape = (ROW_BLOCK, ROW_BLOCK)
    eye = (lax.broadcasted_iota(jnp.int32, shape, 0) == lax.broadcasted_iota(jnp.int32, shape, 1)).astype(F32)
    mul = lambda left, right: precise(left, right, ((1,), (0,)))
    blocks = range(out.shape[0])
    currents, scales, totals = [], [], []
    for n in blocks:
        gram = refs[0][n]
        for ref in refs[1:count]:
            gram = gram + ref[n].astype(F32)
        square = jnp.sum(jnp.sum(gram * eye, axis=1, keepdims=True), axis=0, keepdims=True)
        scale = 1.0 / (jnp.sqrt(square) + NORM_EPS)
        scales.append(scale)
        currents.append(gram * (scale * scale))
    for step in range(NS_STEPS):
        factors = [NS_A * eye + NS_B * a + NS_C * mul(a, a) for a in currents]
        totals = factors if step == 0 else [mul(f, t) for f, t in zip(factors, totals)]
        if step + 1 < NS_STEPS:
            currents = [mul(f, a) for f, a in zip(factors, currents)]
            currents = [mul(a, f) for f, a in zip(factors, currents)]
    for n in blocks:
        out[n] = totals[n] * scales[n]


def polynomial(parts):
    vmem = pl.BlockSpec(memory_space=pltpu.VMEM)
    return pl.pallas_call(
        functools.partial(polynomial_kernel, len(parts)),
        out_shape=jax.ShapeDtypeStruct(parts[0].shape, F32),
        in_specs=[vmem] * len(parts),
        out_specs=vmem,
        compiler_params=pltpu.CompilerParams(vmem_limit_bytes=VMEM_LIMIT),
        name="polynomial",
    )(*parts)


def muon_apply_kernel(rates, placed, spots_ref, *refs):
    count = len(rates)
    parts, momenta, masters = refs[:4], refs[4 : 4 + count], refs[4 + count : 4 + 2 * count]
    outs, factors = refs[4 + 2 * count : 4 + 3 * count], refs[4 + 3 * count]
    for n in range(4):
        factors[n] = parts[n][...]
    zs = factors.shape[1]
    for matrix, block, z, x, core, place_in in placed:
        part = slice(block * ROW_BLOCK, (block + 1) * ROW_BLOCK)
        away = 2 * lax.rem(spots_ref[2] + core, 2) + lax.rem(spots_ref[1] + x, 2)
        factor = factors[away, lax.rem(zs + z - spots_ref[0], zs), place_in]
        direction = precise(momenta[matrix][:, part], factor, ((1,), (1,)))
        outs[matrix][:, part] = masters[matrix][:, part] * (1.0 - WEIGHT_SHRINK) - rates[matrix] * direction


def muon_apply(spots, factors, momenta, masters, rates, placed):
    vmem = pl.BlockSpec(memory_space=pltpu.VMEM)
    return pl.pallas_call(
        functools.partial(muon_apply_kernel, rates, placed),
        out_shape=[jax.ShapeDtypeStruct(master.shape, F32) for master in masters],
        in_specs=[pl.BlockSpec(memory_space=pltpu.SMEM)] + [vmem] * (4 + 2 * len(masters)),
        out_specs=[vmem] * len(masters),
        scratch_shapes=[pltpu.VMEM((4,) + factors[0].shape, F32)],
        compiler_params=pltpu.CompilerParams(vmem_limit_bytes=VMEM_LIMIT),
        name="muon_apply",
    )(spots, *factors, *momenta, *masters)


def body(net, tokens, conditioning, heights, widths, upstream, *state):
    masters, momenta = state[0:5], state[5:10]
    biases, bias_first, bias_second = state[10:13]
    w_qkv, w_proj, w_fc1, w_fc2, w_ada = masters
    micro, local, rows, width = tokens.shape
    count = micro * local
    head_dim = width // HEADS
    hidden = w_fc1.shape[1] * net.dp
    seq, dp = net.seq, net.dp
    y = net.y.digit()

    bounds = [0, 6 * width, 7 * width, 8 * width, 9 * width, 9 * width + hidden, 10 * width + hidden]

    n_qkv, n_proj, n_fc1, n_fc2 = [w.shape[1] for w in (w_qkv, w_proj, w_fc1, w_fc2)]
    unit = math.gcd(math.gcd(n_qkv, n_proj), 8)
    unit_qkv, layout_qkv = math.gcd(n_qkv, 8), [(n_qkv, 1)]
    own_tokens = tokens.reshape(count, rows, width)
    wires = net.y.gather(net.wire([w_qkv, w_proj]))

    ada_rows, ada_cols = w_ada.shape
    cond = conditioning.astype(F32).reshape(count, width)
    cond_act, silu_back = jax.vjp(sigmoid_linear, cond)
    cond_low = cond_act.astype(BF).astype(F32)
    cond_parts = jnp.transpose(cond_low.reshape(count, seq, ada_rows), (1, 0, 2)).reshape(seq, -1)
    parcel = jnp.concatenate([jnp.broadcast_to(biases, (seq,) + biases.shape), cond_parts], axis=1)
    parcel = net.to_all(tie(jnp.broadcast_to(parcel[None], (dp,) + parcel.shape), wires[0]))
    cond_all = parcel[:, 0, biases.shape[0] :].reshape(dp * count, ada_rows).astype(BF)
    first = Staged(net.gather_steps(net.joined(wires, unit, width), [(n_qkv, 1), (n_proj, 1)], 0.45))
    sent = first.advance()
    token_pieces = [net.y.gather(tie(own_tokens[0], *sent))]

    low_ada = w_ada.astype(BF)
    partial = jnp.dot(tie(cond_all, *sent), low_ada, preferred_element_type=F32).reshape(dp, 1, count, ada_cols)
    partial = jnp.broadcast_to(partial, (dp, seq, count, ada_cols))
    received = net.to_all(partial)
    first.advance(partial)
    sent = first.advance(received)
    received, parcel = tie(received, *sent), tie(parcel, *sent)
    received = jnp.sum(received, axis=1)
    bias_full = parcel[:, :, : biases.shape[0]].reshape(-1)
    b_ada, b_q, b_v, b_proj, b_fc1, b_fc2 = [bias_full[bounds[i] : bounds[i + 1]] for i in range(6)]
    modulation = jnp.transpose(received, (1, 0, 2)).reshape(count, dp * ada_cols) + b_ada
    shift_one, scale_one, gate_one, shift_two, scale_two, gate_two = jnp.split(
        modulation[:, None, :], 6, axis=-1
    )
    t_qkv, t_proj = first.finish(modulation)[0]
    wires = net.y.gather(tie(net.wire([w_fc1]), token_pieces[0][-1], *sent))
    wires = wires[:1] + [tie(wire, t_qkv) for wire in wires[1:]]
    t_fc1 = lax.all_gather(net.rows(wires), "dp", axis=0, tiled=True)
    for i in range(1, count):
        token_pieces.append(net.y.gather(tie(own_tokens[i], wires[-1])))

    lengths = (heights * widths).reshape(count).astype(jnp.int32)
    offsets = jnp.stack([((y + s) % seq) * rows for s in range(seq)]).astype(jnp.int32)
    normed_all, inverse_all, attn_all, queries, keys, values, attended_low, log_total = [[] for _ in range(8)]
    for i in range(count):
        normed, inverse = layer_norm(jnp.concatenate(token_pieces[i], axis=0).astype(F32))
        attn = (normed * (1.0 + scale_one[i]) + shift_one[i]).astype(BF)
        queries.append((dot_t(attn[None, :rows], t_qkv[:width]) + b_q).astype(BF))
        keys.append(dot_t(attn[None], t_qkv[width : 2 * width]).astype(BF))
        values.append((dot_t(attn[None], t_qkv[2 * width :]) + b_v).astype(BF))
        mixed, lse = attend(lengths[i : i + 1], offsets, queries[i], keys[i], values[i], HEADS, 512)
        if i == 0:
            token_pieces[1:] = [each[:1] + [tie(a, mixed) for a in each[1:]] for each in token_pieces[1:]]
            last_piece = token_pieces[-1][-1] if count > 1 else mixed
            wires = net.y.gather(tie(net.wire([w_fc2]), last_piece))
        normed_all.append(normed[:rows])
        inverse_all.append(inverse[:rows])
        attn_all.append(attn)
        attended_low.append(mixed[0])
        log_total.append(lse)
    wires = wires[:1] + [tie(wire, keys[-1]) for wire in wires[1:]]
    t_fc2 = lax.all_gather(net.rows(wires), "dp", axis=0, tiled=True)
    attended_low = jnp.stack(attended_low)

    inputs = own_tokens.astype(F32)
    branch_one = dot_t(attended_low, t_proj) + b_proj
    mixed_one = inputs + gate_one * branch_one
    normed_two, inverse_two = layer_norm(mixed_one)
    ffn_in = (normed_two * (1.0 + scale_two) + shift_two).astype(BF)
    pre_act = dot_t(ffn_in, t_fc1) + b_fc1
    activated, gelu_back = jax.vjp(gelu_tanh, pre_act)
    activated_low = activated.astype(BF)
    grad_out = upstream.reshape(count, rows, width).astype(F32)
    grad_branch_two = (gate_two * grad_out).astype(BF)
    flat = lambda array: array.reshape(-1, array.shape[-1])
    term_fc2 = outer(grad_branch_two, activated_low)
    sum_fc2 = net.scatter(term_fc2)
    branch_two = dot_t(tie(activated_low, term_fc2), t_fc2) + b_fc2
    grad_branch_two = tie(grad_branch_two, term_fc2)
    result = (mixed_one + gate_two * branch_two).astype(BF)

    grad_gate_two = jnp.sum(branch_two * grad_out, axis=1)
    bias_fc2 = jnp.sum(grad_branch_two.astype(F32), axis=(0, 1))
    grad_pre = gelu_back(dot(grad_branch_two, t_fc2))[0].astype(BF)
    term_fc1 = outer(grad_pre, ffn_in)
    grad_pre = tie(grad_pre, term_fc1)
    bias_fc1 = jnp.sum(grad_pre.astype(F32), axis=(0, 1))
    grad_ffn_in = dot(grad_pre, t_fc1)
    grad_shift_two = jnp.sum(grad_ffn_in, axis=1)
    grad_scale_two = jnp.sum(grad_ffn_in * normed_two, axis=1)
    grad_mixed = grad_out + norm_back(normed_two, inverse_two, grad_ffn_in * (1.0 + scale_two))
    grad_gate_one = jnp.sum(branch_one * grad_mixed, axis=1)
    grad_branch_one = (gate_one * grad_mixed).astype(BF)
    bias_proj = jnp.sum(grad_branch_one.astype(F32), axis=(0, 1))
    grad_attended = dot(grad_branch_one, t_proj).astype(BF)
    term_fc1 = tie(term_fc1, sum_fc2, grad_attended)
    sum_fc1 = net.scatter(term_fc1)
    term_proj = tie(outer(grad_branch_one, attended_low), term_fc1)
    sum_proj = net.scatter(term_proj)
    grad_attended = tie(grad_attended, term_proj)

    def far_steps(dk, dv):
        part = dot(dk[:, rows:], t_qkv[width : 2 * width]) + dot(dv[:, rows:], t_qkv[2 * width :])
        part = part.astype(BF)[0]
        blank = jnp.zeros((rows, width), BF)
        return Staged(net.y.scatter_steps(lambda s: blank if s == 0 else part[(s - 1) * rows : s * rows]))

    grad_q, grad_k, grad_v, far_parts = [], [], [], []
    turned = [momentum.T for momentum in momenta]
    sent = []
    for i in range(count):
        dq, dk, dv = attend_back(
            lengths[i : i + 1], offsets, queries[i], keys[i], values[i], attended_low[i : i + 1],
            grad_attended[i : i + 1], log_total[i], HEADS, 512, sent,
        )
        sent = []
        grad_q.append(dq)
        grad_k.append(dk)
        grad_v.append(dv)
        if i + 1 < count:
            far_parts.append(far_steps(dk, dv))
            sent = sent + far_parts[-1].advance()
    unit_last = math.gcd(n_qkv, 8)
    (term_last,) = shard_outer(
        net.spots(),
        [flat(each) for each in grad_q + grad_k + grad_v]
        + [attn[:rows] for attn in attn_all]
        + attn_all,
        [([n * count + i for i in range(count)], 0, width) for n in range(5)],
        [(0, 3, n_qkv, 0), (1, 4, n_qkv, 0), (2, 4, n_qkv, 0)],
        net.z.size, width, unit_last, n_qkv // unit_last, sent, split=False,
    )
    sum_last = net.scatter(term_last.reshape(dp * n_qkv, width))
    grad_k[-1] = tie(grad_k[-1], term_last)
    far_parts.append(far_steps(grad_k[-1], grad_v[-1]))
    sent = far_parts[-1].advance()
    halves = Staged(lockstep(*[net.halves_steps(tie(each, *sent)) for each in (sum_fc2, sum_fc1, sum_proj)]))
    sent = sent + halves.advance()
    grad_q[0] = tie(grad_q[0], *sent)
    bias_q = sum(jnp.sum(each.astype(F32), axis=(0, 1)) for each in grad_q)
    bias_v = sum(jnp.sum(each.astype(F32), axis=(0, 1)) for each in grad_v)
    own_part = jnp.concatenate(
        [
            dot(grad_q[i], t_qkv[:width])
            + dot(grad_k[i][:, :rows], t_qkv[width : 2 * width])
            + dot(grad_v[i][:, :rows], t_qkv[2 * width :])
            for i in range(count)
        ],
        axis=0,
    )
    matrices = (w_qkv, w_proj, w_fc1, w_fc2, w_ada)
    per = -(-sum(matrix.shape[0] // ROW_BLOCK for matrix in matrices) // dp)
    spread_early = (per, 0)
    early_blocks = (w_fc2.shape[0] + w_fc1.shape[0] + w_proj.shape[0]) // ROW_BLOCK
    spread_last = (per, -(-early_blocks // per))
    far_sum = jnp.stack([steps_of.finish() for steps_of in far_parts])
    grad_attn_in = own_part + far_sum
    normed_one, inverse_one = jnp.stack(normed_all), jnp.stack(inverse_all)
    grad_shift_one = jnp.sum(grad_attn_in, axis=1)
    grad_scale_one = jnp.sum(grad_attn_in * normed_one, axis=1)
    grad_inputs = grad_mixed + norm_back(normed_one, inverse_one, grad_attn_in * (1.0 + scale_one))
    grad_inputs = grad_inputs.astype(BF).reshape(tokens.shape)

    grad_mod_local = jnp.concatenate(
        [grad_shift_one, grad_scale_one, grad_gate_one, grad_shift_two, grad_scale_two, grad_gate_two], axis=-1
    )
    bias_ada = jnp.sum(grad_mod_local, axis=0)
    sent = jnp.transpose(grad_mod_local.reshape(count, dp, 1, ada_cols), (1, 2, 0, 3))
    sent = jnp.broadcast_to(sent, (dp, seq, count, ada_cols))
    mod_parts = net.to_all(sent)
    mod_parts = tie(mod_parts, sent)
    mod_cols = jnp.sum(mod_parts, axis=1).astype(BF).reshape(dp * count, ada_cols)
    shard_ada = jnp.einsum("sr,sc->cr", cond_all, mod_cols, preferred_element_type=F32)

    cond_part = jnp.einsum("sc,rc->sr", mod_cols, low_ada, preferred_element_type=F32)
    cond_part = jnp.broadcast_to(cond_part.reshape(dp, 1, -1), (dp, seq, count * ada_rows))
    term_bias = jnp.concatenate([bias_ada, bias_q, bias_v, bias_proj, bias_fc1, bias_fc2])
    parcel = jnp.concatenate([term_bias.reshape(dp, seq, -1), cond_part], axis=-1)
    got_parcel = net.to_all(parcel)

    sums = halves.finish(parcel)
    blank = jnp.zeros((2, net.z.size, per, ROW_BLOCK, ROW_BLOCK), F32)
    (next_fc2, next_fc1, next_proj), *early = muon_gram(
        net.spots(),
        [(sums[0], [turned[3]]), (sums[1], [turned[2]]), (sums[2], [turned[1]])],
        spread_early, (blank, blank),
    )
    got_parcel = tie(got_parcel, early[0])
    halves = Staged(net.halves_steps(tie(sum_last, got_parcel)))
    sent = halves.advance()
    total = halves.finish(shard_ada)
    (next_qkv, next_ada), *grams = muon_gram(
        net.spots(), [(total, [turned[0]]), (shard_ada, [turned[4]])], spread_last, early
    )
    grams = Staged(net.gram_steps(*grams))
    sent = grams.advance()
    parcel = tie(got_parcel, *sent)
    while not grams.done:
        sent = grams.advance(sent[0])
    gathered = Staged(net.muon_gather_steps(grams.result))
    sent = gathered.advance()
    while not gathered.done:
        sent = gathered.advance(sent[0])
    momenta_in = [next_fc2, next_fc1, next_proj, next_qkv, next_ada]
    heights_of = [momentum.shape[1] // ROW_BLOCK for momentum in momenta_in]
    placed = block_spots(heights_of[:3], spread_early)
    placed += [(3 + spot[0],) + spot[1:] for spot in block_spots(heights_of[3:], spread_last)]
    new_fc2, new_fc1, new_proj, new_qkv, new_ada = muon_apply(
        net.spots(), gathered.result, momenta_in, [w.T for w in (w_fc2, w_fc1, w_proj, w_qkv, w_ada)],
        [math.sqrt(width / hidden), math.sqrt(hidden / width), 1.0, math.sqrt(3.0), math.sqrt(6.0)], placed,
    )

    size = biases.shape[0]
    grad_bias = jnp.sum(parcel[..., :size], axis=(0, 1))
    cond_part = jnp.sum(parcel[..., size:], axis=0).reshape(seq, count, ada_rows)
    grad_cond = silu_back(jnp.transpose(cond_part, (1, 0, 2)).reshape(count, width))[0]
    next_first = BETA_FIRST * bias_first + (1.0 - BETA_FIRST) * grad_bias
    next_second = BETA_SECOND * bias_second + (1.0 - BETA_SECOND) * grad_bias * grad_bias
    first_hat = next_first / (1.0 - BETA_FIRST**STEP_COUNT)
    second_hat = next_second / (1.0 - BETA_SECOND**STEP_COUNT)
    new_biases = biases * (1.0 - ADAM_RATE * ADAM_DECAY) - ADAM_RATE * first_hat / (
        jnp.sqrt(second_hat) + ADAM_EPS
    )
    return (
        result.reshape(tokens.shape),
        grad_inputs,
        grad_cond.reshape(conditioning.shape),
        new_qkv.T, new_proj.T, new_fc1.T, new_fc2.T, new_ada.T,
        next_qkv.T, next_proj.T, next_fc1.T, next_fc2.T, next_ada.T,
        new_biases,
        next_first,
        next_second,
    )


def solution(mesh):
    rows = P(None, "dp", "seq", None)
    matrix = P("seq", "dp")
    flat = P(("dp", "seq"))
    in_specs = (rows, P(None, "dp", None), P(None, "dp"), P(None, "dp"), rows) + (matrix,) * 10 + (flat,) * 3
    out_specs = (rows, rows, P(None, "dp", None)) + (matrix,) * 10 + (flat,) * 3
    return jax.shard_map(
        functools.partial(body, Net(mesh)), mesh=mesh, in_specs=in_specs, out_specs=out_specs, check_vma=False
    )
```

```python
import functools
import math

import jax
import jax.numpy as jnp
from jax import lax
from jax.experimental import pallas as pl
from jax.experimental.pallas import tpu as pltpu
from jax.sharding import PartitionSpec as P

HEADS = 16
ROW_BLOCK = 144
NS_STEPS = 5
STEP_COUNT = 10

PRECISE = lax.Precision.HIGHEST
LN_EPS = 1e-06
MASKED = -1e30
NS_A = 3.4445
NS_B = -4.775
NS_C = 2.0315
MUON_DECAY = 0.5
WEIGHT_SHRINK = 0.0001
NORM_EPS = 1e-07
BETA_FIRST = 0.9
BETA_SECOND = 0.999
ADAM_RATE = 0.1
ADAM_DECAY = 0.01
ADAM_EPS = 1e-08
BF = jnp.bfloat16
F32 = jnp.float32
VMEM_LIMIT = 60 * 2**20


class Ring:
    def __init__(self, name, total, stride, size):
        self.name, self.total, self.stride, self.size = name, total, stride, size

    def digit(self):
        return (lax.axis_index(self.name) // self.stride) % self.size

    def send(self, value, shift):
        pairs = []
        for i in range(self.total):
            d = (i // self.stride) % self.size
            pairs.append((i, i + ((d + shift) % self.size - d) * self.stride))
        return lax.ppermute(value, self.name, pairs)

    def gather(self, value, far=1):
        n = self.size
        blocks = [value] + [None] * (n - 1)
        if n == 2:
            blocks[1] = self.send(value, 1)
        elif n > 2:
            low = high = value
            for t in range(1, n // 2):
                low, high = self.send(low, 1), self.send(high, -1)
                blocks[n - t], blocks[t] = low, high
            blocks[n // 2] = self.send(low, 1) if far == 1 else self.send(high, -1)
        return blocks

    def gather_steps(self, value, far=1):
        n = self.size
        blocks = [value] + [None] * (n - 1)
        if n == 2:
            blocks[1] = self.send(value, 1)
            anchor = yield [value]
            blocks[1] = tie(blocks[1], anchor)
            return blocks
        low = high = value
        for t in range(1, n // 2):
            sent = [low, high]
            low, high = self.send(low, 1), self.send(high, -1)
            anchor = yield sent
            low, high = tie(low, anchor), tie(high, anchor)
            blocks[n - t], blocks[t] = low, high
        sent = [low if far == 1 else high]
        last = self.send(sent[0], far)
        anchor = yield sent
        blocks[n // 2] = tie(last, anchor)
        return blocks

    def scatter_steps(self, block_of, far=1):
        n = self.size
        if n == 1:
            return block_of(0).astype(F32)
        if n == 2:
            sent = block_of(1)
            got = self.send(sent, 1)
            anchor = yield [sent]
            return block_of(0).astype(F32) + tie(got, anchor).astype(F32)
        sent = block_of(n // 2)
        got = self.send(sent, far)
        anchor = yield [sent]
        low, high = (tie(got, anchor), None) if far == 1 else (None, tie(got, anchor))
        for t in range(n // 2 - 1, 0, -1):
            up, down = block_of(t), block_of(n - t)
            if low is not None:
                up = (up.astype(F32) + low.astype(F32)).astype(up.dtype)
            if high is not None:
                down = (down.astype(F32) + high.astype(F32)).astype(down.dtype)
            low, high = self.send(up, 1), self.send(down, -1)
            anchor = yield [up, down]
            low, high = tie(low, anchor), tie(high, anchor)
        return block_of(0).astype(F32) + low.astype(F32) + high.astype(F32)


def tie(value, *earlier):
    earlier = [array for array in earlier if array is not None]
    if not earlier:
        return value
    anywhere = pl.BlockSpec(memory_space=pl.ANY)
    return pl.pallas_call(
        lambda *refs: None,
        out_shape=jax.ShapeDtypeStruct(value.shape, value.dtype),
        in_specs=[anywhere] * (1 + len(earlier)),
        out_specs=anywhere,
        input_output_aliases={0: 0},
        name="tie",
    )(value, *earlier)


def lockstep(*steps):
    results = [None] * len(steps)
    alive = dict(enumerate(steps))
    anchor = None
    while alive:
        sent = []
        for n, step in list(alive.items()):
            try:
                sent += step.send(anchor)
            except StopIteration as stop:
                results[n] = stop.value
                del alive[n]
        if alive:
            anchor = yield sent
    return results


class Staged:
    def __init__(self, steps):
        self.steps, self.result, self.started, self.done = steps, None, False, False

    def advance(self, anchor=None):
        if self.done:
            return []
        try:
            sent = self.steps.send(anchor if self.started else None)
            self.started = True
            return sent
        except StopIteration as stop:
            self.result, self.done = stop.value, True
            return []

    def finish(self, anchor=None):
        while not self.done:
            self.advance(anchor)
        return self.result


def place_kernel(zs, ga, parts, count, outs, *refs):
    spots, sources = refs[0], refs[1 : 1 + count]
    outputs, (full, in_sems, out_sems) = refs[1 + count : 1 + count + outs], refs[1 + count + outs :]
    g = full.shape[3]
    half = count // 2
    shards = []
    for sc in range(2):
        for sx in range(2):
            for sz in range(zs):
                where = (lax.rem(spots[0] + sz, zs), lax.rem(spots[1] + sx, 2), lax.rem(spots[2] + sc, 2))
                n = 2 * len(shards)
                line, pair = sources[sc * half + sx].at[sz], sources[sc * half + 2 + sz].at[sx]
                copies = [
                    pltpu.make_async_copy(line, full.at[(*where, pl.ds(0, ga))], in_sems.at[n]),
                    pltpu.make_async_copy(pair, full.at[(*where, pl.ds(ga, g - ga))], in_sems.at[n + 1]),
                ]
                for copy in copies:
                    copy.start()
                shards.append((where, copies))
    exits = []
    for where, copies in shards:
        for copy in copies:
            copy.wait()
        for output, start, size, column, depth in parts:
            target = outputs[output].at[(*where, slice(None), slice(None), pl.ds(column, depth))]
            copy = pltpu.make_async_copy(
                full.at[(*where, pl.ds(start, size))], target, out_sems.at[len(exits)]
            )
            copy.start()
            exits.append(copy)
    for copy in exits:
        copy.wait()


def place(spots, sources, shape, ga, parts, shapes):
    zs = shape[0]
    moved = math.prod(shape) * 2
    return pl.pallas_call(
        functools.partial(place_kernel, zs, ga, parts, len(sources), len(shapes)),
        out_shape=[jax.ShapeDtypeStruct(each, BF) for each in shapes],
        in_specs=[pl.BlockSpec(memory_space=pltpu.SMEM)]
        + [pl.BlockSpec(memory_space=pl.ANY)] * len(sources),
        out_specs=[pl.BlockSpec(memory_space=pl.ANY)] * len(shapes),
        scratch_shapes=[
            pltpu.VMEM(shape, BF),
            pltpu.SemaphoreType.DMA((8 * zs,)),
            pltpu.SemaphoreType.DMA((4 * zs * len(parts),)),
        ],
        compiler_params=pltpu.CompilerParams(vmem_limit_bytes=VMEM_LIMIT),
        cost_estimate=pl.CostEstimate(flops=0, bytes_accessed=2 * moved, transcendentals=0),
        name="place",
    )(spots, *sources)


class Net:
    def __init__(self, mesh):
        dp, seq = mesh.shape["dp"], mesh.shape["seq"]
        self.dp, self.seq = dp, seq
        self.core = Ring("dp", dp, 1, 2)
        self.x = Ring("dp", dp, 2, 2)
        self.z = Ring("dp", dp, 4, dp // 4)
        self.y = Ring("seq", seq, 1, seq)

    def spots(self):
        return jnp.stack([self.z.digit(), self.x.digit(), self.core.digit()]).astype(jnp.int32)


    def wire(self, shards):
        turned = [shard.astype(BF).T for shard in shards]
        return turned[0] if len(turned) == 1 else jnp.concatenate(turned, axis=0)

    def rows(self, wires):
        if self.seq == 2:
            own, other = wires
            return jnp.where(
                self.y.digit() == 0,
                jnp.concatenate([own, other], axis=1),
                jnp.concatenate([other, own], axis=1),
            )
        order = (jnp.arange(self.seq) - self.y.digit()) % self.seq
        full = jnp.take(jnp.stack(wires), order, axis=0)
        return jnp.transpose(full, (1, 0, 2)).reshape(full.shape[1], -1)

    def joined(self, wires, unit, depth):
        full = self.rows(wires)
        return full.reshape(full.shape[0] // unit, unit, depth)

    def scatter(self, term):
        return lax.psum_scatter(term, "dp", scatter_dimension=0, tiled=True)

    def halves_steps(self, term):
        y = self.y.digit()
        blocks = term.reshape(term.shape[0], self.seq, -1)
        return (
            yield from self.y.scatter_steps(
                lambda s: lax.dynamic_index_in_dim(blocks, (y + s) % self.seq, 1, keepdims=False)
            )
        )

    def gather_steps(self, units, layout, part):
        g, unit, depth = units.shape
        zs = self.z.size
        ga = max(1, int(part * g))
        first, second = units[:ga], units[ga:]

        def line_steps():
            blocks = yield from self.z.gather_steps(first, 1)
            line = jnp.stack(blocks)
            return (yield from self.x.gather_steps(line))

        def pair_steps():
            blocks = yield from self.x.gather_steps(second)
            return (yield from self.z.gather_steps(jnp.stack(blocks), -1))

        lines, pairs = yield from lockstep(line_steps(), pair_steps())
        pieces = lines + pairs
        others = [self.core.send(piece, 1) for piece in pieces]
        anchor = yield pieces
        sources = pieces + [tie(other, anchor) for other in others]
        parts, shapes, start = [], [], 0
        for n, (rows, blocks) in enumerate(layout):
            size = rows // unit
            shapes.append((zs, 2, 2, size, unit, blocks * depth))
            for j in range(blocks):
                parts.append((n, start, size, j * depth, depth))
                start += size
        full = place(self.spots(), sources, (zs, 2, 2, g, unit, depth), ga, parts, shapes)
        return [f.reshape(-1, f.shape[-1]) for f in full], lines[1:] + pairs[1:]


    def gram_steps(self, own, other):
        got = self.core.send(other, 1)
        anchor = yield [other]
        half = own + tie(got, anchor)
        sent = half[1].astype(BF)
        got = self.x.send(sent, 1)
        anchor = yield [sent]
        kept = half[0] + tie(got, anchor).astype(F32)
        sent = [kept[shift].astype(BF) for shift in range(1, self.z.size)]
        got = [self.z.send(each, shift) for shift, each in enumerate(sent, 1)]
        anchor = yield sent
        return [kept[0]] + [tie(each, anchor) for each in got]

    def muon_gather_steps(self, parts):
        factor = polynomial(parts)
        got = [self.z.send(factor, -shift) for shift in range(1, self.z.size)]
        anchor = yield [factor]
        line = jnp.stack([factor] + [tie(each, anchor) for each in got])
        got = self.x.send(line, 1)
        anchor = yield [line]
        pair = [line, tie(got, anchor)]
        others = [self.core.send(each, 1) for each in pair]
        anchor = yield pair
        return pair + [tie(each, anchor) for each in others]


    def to_all(self, value):
        flat = value.reshape((self.dp * self.seq,) + value.shape[2:])
        return lax.all_to_all(flat, ("dp", "seq"), 0, 0, tiled=True).reshape(value.shape)

    def to_dp(self, value):
        return lax.all_to_all(value, "dp", 0, 0, tiled=True)


def layer_norm(values):
    centered = values - jnp.mean(values, axis=-1, keepdims=True)
    inverse = lax.rsqrt(jnp.mean(centered * centered, axis=-1, keepdims=True) + LN_EPS)
    return (centered * inverse, inverse)


def norm_back(normed, inverse, grad):
    mean_grad = jnp.mean(grad, axis=-1, keepdims=True)
    mean_cross = jnp.mean(grad * normed, axis=-1, keepdims=True)
    return inverse * (grad - mean_grad - normed * mean_cross)


def sigmoid_linear(values):
    return values * jax.nn.sigmoid(values)


def dot_t(left, right):
    return jnp.einsum("srk,nk->srn", left, right, preferred_element_type=F32)


def dot(left, right):
    return jnp.einsum("srn,nk->srk", left, right, preferred_element_type=F32)


GELU_SCALE = math.sqrt(2.0 / math.pi)
GELU_CUBE = 0.044715


def hidden_kernel(x_ref, w_ref, b_ref, act_ref, slope_ref):
    value = nt(x_ref[...], w_ref[...]) + b_ref[...]
    square = value * value
    bend = jnp.tanh(value * (GELU_SCALE + (GELU_SCALE * GELU_CUBE) * square))
    half = 0.5 + 0.5 * bend
    act_ref[...] = (value * half).astype(BF)
    steep = (0.5 * value) * (GELU_SCALE + (3.0 * GELU_SCALE * GELU_CUBE) * square)
    slope_ref[...] = (half + steep * (1.0 - bend * bend)).astype(BF)


def hidden_forward(x, w, bias):
    rows, depth = x.shape
    n = w.shape[0]
    tile = math.gcd(n, 512)
    out = pl.BlockSpec((rows, tile), lambda i: (0, i))
    return pl.pallas_call(
        hidden_kernel,
        grid=(n // tile,),
        in_specs=[
            pl.BlockSpec((rows, depth), lambda i: (0, 0)),
            pl.BlockSpec((tile, depth), lambda i: (i, 0)),
            pl.BlockSpec((1, tile), lambda i: (0, i)),
        ],
        out_specs=[out, out],
        out_shape=[jax.ShapeDtypeStruct((rows, n), BF)] * 2,
        compiler_params=pltpu.CompilerParams(vmem_limit_bytes=VMEM_LIMIT),
        cost_estimate=pl.CostEstimate(
            flops=2 * rows * n * depth, bytes_accessed=2 * (rows + n) * depth + 4 * rows * n, transcendentals=rows * n
        ),
        name="hidden_forward",
    )(x, w, bias.reshape(1, n))


def hidden_back_kernel(g_ref, w_ref, slope_ref, out_ref, bias_ref):
    grad = (nn(g_ref[...], w_ref[...]) * slope_ref[...].astype(F32)).astype(BF)
    out_ref[...] = grad
    bias_ref[...] = jnp.sum(grad.astype(F32), axis=0, keepdims=True)


def hidden_backward(grad, w, slope):
    rows, depth = grad.shape
    n = w.shape[1]
    tile = math.gcd(n, 512)
    out = pl.BlockSpec((rows, tile), lambda i: (0, i))
    result, bias = pl.pallas_call(
        hidden_back_kernel,
        grid=(n // tile,),
        in_specs=[
            pl.BlockSpec((rows, depth), lambda i: (0, 0)),
            pl.BlockSpec((depth, tile), lambda i: (0, i)),
            out,
        ],
        out_specs=[out, pl.BlockSpec((1, tile), lambda i: (0, i))],
        out_shape=[jax.ShapeDtypeStruct((rows, n), BF), jax.ShapeDtypeStruct((1, n), F32)],
        compiler_params=pltpu.CompilerParams(vmem_limit_bytes=VMEM_LIMIT),
        cost_estimate=pl.CostEstimate(
            flops=2 * rows * n * depth, bytes_accessed=2 * (rows + n) * depth + 4 * rows * n, transcendentals=0
        ),
        name="hidden_backward",
    )(grad, w, slope)
    return result, bias[0]


def outer(left, right):
    return jnp.einsum("srn,srk->nk", left, right, preferred_element_type=F32).astype(BF)


def shard_outer_kernel(plan, counts, tile, split, spots_ref, *refs):
    outs = 2 if split else 1
    inputs, where = refs[: counts[0]], refs[counts[1] : counts[1] + outs]
    buffers = refs[counts[1] + outs : counts[1] + outs + len(plan["loads"])]
    acc, in_sems, out_sems = refs[counts[1] + outs + len(plan["loads"]) :]
    loads = []
    for n, (sources, start, size) in enumerate(plan["loads"]):
        row, copies = 0, []
        for m, source in enumerate(sources):
            rows = inputs[source].shape[0]
            window = inputs[source].at[:, pl.ds(start, size)]
            copies.append(pltpu.make_async_copy(window, buffers[n].at[pl.ds(row, rows)], in_sems.at[n, m]))
            copies[-1].start()
            row += rows
        loads.append(copies)
    ready = set()
    shipped = []
    unit = acc.shape[1]
    for left, right, base, ships in plan["parts"]:
        for n in (left, right):
            if n not in ready:
                for copy in loads[n]:
                    copy.wait()
                ready.add(n)
        width = buffers[left].shape[1]
        step = tile if width % tile == 0 else width

        @pl.loop(0, width // step)
        def _(t):
            block = buffers[left][:, pl.ds(pl.multiple_of(t * step, step), step)]
            product = lax.dot_general(
                block, buffers[right][...], (((0,), (0,)), ((), ())), preferred_element_type=F32
            )
            product = product.reshape(step // unit, unit, product.shape[1]).astype(BF)
            acc[pl.ds(base + t * (step // unit), step // unit)] = product

        for core, z, x, row, target, size in ships:
            spot = (z, x) if split else (z, x, core)
            places = [ref.at[(*spot, pl.ds(target, size))] for ref in where]
            copies = [
                pltpu.make_async_copy(acc.at[pl.ds(row, size)], each, out_sems.at[len(shipped)]) for each in places
            ]
            shipped.append((core, copies))
            on_own_core(split, spots_ref, core, [copy.start for copy in copies])
    for core, copies in shipped:
        on_own_core(split, spots_ref, core, [copy.wait for copy in copies])


def on_own_core(split, spots_ref, core, actions):
    if not split:
        actions[0]()
        return

    @pl.when(spots_ref[2] == core)
    def _():
        actions[0]()

    @pl.when(spots_ref[2] != core)
    def _():
        actions[1]()


def shard_outer(spots, inputs, loads, parts, zs, depth, unit, shard_units, deps=(), tile=384, split=True):
    dp = zs * 4
    plan_parts, base, row, placed = [], 0, 0, {}
    begun = {}
    for left, right, rows, first in parts:
        if first not in begun:
            begun[first] = (base, 0)
        start, shipped = begun[first]
        width = loads[left][2]
        size = rows // unit
        end = base + width // unit
        ships = []
        while shipped < dp and start + (shipped + 1) * size <= end:
            core, x, z = shipped % 2, shipped // 2 % 2, shipped // 4
            ships.append((core, z, x, start + shipped * size, first, size))
            shipped += 1
        begun[first] = (start, shipped)
        plan_parts.append((left, right, base, ships))
        base = end
    total = sum(len(part[3]) for part in plan_parts)
    shape = (zs, 2, shard_units, unit, depth) if split else (zs, 2, 2, shard_units, unit, depth)
    outs = [jax.ShapeDtypeStruct(shape, BF)] * (2 if split else 1)
    anywhere = pl.BlockSpec(memory_space=pl.ANY)
    heights = [sum(inputs[source].shape[0] for source in sources) for sources, _, _ in loads]
    flops = sum(2 * heights[p[0]] * loads[p[0]][2] * loads[p[1]][2] for p in parts)
    return pl.pallas_call(
        functools.partial(
            shard_outer_kernel, {"loads": loads, "parts": plan_parts}, (len(inputs), len(inputs) + len(deps)), tile, split
        ),
        out_shape=outs,
        in_specs=[pl.BlockSpec(memory_space=pltpu.SMEM)] + [anywhere] * (len(inputs) + len(deps)),
        out_specs=[anywhere] * len(outs),
        scratch_shapes=[pltpu.VMEM((height, load[2]), BF) for height, load in zip(heights, loads)]
        + [
            pltpu.VMEM((base, unit, depth), BF),
            pltpu.SemaphoreType.DMA((len(loads), max(len(load[0]) for load in loads))),
            pltpu.SemaphoreType.DMA((total,)),
        ],
        compiler_params=pltpu.CompilerParams(vmem_limit_bytes=VMEM_LIMIT),
        cost_estimate=pl.CostEstimate(flops=flops, bytes_accessed=2 * base * unit * depth, transcendentals=0),
        name="shard_outer",
    )(spots, *inputs, *deps)


LANES = 128
LOG2E = math.log2(math.e)


def padded(block, column=None):
    rows, depth = block.shape
    if column is None:
        return jnp.concatenate([block, jnp.zeros((rows, LANES - depth), block.dtype)], axis=1)
    rest = jnp.zeros((rows, LANES - depth - 1), block.dtype)
    return jnp.concatenate([block, column.astype(block.dtype), rest], axis=1)


def mask_column(lengths_ref, offsets_ref, sample, total, rows):
    place = lax.broadcasted_iota(jnp.int32, (total, 1), 0)
    position = place
    for s in range(total // rows):
        position = jnp.where(place // rows == s, place - s * rows + offsets_ref[s], position)
    return jnp.where(position < lengths_ref[sample], 0.0, MASKED)


def nt(left, right):
    return lax.dot_general(left, right, (((1,), (1,)), ((), ())), preferred_element_type=F32)


def nn(left, right):
    return jnp.dot(left, right, preferred_element_type=F32)


def without(kernel, start, count, *fixed):
    def run(*refs):
        kernel(*fixed, *refs[:start], *refs[start + count :])

    return run


def attend_kernel(heads, chunk, lengths_ref, offsets_ref, q_ref, k_ref, v_ref, o_ref, lse_ref, q_s, k_s, vt_s, o_s):
    rows, width = q_ref.shape[1:]
    total = k_ref.shape[1]
    depth = width // heads
    factor = depth**-0.5 * LOG2E
    mask = mask_column(lengths_ref, offsets_ref, pl.program_id(0), total, rows)
    ones = jnp.ones((rows, 1), F32)
    for h in range(heads):
        span = slice(h * depth, (h + 1) * depth)
        q_s[h] = padded(q_ref[0, :, span], ones)
        k_s[h] = padded(k_ref[0, :, span], mask)
        vt_s[h] = jnp.transpose(v_ref[0, :, span])

    def one_head(h, carry):
        peak = jnp.full((1, rows), MASKED, F32)
        sums = jnp.zeros((1, rows), F32)
        mixed = jnp.zeros((depth, rows), F32)
        for c in range(total // chunk):
            part = slice(c * chunk, (c + 1) * chunk)
            scores = nt(k_s[h, part], q_s[h])
            higher = jnp.maximum(peak, jnp.max(scores, axis=0, keepdims=True))
            weights = jnp.exp2((scores - higher) * factor)
            if c == 0:
                sums = jnp.sum(weights, axis=0, keepdims=True)
                mixed = nn(vt_s[h, :, part], weights.astype(BF))
            else:
                shrink = jnp.exp2((peak - higher) * factor)
                sums = sums * shrink + jnp.sum(weights, axis=0, keepdims=True)
                mixed = mixed * shrink + nn(vt_s[h, :, part], weights.astype(BF))
            peak = higher
        o_s[h] = jnp.transpose(mixed / sums)
        lse_ref[0, h] = peak * factor + jnp.log2(sums)
        return carry

    lax.fori_loop(0, heads, one_head, 0, unroll=4)
    for h in range(heads):
        o_ref[0, :, h * depth : (h + 1) * depth] = o_s[h].astype(BF)


def attend(lengths, offsets, queries, keys, values, heads, tile, deps=()):
    count, rows, width = queries.shape
    total = keys.shape[1]
    depth = width // heads
    tile = min(tile, total)
    pick = lambda i, *_: (i, 0, 0)
    return pl.pallas_call(
        without(attend_kernel, 5, len(deps), heads, tile),
        grid_spec=pltpu.PrefetchScalarGridSpec(
            num_scalar_prefetch=2,
            grid=(count,),
            in_specs=[
                pl.BlockSpec((1, rows, width), pick),
                pl.BlockSpec((1, total, width), pick),
                pl.BlockSpec((1, total, width), pick),
            ]
            + [pl.BlockSpec(memory_space=pl.ANY)] * len(deps),
            out_specs=[
                pl.BlockSpec((1, rows, width), pick),
                pl.BlockSpec((1, heads, 1, rows), lambda i, *_: (i, 0, 0, 0)),
            ],
            scratch_shapes=[
                pltpu.VMEM((heads, rows, LANES), BF),
                pltpu.VMEM((heads, total, LANES), BF),
                pltpu.VMEM((heads, depth, total), BF),
                pltpu.VMEM((heads, rows, depth), F32),
            ],
        ),
        out_shape=[
            jax.ShapeDtypeStruct((count, rows, width), BF),
            jax.ShapeDtypeStruct((count, heads, 1, rows), F32),
        ],
        compiler_params=pltpu.CompilerParams(vmem_limit_bytes=VMEM_LIMIT),
        cost_estimate=pl.CostEstimate(
            flops=4 * count * heads * rows * total * LANES,
            bytes_accessed=2 * count * width * (2 * rows + 2 * total),
            transcendentals=count * heads * rows * total,
        ),
        name="attend",
    )(lengths, offsets, queries, keys, values, *deps)


def attend_back_kernel(
    heads, chunk, lengths_ref, offsets_ref, q_ref, k_ref, v_ref, o_ref, g_ref, lse_ref,
    dq_ref, dk_ref, dv_ref, q_s, k_s, kt_s, v_s, g_s, delta_s, dq_s, dk_s, dv_s
):
    rows, width = q_ref.shape[1:]
    total = k_ref.shape[1]
    depth = width // heads
    scale = depth**-0.5
    factor = scale * LOG2E
    mask = mask_column(lengths_ref, offsets_ref, pl.program_id(0), total, rows)
    ones = jnp.ones((rows, 1), F32)
    cross = jnp.transpose(g_ref[0].astype(F32) * o_ref[0].astype(F32))
    for h in range(heads):
        span = slice(h * depth, (h + 1) * depth)
        delta_s[h] = jnp.sum(cross[span], axis=0, keepdims=True)
        q_s[h] = padded(q_ref[0, :, span], ones)
        k_s[h] = padded(k_ref[0, :, span], mask)
        kt_s[h] = jnp.transpose(k_ref[0, :, span])
        g_s[h] = padded(g_ref[0, :, span])
        v_s[h] = padded(v_ref[0, :, span])

    def one_head(h, carry):
        dq = jnp.zeros((depth, rows), F32)
        for c in range(total // chunk):
            part = slice(c * chunk, (c + 1) * chunk)
            probs = jnp.exp2(nt(k_s[h, part], q_s[h]) * factor - lse_ref[0, h])
            slopes = (probs * (nt(v_s[h, part], g_s[h]) - delta_s[h])).astype(BF)
            dv_s[h, part] = nn(probs.astype(BF), g_s[h]).astype(BF)
            dk_s[h, part] = (nn(slopes, q_s[h]) * scale).astype(BF)
            dq = dq + nn(kt_s[h, :, part], slopes)
        dq_s[h] = jnp.transpose(dq * scale)
        return carry

    lax.fori_loop(0, heads, one_head, 0, unroll=4)
    for h in range(heads):
        span = slice(h * depth, (h + 1) * depth)
        dq_ref[0, :, span] = dq_s[h].astype(BF)
        dk_ref[0, :, span] = dk_s[h][:, :depth]
        dv_ref[0, :, span] = dv_s[h][:, :depth]


def attend_back(lengths, offsets, queries, keys, values, mixed, grads, lse, heads, tile, deps=()):
    count, rows, width = queries.shape
    total = keys.shape[1]
    depth = width // heads
    tile = min(tile, total)
    pick = lambda i, *_: (i, 0, 0)
    near = pl.BlockSpec((1, rows, width), pick)
    far = pl.BlockSpec((1, total, width), pick)
    return pl.pallas_call(
        without(attend_back_kernel, 8, len(deps), heads, tile),
        grid_spec=pltpu.PrefetchScalarGridSpec(
            num_scalar_prefetch=2,
            grid=(count,),
            in_specs=[near, far, far, near, near, pl.BlockSpec((1, heads, 1, rows), lambda i, *_: (i, 0, 0, 0))]
            + [pl.BlockSpec(memory_space=pl.ANY)] * len(deps),
            out_specs=[near, far, far],
            scratch_shapes=[
                pltpu.VMEM((heads, rows, LANES), BF),
                pltpu.VMEM((heads, total, LANES), BF),
                pltpu.VMEM((heads, depth, total), BF),
                pltpu.VMEM((heads, total, LANES), BF),
                pltpu.VMEM((heads, rows, LANES), BF),
                pltpu.VMEM((heads, 1, rows), F32),
                pltpu.VMEM((heads, rows, depth), F32),
                pltpu.VMEM((heads, total, LANES), BF),
                pltpu.VMEM((heads, total, LANES), BF),
            ],
        ),
        out_shape=[
            jax.ShapeDtypeStruct((count, rows, width), BF),
            jax.ShapeDtypeStruct((count, total, width), BF),
            jax.ShapeDtypeStruct((count, total, width), BF),
        ],
        compiler_params=pltpu.CompilerParams(vmem_limit_bytes=VMEM_LIMIT),
        cost_estimate=pl.CostEstimate(
            flops=10 * count * heads * rows * total * LANES,
            bytes_accessed=2 * count * width * (4 * rows + 4 * total),
            transcendentals=count * heads * rows * total,
        ),
        name="attend_back",
    )(lengths, offsets, queries, keys, values, mixed, grads, lse, *deps)


def block_spots(counts, spread):
    per, first = spread
    spots = []
    for matrix, count in enumerate(counts):
        for block in range(count):
            device, place_in = divmod(len(spots), per)
            device += first
            spots.append((matrix, block, device // 4, device // 2 % 2, device % 2, place_in))
    return spots


EXTRA = ROW_BLOCK - 128
PACKED = (ROW_BLOCK + EXTRA, 128)


def packed(block):
    corner = block[128:, 128:]
    corner = jnp.concatenate([corner, jnp.zeros((EXTRA, 128 - EXTRA), block.dtype)], axis=1)
    return jnp.concatenate([block[:, :128], corner], axis=0)


def unpacked(block):
    side = jnp.transpose(block[128:ROW_BLOCK])
    right = jnp.concatenate([side, block[ROW_BLOCK:, :EXTRA]], axis=0)
    return jnp.concatenate([block[:ROW_BLOCK], right], axis=1)


def precise(left, right, dims):
    return lax.dot_general(left, right, (dims, ((), ())), precision=PRECISE, preferred_element_type=F32)


def muon_gram_kernel(groups, spread, spots_ref, base_own, base_other, *refs):
    count = sum(groups)
    sums, momenta = refs[: len(groups)], refs[len(groups) : len(groups) + count]
    outs = refs[len(groups) + count : len(groups) + 2 * count]
    own_ref, other_ref, grams, sems = refs[len(groups) + 2 * count :]
    n = 0
    for matrices, sum_ref in zip(groups, sums):
        start = 0
        for _ in range(matrices):
            size = momenta[n].shape[0]
            outs[n][...] = MUON_DECAY * momenta[n][...] + sum_ref[start : start + size]
            start += size
            n += 1
    zs = own_ref.shape[1]
    spots = block_spots([out.shape[1] // ROW_BLOCK for out in outs], spread)
    copies = []
    for n, (matrix, block, z, x, core, place_in) in enumerate(spots):
        turned = outs[matrix][:, block * ROW_BLOCK : (block + 1) * ROW_BLOCK]
        grams[n] = packed(precise(turned, turned, ((0,), (0,))))
        away = (lax.rem(spots_ref[1] + x, 2), lax.rem(zs + z - spots_ref[0], zs), place_in)
        pair = [pltpu.make_async_copy(grams.at[n], ref.at[away], sems.at[n]) for ref in (own_ref, other_ref)]
        on_own_core(True, spots_ref, core, [copy.start for copy in pair])
        copies.append((core, pair))
    for core, pair in copies:
        on_own_core(True, spots_ref, core, [copy.wait for copy in pair])


def muon_gram(spots, groups, spread, base):
    momenta = [momentum for _, each in groups for momentum in each]
    terms = jax.ShapeDtypeStruct(base[0].shape, F32)
    vmem, anywhere = pl.BlockSpec(memory_space=pltpu.VMEM), pl.BlockSpec(memory_space=pl.ANY)
    blocks = len(block_spots([momentum.shape[1] // ROW_BLOCK for momentum in momenta], spread))
    outs = pl.pallas_call(
        functools.partial(muon_gram_kernel, [len(each) for _, each in groups], spread),
        out_shape=[jax.ShapeDtypeStruct(momentum.shape, F32) for momentum in momenta] + [terms, terms],
        in_specs=[pl.BlockSpec(memory_space=pltpu.SMEM), anywhere, anywhere]
        + [vmem] * (len(groups) + len(momenta)),
        out_specs=[vmem] * len(momenta) + [anywhere, anywhere],
        input_output_aliases={1: len(momenta), 2: len(momenta) + 1},
        scratch_shapes=[
            pltpu.VMEM((blocks,) + PACKED, F32),
            pltpu.SemaphoreType.DMA((blocks,)),
        ],
        compiler_params=pltpu.CompilerParams(vmem_limit_bytes=VMEM_LIMIT),
        name="muon_gram",
    )(spots, *base, *[group[0] for group in groups], *momenta)
    return outs[:-2], outs[-2], outs[-1]


def polynomial_kernel(count, *refs):
    out = refs[count]
    shape = (ROW_BLOCK, ROW_BLOCK)
    eye = (lax.broadcasted_iota(jnp.int32, shape, 0) == lax.broadcasted_iota(jnp.int32, shape, 1)).astype(F32)
    mul = lambda left, right: precise(left, right, ((1,), (0,)))
    blocks = range(out.shape[0])
    currents, scales, totals = [], [], []
    for n in blocks:
        gram = refs[0][n]
        for ref in refs[1:count]:
            gram = gram + ref[n].astype(F32)
        gram = unpacked(gram)
        square = jnp.sum(jnp.sum(gram * eye, axis=1, keepdims=True), axis=0, keepdims=True)
        scale = 1.0 / (jnp.sqrt(square) + NORM_EPS)
        scales.append(scale)
        currents.append(gram * (scale * scale))
    for step in range(NS_STEPS):
        factors = [NS_A * eye + NS_B * a + NS_C * mul(a, a) for a in currents]
        totals = factors if step == 0 else [mul(f, t) for f, t in zip(factors, totals)]
        if step + 1 < NS_STEPS:
            currents = [mul(f, a) for f, a in zip(factors, currents)]
            currents = [mul(a, f) for f, a in zip(factors, currents)]
    for n in blocks:
        out[n] = packed(totals[n] * scales[n])


def polynomial(parts):
    vmem = pl.BlockSpec(memory_space=pltpu.VMEM)
    return pl.pallas_call(
        functools.partial(polynomial_kernel, len(parts)),
        out_shape=jax.ShapeDtypeStruct(parts[0].shape, F32),
        in_specs=[vmem] * len(parts),
        out_specs=vmem,
        compiler_params=pltpu.CompilerParams(vmem_limit_bytes=VMEM_LIMIT),
        name="polynomial",
    )(*parts)


def muon_apply_kernel(rates, placed, spots_ref, *refs):
    count = len(rates)
    parts, momenta, masters = refs[:4], refs[4 : 4 + count], refs[4 + count : 4 + 2 * count]
    outs, factors = refs[4 + 2 * count : 4 + 3 * count], refs[4 + 3 * count]
    for n in range(4):
        factors[n] = parts[n][...]
    zs = factors.shape[1]
    for matrix, block, z, x, core, place_in in placed:
        part = slice(block * ROW_BLOCK, (block + 1) * ROW_BLOCK)
        away = 2 * lax.rem(spots_ref[2] + core, 2) + lax.rem(spots_ref[1] + x, 2)
        factor = unpacked(factors[away, lax.rem(zs + z - spots_ref[0], zs), place_in])
        direction = precise(momenta[matrix][:, part], factor, ((1,), (1,)))
        outs[matrix][:, part] = masters[matrix][:, part] * (1.0 - WEIGHT_SHRINK) - rates[matrix] * direction


def muon_apply(spots, factors, momenta, masters, rates, placed):
    vmem = pl.BlockSpec(memory_space=pltpu.VMEM)
    return pl.pallas_call(
        functools.partial(muon_apply_kernel, rates, placed),
        out_shape=[jax.ShapeDtypeStruct(master.shape, F32) for master in masters],
        in_specs=[pl.BlockSpec(memory_space=pltpu.SMEM)] + [vmem] * (4 + 2 * len(masters)),
        out_specs=[vmem] * len(masters),
        scratch_shapes=[pltpu.VMEM((4,) + factors[0].shape, F32)],
        compiler_params=pltpu.CompilerParams(vmem_limit_bytes=VMEM_LIMIT),
        name="muon_apply",
    )(spots, *factors, *momenta, *masters)


def body(net, tokens, conditioning, heights, widths, upstream, *state):
    masters, momenta = state[0:5], state[5:10]
    biases, bias_first, bias_second = state[10:13]
    w_qkv, w_proj, w_fc1, w_fc2, w_ada = masters
    micro, local, rows, width = tokens.shape
    count = micro * local
    head_dim = width // HEADS
    hidden = w_fc1.shape[1] * net.dp
    seq, dp = net.seq, net.dp
    y = net.y.digit()

    bounds = [0, 6 * width, 7 * width, 8 * width, 9 * width, 9 * width + hidden, 10 * width + hidden]

    n_qkv, n_proj, n_fc1, n_fc2 = [w.shape[1] for w in (w_qkv, w_proj, w_fc1, w_fc2)]
    unit = math.gcd(math.gcd(n_qkv, n_proj), 8)
    unit_qkv, layout_qkv = math.gcd(n_qkv, 8), [(n_qkv, 1)]
    own_tokens = tokens.reshape(count, rows, width)
    wires = net.y.gather(net.wire([w_qkv, w_proj]))

    ada_rows, ada_cols = w_ada.shape
    cond = conditioning.astype(F32).reshape(count, width)
    cond_act, silu_back = jax.vjp(sigmoid_linear, cond)
    cond_low = cond_act.astype(BF).astype(F32)
    cond_parts = jnp.transpose(cond_low.reshape(count, seq, ada_rows), (1, 0, 2)).reshape(seq, -1)
    parcel = jnp.concatenate([jnp.broadcast_to(biases, (seq,) + biases.shape), cond_parts], axis=1)
    parcel = net.to_all(tie(jnp.broadcast_to(parcel[None], (dp,) + parcel.shape), wires[0]))
    cond_all = parcel[:, 0, biases.shape[0] :].reshape(dp * count, ada_rows).astype(BF)
    first = Staged(net.gather_steps(net.joined(wires, unit, width), [(n_qkv, 1), (n_proj, 1)], 0.45))
    sent = first.advance()
    token_pieces = [net.y.gather(tie(own_tokens[0], *sent))]

    low_ada = w_ada.astype(BF)
    partial = jnp.dot(tie(cond_all, *sent), low_ada, preferred_element_type=F32).reshape(dp, 1, count, ada_cols)
    partial = jnp.broadcast_to(partial, (dp, seq, count, ada_cols))
    received = net.to_all(partial)
    first.advance(partial)
    sent = first.advance(received)
    received, parcel = tie(received, *sent), tie(parcel, *sent)
    received = jnp.sum(received, axis=1)
    bias_full = parcel[:, :, : biases.shape[0]].reshape(-1)
    b_ada, b_q, b_v, b_proj, b_fc1, b_fc2 = [bias_full[bounds[i] : bounds[i + 1]] for i in range(6)]
    modulation = jnp.transpose(received, (1, 0, 2)).reshape(count, dp * ada_cols) + b_ada
    shift_one, scale_one, gate_one, shift_two, scale_two, gate_two = jnp.split(
        modulation[:, None, :], 6, axis=-1
    )
    t_qkv, t_proj = first.finish(modulation)[0]
    wires = net.y.gather(tie(net.wire([w_fc1]), token_pieces[0][-1], *sent))
    wires = wires[:1] + [tie(wire, t_qkv) for wire in wires[1:]]
    t_fc1 = lax.all_gather(net.rows(wires), "dp", axis=0, tiled=True)
    for i in range(1, count):
        token_pieces.append(net.y.gather(tie(own_tokens[i], wires[-1])))

    lengths = (heights * widths).reshape(count).astype(jnp.int32)
    offsets = jnp.stack([((y + s) % seq) * rows for s in range(seq)]).astype(jnp.int32)
    normed_all, inverse_all, attn_all, queries, keys, values, attended_low, log_total = [[] for _ in range(8)]
    for i in range(count):
        normed, inverse = layer_norm(jnp.concatenate(token_pieces[i], axis=0).astype(F32))
        attn = (normed * (1.0 + scale_one[i]) + shift_one[i]).astype(BF)
        queries.append((dot_t(attn[None, :rows], t_qkv[:width]) + b_q).astype(BF))
        keys.append(dot_t(attn[None], t_qkv[width : 2 * width]).astype(BF))
        values.append((dot_t(attn[None], t_qkv[2 * width :]) + b_v).astype(BF))
        mixed, lse = attend(lengths[i : i + 1], offsets, queries[i], keys[i], values[i], HEADS, 512)
        if i == 0:
            token_pieces[1:] = [each[:1] + [tie(a, mixed) for a in each[1:]] for each in token_pieces[1:]]
            last_piece = token_pieces[-1][-1] if count > 1 else mixed
            wires = net.y.gather(tie(net.wire([w_fc2]), last_piece))
        normed_all.append(normed[:rows])
        inverse_all.append(inverse[:rows])
        attn_all.append(attn)
        attended_low.append(mixed[0])
        log_total.append(lse)
    wires = wires[:1] + [tie(wire, keys[-1]) for wire in wires[1:]]
    t_fc2 = lax.all_gather(net.rows(wires), "dp", axis=0, tiled=True)
    attended_low = jnp.stack(attended_low)

    inputs = own_tokens.astype(F32)
    branch_one = dot_t(attended_low, t_proj) + b_proj
    mixed_one = inputs + gate_one * branch_one
    normed_two, inverse_two = layer_norm(mixed_one)
    ffn_in = (normed_two * (1.0 + scale_two) + shift_two).astype(BF)
    flat = lambda array: array.reshape(-1, array.shape[-1])
    activated_low, slope = hidden_forward(flat(ffn_in), t_fc1, b_fc1)
    activated_low = activated_low.reshape(count, rows, hidden)
    grad_out = upstream.reshape(count, rows, width).astype(F32)
    grad_branch_two = (gate_two * grad_out).astype(BF)
    term_fc2 = outer(grad_branch_two, activated_low)
    sum_fc2 = net.scatter(term_fc2)
    branch_two = dot_t(tie(activated_low, term_fc2), t_fc2) + b_fc2
    grad_branch_two = tie(grad_branch_two, term_fc2)
    result = (mixed_one + gate_two * branch_two).astype(BF)

    grad_gate_two = jnp.sum(branch_two * grad_out, axis=1)
    bias_fc2 = jnp.sum(grad_branch_two.astype(F32), axis=(0, 1))
    grad_pre, bias_fc1 = hidden_backward(flat(grad_branch_two), t_fc2, slope)
    grad_pre = grad_pre.reshape(count, rows, hidden)
    grad_ffn_in = dot(grad_pre, t_fc1)
    grad_shift_two = jnp.sum(grad_ffn_in, axis=1)
    grad_scale_two = jnp.sum(grad_ffn_in * normed_two, axis=1)
    grad_mixed = grad_out + norm_back(normed_two, inverse_two, grad_ffn_in * (1.0 + scale_two))
    grad_gate_one = jnp.sum(branch_one * grad_mixed, axis=1)
    grad_branch_one = (gate_one * grad_mixed).astype(BF)
    bias_proj = jnp.sum(grad_branch_one.astype(F32), axis=(0, 1))
    grad_attended = dot(grad_branch_one, t_proj).astype(BF)
    unit_mid = math.gcd(math.gcd(n_proj, n_fc1), 8)
    (term_mid,) = shard_outer(
        net.spots(),
        [flat(grad_pre), flat(ffn_in), flat(grad_branch_one), flat(attended_low)],
        [([2], 0, width), ([3], 0, width), ([1], 0, width)]
        + [([0], j * width, width) for j in range(hidden // width)],
        [(0, 1, n_proj, 0)] + [(3 + j, 2, n_fc1, n_proj // unit_mid) for j in range(hidden // width)],
        net.z.size, width, unit_mid, (n_proj + n_fc1) // unit_mid, split=False,
    )
    term_mid = tie(term_mid, sum_fc2, grad_attended)
    sum_mid = net.scatter(term_mid.reshape(dp * (n_proj + n_fc1), width))
    grad_attended = tie(grad_attended, term_mid)

    def far_steps(dk, dv):
        part = dot(dk[:, rows:], t_qkv[width : 2 * width]) + dot(dv[:, rows:], t_qkv[2 * width :])
        part = part.astype(BF)[0]
        blank = jnp.zeros((rows, width), BF)
        return Staged(net.y.scatter_steps(lambda s: blank if s == 0 else part[(s - 1) * rows : s * rows]))

    grad_q, grad_k, grad_v, far_parts = [], [], [], []
    turned = [momentum.T for momentum in momenta]
    sent = []
    for i in range(count):
        dq, dk, dv = attend_back(
            lengths[i : i + 1], offsets, queries[i], keys[i], values[i], attended_low[i : i + 1],
            grad_attended[i : i + 1], log_total[i], HEADS, 512, sent,
        )
        sent = []
        grad_q.append(dq)
        grad_k.append(dk)
        grad_v.append(dv)
        if i + 1 < count:
            far_parts.append(far_steps(dk, dv))
            sent = sent + far_parts[-1].advance()
    unit_last = math.gcd(n_qkv, 8)
    (term_last,) = shard_outer(
        net.spots(),
        [flat(each) for each in grad_q + grad_k + grad_v]
        + [attn[:rows] for attn in attn_all]
        + attn_all,
        [([n * count + i for i in range(count)], 0, width) for n in range(5)],
        [(0, 3, n_qkv, 0), (1, 4, n_qkv, 0), (2, 4, n_qkv, 0)],
        net.z.size, width, unit_last, n_qkv // unit_last, sent, split=False,
    )
    sum_last = net.scatter(term_last.reshape(dp * n_qkv, width))
    grad_k[-1] = tie(grad_k[-1], term_last)
    far_parts.append(far_steps(grad_k[-1], grad_v[-1]))
    sent = far_parts[-1].advance()
    halves = Staged(lockstep(*[net.halves_steps(tie(each, *sent)) for each in (sum_fc2, sum_mid)]))
    sent = sent + halves.advance()
    grad_q[0] = tie(grad_q[0], *sent)
    bias_q = sum(jnp.sum(each.astype(F32), axis=(0, 1)) for each in grad_q)
    bias_v = sum(jnp.sum(each.astype(F32), axis=(0, 1)) for each in grad_v)
    own_part = jnp.concatenate(
        [
            dot(grad_q[i], t_qkv[:width])
            + dot(grad_k[i][:, :rows], t_qkv[width : 2 * width])
            + dot(grad_v[i][:, :rows], t_qkv[2 * width :])
            for i in range(count)
        ],
        axis=0,
    )
    matrices = (w_qkv, w_proj, w_fc1, w_fc2, w_ada)
    per = -(-sum(matrix.shape[0] // ROW_BLOCK for matrix in matrices) // dp)
    spread_early = (per, 0)
    early_blocks = (w_fc2.shape[0] + w_fc1.shape[0] + w_proj.shape[0]) // ROW_BLOCK
    spread_last = (per, -(-early_blocks // per))
    far_sum = jnp.stack([steps_of.finish() for steps_of in far_parts])
    grad_attn_in = own_part + far_sum
    normed_one, inverse_one = jnp.stack(normed_all), jnp.stack(inverse_all)
    grad_shift_one = jnp.sum(grad_attn_in, axis=1)
    grad_scale_one = jnp.sum(grad_attn_in * normed_one, axis=1)
    grad_inputs = grad_mixed + norm_back(normed_one, inverse_one, grad_attn_in * (1.0 + scale_one))
    grad_inputs = grad_inputs.astype(BF).reshape(tokens.shape)

    grad_mod_local = jnp.concatenate(
        [grad_shift_one, grad_scale_one, grad_gate_one, grad_shift_two, grad_scale_two, grad_gate_two], axis=-1
    )
    bias_ada = jnp.sum(grad_mod_local, axis=0)
    sent = jnp.transpose(grad_mod_local.reshape(count, dp, 1, ada_cols), (1, 2, 0, 3))
    sent = jnp.broadcast_to(sent, (dp, seq, count, ada_cols))
    mod_parts = net.to_all(sent)
    mod_parts = tie(mod_parts, sent)
    mod_cols = jnp.sum(mod_parts, axis=1).astype(BF).reshape(dp * count, ada_cols)
    shard_ada = jnp.einsum("sr,sc->cr", cond_all, mod_cols, preferred_element_type=F32)

    cond_part = jnp.einsum("sc,rc->sr", mod_cols, low_ada, preferred_element_type=F32)
    cond_part = jnp.broadcast_to(cond_part.reshape(dp, 1, -1), (dp, seq, count * ada_rows))
    term_bias = jnp.concatenate([bias_ada, bias_q, bias_v, bias_proj, bias_fc1, bias_fc2])
    parcel = jnp.concatenate([term_bias.reshape(dp, seq, -1), cond_part], axis=-1)
    got_parcel = net.to_all(parcel)

    sums = halves.finish(parcel)
    blank = jnp.zeros((2, net.z.size, per) + PACKED, F32)
    (next_fc2, next_proj, next_fc1), *early = muon_gram(
        net.spots(), [(sums[0], [turned[3]]), (sums[1], [turned[1], turned[2]])], spread_early, (blank, blank)
    )
    got_parcel = tie(got_parcel, early[0])
    halves = Staged(net.halves_steps(tie(sum_last, got_parcel)))
    sent = halves.advance()
    total = halves.finish(shard_ada)
    (next_qkv, next_ada), *grams = muon_gram(
        net.spots(), [(total, [turned[0]]), (shard_ada, [turned[4]])], spread_last, early
    )
    grams = Staged(net.gram_steps(*grams))
    sent = grams.advance()
    parcel = tie(got_parcel, *sent)
    while not grams.done:
        sent = grams.advance(sent[0])
    gathered = Staged(net.muon_gather_steps(grams.result))
    sent = gathered.advance()
    while not gathered.done:
        sent = gathered.advance(sent[0])
    momenta_in = [next_fc2, next_proj, next_fc1, next_qkv, next_ada]
    heights_of = [momentum.shape[1] // ROW_BLOCK for momentum in momenta_in]
    placed = block_spots(heights_of[:3], spread_early)
    placed += [(3 + spot[0],) + spot[1:] for spot in block_spots(heights_of[3:], spread_last)]
    new_fc2, new_proj, new_fc1, new_qkv, new_ada = muon_apply(
        net.spots(), gathered.result, momenta_in, [w.T for w in (w_fc2, w_proj, w_fc1, w_qkv, w_ada)],
        [math.sqrt(width / hidden), 1.0, math.sqrt(hidden / width), math.sqrt(3.0), math.sqrt(6.0)], placed,
    )

    size = biases.shape[0]
    grad_bias = jnp.sum(parcel[..., :size], axis=(0, 1))
    cond_part = jnp.sum(parcel[..., size:], axis=0).reshape(seq, count, ada_rows)
    grad_cond = silu_back(jnp.transpose(cond_part, (1, 0, 2)).reshape(count, width))[0]
    next_first = BETA_FIRST * bias_first + (1.0 - BETA_FIRST) * grad_bias
    next_second = BETA_SECOND * bias_second + (1.0 - BETA_SECOND) * grad_bias * grad_bias
    first_hat = next_first / (1.0 - BETA_FIRST**STEP_COUNT)
    second_hat = next_second / (1.0 - BETA_SECOND**STEP_COUNT)
    new_biases = biases * (1.0 - ADAM_RATE * ADAM_DECAY) - ADAM_RATE * first_hat / (
        jnp.sqrt(second_hat) + ADAM_EPS
    )
    return (
        result.reshape(tokens.shape),
        grad_inputs,
        grad_cond.reshape(conditioning.shape),
        new_qkv.T, new_proj.T, new_fc1.T, new_fc2.T, new_ada.T,
        next_qkv.T, next_proj.T, next_fc1.T, next_fc2.T, next_ada.T,
        new_biases,
        next_first,
        next_second,
    )


def solution(mesh):
    rows = P(None, "dp", "seq", None)
    matrix = P("seq", "dp")
    flat = P(("dp", "seq"))
    in_specs = (rows, P(None, "dp", None), P(None, "dp"), P(None, "dp"), rows) + (matrix,) * 10 + (flat,) * 3
    out_specs = (rows, rows, P(None, "dp", None)) + (matrix,) * 10 + (flat,) * 3
    return jax.shard_map(
        functools.partial(body, Net(mesh)), mesh=mesh, in_specs=in_specs, out_specs=out_specs, check_vma=False
    )
```

```python
import functools
import math

import jax
import jax.numpy as jnp
from jax import lax
from jax.experimental import pallas as pl
from jax.experimental.pallas import tpu as pltpu
from jax.sharding import PartitionSpec as P

HEADS = 16
ROW_BLOCK = 144
NS_STEPS = 5
STEP_COUNT = 10

PRECISE = lax.Precision.HIGHEST
LN_EPS = 1e-06
MASKED = -1e30
NS_A = 3.4445
NS_B = -4.775
NS_C = 2.0315
MUON_DECAY = 0.5
WEIGHT_SHRINK = 0.0001
NORM_EPS = 1e-07
BETA_FIRST = 0.9
BETA_SECOND = 0.999
ADAM_RATE = 0.1
ADAM_DECAY = 0.01
ADAM_EPS = 1e-08
BF = jnp.bfloat16
F32 = jnp.float32
VMEM_LIMIT = 60 * 2**20


class Ring:
    def __init__(self, name, total, stride, size):
        self.name, self.total, self.stride, self.size = name, total, stride, size

    def digit(self):
        return (lax.axis_index(self.name) // self.stride) % self.size

    def send(self, value, shift):
        pairs = []
        for i in range(self.total):
            d = (i // self.stride) % self.size
            pairs.append((i, i + ((d + shift) % self.size - d) * self.stride))
        return lax.ppermute(value, self.name, pairs)

    def gather(self, value, far=1):
        n = self.size
        blocks = [value] + [None] * (n - 1)
        if n == 2:
            blocks[1] = self.send(value, 1)
        elif n > 2:
            low = high = value
            for t in range(1, n // 2):
                low, high = self.send(low, 1), self.send(high, -1)
                blocks[n - t], blocks[t] = low, high
            blocks[n // 2] = self.send(low, 1) if far == 1 else self.send(high, -1)
        return blocks

    def gather_steps(self, value, far=1):
        n = self.size
        blocks = [value] + [None] * (n - 1)
        if n == 2:
            blocks[1] = self.send(value, 1)
            anchor = yield [value]
            blocks[1] = tie(blocks[1], anchor)
            return blocks
        low = high = value
        for t in range(1, n // 2):
            sent = [low, high]
            low, high = self.send(low, 1), self.send(high, -1)
            anchor = yield sent
            low, high = tie(low, anchor), tie(high, anchor)
            blocks[n - t], blocks[t] = low, high
        sent = [low if far == 1 else high]
        last = self.send(sent[0], far)
        anchor = yield sent
        blocks[n // 2] = tie(last, anchor)
        return blocks

    def scatter_steps(self, block_of, far=1):
        n = self.size
        if n == 1:
            return block_of(0).astype(F32)
        if n == 2:
            sent = block_of(1)
            got = self.send(sent, 1)
            anchor = yield [sent]
            return block_of(0).astype(F32) + tie(got, anchor).astype(F32)
        sent = block_of(n // 2)
        got = self.send(sent, far)
        anchor = yield [sent]
        low, high = (tie(got, anchor), None) if far == 1 else (None, tie(got, anchor))
        for t in range(n // 2 - 1, 0, -1):
            up, down = block_of(t), block_of(n - t)
            if low is not None:
                up = (up.astype(F32) + low.astype(F32)).astype(up.dtype)
            if high is not None:
                down = (down.astype(F32) + high.astype(F32)).astype(down.dtype)
            low, high = self.send(up, 1), self.send(down, -1)
            anchor = yield [up, down]
            low, high = tie(low, anchor), tie(high, anchor)
        return block_of(0).astype(F32) + low.astype(F32) + high.astype(F32)


def tie(value, *earlier):
    earlier = [array for array in earlier if array is not None]
    if not earlier:
        return value
    anywhere = pl.BlockSpec(memory_space=pl.ANY)
    return pl.pallas_call(
        lambda *refs: None,
        out_shape=jax.ShapeDtypeStruct(value.shape, value.dtype),
        in_specs=[anywhere] * (1 + len(earlier)),
        out_specs=anywhere,
        input_output_aliases={0: 0},
        name="tie",
    )(value, *earlier)


def lockstep(*steps):
    results = [None] * len(steps)
    alive = dict(enumerate(steps))
    anchor = None
    while alive:
        sent = []
        for n, step in list(alive.items()):
            try:
                sent += step.send(anchor)
            except StopIteration as stop:
                results[n] = stop.value
                del alive[n]
        if alive:
            anchor = yield sent
    return results


class Staged:
    def __init__(self, steps):
        self.steps, self.result, self.started, self.done = steps, None, False, False

    def advance(self, anchor=None):
        if self.done:
            return []
        try:
            sent = self.steps.send(anchor if self.started else None)
            self.started = True
            return sent
        except StopIteration as stop:
            self.result, self.done = stop.value, True
            return []

    def finish(self, anchor=None):
        while not self.done:
            self.advance(anchor)
        return self.result


def place_kernel(zs, ga, parts, count, outs, *refs):
    spots, sources = refs[0], refs[1 : 1 + count]
    outputs, (full, in_sems, out_sems) = refs[1 + count : 1 + count + outs], refs[1 + count + outs :]
    g = full.shape[3]
    half = count // 2
    shards = []
    for sc in range(2):
        for sx in range(2):
            for sz in range(zs):
                where = (lax.rem(spots[0] + sz, zs), lax.rem(spots[1] + sx, 2), lax.rem(spots[2] + sc, 2))
                n = 2 * len(shards)
                line, pair = sources[sc * half + sx].at[sz], sources[sc * half + 2 + sz].at[sx]
                copies = [
                    pltpu.make_async_copy(line, full.at[(*where, pl.ds(0, ga))], in_sems.at[n]),
                    pltpu.make_async_copy(pair, full.at[(*where, pl.ds(ga, g - ga))], in_sems.at[n + 1]),
                ]
                for copy in copies:
                    copy.start()
                shards.append((where, copies))
    exits = []
    for where, copies in shards:
        for copy in copies:
            copy.wait()
        for output, start, size, column, depth in parts:
            target = outputs[output].at[(*where, slice(None), slice(None), pl.ds(column, depth))]
            copy = pltpu.make_async_copy(
                full.at[(*where, pl.ds(start, size))], target, out_sems.at[len(exits)]
            )
            copy.start()
            exits.append(copy)
    for copy in exits:
        copy.wait()


def place(spots, sources, shape, ga, parts, shapes):
    zs = shape[0]
    moved = math.prod(shape) * 2
    return pl.pallas_call(
        functools.partial(place_kernel, zs, ga, parts, len(sources), len(shapes)),
        out_shape=[jax.ShapeDtypeStruct(each, BF) for each in shapes],
        in_specs=[pl.BlockSpec(memory_space=pltpu.SMEM)]
        + [pl.BlockSpec(memory_space=pl.ANY)] * len(sources),
        out_specs=[pl.BlockSpec(memory_space=pl.ANY)] * len(shapes),
        scratch_shapes=[
            pltpu.VMEM(shape, BF),
            pltpu.SemaphoreType.DMA((8 * zs,)),
            pltpu.SemaphoreType.DMA((4 * zs * len(parts),)),
        ],
        compiler_params=pltpu.CompilerParams(vmem_limit_bytes=VMEM_LIMIT),
        cost_estimate=pl.CostEstimate(flops=0, bytes_accessed=2 * moved, transcendentals=0),
        name="place",
    )(spots, *sources)


class Net:
    def __init__(self, mesh):
        dp, seq = mesh.shape["dp"], mesh.shape["seq"]
        self.dp, self.seq = dp, seq
        self.core = Ring("dp", dp, 1, 2)
        self.x = Ring("dp", dp, 2, 2)
        self.z = Ring("dp", dp, 4, dp // 4)
        self.y = Ring("seq", seq, 1, seq)

    def spots(self):
        return jnp.stack([self.z.digit(), self.x.digit(), self.core.digit()]).astype(jnp.int32)


    def wire(self, shards):
        turned = [shard.astype(BF).T for shard in shards]
        return turned[0] if len(turned) == 1 else jnp.concatenate(turned, axis=0)

    def rows(self, wires):
        if self.seq == 2:
            own, other = wires
            return jnp.where(
                self.y.digit() == 0,
                jnp.concatenate([own, other], axis=1),
                jnp.concatenate([other, own], axis=1),
            )
        order = (jnp.arange(self.seq) - self.y.digit()) % self.seq
        full = jnp.take(jnp.stack(wires), order, axis=0)
        return jnp.transpose(full, (1, 0, 2)).reshape(full.shape[1], -1)

    def joined(self, wires, unit, depth):
        full = self.rows(wires)
        return full.reshape(full.shape[0] // unit, unit, depth)

    def scatter(self, term):
        return lax.psum_scatter(term, "dp", scatter_dimension=0, tiled=True)

    def halves_steps(self, term):
        y = self.y.digit()
        blocks = term.reshape(term.shape[0], self.seq, -1)
        return (
            yield from self.y.scatter_steps(
                lambda s: lax.dynamic_index_in_dim(blocks, (y + s) % self.seq, 1, keepdims=False)
            )
        )

    def gather_steps(self, units, layout, part):
        g, unit, depth = units.shape
        zs = self.z.size
        ga = max(1, int(part * g))
        first, second = units[:ga], units[ga:]

        def line_steps():
            blocks = yield from self.z.gather_steps(first, 1)
            line = jnp.stack(blocks)
            return (yield from self.x.gather_steps(line))

        def pair_steps():
            blocks = yield from self.x.gather_steps(second)
            return (yield from self.z.gather_steps(jnp.stack(blocks), -1))

        lines, pairs = yield from lockstep(line_steps(), pair_steps())
        pieces = lines + pairs
        others = [self.core.send(piece, 1) for piece in pieces]
        anchor = yield pieces
        sources = pieces + [tie(other, anchor) for other in others]
        parts, shapes, start = [], [], 0
        for n, (rows, blocks) in enumerate(layout):
            size = rows // unit
            shapes.append((zs, 2, 2, size, unit, blocks * depth))
            for j in range(blocks):
                parts.append((n, start, size, j * depth, depth))
                start += size
        full = place(self.spots(), sources, (zs, 2, 2, g, unit, depth), ga, parts, shapes)
        return [f.reshape(-1, f.shape[-1]) for f in full], lines[1:] + pairs[1:]


    def gram_steps(self, own, other):
        got = self.core.send(other, 1)
        anchor = yield [other]
        half = own + tie(got, anchor)
        sent = half[1].astype(BF)
        got = self.x.send(sent, 1)
        anchor = yield [sent]
        kept = half[0] + tie(got, anchor).astype(F32)
        sent = [kept[shift].astype(BF) for shift in range(1, self.z.size)]
        got = [self.z.send(each, shift) for shift, each in enumerate(sent, 1)]
        anchor = yield sent
        return [kept[0]] + [tie(each, anchor) for each in got]

    def muon_gather_steps(self, parts):
        factor = polynomial(parts)
        got = [self.z.send(factor, -shift) for shift in range(1, self.z.size)]
        anchor = yield [factor]
        line = jnp.stack([factor] + [tie(each, anchor) for each in got])
        got = self.x.send(line, 1)
        anchor = yield [line]
        pair = [line, tie(got, anchor)]
        others = [self.core.send(each, 1) for each in pair]
        anchor = yield pair
        return pair + [tie(each, anchor) for each in others]


    def to_all(self, value):
        flat = value.reshape((self.dp * self.seq,) + value.shape[2:])
        return lax.all_to_all(flat, ("dp", "seq"), 0, 0, tiled=True).reshape(value.shape)

    def to_dp(self, value):
        return lax.all_to_all(value, "dp", 0, 0, tiled=True)


def layer_norm(values):
    centered = values - jnp.mean(values, axis=-1, keepdims=True)
    inverse = lax.rsqrt(jnp.mean(centered * centered, axis=-1, keepdims=True) + LN_EPS)
    return (centered * inverse, inverse)


def norm_back(normed, inverse, grad):
    mean_grad = jnp.mean(grad, axis=-1, keepdims=True)
    mean_cross = jnp.mean(grad * normed, axis=-1, keepdims=True)
    return inverse * (grad - mean_grad - normed * mean_cross)


def sigmoid_linear(values):
    return values * jax.nn.sigmoid(values)


def dot_t(left, right):
    return jnp.einsum("srk,nk->srn", left, right, preferred_element_type=F32)


def dot(left, right):
    return jnp.einsum("srn,nk->srk", left, right, preferred_element_type=F32)


GELU_SCALE = math.sqrt(2.0 / math.pi)
GELU_CUBE = 0.044715


def row_parts(rows):
    step = rows // 4 if rows % 64 == 0 else rows
    return [slice(start, start + step) for start in range(0, rows, step)]


def hidden_kernel(x_ref, w_ref, b_ref, act_ref, slope_ref):
    for part in row_parts(x_ref.shape[0]):
        value = nt(x_ref[part], w_ref[...]) + b_ref[...]
        square = value * value
        bend = jnp.tanh(value * (GELU_SCALE + (GELU_SCALE * GELU_CUBE) * square))
        half = 0.5 + 0.5 * bend
        act_ref[part] = (value * half).astype(BF)
        steep = (0.5 * value) * (GELU_SCALE + (3.0 * GELU_SCALE * GELU_CUBE) * square)
        slope_ref[part] = (half + steep * (1.0 - bend * bend)).astype(BF)


def hidden_forward(x, w, bias):
    rows, depth = x.shape
    n = w.shape[0]
    tile = math.gcd(n, 512)
    out = pl.BlockSpec((rows, tile), lambda i: (0, i))
    return pl.pallas_call(
        hidden_kernel,
        grid=(n // tile,),
        in_specs=[
            pl.BlockSpec((rows, depth), lambda i: (0, 0)),
            pl.BlockSpec((tile, depth), lambda i: (i, 0)),
            pl.BlockSpec((1, tile), lambda i: (0, i)),
        ],
        out_specs=[out, out],
        out_shape=[jax.ShapeDtypeStruct((rows, n), BF)] * 2,
        compiler_params=pltpu.CompilerParams(vmem_limit_bytes=VMEM_LIMIT),
        cost_estimate=pl.CostEstimate(
            flops=2 * rows * n * depth, bytes_accessed=2 * (rows + n) * depth + 4 * rows * n, transcendentals=rows * n
        ),
        name="hidden_forward",
    )(x, w, bias.reshape(1, n))


def hidden_back_kernel(g_ref, w_ref, slope_ref, out_ref, bias_ref):
    total = 0.0
    for part in row_parts(g_ref.shape[0]):
        grad = (nn(g_ref[part], w_ref[...]) * slope_ref[part].astype(F32)).astype(BF)
        out_ref[part] = grad
        total = total + jnp.sum(grad.astype(F32), axis=0, keepdims=True)
    bias_ref[...] = total


def hidden_backward(grad, w, slope):
    rows, depth = grad.shape
    n = w.shape[1]
    tile = math.gcd(n, 512)
    out = pl.BlockSpec((rows, tile), lambda i: (0, i))
    result, bias = pl.pallas_call(
        hidden_back_kernel,
        grid=(n // tile,),
        in_specs=[
            pl.BlockSpec((rows, depth), lambda i: (0, 0)),
            pl.BlockSpec((depth, tile), lambda i: (0, i)),
            out,
        ],
        out_specs=[out, pl.BlockSpec((1, tile), lambda i: (0, i))],
        out_shape=[jax.ShapeDtypeStruct((rows, n), BF), jax.ShapeDtypeStruct((1, n), F32)],
        compiler_params=pltpu.CompilerParams(vmem_limit_bytes=VMEM_LIMIT),
        cost_estimate=pl.CostEstimate(
            flops=2 * rows * n * depth, bytes_accessed=2 * (rows + n) * depth + 4 * rows * n, transcendentals=0
        ),
        name="hidden_backward",
    )(grad, w, slope)
    return result, bias[0]


def outer(left, right):
    return jnp.einsum("srn,srk->nk", left, right, preferred_element_type=F32).astype(BF)


def shard_outer_kernel(plan, counts, tile, split, spots_ref, *refs):
    outs = 2 if split else 1
    inputs, where = refs[: counts[0]], refs[counts[1] : counts[1] + outs]
    buffers = refs[counts[1] + outs : counts[1] + outs + len(plan["loads"])]
    acc, in_sems, out_sems = refs[counts[1] + outs + len(plan["loads"]) :]
    loads = []
    for n, (sources, start, size) in enumerate(plan["loads"]):
        row, copies = 0, []
        for m, source in enumerate(sources):
            rows = inputs[source].shape[0]
            window = inputs[source].at[:, pl.ds(start, size)]
            copies.append(pltpu.make_async_copy(window, buffers[n].at[pl.ds(row, rows)], in_sems.at[n, m]))
            copies[-1].start()
            row += rows
        loads.append(copies)
    ready = set()
    shipped = []
    unit = acc.shape[1]
    for left, right, base, ships in plan["parts"]:
        for n in (left, right):
            if n not in ready:
                for copy in loads[n]:
                    copy.wait()
                ready.add(n)
        width = buffers[left].shape[1]
        step = tile if width % tile == 0 else width

        @pl.loop(0, width // step)
        def _(t):
            block = buffers[left][:, pl.ds(pl.multiple_of(t * step, step), step)]
            product = lax.dot_general(
                block, buffers[right][...], (((0,), (0,)), ((), ())), preferred_element_type=F32
            )
            product = product.reshape(step // unit, unit, product.shape[1]).astype(BF)
            acc[pl.ds(base + t * (step // unit), step // unit)] = product

        for core, z, x, row, target, size in ships:
            spot = (z, x) if split else (z, x, core)
            places = [ref.at[(*spot, pl.ds(target, size))] for ref in where]
            copies = [
                pltpu.make_async_copy(acc.at[pl.ds(row, size)], each, out_sems.at[len(shipped)]) for each in places
            ]
            shipped.append((core, copies))
            on_own_core(split, spots_ref, core, [copy.start for copy in copies])
    for core, copies in shipped:
        on_own_core(split, spots_ref, core, [copy.wait for copy in copies])


def on_own_core(split, spots_ref, core, actions):
    if not split:
        actions[0]()
        return

    @pl.when(spots_ref[2] == core)
    def _():
        actions[0]()

    @pl.when(spots_ref[2] != core)
    def _():
        actions[1]()


def shard_outer(spots, inputs, loads, parts, zs, depth, unit, shard_units, deps=(), tile=384, split=True):
    dp = zs * 4
    plan_parts, base, row, placed = [], 0, 0, {}
    begun = {}
    for left, right, rows, first in parts:
        if first not in begun:
            begun[first] = (base, 0)
        start, shipped = begun[first]
        width = loads[left][2]
        size = rows // unit
        end = base + width // unit
        ships = []
        while shipped < dp and start + (shipped + 1) * size <= end:
            core, x, z = shipped % 2, shipped // 2 % 2, shipped // 4
            ships.append((core, z, x, start + shipped * size, first, size))
            shipped += 1
        begun[first] = (start, shipped)
        plan_parts.append((left, right, base, ships))
        base = end
    total = sum(len(part[3]) for part in plan_parts)
    shape = (zs, 2, shard_units, unit, depth) if split else (zs, 2, 2, shard_units, unit, depth)
    outs = [jax.ShapeDtypeStruct(shape, BF)] * (2 if split else 1)
    anywhere = pl.BlockSpec(memory_space=pl.ANY)
    heights = [sum(inputs[source].shape[0] for source in sources) for sources, _, _ in loads]
    flops = sum(2 * heights[p[0]] * loads[p[0]][2] * loads[p[1]][2] for p in parts)
    return pl.pallas_call(
        functools.partial(
            shard_outer_kernel, {"loads": loads, "parts": plan_parts}, (len(inputs), len(inputs) + len(deps)), tile, split
        ),
        out_shape=outs,
        in_specs=[pl.BlockSpec(memory_space=pltpu.SMEM)] + [anywhere] * (len(inputs) + len(deps)),
        out_specs=[anywhere] * len(outs),
        scratch_shapes=[pltpu.VMEM((height, load[2]), BF) for height, load in zip(heights, loads)]
        + [
            pltpu.VMEM((base, unit, depth), BF),
            pltpu.SemaphoreType.DMA((len(loads), max(len(load[0]) for load in loads))),
            pltpu.SemaphoreType.DMA((total,)),
        ],
        compiler_params=pltpu.CompilerParams(vmem_limit_bytes=VMEM_LIMIT),
        cost_estimate=pl.CostEstimate(flops=flops, bytes_accessed=2 * base * unit * depth, transcendentals=0),
        name="shard_outer",
    )(spots, *inputs, *deps)


LANES = 128
LOG2E = math.log2(math.e)


def padded(block, column=None):
    rows, depth = block.shape
    if column is None:
        return jnp.concatenate([block, jnp.zeros((rows, LANES - depth), block.dtype)], axis=1)
    rest = jnp.zeros((rows, LANES - depth - 1), block.dtype)
    return jnp.concatenate([block, column.astype(block.dtype), rest], axis=1)


def mask_column(lengths_ref, offsets_ref, sample, total, rows):
    place = lax.broadcasted_iota(jnp.int32, (total, 1), 0)
    position = place
    for s in range(total // rows):
        position = jnp.where(place // rows == s, place - s * rows + offsets_ref[s], position)
    return jnp.where(position < lengths_ref[sample], 0.0, MASKED)


def nt(left, right):
    return lax.dot_general(left, right, (((1,), (1,)), ((), ())), preferred_element_type=F32)


def nn(left, right):
    return jnp.dot(left, right, preferred_element_type=F32)


def without(kernel, start, count, *fixed):
    def run(*refs):
        kernel(*fixed, *refs[:start], *refs[start + count :])

    return run


def attend_kernel(heads, chunk, lengths_ref, offsets_ref, q_ref, k_ref, v_ref, o_ref, lse_ref, q_s, k_s, vt_s, o_s):
    rows, width = q_ref.shape[1:]
    total = k_ref.shape[1]
    depth = width // heads
    factor = depth**-0.5 * LOG2E
    mask = mask_column(lengths_ref, offsets_ref, pl.program_id(0), total, rows)
    q_blank = padded(jnp.zeros((rows, depth), BF), jnp.ones((rows, 1), F32))
    k_blank = padded(jnp.zeros((total, depth), BF), mask)
    turned = jnp.transpose(v_ref[0].astype(F32))
    for h in range(heads):
        span = slice(h * depth, (h + 1) * depth)
        q_s[h] = q_blank
        k_s[h] = k_blank
        q_s[h, :, :depth] = q_ref[0, :, span]
        k_s[h, :, :depth] = k_ref[0, :, span]
        vt_s[h] = turned[span].astype(BF)

    def one_head(h, carry):
        peak = jnp.full((1, rows), MASKED, F32)
        sums = jnp.zeros((1, rows), F32)
        mixed = jnp.zeros((depth, rows), F32)
        for c in range(total // chunk):
            part = slice(c * chunk, (c + 1) * chunk)
            scores = nt(k_s[h, part], q_s[h])
            higher = jnp.maximum(peak, jnp.max(scores, axis=0, keepdims=True))
            weights = jnp.exp2((scores - higher) * factor)
            if c == 0:
                sums = jnp.sum(weights, axis=0, keepdims=True)
                mixed = nn(vt_s[h, :, part], weights.astype(BF))
            else:
                shrink = jnp.exp2((peak - higher) * factor)
                sums = sums * shrink + jnp.sum(weights, axis=0, keepdims=True)
                mixed = mixed * shrink + nn(vt_s[h, :, part], weights.astype(BF))
            peak = higher
        o_s[h] = jnp.transpose(mixed / sums)
        lse_ref[0, h] = peak * factor + jnp.log2(sums)
        return carry

    lax.fori_loop(0, heads, one_head, 0, unroll=4)
    for h in range(heads):
        o_ref[0, :, h * depth : (h + 1) * depth] = o_s[h].astype(BF)


def attend(lengths, offsets, queries, keys, values, heads, tile, deps=()):
    count, rows, width = queries.shape
    total = keys.shape[1]
    depth = width // heads
    tile = min(tile, total)
    pick = lambda i, *_: (i, 0, 0)
    return pl.pallas_call(
        without(attend_kernel, 5, len(deps), heads, tile),
        grid_spec=pltpu.PrefetchScalarGridSpec(
            num_scalar_prefetch=2,
            grid=(count,),
            in_specs=[
                pl.BlockSpec((1, rows, width), pick),
                pl.BlockSpec((1, total, width), pick),
                pl.BlockSpec((1, total, width), pick),
            ]
            + [pl.BlockSpec(memory_space=pl.ANY)] * len(deps),
            out_specs=[
                pl.BlockSpec((1, rows, width), pick),
                pl.BlockSpec((1, heads, 1, rows), lambda i, *_: (i, 0, 0, 0)),
            ],
            scratch_shapes=[
                pltpu.VMEM((heads, rows, LANES), BF),
                pltpu.VMEM((heads, total, LANES), BF),
                pltpu.VMEM((heads, depth, total), BF),
                pltpu.VMEM((heads, rows, depth), F32),
            ],
        ),
        out_shape=[
            jax.ShapeDtypeStruct((count, rows, width), BF),
            jax.ShapeDtypeStruct((count, heads, 1, rows), F32),
        ],
        compiler_params=pltpu.CompilerParams(vmem_limit_bytes=VMEM_LIMIT),
        cost_estimate=pl.CostEstimate(
            flops=4 * count * heads * rows * total * LANES,
            bytes_accessed=2 * count * width * (2 * rows + 2 * total),
            transcendentals=count * heads * rows * total,
        ),
        name="attend",
    )(lengths, offsets, queries, keys, values, *deps)


def attend_back_kernel(
    heads, chunk, lengths_ref, offsets_ref, q_ref, k_ref, v_ref, o_ref, g_ref, lse_ref,
    dq_ref, dk_ref, dv_ref, q_s, k_s, kt_s, v_s, g_s, delta_s, dq_s, dk_s, dv_s
):
    rows, width = q_ref.shape[1:]
    total = k_ref.shape[1]
    depth = width // heads
    scale = depth**-0.5
    factor = scale * LOG2E
    mask = mask_column(lengths_ref, offsets_ref, pl.program_id(0), total, rows)
    ones = jnp.ones((rows, 1), F32)
    cross = jnp.transpose(g_ref[0].astype(F32) * o_ref[0].astype(F32))
    for h in range(heads):
        span = slice(h * depth, (h + 1) * depth)
        delta_s[h] = jnp.sum(cross[span], axis=0, keepdims=True)
        q_s[h] = padded(q_ref[0, :, span], ones)
        k_s[h] = padded(k_ref[0, :, span], mask)
        kt_s[h] = jnp.transpose(k_ref[0, :, span])
        g_s[h] = padded(g_ref[0, :, span])
        v_s[h] = padded(v_ref[0, :, span])

    def one_head(h, carry):
        dq = jnp.zeros((depth, rows), F32)
        for c in range(total // chunk):
            part = slice(c * chunk, (c + 1) * chunk)
            probs = jnp.exp2(nt(k_s[h, part], q_s[h]) * factor - lse_ref[0, h])
            slopes = (probs * (nt(v_s[h, part], g_s[h]) - delta_s[h])).astype(BF)
            dv_s[h, part] = nn(probs.astype(BF), g_s[h]).astype(BF)
            dk_s[h, part] = (nn(slopes, q_s[h]) * scale).astype(BF)
            dq = dq + nn(kt_s[h, :, part], slopes)
        dq_s[h] = jnp.transpose(dq * scale)
        return carry

    lax.fori_loop(0, heads, one_head, 0, unroll=4)
    for h in range(heads):
        span = slice(h * depth, (h + 1) * depth)
        dq_ref[0, :, span] = dq_s[h].astype(BF)
        dk_ref[0, :, span] = dk_s[h][:, :depth]
        dv_ref[0, :, span] = dv_s[h][:, :depth]


def attend_back(lengths, offsets, queries, keys, values, mixed, grads, sample, lse, heads, tile, deps=()):
    count, rows, width = queries.shape
    total = keys.shape[1]
    depth = width // heads
    tile = min(tile, total)
    pick = lambda i, *_: (i, 0, 0)
    near = pl.BlockSpec((1, rows, width), pick)
    picked = pl.BlockSpec((1, rows, width), lambda i, *_: (sample + i, 0, 0))
    far = pl.BlockSpec((1, total, width), pick)
    return pl.pallas_call(
        without(attend_back_kernel, 8, len(deps), heads, tile),
        grid_spec=pltpu.PrefetchScalarGridSpec(
            num_scalar_prefetch=2,
            grid=(count,),
            in_specs=[near, far, far, near, picked, pl.BlockSpec((1, heads, 1, rows), lambda i, *_: (i, 0, 0, 0))]
            + [pl.BlockSpec(memory_space=pl.ANY)] * len(deps),
            out_specs=[near, far, far],
            scratch_shapes=[
                pltpu.VMEM((heads, rows, LANES), BF),
                pltpu.VMEM((heads, total, LANES), BF),
                pltpu.VMEM((heads, depth, total), BF),
                pltpu.VMEM((heads, total, LANES), BF),
                pltpu.VMEM((heads, rows, LANES), BF),
                pltpu.VMEM((heads, 1, rows), F32),
                pltpu.VMEM((heads, rows, depth), F32),
                pltpu.VMEM((heads, total, LANES), BF),
                pltpu.VMEM((heads, total, LANES), BF),
            ],
        ),
        out_shape=[
            jax.ShapeDtypeStruct((count, rows, width), BF),
            jax.ShapeDtypeStruct((count, total, width), BF),
            jax.ShapeDtypeStruct((count, total, width), BF),
        ],
        compiler_params=pltpu.CompilerParams(vmem_limit_bytes=VMEM_LIMIT),
        cost_estimate=pl.CostEstimate(
            flops=10 * count * heads * rows * total * LANES,
            bytes_accessed=2 * count * width * (4 * rows + 4 * total),
            transcendentals=count * heads * rows * total,
        ),
        name="attend_back",
    )(lengths, offsets, queries, keys, values, mixed, grads, lse, *deps)


def block_spots(counts, spread):
    per, first = spread
    spots = []
    for matrix, count in enumerate(counts):
        for block in range(count):
            device, place_in = divmod(len(spots), per)
            device += first
            spots.append((matrix, block, device // 4, device // 2 % 2, device % 2, place_in))
    return spots


EXTRA = ROW_BLOCK - 128
PACKED = (ROW_BLOCK + EXTRA, 128)


def packed(block):
    corner = block[128:, 128:]
    corner = jnp.concatenate([corner, jnp.zeros((EXTRA, 128 - EXTRA), block.dtype)], axis=1)
    return jnp.concatenate([block[:, :128], corner], axis=0)


def unpacked(block):
    side = jnp.transpose(block[128:ROW_BLOCK])
    right = jnp.concatenate([side, block[ROW_BLOCK:, :EXTRA]], axis=0)
    return jnp.concatenate([block[:ROW_BLOCK], right], axis=1)


def precise(left, right, dims):
    return lax.dot_general(left, right, (dims, ((), ())), precision=PRECISE, preferred_element_type=F32)


def muon_gram_kernel(groups, spread, spots_ref, base_own, base_other, *refs):
    count = sum(groups)
    sums, momenta = refs[: len(groups)], refs[len(groups) : len(groups) + count]
    outs = refs[len(groups) + count : len(groups) + 2 * count]
    own_ref, other_ref, grams, sems = refs[len(groups) + 2 * count :]
    n = 0
    for matrices, sum_ref in zip(groups, sums):
        start = 0
        for _ in range(matrices):
            size = momenta[n].shape[0]
            outs[n][...] = MUON_DECAY * momenta[n][...] + sum_ref[start : start + size]
            start += size
            n += 1
    zs = own_ref.shape[1]
    spots = block_spots([out.shape[1] // ROW_BLOCK for out in outs], spread)
    copies = []
    for n, (matrix, block, z, x, core, place_in) in enumerate(spots):
        turned = outs[matrix][:, block * ROW_BLOCK : (block + 1) * ROW_BLOCK]
        grams[n] = packed(precise(turned, turned, ((0,), (0,))))
        away = (lax.rem(spots_ref[1] + x, 2), lax.rem(zs + z - spots_ref[0], zs), place_in)
        pair = [pltpu.make_async_copy(grams.at[n], ref.at[away], sems.at[n]) for ref in (own_ref, other_ref)]
        on_own_core(True, spots_ref, core, [copy.start for copy in pair])
        copies.append((core, pair))
    for core, pair in copies:
        on_own_core(True, spots_ref, core, [copy.wait for copy in pair])


def muon_gram(spots, groups, spread, base):
    momenta = [momentum for _, each in groups for momentum in each]
    terms = jax.ShapeDtypeStruct(base[0].shape, F32)
    vmem, anywhere = pl.BlockSpec(memory_space=pltpu.VMEM), pl.BlockSpec(memory_space=pl.ANY)
    blocks = len(block_spots([momentum.shape[1] // ROW_BLOCK for momentum in momenta], spread))
    outs = pl.pallas_call(
        functools.partial(muon_gram_kernel, [len(each) for _, each in groups], spread),
        out_shape=[jax.ShapeDtypeStruct(momentum.shape, F32) for momentum in momenta] + [terms, terms],
        in_specs=[pl.BlockSpec(memory_space=pltpu.SMEM), anywhere, anywhere]
        + [vmem] * (len(groups) + len(momenta)),
        out_specs=[vmem] * len(momenta) + [anywhere, anywhere],
        input_output_aliases={1: len(momenta), 2: len(momenta) + 1},
        scratch_shapes=[
            pltpu.VMEM((blocks,) + PACKED, F32),
            pltpu.SemaphoreType.DMA((blocks,)),
        ],
        compiler_params=pltpu.CompilerParams(vmem_limit_bytes=VMEM_LIMIT),
        name="muon_gram",
    )(spots, *base, *[group[0] for group in groups], *momenta)
    return outs[:-2], outs[-2], outs[-1]


def polynomial_kernel(count, *refs):
    out = refs[count]
    shape = (ROW_BLOCK, ROW_BLOCK)
    eye = (lax.broadcasted_iota(jnp.int32, shape, 0) == lax.broadcasted_iota(jnp.int32, shape, 1)).astype(F32)
    mul = lambda left, right: precise(left, right, ((1,), (0,)))
    blocks = range(out.shape[0])
    currents, scales, totals = [], [], []
    for n in blocks:
        gram = refs[0][n]
        for ref in refs[1:count]:
            gram = gram + ref[n].astype(F32)
        gram = unpacked(gram)
        square = jnp.sum(jnp.sum(gram * eye, axis=1, keepdims=True), axis=0, keepdims=True)
        scale = 1.0 / (jnp.sqrt(square) + NORM_EPS)
        scales.append(scale)
        currents.append(gram * (scale * scale))
    for step in range(NS_STEPS):
        factors = [NS_A * eye + NS_B * a + NS_C * mul(a, a) for a in currents]
        totals = factors if step == 0 else [mul(f, t) for f, t in zip(factors, totals)]
        if step + 1 < NS_STEPS:
            currents = [mul(f, a) for f, a in zip(factors, currents)]
            currents = [mul(a, f) for f, a in zip(factors, currents)]
    for n in blocks:
        out[n] = packed(totals[n] * scales[n])


def polynomial(parts):
    vmem = pl.BlockSpec(memory_space=pltpu.VMEM)
    return pl.pallas_call(
        functools.partial(polynomial_kernel, len(parts)),
        out_shape=jax.ShapeDtypeStruct(parts[0].shape, F32),
        in_specs=[vmem] * len(parts),
        out_specs=vmem,
        compiler_params=pltpu.CompilerParams(vmem_limit_bytes=VMEM_LIMIT),
        name="polynomial",
    )(*parts)


def muon_apply_kernel(rates, placed, spots_ref, *refs):
    count = len(rates)
    parts, momenta, masters = refs[:4], refs[4 : 4 + count], refs[4 + count : 4 + 2 * count]
    outs, factors = refs[4 + 2 * count : 4 + 3 * count], refs[4 + 3 * count]
    for n in range(4):
        factors[n] = parts[n][...]
    zs = factors.shape[1]
    for matrix, block, z, x, core, place_in in placed:
        part = slice(block * ROW_BLOCK, (block + 1) * ROW_BLOCK)
        away = 2 * lax.rem(spots_ref[2] + core, 2) + lax.rem(spots_ref[1] + x, 2)
        factor = unpacked(factors[away, lax.rem(zs + z - spots_ref[0], zs), place_in])
        direction = precise(momenta[matrix][:, part], factor, ((1,), (1,)))
        outs[matrix][:, part] = masters[matrix][:, part] * (1.0 - WEIGHT_SHRINK) - rates[matrix] * direction


def muon_apply(spots, factors, momenta, masters, rates, placed):
    vmem = pl.BlockSpec(memory_space=pltpu.VMEM)
    return pl.pallas_call(
        functools.partial(muon_apply_kernel, rates, placed),
        out_shape=[jax.ShapeDtypeStruct(master.shape, F32) for master in masters],
        in_specs=[pl.BlockSpec(memory_space=pltpu.SMEM)] + [vmem] * (4 + 2 * len(masters)),
        out_specs=[vmem] * len(masters),
        scratch_shapes=[pltpu.VMEM((4,) + factors[0].shape, F32)],
        compiler_params=pltpu.CompilerParams(vmem_limit_bytes=VMEM_LIMIT),
        name="muon_apply",
    )(spots, *factors, *momenta, *masters)


def body(net, tokens, conditioning, heights, widths, upstream, *state):
    masters, momenta = state[0:5], state[5:10]
    biases, bias_first, bias_second = state[10:13]
    w_qkv, w_proj, w_fc1, w_fc2, w_ada = masters
    micro, local, rows, width = tokens.shape
    count = micro * local
    head_dim = width // HEADS
    hidden = w_fc1.shape[1] * net.dp
    seq, dp = net.seq, net.dp
    y = net.y.digit()

    bounds = [0, 6 * width, 7 * width, 8 * width, 9 * width, 9 * width + hidden, 10 * width + hidden]

    n_qkv, n_proj, n_fc1, n_fc2 = [w.shape[1] for w in (w_qkv, w_proj, w_fc1, w_fc2)]
    unit = math.gcd(math.gcd(n_qkv, n_proj), 8)
    unit_qkv, layout_qkv = math.gcd(n_qkv, 8), [(n_qkv, 1)]
    own_tokens = tokens.reshape(count, rows, width)
    wires = net.y.gather(net.wire([w_qkv, w_proj]))

    ada_rows, ada_cols = w_ada.shape
    cond = conditioning.astype(F32).reshape(count, width)
    cond_act, silu_back = jax.vjp(sigmoid_linear, cond)
    cond_low = cond_act.astype(BF).astype(F32)
    cond_parts = jnp.transpose(cond_low.reshape(count, seq, ada_rows), (1, 0, 2)).reshape(seq, -1)
    parcel = jnp.concatenate([jnp.broadcast_to(biases, (seq,) + biases.shape), cond_parts], axis=1)
    parcel = net.to_all(tie(jnp.broadcast_to(parcel[None], (dp,) + parcel.shape), wires[0]))
    cond_all = parcel[:, 0, biases.shape[0] :].reshape(dp * count, ada_rows).astype(BF)
    first = Staged(net.gather_steps(net.joined(wires, unit, width), [(n_qkv, 1), (n_proj, 1)], 0.45))
    sent = first.advance()
    token_pieces = [net.y.gather(tie(own_tokens[0], *sent))]

    low_ada = w_ada.astype(BF)
    partial = jnp.dot(tie(cond_all, *sent), low_ada, preferred_element_type=F32).reshape(dp, 1, count, ada_cols)
    partial = jnp.broadcast_to(partial, (dp, seq, count, ada_cols))
    received = net.to_all(partial)
    first.advance(partial)
    sent = first.advance(received)
    received, parcel = tie(received, *sent), tie(parcel, *sent)
    received = jnp.sum(received, axis=1)
    bias_full = parcel[:, :, : biases.shape[0]].reshape(-1)
    b_ada, b_q, b_v, b_proj, b_fc1, b_fc2 = [bias_full[bounds[i] : bounds[i + 1]] for i in range(6)]
    modulation = jnp.transpose(received, (1, 0, 2)).reshape(count, dp * ada_cols) + b_ada
    shift_one, scale_one, gate_one, shift_two, scale_two, gate_two = jnp.split(
        modulation[:, None, :], 6, axis=-1
    )
    first.advance(modulation)
    norms, attn_all = [], []

    def norm_one(i):
        normed, inverse = layer_norm(jnp.concatenate(token_pieces[i], axis=0).astype(F32))
        norms.append((normed[:rows], inverse[:rows]))
        attn_all.append((normed * (1.0 + scale_one[i]) + shift_one[i]).astype(BF))

    norm_one(0)
    t_qkv, t_proj = first.finish(attn_all[0])[0]
    wires = net.y.gather(tie(net.wire([w_fc1]), token_pieces[0][-1], *sent))
    wires = wires[:1] + [tie(wire, t_qkv) for wire in wires[1:]]
    t_fc1 = lax.all_gather(net.rows(wires), "dp", axis=0, tiled=True)
    for i in range(1, count):
        token_pieces.append(net.y.gather(tie(own_tokens[i], wires[-1])))

    lengths = (heights * widths).reshape(count).astype(jnp.int32)
    offsets = jnp.stack([((y + s) % seq) * rows for s in range(seq)]).astype(jnp.int32)
    queries, keys, values, attended, log_total = [[] for _ in range(5)]
    for i in range(count):
        if i > 0:
            norm_one(i)
        attn = attn_all[i]
        queries.append((dot_t(attn[None, :rows], t_qkv[:width]) + b_q).astype(BF))
        keys.append(dot_t(attn[None], t_qkv[width : 2 * width]).astype(BF))
        values.append((dot_t(attn[None], t_qkv[2 * width :]) + b_v).astype(BF))
        mixed, lse = attend(lengths[i : i + 1], offsets, queries[i], keys[i], values[i], HEADS, 512)
        if i == 0:
            token_pieces[1:] = [each[:1] + [tie(a, mixed) for a in each[1:]] for each in token_pieces[1:]]
            last_piece = token_pieces[-1][-1] if count > 1 else mixed
            wires = net.y.gather(tie(net.wire([w_fc2]), last_piece))
        attended.append(mixed)
        log_total.append(lse)
    wires = wires[:1] + [tie(wire, keys[-1]) for wire in wires[1:]]
    t_fc2 = lax.all_gather(net.rows(wires), "dp", axis=0, tiled=True)
    attended_low = jnp.concatenate(attended, axis=0)

    inputs = own_tokens.astype(F32)
    branch_one = dot_t(attended_low, t_proj) + b_proj
    mixed_one = inputs + gate_one * branch_one
    normed_two, inverse_two = layer_norm(mixed_one)
    ffn_in = (normed_two * (1.0 + scale_two) + shift_two).astype(BF)
    flat = lambda array: array.reshape(-1, array.shape[-1])
    activated_low, slope = hidden_forward(flat(ffn_in), t_fc1, b_fc1)
    activated_low = activated_low.reshape(count, rows, hidden)
    grad_out = upstream.reshape(count, rows, width).astype(F32)
    grad_branch_two = (gate_two * grad_out).astype(BF)
    term_fc2 = outer(grad_branch_two, activated_low)
    sum_fc2 = net.scatter(term_fc2)
    branch_two = dot_t(tie(activated_low, term_fc2), t_fc2) + b_fc2
    grad_branch_two = tie(grad_branch_two, term_fc2)
    result = (mixed_one + gate_two * branch_two).astype(BF)

    grad_gate_two = jnp.sum(branch_two * grad_out, axis=1)
    bias_fc2 = jnp.sum(grad_branch_two.astype(F32), axis=(0, 1))
    grad_pre, bias_fc1 = hidden_backward(flat(grad_branch_two), t_fc2, slope)
    grad_pre = grad_pre.reshape(count, rows, hidden)
    grad_ffn_in = dot(grad_pre, t_fc1)
    grad_shift_two = jnp.sum(grad_ffn_in, axis=1)
    grad_scale_two = jnp.sum(grad_ffn_in * normed_two, axis=1)
    grad_mixed = grad_out + norm_back(normed_two, inverse_two, grad_ffn_in * (1.0 + scale_two))
    grad_gate_one = jnp.sum(branch_one * grad_mixed, axis=1)
    grad_branch_one = (gate_one * grad_mixed).astype(BF)
    bias_proj = jnp.sum(grad_branch_one.astype(F32), axis=(0, 1))
    grad_attended = dot(grad_branch_one, t_proj).astype(BF)
    unit_mid = math.gcd(math.gcd(n_proj, n_fc1), 8)
    (term_mid,) = shard_outer(
        net.spots(),
        [flat(grad_pre), flat(ffn_in), flat(grad_branch_one), flat(attended_low)],
        [([2], 0, width), ([3], 0, width), ([1], 0, width)]
        + [([0], j * width, width) for j in range(hidden // width)],
        [(0, 1, n_proj, 0)] + [(3 + j, 2, n_fc1, n_proj // unit_mid) for j in range(hidden // width)],
        net.z.size, width, unit_mid, (n_proj + n_fc1) // unit_mid, split=False,
    )
    term_mid = tie(term_mid, sum_fc2, grad_attended)
    sum_mid = net.scatter(term_mid.reshape(dp * (n_proj + n_fc1), width))
    grad_attended = tie(grad_attended, term_mid)

    def far_steps(dk, dv):
        part = dot(dk[:, rows:], t_qkv[width : 2 * width]) + dot(dv[:, rows:], t_qkv[2 * width :])
        part = part.astype(BF)[0]
        blank = jnp.zeros((rows, width), BF)
        return Staged(net.y.scatter_steps(lambda s: blank if s == 0 else part[(s - 1) * rows : s * rows]))

    grad_q, grad_k, grad_v, far_parts = [], [], [], []
    turned = [momentum.T for momentum in momenta]
    sent = []
    for i in range(count):
        dq, dk, dv = attend_back(
            lengths[i : i + 1], offsets, queries[i], keys[i], values[i], attended[i],
            grad_attended, i, log_total[i], HEADS, 512, sent,
        )
        sent = []
        grad_q.append(dq)
        grad_k.append(dk)
        grad_v.append(dv)
        if i + 1 < count:
            far_parts.append(far_steps(dk, dv))
            sent = sent + far_parts[-1].advance()
    unit_last = math.gcd(n_qkv, 8)
    (term_last,) = shard_outer(
        net.spots(),
        [flat(each) for each in grad_q + grad_k + grad_v]
        + [attn[:rows] for attn in attn_all]
        + attn_all,
        [([n * count + i for i in range(count)], 0, width) for n in range(5)],
        [(0, 3, n_qkv, 0), (1, 4, n_qkv, 0), (2, 4, n_qkv, 0)],
        net.z.size, width, unit_last, n_qkv // unit_last, sent, split=False,
    )
    sum_last = net.scatter(term_last.reshape(dp * n_qkv, width))
    grad_k[-1] = tie(grad_k[-1], term_last)
    far_parts.append(far_steps(grad_k[-1], grad_v[-1]))
    sent = far_parts[-1].advance()
    halves = Staged(lockstep(*[net.halves_steps(tie(each, *sent)) for each in (sum_fc2, sum_mid)]))
    sent = sent + halves.advance()
    grad_q[0] = tie(grad_q[0], *sent)
    bias_q = sum(jnp.sum(each.astype(F32), axis=(0, 1)) for each in grad_q)
    bias_v = sum(jnp.sum(each.astype(F32), axis=(0, 1)) for each in grad_v)
    own_part = [
        dot(grad_q[i], t_qkv[:width])
        + dot(grad_k[i][:, :rows], t_qkv[width : 2 * width])
        + dot(grad_v[i][:, :rows], t_qkv[2 * width :])
        for i in range(count)
    ]
    grad_shift_one, grad_scale_one, grad_inputs = [], [], []
    for i, (normed, inverse) in enumerate(norms):
        grad_attn_in = own_part[i][0] + far_parts[i].finish()
        grad_shift_one.append(jnp.sum(grad_attn_in, axis=0))
        grad_scale_one.append(jnp.sum(grad_attn_in * normed, axis=0))
        grad_in = grad_mixed[i] + norm_back(normed, inverse, grad_attn_in * (1.0 + scale_one[i]))
        grad_inputs.append(grad_in.astype(BF))
    grad_shift_one, grad_scale_one = jnp.stack(grad_shift_one), jnp.stack(grad_scale_one)
    grad_inputs = jnp.stack(grad_inputs).reshape(tokens.shape)

    matrices = (w_qkv, w_proj, w_fc1, w_fc2, w_ada)
    per = -(-sum(matrix.shape[0] // ROW_BLOCK for matrix in matrices) // dp)
    spread_early = (per, 0)
    early_blocks = (w_fc2.shape[0] + w_fc1.shape[0] + w_proj.shape[0]) // ROW_BLOCK
    spread_last = (per, -(-early_blocks // per))

    grad_mod_local = jnp.concatenate(
        [grad_shift_one, grad_scale_one, grad_gate_one, grad_shift_two, grad_scale_two, grad_gate_two], axis=-1
    )
    bias_ada = jnp.sum(grad_mod_local, axis=0)
    sent = jnp.transpose(grad_mod_local.reshape(count, dp, 1, ada_cols), (1, 2, 0, 3))
    sent = jnp.broadcast_to(sent, (dp, seq, count, ada_cols))
    mod_parts = net.to_all(sent)
    mod_parts = tie(mod_parts, sent)
    mod_cols = jnp.sum(mod_parts, axis=1).astype(BF).reshape(dp * count, ada_cols)
    shard_ada = jnp.einsum("sr,sc->cr", cond_all, mod_cols, preferred_element_type=F32)

    cond_part = jnp.einsum("sc,rc->sr", mod_cols, low_ada, preferred_element_type=F32)
    cond_part = jnp.broadcast_to(cond_part.reshape(dp, 1, -1), (dp, seq, count * ada_rows))
    term_bias = jnp.concatenate([bias_ada, bias_q, bias_v, bias_proj, bias_fc1, bias_fc2])
    parcel = jnp.concatenate([term_bias.reshape(dp, seq, -1), cond_part], axis=-1)
    got_parcel = net.to_all(parcel)

    sums = halves.finish(parcel)
    blank = jnp.zeros((2, net.z.size, per) + PACKED, F32)
    (next_fc2, next_proj, next_fc1), *early = muon_gram(
        net.spots(), [(sums[0], [turned[3]]), (sums[1], [turned[1], turned[2]])], spread_early, (blank, blank)
    )
    got_parcel = tie(got_parcel, early[0])
    halves = Staged(net.halves_steps(tie(sum_last, got_parcel)))
    sent = halves.advance()
    total = halves.finish(shard_ada)
    (next_qkv, next_ada), *grams = muon_gram(
        net.spots(), [(total, [turned[0]]), (shard_ada, [turned[4]])], spread_last, early
    )
    grams = Staged(net.gram_steps(*grams))
    sent = grams.advance()
    parcel = tie(got_parcel, *sent)
    while not grams.done:
        sent = grams.advance(sent[0])
    gathered = Staged(net.muon_gather_steps(grams.result))
    sent = gathered.advance()
    while not gathered.done:
        sent = gathered.advance(sent[0])
    momenta_in = [next_fc2, next_proj, next_fc1, next_qkv, next_ada]
    heights_of = [momentum.shape[1] // ROW_BLOCK for momentum in momenta_in]
    placed = block_spots(heights_of[:3], spread_early)
    placed += [(3 + spot[0],) + spot[1:] for spot in block_spots(heights_of[3:], spread_last)]
    new_fc2, new_proj, new_fc1, new_qkv, new_ada = muon_apply(
        net.spots(), gathered.result, momenta_in, [w.T for w in (w_fc2, w_proj, w_fc1, w_qkv, w_ada)],
        [math.sqrt(width / hidden), 1.0, math.sqrt(hidden / width), math.sqrt(3.0), math.sqrt(6.0)], placed,
    )

    size = biases.shape[0]
    grad_bias = jnp.sum(parcel[..., :size], axis=(0, 1))
    cond_part = jnp.sum(parcel[..., size:], axis=0).reshape(seq, count, ada_rows)
    grad_cond = silu_back(jnp.transpose(cond_part, (1, 0, 2)).reshape(count, width))[0]
    next_first = BETA_FIRST * bias_first + (1.0 - BETA_FIRST) * grad_bias
    next_second = BETA_SECOND * bias_second + (1.0 - BETA_SECOND) * grad_bias * grad_bias
    first_hat = next_first / (1.0 - BETA_FIRST**STEP_COUNT)
    second_hat = next_second / (1.0 - BETA_SECOND**STEP_COUNT)
    new_biases = biases * (1.0 - ADAM_RATE * ADAM_DECAY) - ADAM_RATE * first_hat / (
        jnp.sqrt(second_hat) + ADAM_EPS
    )
    return (
        result.reshape(tokens.shape),
        grad_inputs,
        grad_cond.reshape(conditioning.shape),
        new_qkv.T, new_proj.T, new_fc1.T, new_fc2.T, new_ada.T,
        next_qkv.T, next_proj.T, next_fc1.T, next_fc2.T, next_ada.T,
        new_biases,
        next_first,
        next_second,
    )


def solution(mesh):
    rows = P(None, "dp", "seq", None)
    matrix = P("seq", "dp")
    flat = P(("dp", "seq"))
    in_specs = (rows, P(None, "dp", None), P(None, "dp"), P(None, "dp"), rows) + (matrix,) * 10 + (flat,) * 3
    out_specs = (rows, rows, P(None, "dp", None)) + (matrix,) * 10 + (flat,) * 3
    return jax.shard_map(
        functools.partial(body, Net(mesh)), mesh=mesh, in_specs=in_specs, out_specs=out_specs, check_vma=False
    )
```

```python
import functools
import math

import jax
import jax.numpy as jnp
from jax import lax
from jax.experimental import pallas as pl
from jax.experimental.pallas import tpu as pltpu
from jax.sharding import PartitionSpec as P

HEADS = 16
ROW_BLOCK = 144
NS_STEPS = 5
STEP_COUNT = 10

PRECISE = lax.Precision.HIGHEST
LN_EPS = 1e-06
MASKED = -1e30
NS_A = 3.4445
NS_B = -4.775
NS_C = 2.0315
MUON_DECAY = 0.5
WEIGHT_SHRINK = 0.0001
NORM_EPS = 1e-07
BETA_FIRST = 0.9
BETA_SECOND = 0.999
ADAM_RATE = 0.1
ADAM_DECAY = 0.01
ADAM_EPS = 1e-08
BF = jnp.bfloat16
F32 = jnp.float32
VMEM_LIMIT = 60 * 2**20


class Ring:
    def __init__(self, name, total, stride, size):
        self.name, self.total, self.stride, self.size = name, total, stride, size

    def digit(self):
        return (lax.axis_index(self.name) // self.stride) % self.size

    def send(self, value, shift):
        pairs = []
        for i in range(self.total):
            d = (i // self.stride) % self.size
            pairs.append((i, i + ((d + shift) % self.size - d) * self.stride))
        return lax.ppermute(value, self.name, pairs)

    def gather(self, value, far=1):
        n = self.size
        blocks = [value] + [None] * (n - 1)
        if n == 2:
            blocks[1] = self.send(value, 1)
        elif n > 2:
            low = high = value
            for t in range(1, n // 2):
                low, high = self.send(low, 1), self.send(high, -1)
                blocks[n - t], blocks[t] = low, high
            blocks[n // 2] = self.send(low, 1) if far == 1 else self.send(high, -1)
        return blocks

    def gather_steps(self, value, far=1):
        n = self.size
        blocks = [value] + [None] * (n - 1)
        if n == 2:
            blocks[1] = self.send(value, 1)
            anchor = yield [value]
            blocks[1] = tie(blocks[1], anchor)
            return blocks
        low = high = value
        for t in range(1, n // 2):
            sent = [low, high]
            low, high = self.send(low, 1), self.send(high, -1)
            anchor = yield sent
            low, high = tie(low, anchor), tie(high, anchor)
            blocks[n - t], blocks[t] = low, high
        sent = [low if far == 1 else high]
        last = self.send(sent[0], far)
        anchor = yield sent
        blocks[n // 2] = tie(last, anchor)
        return blocks

    def scatter_steps(self, block_of, far=1):
        n = self.size
        if n == 1:
            return block_of(0).astype(F32)
        if n == 2:
            sent = block_of(1)
            got = self.send(sent, 1)
            anchor = yield [sent]
            return block_of(0).astype(F32) + tie(got, anchor).astype(F32)
        sent = block_of(n // 2)
        got = self.send(sent, far)
        anchor = yield [sent]
        low, high = (tie(got, anchor), None) if far == 1 else (None, tie(got, anchor))
        for t in range(n // 2 - 1, 0, -1):
            up, down = block_of(t), block_of(n - t)
            if low is not None:
                up = (up.astype(F32) + low.astype(F32)).astype(up.dtype)
            if high is not None:
                down = (down.astype(F32) + high.astype(F32)).astype(down.dtype)
            low, high = self.send(up, 1), self.send(down, -1)
            anchor = yield [up, down]
            low, high = tie(low, anchor), tie(high, anchor)
        return block_of(0).astype(F32) + low.astype(F32) + high.astype(F32)


def tie(value, *earlier):
    earlier = [array for array in earlier if array is not None]
    if not earlier:
        return value
    anywhere = pl.BlockSpec(memory_space=pl.ANY)
    return pl.pallas_call(
        lambda *refs: None,
        out_shape=jax.ShapeDtypeStruct(value.shape, value.dtype),
        in_specs=[anywhere] * (1 + len(earlier)),
        out_specs=anywhere,
        input_output_aliases={0: 0},
        name="tie",
    )(value, *earlier)


def lockstep(*steps):
    results = [None] * len(steps)
    alive = dict(enumerate(steps))
    anchor = None
    while alive:
        sent = []
        for n, step in list(alive.items()):
            try:
                sent += step.send(anchor)
            except StopIteration as stop:
                results[n] = stop.value
                del alive[n]
        if alive:
            anchor = yield sent
    return results


class Staged:
    def __init__(self, steps):
        self.steps, self.result, self.started, self.done = steps, None, False, False

    def advance(self, anchor=None):
        if self.done:
            return []
        try:
            sent = self.steps.send(anchor if self.started else None)
            self.started = True
            return sent
        except StopIteration as stop:
            self.result, self.done = stop.value, True
            return []

    def finish(self, anchor=None):
        while not self.done:
            self.advance(anchor)
        return self.result


def place_kernel(zs, ga, parts, count, outs, *refs):
    spots, sources = refs[0], refs[1 : 1 + count]
    outputs, (full, in_sems, out_sems) = refs[1 + count : 1 + count + outs], refs[1 + count + outs :]
    g = full.shape[3]
    half = count // 2
    shards = []
    for sc in range(2):
        for sx in range(2):
            for sz in range(zs):
                where = (lax.rem(spots[0] + sz, zs), lax.rem(spots[1] + sx, 2), lax.rem(spots[2] + sc, 2))
                n = 2 * len(shards)
                line, pair = sources[sc * half + sx].at[sz], sources[sc * half + 2 + sz].at[sx]
                copies = [
                    pltpu.make_async_copy(line, full.at[(*where, pl.ds(0, ga))], in_sems.at[n]),
                    pltpu.make_async_copy(pair, full.at[(*where, pl.ds(ga, g - ga))], in_sems.at[n + 1]),
                ]
                for copy in copies:
                    copy.start()
                shards.append((where, copies))
    exits = []
    for where, copies in shards:
        for copy in copies:
            copy.wait()
        for output, start, size, column, depth in parts:
            target = outputs[output].at[(*where, slice(None), slice(None), pl.ds(column, depth))]
            copy = pltpu.make_async_copy(
                full.at[(*where, pl.ds(start, size))], target, out_sems.at[len(exits)]
            )
            copy.start()
            exits.append(copy)
    for copy in exits:
        copy.wait()


def place(spots, sources, shape, ga, parts, shapes):
    zs = shape[0]
    moved = math.prod(shape) * 2
    return pl.pallas_call(
        functools.partial(place_kernel, zs, ga, parts, len(sources), len(shapes)),
        out_shape=[jax.ShapeDtypeStruct(each, BF) for each in shapes],
        in_specs=[pl.BlockSpec(memory_space=pltpu.SMEM)]
        + [pl.BlockSpec(memory_space=pl.ANY)] * len(sources),
        out_specs=[pl.BlockSpec(memory_space=pl.ANY)] * len(shapes),
        scratch_shapes=[
            pltpu.VMEM(shape, BF),
            pltpu.SemaphoreType.DMA((8 * zs,)),
            pltpu.SemaphoreType.DMA((4 * zs * len(parts),)),
        ],
        compiler_params=pltpu.CompilerParams(vmem_limit_bytes=VMEM_LIMIT),
        cost_estimate=pl.CostEstimate(flops=0, bytes_accessed=2 * moved, transcendentals=0),
        name="place",
    )(spots, *sources)


class Net:
    def __init__(self, mesh):
        dp, seq = mesh.shape["dp"], mesh.shape["seq"]
        self.dp, self.seq = dp, seq
        self.core = Ring("dp", dp, 1, 2)
        self.x = Ring("dp", dp, 2, 2)
        self.z = Ring("dp", dp, 4, dp // 4)
        self.y = Ring("seq", seq, 1, seq)

    def spots(self):
        return jnp.stack([self.z.digit(), self.x.digit(), self.core.digit()]).astype(jnp.int32)


    def wire(self, shards):
        turned = [shard.astype(BF).T for shard in shards]
        return turned[0] if len(turned) == 1 else jnp.concatenate(turned, axis=0)

    def rows(self, wires):
        if self.seq == 2:
            own, other = wires
            return jnp.where(
                self.y.digit() == 0,
                jnp.concatenate([own, other], axis=1),
                jnp.concatenate([other, own], axis=1),
            )
        order = (jnp.arange(self.seq) - self.y.digit()) % self.seq
        full = jnp.take(jnp.stack(wires), order, axis=0)
        return jnp.transpose(full, (1, 0, 2)).reshape(full.shape[1], -1)

    def joined(self, wires, unit, depth):
        full = self.rows(wires)
        return full.reshape(full.shape[0] // unit, unit, depth)

    def scatter(self, term):
        return lax.psum_scatter(term, "dp", scatter_dimension=0, tiled=True)

    def scatter_chips(self, term):
        groups = [list(range(core, self.dp, 2)) for core in range(2)]
        return lax.psum_scatter(term, "dp", scatter_dimension=0, tiled=True, axis_index_groups=groups)

    def halves_steps(self, term):
        y = self.y.digit()
        blocks = term.reshape(term.shape[0], self.seq, -1)
        return (
            yield from self.y.scatter_steps(
                lambda s: lax.dynamic_index_in_dim(blocks, (y + s) % self.seq, 1, keepdims=False)
            )
        )

    def gather_steps(self, units, layout, part):
        g, unit, depth = units.shape
        zs = self.z.size
        ga = max(1, int(part * g))
        first, second = units[:ga], units[ga:]

        def line_steps():
            blocks = yield from self.z.gather_steps(first, 1)
            line = jnp.stack(blocks)
            return (yield from self.x.gather_steps(line))

        def pair_steps():
            blocks = yield from self.x.gather_steps(second)
            return (yield from self.z.gather_steps(jnp.stack(blocks), -1))

        lines, pairs = yield from lockstep(line_steps(), pair_steps())
        pieces = lines + pairs
        others = [self.core.send(piece, 1) for piece in pieces]
        anchor = yield pieces
        sources = pieces + [tie(other, anchor) for other in others]
        parts, shapes, start = [], [], 0
        for n, (rows, blocks) in enumerate(layout):
            size = rows // unit
            shapes.append((zs, 2, 2, size, unit, blocks * depth))
            for j in range(blocks):
                parts.append((n, start, size, j * depth, depth))
                start += size
        full = place(self.spots(), sources, (zs, 2, 2, g, unit, depth), ga, parts, shapes)
        return [f.reshape(-1, f.shape[-1]) for f in full], lines[1:] + pairs[1:]


    def gram_steps(self, own, other):
        got = self.core.send(other, 1)
        anchor = yield [other]
        half = own + tie(got, anchor)
        sent = half[1]
        got = self.x.send(sent, 1)
        anchor = yield [sent]
        kept = half[0] + tie(got, anchor)
        sent = [kept[shift] for shift in range(1, self.z.size)]
        got = [self.z.send(each, shift) for shift, each in enumerate(sent, 1)]
        anchor = yield sent
        return [kept[0]] + [tie(each, anchor) for each in got]

    def muon_gather_steps(self, parts):
        factor = polynomial(parts)
        got = [self.z.send(factor, -shift) for shift in range(1, self.z.size)]
        anchor = yield [factor]
        line = jnp.stack([factor] + [tie(each, anchor) for each in got])
        got = self.x.send(line, 1)
        anchor = yield [line]
        pair = [line, tie(got, anchor)]
        others = [self.core.send(each, 1) for each in pair]
        anchor = yield pair
        return pair + [tie(each, anchor) for each in others]


    def to_all(self, value):
        flat = value.reshape((self.dp * self.seq,) + value.shape[2:])
        return lax.all_to_all(flat, ("dp", "seq"), 0, 0, tiled=True).reshape(value.shape)

    def to_dp(self, value):
        return lax.all_to_all(value, "dp", 0, 0, tiled=True)


def layer_norm(values):
    centered = values - jnp.mean(values, axis=-1, keepdims=True)
    inverse = lax.rsqrt(jnp.mean(centered * centered, axis=-1, keepdims=True) + LN_EPS)
    return (centered * inverse, inverse)


def norm_back(normed, inverse, grad):
    mean_grad = jnp.mean(grad, axis=-1, keepdims=True)
    mean_cross = jnp.mean(grad * normed, axis=-1, keepdims=True)
    return inverse * (grad - mean_grad - normed * mean_cross)


def sigmoid_linear(values):
    return values * jax.nn.sigmoid(values)


def dot_t(left, right):
    return jnp.einsum("srk,nk->srn", left, right, preferred_element_type=F32)


def dot(left, right):
    return jnp.einsum("srn,nk->srk", left, right, preferred_element_type=F32)


GELU_SCALE = math.sqrt(2.0 / math.pi)
GELU_CUBE = 0.044715


def row_parts(rows):
    step = rows // 4 if rows % 64 == 0 else rows
    return [slice(start, start + step) for start in range(0, rows, step)]


def hidden_kernel(x_ref, w_ref, b_ref, act_ref, slope_ref):
    for part in row_parts(x_ref.shape[0]):
        value = nt(x_ref[part], w_ref[...]) + b_ref[...]
        square = value * value
        bend = jnp.tanh(value * (GELU_SCALE + (GELU_SCALE * GELU_CUBE) * square))
        half = 0.5 + 0.5 * bend
        act_ref[part] = (value * half).astype(BF)
        steep = (0.5 * value) * (GELU_SCALE + (3.0 * GELU_SCALE * GELU_CUBE) * square)
        slope_ref[part] = (half + steep * (1.0 - bend * bend)).astype(BF)


def hidden_forward(x, w, bias):
    rows, depth = x.shape
    n = w.shape[0]
    tile = math.gcd(n, 512)
    out = pl.BlockSpec((rows, tile), lambda i: (0, i))
    return pl.pallas_call(
        hidden_kernel,
        grid=(n // tile,),
        in_specs=[
            pl.BlockSpec((rows, depth), lambda i: (0, 0)),
            pl.BlockSpec((tile, depth), lambda i: (i, 0)),
            pl.BlockSpec((1, tile), lambda i: (0, i)),
        ],
        out_specs=[out, out],
        out_shape=[jax.ShapeDtypeStruct((rows, n), BF)] * 2,
        compiler_params=pltpu.CompilerParams(vmem_limit_bytes=VMEM_LIMIT),
        cost_estimate=pl.CostEstimate(
            flops=2 * rows * n * depth, bytes_accessed=2 * (rows + n) * depth + 4 * rows * n, transcendentals=rows * n
        ),
        name="hidden_forward",
    )(x, w, bias.reshape(1, n))


def hidden_back_kernel(g_ref, w_ref, slope_ref, out_ref, bias_ref):
    total = 0.0
    for part in row_parts(g_ref.shape[0]):
        grad = (nn(g_ref[part], w_ref[...]) * slope_ref[part].astype(F32)).astype(BF)
        out_ref[part] = grad
        total = total + jnp.sum(grad.astype(F32), axis=0, keepdims=True)
    bias_ref[...] = total


def hidden_backward(grad, w, slope):
    rows, depth = grad.shape
    n = w.shape[1]
    tile = math.gcd(n, 512)
    out = pl.BlockSpec((rows, tile), lambda i: (0, i))
    result, bias = pl.pallas_call(
        hidden_back_kernel,
        grid=(n // tile,),
        in_specs=[
            pl.BlockSpec((rows, depth), lambda i: (0, 0)),
            pl.BlockSpec((depth, tile), lambda i: (0, i)),
            out,
        ],
        out_specs=[out, pl.BlockSpec((1, tile), lambda i: (0, i))],
        out_shape=[jax.ShapeDtypeStruct((rows, n), BF), jax.ShapeDtypeStruct((1, n), F32)],
        compiler_params=pltpu.CompilerParams(vmem_limit_bytes=VMEM_LIMIT),
        cost_estimate=pl.CostEstimate(
            flops=2 * rows * n * depth, bytes_accessed=2 * (rows + n) * depth + 4 * rows * n, transcendentals=0
        ),
        name="hidden_backward",
    )(grad, w, slope)
    return result, bias[0]


def outer(left, right):
    return jnp.einsum("srn,srk->nk", left, right, preferred_element_type=F32).astype(BF)


def shard_outer_kernel(plan, counts, tile, split, spots_ref, *refs):
    outs = 2 if split else 1
    inputs, where = refs[: counts[0]], refs[counts[1] : counts[1] + outs]
    buffers = refs[counts[1] + outs : counts[1] + outs + len(plan["loads"])]
    acc, in_sems, out_sems = refs[counts[1] + outs + len(plan["loads"]) :]
    loads = []
    for n, (sources, start, size) in enumerate(plan["loads"]):
        row, copies = 0, []
        for m, source in enumerate(sources):
            rows = inputs[source].shape[0]
            window = inputs[source].at[:, pl.ds(start, size)]
            copies.append(pltpu.make_async_copy(window, buffers[n].at[pl.ds(row, rows)], in_sems.at[n, m]))
            copies[-1].start()
            row += rows
        loads.append(copies)
    ready = set()
    shipped = []
    unit = acc.shape[1]
    for left, right, base, ships in plan["parts"]:
        for n in (left, right):
            if n not in ready:
                for copy in loads[n]:
                    copy.wait()
                ready.add(n)
        width = buffers[left].shape[1]
        step = tile if width % tile == 0 else width

        @pl.loop(0, width // step)
        def _(t):
            block = buffers[left][:, pl.ds(pl.multiple_of(t * step, step), step)]
            product = lax.dot_general(
                block, buffers[right][...], (((0,), (0,)), ((), ())), preferred_element_type=F32
            )
            product = product.reshape(step // unit, unit, product.shape[1]).astype(BF)
            acc[pl.ds(base + t * (step // unit), step // unit)] = product

        for core, z, x, row, target, size in ships:
            spot = (z, x) if split else (z, x, core)
            places = [ref.at[(*spot, pl.ds(target, size))] for ref in where]
            copies = [
                pltpu.make_async_copy(acc.at[pl.ds(row, size)], each, out_sems.at[len(shipped)]) for each in places
            ]
            shipped.append((core, copies))
            on_own_core(split, spots_ref, core, [copy.start for copy in copies])
    for core, copies in shipped:
        on_own_core(split, spots_ref, core, [copy.wait for copy in copies])


def on_own_core(split, spots_ref, core, actions):
    if not split:
        actions[0]()
        return

    @pl.when(spots_ref[2] == core)
    def _():
        actions[0]()

    @pl.when(spots_ref[2] != core)
    def _():
        actions[1]()


def shard_outer(spots, inputs, loads, parts, zs, depth, unit, shard_units, deps=(), tile=384, split=True):
    dp = zs * 4
    plan_parts, base, row, placed = [], 0, 0, {}
    begun = {}
    for left, right, rows, first in parts:
        if first not in begun:
            begun[first] = (base, 0)
        start, shipped = begun[first]
        width = loads[left][2]
        size = rows // unit
        end = base + width // unit
        ships = []
        while shipped < dp and start + (shipped + 1) * size <= end:
            core, x, z = shipped % 2, shipped // 2 % 2, shipped // 4
            ships.append((core, z, x, start + shipped * size, first, size))
            shipped += 1
        begun[first] = (start, shipped)
        plan_parts.append((left, right, base, ships))
        base = end
    total = sum(len(part[3]) for part in plan_parts)
    shape = (zs, 2, shard_units, unit, depth) if split else (zs, 2, 2, shard_units, unit, depth)
    outs = [jax.ShapeDtypeStruct(shape, BF)] * (2 if split else 1)
    anywhere = pl.BlockSpec(memory_space=pl.ANY)
    heights = [sum(inputs[source].shape[0] for source in sources) for sources, _, _ in loads]
    flops = sum(2 * heights[p[0]] * loads[p[0]][2] * loads[p[1]][2] for p in parts)
    return pl.pallas_call(
        functools.partial(
            shard_outer_kernel, {"loads": loads, "parts": plan_parts}, (len(inputs), len(inputs) + len(deps)), tile, split
        ),
        out_shape=outs,
        in_specs=[pl.BlockSpec(memory_space=pltpu.SMEM)] + [anywhere] * (len(inputs) + len(deps)),
        out_specs=[anywhere] * len(outs),
        scratch_shapes=[pltpu.VMEM((height, load[2]), BF) for height, load in zip(heights, loads)]
        + [
            pltpu.VMEM((base, unit, depth), BF),
            pltpu.SemaphoreType.DMA((len(loads), max(len(load[0]) for load in loads))),
            pltpu.SemaphoreType.DMA((total,)),
        ],
        compiler_params=pltpu.CompilerParams(vmem_limit_bytes=VMEM_LIMIT),
        cost_estimate=pl.CostEstimate(flops=flops, bytes_accessed=2 * base * unit * depth, transcendentals=0),
        name="shard_outer",
    )(spots, *inputs, *deps)


LANES = 128
LOG2E = math.log2(math.e)


def padded(block, column=None):
    rows, depth = block.shape
    if column is None:
        return jnp.concatenate([block, jnp.zeros((rows, LANES - depth), block.dtype)], axis=1)
    rest = jnp.zeros((rows, LANES - depth - 1), block.dtype)
    return jnp.concatenate([block, column.astype(block.dtype), rest], axis=1)


def mask_column(lengths_ref, offsets_ref, sample, total, rows):
    place = lax.broadcasted_iota(jnp.int32, (total, 1), 0)
    position = place
    for s in range(total // rows):
        position = jnp.where(place // rows == s, place - s * rows + offsets_ref[s], position)
    return jnp.where(position < lengths_ref[sample], 0.0, MASKED)


def nt(left, right):
    return lax.dot_general(left, right, (((1,), (1,)), ((), ())), preferred_element_type=F32)


def nn(left, right):
    return jnp.dot(left, right, preferred_element_type=F32)


def without(kernel, start, count, *fixed):
    def run(*refs):
        kernel(*fixed, *refs[:start], *refs[start + count :])

    return run


def attend_kernel(heads, chunk, lengths_ref, offsets_ref, q_ref, k_ref, v_ref, o_ref, lse_ref, q_s, k_s, vt_s, o_s):
    rows, width = q_ref.shape[1:]
    total = k_ref.shape[1]
    depth = width // heads
    factor = depth**-0.5 * LOG2E
    mask = mask_column(lengths_ref, offsets_ref, pl.program_id(0), total, rows)
    q_blank = padded(jnp.zeros((rows, depth), BF), jnp.ones((rows, 1), F32))
    k_blank = padded(jnp.zeros((total, depth), BF), mask)
    turned = jnp.transpose(v_ref[0].astype(F32))
    for h in range(heads):
        span = slice(h * depth, (h + 1) * depth)
        q_s[h] = q_blank
        k_s[h] = k_blank
        q_s[h, :, :depth] = q_ref[0, :, span]
        k_s[h, :, :depth] = k_ref[0, :, span]
        vt_s[h] = turned[span].astype(BF)

    def one_head(h, carry):
        peak = jnp.full((1, rows), MASKED, F32)
        sums = jnp.zeros((1, rows), F32)
        mixed = jnp.zeros((depth, rows), F32)
        for c in range(total // chunk):
            part = slice(c * chunk, (c + 1) * chunk)
            scores = nt(k_s[h, part], q_s[h])
            higher = jnp.maximum(peak, jnp.max(scores, axis=0, keepdims=True))
            weights = jnp.exp2((scores - higher) * factor)
            if c == 0:
                sums = jnp.sum(weights, axis=0, keepdims=True)
                mixed = nn(vt_s[h, :, part], weights.astype(BF))
            else:
                shrink = jnp.exp2((peak - higher) * factor)
                sums = sums * shrink + jnp.sum(weights, axis=0, keepdims=True)
                mixed = mixed * shrink + nn(vt_s[h, :, part], weights.astype(BF))
            peak = higher
        o_s[h] = jnp.transpose(mixed / sums)
        lse_ref[0, h] = peak * factor + jnp.log2(sums)
        return carry

    lax.fori_loop(0, heads, one_head, 0, unroll=4)
    for h in range(heads):
        o_ref[0, :, h * depth : (h + 1) * depth] = o_s[h].astype(BF)


def attend(lengths, offsets, queries, keys_values, heads, tile, deps=()):
    count, rows, width = queries.shape
    total = keys_values.shape[1]
    depth = width // heads
    tile = min(tile, total)
    pick = lambda i, *_: (i, 0, 0)
    return pl.pallas_call(
        without(attend_kernel, 5, len(deps), heads, tile),
        grid_spec=pltpu.PrefetchScalarGridSpec(
            num_scalar_prefetch=2,
            grid=(count,),
            in_specs=[
                pl.BlockSpec((1, rows, width), pick),
                pl.BlockSpec((1, total, width), pick),
                pl.BlockSpec((1, total, width), lambda i, *_: (i, 0, 1)),
            ]
            + [pl.BlockSpec(memory_space=pl.ANY)] * len(deps),
            out_specs=[
                pl.BlockSpec((1, rows, width), pick),
                pl.BlockSpec((1, heads, 1, rows), lambda i, *_: (i, 0, 0, 0)),
            ],
            scratch_shapes=[
                pltpu.VMEM((heads, rows, LANES), BF),
                pltpu.VMEM((heads, total, LANES), BF),
                pltpu.VMEM((heads, depth, total), BF),
                pltpu.VMEM((heads, rows, depth), F32),
            ],
        ),
        out_shape=[
            jax.ShapeDtypeStruct((count, rows, width), BF),
            jax.ShapeDtypeStruct((count, heads, 1, rows), F32),
        ],
        compiler_params=pltpu.CompilerParams(vmem_limit_bytes=VMEM_LIMIT),
        cost_estimate=pl.CostEstimate(
            flops=4 * count * heads * rows * total * LANES,
            bytes_accessed=2 * count * width * (2 * rows + 2 * total),
            transcendentals=count * heads * rows * total,
        ),
        name="attend",
    )(lengths, offsets, queries, keys_values, keys_values, *deps)


def attend_back_kernel(
    heads, chunk, lengths_ref, offsets_ref, q_ref, k_ref, v_ref, o_ref, g_ref, lse_ref,
    dq_ref, dk_ref, dv_ref, q_s, k_s, kt_s, v_s, g_s, delta_s, dq_s, dk_s, dv_s
):
    rows, width = q_ref.shape[1:]
    total = k_ref.shape[1]
    depth = width // heads
    scale = depth**-0.5
    factor = scale * LOG2E
    mask = mask_column(lengths_ref, offsets_ref, pl.program_id(0), total, rows)
    ones = jnp.ones((rows, 1), F32)
    cross = jnp.transpose(g_ref[0].astype(F32) * o_ref[0].astype(F32))
    for h in range(heads):
        span = slice(h * depth, (h + 1) * depth)
        delta_s[h] = jnp.sum(cross[span], axis=0, keepdims=True)
        q_s[h] = padded(q_ref[0, :, span], ones)
        k_s[h] = padded(k_ref[0, :, span], mask)
        kt_s[h] = jnp.transpose(k_ref[0, :, span])
        g_s[h] = padded(g_ref[0, :, span])
        v_s[h] = padded(v_ref[0, :, span])

    def one_head(h, carry):
        dq = jnp.zeros((depth, rows), F32)
        for c in range(total // chunk):
            part = slice(c * chunk, (c + 1) * chunk)
            probs = jnp.exp2(nt(k_s[h, part], q_s[h]) * factor - lse_ref[0, h])
            slopes = (probs * (nt(v_s[h, part], g_s[h]) - delta_s[h])).astype(BF)
            dv_s[h, part] = nn(probs.astype(BF), g_s[h]).astype(BF)
            dk_s[h, part] = (nn(slopes, q_s[h]) * scale).astype(BF)
            dq = dq + nn(kt_s[h, :, part], slopes)
        dq_s[h] = jnp.transpose(dq * scale)
        return carry

    lax.fori_loop(0, heads, one_head, 0, unroll=4)
    for h in range(heads):
        span = slice(h * depth, (h + 1) * depth)
        dq_ref[0, :, span] = dq_s[h].astype(BF)
        dk_ref[0, :, span] = dk_s[h][:, :depth]
        dv_ref[0, :, span] = dv_s[h][:, :depth]


def attend_back(lengths, offsets, queries, keys_values, mixed, grads, sample, lse, heads, tile, deps=()):
    count, rows, width = queries.shape
    total = keys_values.shape[1]
    depth = width // heads
    tile = min(tile, total)
    pick = lambda i, *_: (i, 0, 0)
    near = pl.BlockSpec((1, rows, width), pick)
    picked = pl.BlockSpec((1, rows, width), lambda i, *_: (sample + i, 0, 0))
    far = pl.BlockSpec((1, total, width), pick)
    far_values = pl.BlockSpec((1, total, width), lambda i, *_: (i, 0, 1))
    return pl.pallas_call(
        without(attend_back_kernel, 8, len(deps), heads, tile),
        grid_spec=pltpu.PrefetchScalarGridSpec(
            num_scalar_prefetch=2,
            grid=(count,),
            in_specs=[near, far, far_values, near, picked, pl.BlockSpec((1, heads, 1, rows), lambda i, *_: (i, 0, 0, 0))]
            + [pl.BlockSpec(memory_space=pl.ANY)] * len(deps),
            out_specs=[near, far, far],
            scratch_shapes=[
                pltpu.VMEM((heads, rows, LANES), BF),
                pltpu.VMEM((heads, total, LANES), BF),
                pltpu.VMEM((heads, depth, total), BF),
                pltpu.VMEM((heads, total, LANES), BF),
                pltpu.VMEM((heads, rows, LANES), BF),
                pltpu.VMEM((heads, 1, rows), F32),
                pltpu.VMEM((heads, rows, depth), F32),
                pltpu.VMEM((heads, total, LANES), BF),
                pltpu.VMEM((heads, total, LANES), BF),
            ],
        ),
        out_shape=[
            jax.ShapeDtypeStruct((count, rows, width), BF),
            jax.ShapeDtypeStruct((count, total, width), BF),
            jax.ShapeDtypeStruct((count, total, width), BF),
        ],
        compiler_params=pltpu.CompilerParams(vmem_limit_bytes=VMEM_LIMIT),
        cost_estimate=pl.CostEstimate(
            flops=10 * count * heads * rows * total * LANES,
            bytes_accessed=2 * count * width * (4 * rows + 4 * total),
            transcendentals=count * heads * rows * total,
        ),
        name="attend_back",
    )(lengths, offsets, queries, keys_values, keys_values, mixed, grads, lse, *deps)


def block_spots(counts, spread):
    per, first = spread
    spots = []
    for matrix, count in enumerate(counts):
        for block in range(count):
            device, place_in = divmod(len(spots), per)
            device += first
            spots.append((matrix, block, device // 4, device // 2 % 2, device % 2, place_in))
    return spots


EXTRA = ROW_BLOCK - 128
PACKED = (ROW_BLOCK + EXTRA, 128)


def packed(block):
    corner = block[128:, 128:]
    corner = jnp.concatenate([corner, jnp.zeros((EXTRA, 128 - EXTRA), block.dtype)], axis=1)
    return jnp.concatenate([block[:, :128], corner], axis=0)


def unpacked(block):
    side = jnp.transpose(block[128:ROW_BLOCK])
    right = jnp.concatenate([side, block[ROW_BLOCK:, :EXTRA]], axis=0)
    return jnp.concatenate([block[:ROW_BLOCK], right], axis=1)


def precise(left, right, dims):
    return lax.dot_general(left, right, (dims, ((), ())), precision=PRECISE, preferred_element_type=F32)


def muon_gram_kernel(groups, spread, spots_ref, base_own, base_other, *refs):
    count = sum(groups)
    sums, momenta = refs[: len(groups)], refs[len(groups) : len(groups) + count]
    outs = refs[len(groups) + count : len(groups) + 2 * count]
    own_ref, other_ref, grams, sems = refs[len(groups) + 2 * count :]
    n = 0
    for matrices, sum_ref in zip(groups, sums):
        start = 0
        for _ in range(matrices):
            size = momenta[n].shape[0]
            outs[n][...] = MUON_DECAY * momenta[n][...] + sum_ref[start : start + size]
            start += size
            n += 1
    zs = own_ref.shape[1]
    spots = block_spots([out.shape[1] // ROW_BLOCK for out in outs], spread)
    copies = []
    for n, (matrix, block, z, x, core, place_in) in enumerate(spots):
        turned = outs[matrix][:, block * ROW_BLOCK : (block + 1) * ROW_BLOCK]
        grams[n] = packed(precise(turned, turned, ((0,), (0,))))
        away = (lax.rem(spots_ref[1] + x, 2), lax.rem(zs + z - spots_ref[0], zs), place_in)
        pair = [pltpu.make_async_copy(grams.at[n], ref.at[away], sems.at[n]) for ref in (own_ref, other_ref)]
        on_own_core(True, spots_ref, core, [copy.start for copy in pair])
        copies.append((core, pair))
    for core, pair in copies:
        on_own_core(True, spots_ref, core, [copy.wait for copy in pair])


def muon_gram(spots, groups, spread, base):
    momenta = [momentum for _, each in groups for momentum in each]
    terms = jax.ShapeDtypeStruct(base[0].shape, F32)
    vmem, anywhere = pl.BlockSpec(memory_space=pltpu.VMEM), pl.BlockSpec(memory_space=pl.ANY)
    blocks = len(block_spots([momentum.shape[1] // ROW_BLOCK for momentum in momenta], spread))
    outs = pl.pallas_call(
        functools.partial(muon_gram_kernel, [len(each) for _, each in groups], spread),
        out_shape=[jax.ShapeDtypeStruct(momentum.shape, F32) for momentum in momenta] + [terms, terms],
        in_specs=[pl.BlockSpec(memory_space=pltpu.SMEM), anywhere, anywhere]
        + [vmem] * (len(groups) + len(momenta)),
        out_specs=[vmem] * len(momenta) + [anywhere, anywhere],
        input_output_aliases={1: len(momenta), 2: len(momenta) + 1},
        scratch_shapes=[
            pltpu.VMEM((blocks,) + PACKED, F32),
            pltpu.SemaphoreType.DMA((blocks,)),
        ],
        compiler_params=pltpu.CompilerParams(vmem_limit_bytes=VMEM_LIMIT),
        name="muon_gram",
    )(spots, *base, *[group[0] for group in groups], *momenta)
    return outs[:-2], outs[-2], outs[-1]


def polynomial_kernel(count, *refs):
    out = refs[count]
    shape = (ROW_BLOCK, ROW_BLOCK)
    eye = (lax.broadcasted_iota(jnp.int32, shape, 0) == lax.broadcasted_iota(jnp.int32, shape, 1)).astype(F32)
    mul = lambda left, right: precise(left, right, ((1,), (0,)))
    blocks = range(out.shape[0])
    currents, scales, totals = [], [], []
    for n in blocks:
        gram = refs[0][n]
        for ref in refs[1:count]:
            gram = gram + ref[n]
        gram = unpacked(gram)
        square = jnp.sum(jnp.sum(gram * eye, axis=1, keepdims=True), axis=0, keepdims=True)
        scale = 1.0 / (jnp.sqrt(square) + NORM_EPS)
        scales.append(scale)
        currents.append(gram * (scale * scale))
    for step in range(NS_STEPS):
        factors = [NS_A * eye + NS_B * a + NS_C * mul(a, a) for a in currents]
        totals = factors if step == 0 else [mul(f, t) for f, t in zip(factors, totals)]
        if step + 1 < NS_STEPS:
            currents = [mul(f, a) for f, a in zip(factors, currents)]
            currents = [mul(a, f) for f, a in zip(factors, currents)]
    for n in blocks:
        out[n] = packed(totals[n] * scales[n])


def polynomial(parts):
    vmem = pl.BlockSpec(memory_space=pltpu.VMEM)
    return pl.pallas_call(
        functools.partial(polynomial_kernel, len(parts)),
        out_shape=jax.ShapeDtypeStruct(parts[0].shape, F32),
        in_specs=[vmem] * len(parts),
        out_specs=vmem,
        compiler_params=pltpu.CompilerParams(vmem_limit_bytes=VMEM_LIMIT),
        name="polynomial",
    )(*parts)


def muon_apply_kernel(rates, placed, spots_ref, *refs):
    count = len(rates)
    parts, momenta, masters = refs[:4], refs[4 : 4 + count], refs[4 + count : 4 + 2 * count]
    outs, factors = refs[4 + 2 * count : 4 + 3 * count], refs[4 + 3 * count]
    for n in range(4):
        factors[n] = parts[n][...]
    zs = factors.shape[1]
    for matrix, block, z, x, core, place_in in placed:
        part = slice(block * ROW_BLOCK, (block + 1) * ROW_BLOCK)
        away = 2 * lax.rem(spots_ref[2] + core, 2) + lax.rem(spots_ref[1] + x, 2)
        factor = unpacked(factors[away, lax.rem(zs + z - spots_ref[0], zs), place_in])
        direction = precise(momenta[matrix][:, part], factor, ((1,), (1,)))
        outs[matrix][:, part] = masters[matrix][:, part] * (1.0 - WEIGHT_SHRINK) - rates[matrix] * direction


def muon_apply(spots, factors, momenta, masters, rates, placed):
    vmem = pl.BlockSpec(memory_space=pltpu.VMEM)
    return pl.pallas_call(
        functools.partial(muon_apply_kernel, rates, placed),
        out_shape=[jax.ShapeDtypeStruct(master.shape, F32) for master in masters],
        in_specs=[pl.BlockSpec(memory_space=pltpu.SMEM)] + [vmem] * (4 + 2 * len(masters)),
        out_specs=[vmem] * len(masters),
        scratch_shapes=[pltpu.VMEM((4,) + factors[0].shape, F32)],
        compiler_params=pltpu.CompilerParams(vmem_limit_bytes=VMEM_LIMIT),
        name="muon_apply",
    )(spots, *factors, *momenta, *masters)


def body(net, tokens, conditioning, heights, widths, upstream, *state):
    masters, momenta = state[0:5], state[5:10]
    biases, bias_first, bias_second = state[10:13]
    w_qkv, w_proj, w_fc1, w_fc2, w_ada = masters
    micro, local, rows, width = tokens.shape
    count = micro * local
    head_dim = width // HEADS
    hidden = w_fc1.shape[1] * net.dp
    seq, dp = net.seq, net.dp
    y = net.y.digit()

    bounds = [0, 6 * width, 7 * width, 8 * width, 9 * width, 9 * width + hidden, 10 * width + hidden]

    n_qkv, n_proj, n_fc1, n_fc2 = [w.shape[1] for w in (w_qkv, w_proj, w_fc1, w_fc2)]
    unit = math.gcd(math.gcd(n_qkv, n_proj), 8)
    unit_qkv, layout_qkv = math.gcd(n_qkv, 8), [(n_qkv, 1)]
    own_tokens = tokens.reshape(count, rows, width)
    wires = net.y.gather(net.wire([w_qkv, w_proj]))

    ada_rows, ada_cols = w_ada.shape
    cond = conditioning.astype(F32).reshape(count, width)
    cond_act, silu_back = jax.vjp(sigmoid_linear, cond)
    cond_low = cond_act.astype(BF).astype(F32)
    cond_parts = jnp.transpose(cond_low.reshape(count, seq, ada_rows), (1, 0, 2)).reshape(seq, -1)
    parcel = jnp.concatenate([jnp.broadcast_to(biases, (seq,) + biases.shape), cond_parts], axis=1)
    parcel = net.to_all(tie(jnp.broadcast_to(parcel[None], (dp,) + parcel.shape), wires[0]))
    cond_all = parcel[:, 0, biases.shape[0] :].reshape(dp * count, ada_rows).astype(BF)
    first = Staged(net.gather_steps(net.joined(wires, unit, width), [(n_qkv, 1), (n_proj, 1)], 0.45))
    sent = first.advance()
    token_pieces = [net.y.gather(tie(own_tokens[0], *sent))]

    low_ada = w_ada.astype(BF)
    partial = jnp.dot(tie(cond_all, *sent), low_ada, preferred_element_type=F32).reshape(dp, 1, count, ada_cols)
    partial = jnp.broadcast_to(partial, (dp, seq, count, ada_cols))
    received = net.to_all(partial)
    first.advance(partial)
    sent = first.advance(received)
    received, parcel = tie(received, *sent), tie(parcel, *sent)
    received = jnp.sum(received, axis=1)
    bias_full = parcel[:, :, : biases.shape[0]].reshape(-1)
    b_ada, b_q, b_v, b_proj, b_fc1, b_fc2 = [bias_full[bounds[i] : bounds[i + 1]] for i in range(6)]
    modulation = jnp.transpose(received, (1, 0, 2)).reshape(count, dp * ada_cols) + b_ada
    shift_one, scale_one, gate_one, shift_two, scale_two, gate_two = jnp.split(
        modulation[:, None, :], 6, axis=-1
    )
    pieces = first.advance(modulation)
    token_pieces[0] = token_pieces[0][:1] + [tie(each, pieces[-1]) for each in token_pieces[0][1:]]
    norms, attn_all = [], []

    def norm_one(i):
        normed, inverse = layer_norm(jnp.concatenate(token_pieces[i], axis=0).astype(F32))
        norms.append((normed[:rows], inverse[:rows]))
        attn_all.append((normed * (1.0 + scale_one[i]) + shift_one[i]).astype(BF))

    norm_one(0)
    t_qkv, t_proj = first.finish(attn_all[0])[0]
    wires = net.y.gather(tie(net.wire([w_fc1]), token_pieces[0][-1], *sent))
    wires = wires[:1] + [tie(wire, t_qkv) for wire in wires[1:]]
    t_fc1 = lax.all_gather(net.rows(wires), "dp", axis=0, tiled=True)
    for i in range(1, count):
        token_pieces.append(net.y.gather(tie(own_tokens[i], wires[-1])))

    lengths = (heights * widths).reshape(count).astype(jnp.int32)
    offsets = jnp.stack([((y + s) % seq) * rows for s in range(seq)]).astype(jnp.int32)
    queries, keys_values, attended, log_total = [[] for _ in range(4)]
    b_kv = jnp.concatenate([jnp.zeros_like(b_v), b_v])
    for i in range(count):
        if i > 0:
            norm_one(i)
        attn = attn_all[i]
        queries.append((dot_t(attn[None, :rows], t_qkv[:width]) + b_q).astype(BF))
        keys_values.append((dot_t(attn[None], t_qkv[width:]) + b_kv).astype(BF))
        mixed, lse = attend(lengths[i : i + 1], offsets, queries[i], keys_values[i], HEADS, 512)
        if i == 0:
            token_pieces[1:] = [each[:1] + [tie(a, mixed) for a in each[1:]] for each in token_pieces[1:]]
            last_piece = token_pieces[-1][-1] if count > 1 else mixed
            wires = net.y.gather(tie(net.wire([w_fc2]), last_piece))
        attended.append(mixed)
        log_total.append(lse)
    wires = wires[:1] + [tie(wire, keys_values[-1]) for wire in wires[1:]]
    t_fc2 = lax.all_gather(net.rows(wires), "dp", axis=0, tiled=True)
    attended_low = jnp.concatenate(attended, axis=0)

    inputs = own_tokens.astype(F32)
    branch_one = dot_t(attended_low, t_proj) + b_proj
    mixed_one = inputs + gate_one * branch_one
    normed_two, inverse_two = layer_norm(mixed_one)
    ffn_in = (normed_two * (1.0 + scale_two) + shift_two).astype(BF)
    flat = lambda array: array.reshape(-1, array.shape[-1])
    activated_low, slope = hidden_forward(flat(ffn_in), t_fc1, b_fc1)
    activated_low = activated_low.reshape(count, rows, hidden)
    grad_out = upstream.reshape(count, rows, width).astype(F32)
    grad_branch_two = (gate_two * grad_out).astype(BF)
    term_fc2 = outer(grad_branch_two, activated_low)
    sum_fc2 = net.scatter(term_fc2)
    branch_two = dot_t(tie(activated_low, term_fc2), t_fc2) + b_fc2
    grad_branch_two = tie(grad_branch_two, term_fc2)
    result = (mixed_one + gate_two * branch_two).astype(BF)

    grad_gate_two = jnp.sum(branch_two * grad_out, axis=1)
    bias_fc2 = jnp.sum(grad_branch_two.astype(F32), axis=(0, 1))
    grad_pre, bias_fc1 = hidden_backward(flat(grad_branch_two), t_fc2, slope)
    grad_pre = grad_pre.reshape(count, rows, hidden)
    grad_ffn_in = dot(grad_pre, t_fc1)
    grad_shift_two = jnp.sum(grad_ffn_in, axis=1)
    grad_scale_two = jnp.sum(grad_ffn_in * normed_two, axis=1)
    grad_mixed = grad_out + norm_back(normed_two, inverse_two, grad_ffn_in * (1.0 + scale_two))
    grad_gate_one = jnp.sum(branch_one * grad_mixed, axis=1)
    grad_branch_one = (gate_one * grad_mixed).astype(BF)
    bias_proj = jnp.sum(grad_branch_one.astype(F32), axis=(0, 1))
    grad_attended = dot(grad_branch_one, t_proj).astype(BF)
    unit_mid = math.gcd(math.gcd(n_proj, n_fc1), 8)
    own, other = shard_outer(
        net.spots(),
        [flat(grad_pre), flat(ffn_in), flat(grad_branch_one), flat(attended_low)],
        [([2], 0, width), ([3], 0, width), ([1], 0, width)]
        + [([0], j * width, width) for j in range(hidden // width)],
        [(0, 1, n_proj, 0)] + [(3 + j, 2, n_fc1, n_proj // unit_mid) for j in range(hidden // width)],
        net.z.size, width, unit_mid, (n_proj + n_fc1) // unit_mid,
    )
    term_mid = (own.astype(F32) + net.core.send(other, 1).astype(F32)).astype(BF)
    term_mid = tie(term_mid, sum_fc2, grad_attended)
    sum_mid = net.scatter_chips(term_mid.reshape(dp // 2 * (n_proj + n_fc1), width))
    grad_attended = tie(grad_attended, term_mid)

    def far_steps(dk, dv):
        part = dot(dk[:, rows:], t_qkv[width : 2 * width]) + dot(dv[:, rows:], t_qkv[2 * width :])
        part = part.astype(BF)[0]
        blank = jnp.zeros((rows, width), BF)
        return Staged(net.y.scatter_steps(lambda s: blank if s == 0 else part[(s - 1) * rows : s * rows]))

    grad_q, grad_k, grad_v, far_parts = [], [], [], []
    turned = [momentum.T for momentum in momenta]
    sent = []
    for i in range(count):
        dq, dk, dv = attend_back(
            lengths[i : i + 1], offsets, queries[i], keys_values[i], attended[i],
            grad_attended, i, log_total[i], HEADS, 512, sent,
        )
        sent = []
        grad_q.append(dq)
        grad_k.append(dk)
        grad_v.append(dv)
        if i + 1 < count:
            far_parts.append(far_steps(dk, dv))
            sent = sent + far_parts[-1].advance()
    unit_last = math.gcd(n_qkv, 8)
    (term_last,) = shard_outer(
        net.spots(),
        [flat(each) for each in grad_q + grad_k + grad_v]
        + [attn[:rows] for attn in attn_all]
        + attn_all,
        [([n * count + i for i in range(count)], 0, width) for n in range(5)],
        [(0, 3, n_qkv, 0), (1, 4, n_qkv, 0), (2, 4, n_qkv, 0)],
        net.z.size, width, unit_last, n_qkv // unit_last, sent, split=False,
    )
    sum_last = net.scatter(term_last.reshape(dp * n_qkv, width))
    grad_k[-1] = tie(grad_k[-1], term_last)
    far_parts.append(far_steps(grad_k[-1], grad_v[-1]))
    sent = far_parts[-1].advance()
    halves = Staged(lockstep(*[net.halves_steps(tie(each, *sent)) for each in (sum_fc2, sum_mid)]))
    sent = sent + halves.advance()
    grad_q[0] = tie(grad_q[0], *sent)
    bias_q = sum(jnp.sum(each.astype(F32), axis=(0, 1)) for each in grad_q)
    bias_v = sum(jnp.sum(each.astype(F32), axis=(0, 1)) for each in grad_v)
    own_part = [
        dot(grad_q[i], t_qkv[:width])
        + dot(grad_k[i][:, :rows], t_qkv[width : 2 * width])
        + dot(grad_v[i][:, :rows], t_qkv[2 * width :])
        for i in range(count)
    ]
    grad_shift_one, grad_scale_one, grad_inputs = [], [], []
    for i, (normed, inverse) in enumerate(norms):
        grad_attn_in = own_part[i][0] + far_parts[i].finish()
        grad_shift_one.append(jnp.sum(grad_attn_in, axis=0))
        grad_scale_one.append(jnp.sum(grad_attn_in * normed, axis=0))
        grad_in = grad_mixed[i] + norm_back(normed, inverse, grad_attn_in * (1.0 + scale_one[i]))
        grad_inputs.append(grad_in.astype(BF))
    grad_shift_one, grad_scale_one = jnp.stack(grad_shift_one), jnp.stack(grad_scale_one)
    grad_inputs = jnp.stack(grad_inputs).reshape(tokens.shape)

    matrices = (w_qkv, w_proj, w_fc1, w_fc2, w_ada)
    per = -(-sum(matrix.shape[0] // ROW_BLOCK for matrix in matrices) // dp)
    spread_early = (per, 0)
    early_blocks = (w_fc2.shape[0] + w_fc1.shape[0] + w_proj.shape[0]) // ROW_BLOCK
    spread_last = (per, -(-early_blocks // per))

    grad_mod_local = jnp.concatenate(
        [grad_shift_one, grad_scale_one, grad_gate_one, grad_shift_two, grad_scale_two, grad_gate_two], axis=-1
    )
    bias_ada = jnp.sum(grad_mod_local, axis=0)
    sent = jnp.transpose(grad_mod_local.reshape(count, dp, 1, ada_cols), (1, 2, 0, 3))
    sent = jnp.broadcast_to(sent, (dp, seq, count, ada_cols))
    mod_parts = net.to_all(sent)
    mod_parts = tie(mod_parts, sent)
    mod_cols = jnp.sum(mod_parts, axis=1).astype(BF).reshape(dp * count, ada_cols)
    shard_ada = jnp.einsum("sr,sc->cr", cond_all, mod_cols, preferred_element_type=F32)

    cond_part = jnp.einsum("sc,rc->sr", mod_cols, low_ada, preferred_element_type=F32)
    cond_part = jnp.broadcast_to(cond_part.reshape(dp, 1, -1), (dp, seq, count * ada_rows))
    term_bias = jnp.concatenate([bias_ada, bias_q, bias_v, bias_proj, bias_fc1, bias_fc2])
    parcel = jnp.concatenate([term_bias.reshape(dp, seq, -1), cond_part], axis=-1)
    got_parcel = net.to_all(parcel)

    sums = halves.finish(parcel)
    blank = jnp.zeros((2, net.z.size, per) + PACKED, F32)
    (next_fc2, next_proj, next_fc1), *early = muon_gram(
        net.spots(), [(sums[0], [turned[3]]), (sums[1], [turned[1], turned[2]])], spread_early, (blank, blank)
    )
    got_parcel = tie(got_parcel, early[0])
    halves = Staged(net.halves_steps(tie(sum_last, got_parcel)))
    sent = halves.advance()
    total = halves.finish(shard_ada)
    (next_qkv, next_ada), *grams = muon_gram(
        net.spots(), [(total, [turned[0]]), (shard_ada, [turned[4]])], spread_last, early
    )
    grams = Staged(net.gram_steps(*grams))
    sent = grams.advance()
    parcel = tie(got_parcel, *sent)
    while not grams.done:
        sent = grams.advance(sent[0])
    gathered = Staged(net.muon_gather_steps(grams.result))
    sent = gathered.advance()
    while not gathered.done:
        sent = gathered.advance(sent[0])
    momenta_in = [next_fc2, next_proj, next_fc1, next_qkv, next_ada]
    heights_of = [momentum.shape[1] // ROW_BLOCK for momentum in momenta_in]
    placed = block_spots(heights_of[:3], spread_early)
    placed += [(3 + spot[0],) + spot[1:] for spot in block_spots(heights_of[3:], spread_last)]
    new_fc2, new_proj, new_fc1, new_qkv, new_ada = muon_apply(
        net.spots(), gathered.result, momenta_in, [w.T for w in (w_fc2, w_proj, w_fc1, w_qkv, w_ada)],
        [math.sqrt(width / hidden), 1.0, math.sqrt(hidden / width), math.sqrt(3.0), math.sqrt(6.0)], placed,
    )

    size = biases.shape[0]
    grad_bias = jnp.sum(parcel[..., :size], axis=(0, 1))
    cond_part = jnp.sum(parcel[..., size:], axis=0).reshape(seq, count, ada_rows)
    grad_cond = silu_back(jnp.transpose(cond_part, (1, 0, 2)).reshape(count, width))[0]
    next_first = BETA_FIRST * bias_first + (1.0 - BETA_FIRST) * grad_bias
    next_second = BETA_SECOND * bias_second + (1.0 - BETA_SECOND) * grad_bias * grad_bias
    first_hat = next_first / (1.0 - BETA_FIRST**STEP_COUNT)
    second_hat = next_second / (1.0 - BETA_SECOND**STEP_COUNT)
    new_biases = biases * (1.0 - ADAM_RATE * ADAM_DECAY) - ADAM_RATE * first_hat / (
        jnp.sqrt(second_hat) + ADAM_EPS
    )
    return (
        result.reshape(tokens.shape),
        grad_inputs,
        grad_cond.reshape(conditioning.shape),
        new_qkv.T, new_proj.T, new_fc1.T, new_fc2.T, new_ada.T,
        next_qkv.T, next_proj.T, next_fc1.T, next_fc2.T, next_ada.T,
        new_biases,
        next_first,
        next_second,
    )


def solution(mesh):
    rows = P(None, "dp", "seq", None)
    matrix = P("seq", "dp")
    flat = P(("dp", "seq"))
    in_specs = (rows, P(None, "dp", None), P(None, "dp"), P(None, "dp"), rows) + (matrix,) * 10 + (flat,) * 3
    out_specs = (rows, rows, P(None, "dp", None)) + (matrix,) * 10 + (flat,) * 3
    return jax.shard_map(
        functools.partial(body, Net(mesh)), mesh=mesh, in_specs=in_specs, out_specs=out_specs, check_vma=False
    )
```

```python
import functools
import math

import jax
import jax.numpy as jnp
from jax import lax
from jax.experimental import pallas as pl
from jax.experimental.pallas import tpu as pltpu
from jax.sharding import PartitionSpec as P

HEADS = 16
ROW_BLOCK = 144
NS_STEPS = 5
STEP_COUNT = 10

PRECISE = lax.Precision.HIGHEST
LN_EPS = 1e-06
MASKED = -1e30
NS_A = 3.4445
NS_B = -4.775
NS_C = 2.0315
MUON_DECAY = 0.5
WEIGHT_SHRINK = 0.0001
NORM_EPS = 1e-07
BETA_FIRST = 0.9
BETA_SECOND = 0.999
ADAM_RATE = 0.1
ADAM_DECAY = 0.01
ADAM_EPS = 1e-08
BF = jnp.bfloat16
F32 = jnp.float32
VMEM_LIMIT = 60 * 2**20


class Ring:
    def __init__(self, name, total, stride, size):
        self.name, self.total, self.stride, self.size = name, total, stride, size

    def digit(self):
        return (lax.axis_index(self.name) // self.stride) % self.size

    def send(self, value, shift):
        pairs = []
        for i in range(self.total):
            d = (i // self.stride) % self.size
            pairs.append((i, i + ((d + shift) % self.size - d) * self.stride))
        return lax.ppermute(value, self.name, pairs)

    def gather(self, value, far=1):
        n = self.size
        blocks = [value] + [None] * (n - 1)
        if n == 2:
            blocks[1] = self.send(value, 1)
        elif n > 2:
            low = high = value
            for t in range(1, n // 2):
                low, high = self.send(low, 1), self.send(high, -1)
                blocks[n - t], blocks[t] = low, high
            blocks[n // 2] = self.send(low, 1) if far == 1 else self.send(high, -1)
        return blocks

    def gather_steps(self, value, far=1):
        n = self.size
        blocks = [value] + [None] * (n - 1)
        if n == 2:
            blocks[1] = self.send(value, 1)
            anchor = yield [value]
            blocks[1] = tie(blocks[1], anchor)
            return blocks
        low = high = value
        for t in range(1, n // 2):
            sent = [low, high]
            low, high = self.send(low, 1), self.send(high, -1)
            anchor = yield sent
            low, high = tie(low, anchor), tie(high, anchor)
            blocks[n - t], blocks[t] = low, high
        sent = [low if far == 1 else high]
        last = self.send(sent[0], far)
        anchor = yield sent
        blocks[n // 2] = tie(last, anchor)
        return blocks

    def scatter_steps(self, block_of, far=1):
        n = self.size
        if n == 1:
            return block_of(0).astype(F32)
        if n == 2:
            sent = block_of(1)
            got = self.send(sent, 1)
            anchor = yield [sent]
            return block_of(0).astype(F32) + tie(got, anchor).astype(F32)
        sent = block_of(n // 2)
        got = self.send(sent, far)
        anchor = yield [sent]
        low, high = (tie(got, anchor), None) if far == 1 else (None, tie(got, anchor))
        for t in range(n // 2 - 1, 0, -1):
            up, down = block_of(t), block_of(n - t)
            if low is not None:
                up = (up.astype(F32) + low.astype(F32)).astype(up.dtype)
            if high is not None:
                down = (down.astype(F32) + high.astype(F32)).astype(down.dtype)
            low, high = self.send(up, 1), self.send(down, -1)
            anchor = yield [up, down]
            low, high = tie(low, anchor), tie(high, anchor)
        return block_of(0).astype(F32) + low.astype(F32) + high.astype(F32)


def tie(value, *earlier):
    earlier = [array for array in earlier if array is not None]
    if not earlier:
        return value
    anywhere = pl.BlockSpec(memory_space=pl.ANY)
    return pl.pallas_call(
        lambda *refs: None,
        out_shape=jax.ShapeDtypeStruct(value.shape, value.dtype),
        in_specs=[anywhere] * (1 + len(earlier)),
        out_specs=anywhere,
        input_output_aliases={0: 0},
        name="tie",
    )(value, *earlier)


def lockstep(*steps):
    results = [None] * len(steps)
    alive = dict(enumerate(steps))
    anchor = None
    while alive:
        sent = []
        for n, step in list(alive.items()):
            try:
                sent += step.send(anchor)
            except StopIteration as stop:
                results[n] = stop.value
                del alive[n]
        if alive:
            anchor = yield sent
    return results


class Staged:
    def __init__(self, steps):
        self.steps, self.result, self.started, self.done = steps, None, False, False

    def advance(self, anchor=None):
        if self.done:
            return []
        try:
            sent = self.steps.send(anchor if self.started else None)
            self.started = True
            return sent
        except StopIteration as stop:
            self.result, self.done = stop.value, True
            return []

    def finish(self, anchor=None):
        while not self.done:
            self.advance(anchor)
        return self.result


def place_kernel(zs, ga, parts, count, outs, *refs):
    spots, sources = refs[0], refs[1 : 1 + count]
    outputs, (full, in_sems, out_sems) = refs[1 + count : 1 + count + outs], refs[1 + count + outs :]
    g = full.shape[3]
    half = count // 2
    shards = []
    for sc in range(2):
        for sx in range(2):
            for sz in range(zs):
                where = (lax.rem(spots[0] + sz, zs), lax.rem(spots[1] + sx, 2), lax.rem(spots[2] + sc, 2))
                n = 2 * len(shards)
                line, pair = sources[sc * half + sx].at[sz], sources[sc * half + 2 + sz].at[sx]
                copies = [
                    pltpu.make_async_copy(line, full.at[(*where, pl.ds(0, ga))], in_sems.at[n]),
                    pltpu.make_async_copy(pair, full.at[(*where, pl.ds(ga, g - ga))], in_sems.at[n + 1]),
                ]
                for copy in copies:
                    copy.start()
                shards.append((where, copies))
    exits = []
    for where, copies in shards:
        for copy in copies:
            copy.wait()
        for output, start, size, column, depth in parts:
            target = outputs[output].at[(*where, slice(None), slice(None), pl.ds(column, depth))]
            copy = pltpu.make_async_copy(
                full.at[(*where, pl.ds(start, size))], target, out_sems.at[len(exits)]
            )
            copy.start()
            exits.append(copy)
    for copy in exits:
        copy.wait()


def place(spots, sources, shape, ga, parts, shapes):
    zs = shape[0]
    moved = math.prod(shape) * 2
    return pl.pallas_call(
        functools.partial(place_kernel, zs, ga, parts, len(sources), len(shapes)),
        out_shape=[jax.ShapeDtypeStruct(each, BF) for each in shapes],
        in_specs=[pl.BlockSpec(memory_space=pltpu.SMEM)]
        + [pl.BlockSpec(memory_space=pl.ANY)] * len(sources),
        out_specs=[pl.BlockSpec(memory_space=pl.ANY)] * len(shapes),
        scratch_shapes=[
            pltpu.VMEM(shape, BF),
            pltpu.SemaphoreType.DMA((8 * zs,)),
            pltpu.SemaphoreType.DMA((4 * zs * len(parts),)),
        ],
        compiler_params=pltpu.CompilerParams(vmem_limit_bytes=VMEM_LIMIT),
        cost_estimate=pl.CostEstimate(flops=0, bytes_accessed=2 * moved, transcendentals=0),
        name="place",
    )(spots, *sources)


class Net:
    def __init__(self, mesh):
        dp, seq = mesh.shape["dp"], mesh.shape["seq"]
        self.dp, self.seq = dp, seq
        self.core = Ring("dp", dp, 1, 2)
        self.x = Ring("dp", dp, 2, 2)
        self.z = Ring("dp", dp, 4, dp // 4)
        self.y = Ring("seq", seq, 1, seq)

    def spots(self):
        return jnp.stack([self.z.digit(), self.x.digit(), self.core.digit()]).astype(jnp.int32)


    def wire(self, shards):
        turned = [shard.astype(BF).T for shard in shards]
        return turned[0] if len(turned) == 1 else jnp.concatenate(turned, axis=0)

    def rows(self, wires):
        if self.seq == 2:
            own, other = wires
            return jnp.where(
                self.y.digit() == 0,
                jnp.concatenate([own, other], axis=1),
                jnp.concatenate([other, own], axis=1),
            )
        order = (jnp.arange(self.seq) - self.y.digit()) % self.seq
        full = jnp.take(jnp.stack(wires), order, axis=0)
        return jnp.transpose(full, (1, 0, 2)).reshape(full.shape[1], -1)

    def joined(self, wires, unit, depth):
        full = self.rows(wires)
        return full.reshape(full.shape[0] // unit, unit, depth)

    def scatter(self, term):
        return lax.psum_scatter(term, "dp", scatter_dimension=0, tiled=True)

    def scatter_chips(self, term):
        groups = [list(range(core, self.dp, 2)) for core in range(2)]
        return lax.psum_scatter(term, "dp", scatter_dimension=0, tiled=True, axis_index_groups=groups)

    def halves_steps(self, term):
        y = self.y.digit()
        blocks = term.reshape(term.shape[0], self.seq, -1)
        return (
            yield from self.y.scatter_steps(
                lambda s: lax.dynamic_index_in_dim(blocks, (y + s) % self.seq, 1, keepdims=False)
            )
        )

    def gather_steps(self, units, layout, part):
        g, unit, depth = units.shape
        zs = self.z.size
        ga = max(1, int(part * g))
        first, second = units[:ga], units[ga:]

        def line_steps():
            blocks = yield from self.z.gather_steps(first, 1)
            line = jnp.stack(blocks)
            return (yield from self.x.gather_steps(line))

        def pair_steps():
            blocks = yield from self.x.gather_steps(second)
            return (yield from self.z.gather_steps(jnp.stack(blocks), -1))

        lines, pairs = yield from lockstep(line_steps(), pair_steps())
        pieces = lines + pairs
        others = [self.core.send(piece, 1) for piece in pieces]
        anchor = yield pieces
        sources = pieces + [tie(other, anchor) for other in others]
        parts, shapes, start = [], [], 0
        for n, (rows, blocks) in enumerate(layout):
            size = rows // unit
            shapes.append((zs, 2, 2, size, unit, blocks * depth))
            for j in range(blocks):
                parts.append((n, start, size, j * depth, depth))
                start += size
        full = place(self.spots(), sources, (zs, 2, 2, g, unit, depth), ga, parts, shapes)
        return [f.reshape(-1, f.shape[-1]) for f in full], lines[1:] + pairs[1:]


    def gram_steps(self, own, other):
        got = self.core.send(other, 1)
        anchor = yield [other]
        half = own + tie(got, anchor)
        sent = half[1]
        got = self.x.send(sent, 1)
        anchor = yield [sent]
        kept = half[0] + tie(got, anchor)
        sent = [kept[shift] for shift in range(1, self.z.size)]
        got = [self.z.send(each, shift) for shift, each in enumerate(sent, 1)]
        anchor = yield sent
        return [kept[0]] + [tie(each, anchor) for each in got]

    def muon_gather_steps(self, parts):
        factor = polynomial(parts)
        got = [self.z.send(factor, -shift) for shift in range(1, self.z.size)]
        anchor = yield [factor]
        line = jnp.stack([factor] + [tie(each, anchor) for each in got])
        got = self.x.send(line, 1)
        anchor = yield [line]
        pair = [line, tie(got, anchor)]
        others = [self.core.send(each, 1) for each in pair]
        anchor = yield pair
        return pair + [tie(each, anchor) for each in others]


    def to_all(self, value):
        flat = value.reshape((self.dp * self.seq,) + value.shape[2:])
        return lax.all_to_all(flat, ("dp", "seq"), 0, 0, tiled=True).reshape(value.shape)

    def to_dp(self, value):
        return lax.all_to_all(value, "dp", 0, 0, tiled=True)


def layer_norm(values):
    centered = values - jnp.mean(values, axis=-1, keepdims=True)
    inverse = lax.rsqrt(jnp.mean(centered * centered, axis=-1, keepdims=True) + LN_EPS)
    return (centered * inverse, inverse)


def norm_back(normed, inverse, grad):
    mean_grad = jnp.mean(grad, axis=-1, keepdims=True)
    mean_cross = jnp.mean(grad * normed, axis=-1, keepdims=True)
    return inverse * (grad - mean_grad - normed * mean_cross)


def sigmoid_linear(values):
    return values * jax.nn.sigmoid(values)


def dot_t(left, right):
    return jnp.einsum("srk,nk->srn", left, right, preferred_element_type=F32)


def dot(left, right):
    return jnp.einsum("srn,nk->srk", left, right, preferred_element_type=F32)


GELU_SCALE = math.sqrt(2.0 / math.pi)
GELU_CUBE = 0.044715


def row_parts(rows):
    step = rows // 4 if rows % 64 == 0 else rows
    return [slice(start, start + step) for start in range(0, rows, step)]


def hidden_kernel(x_ref, w_ref, b_ref, act_ref, slope_ref):
    for part in row_parts(x_ref.shape[0]):
        value = nt(x_ref[part], w_ref[...]) + b_ref[...]
        square = value * value
        bend = jnp.tanh(value * (GELU_SCALE + (GELU_SCALE * GELU_CUBE) * square))
        half = 0.5 + 0.5 * bend
        act_ref[part] = (value * half).astype(BF)
        steep = (0.5 * value) * (GELU_SCALE + (3.0 * GELU_SCALE * GELU_CUBE) * square)
        slope_ref[part] = (half + steep * (1.0 - bend * bend)).astype(BF)


def hidden_forward(x, w, bias):
    rows, depth = x.shape
    n = w.shape[0]
    tile = math.gcd(n, 512)
    out = pl.BlockSpec((rows, tile), lambda i: (0, i))
    return pl.pallas_call(
        hidden_kernel,
        grid=(n // tile,),
        in_specs=[
            pl.BlockSpec((rows, depth), lambda i: (0, 0)),
            pl.BlockSpec((tile, depth), lambda i: (i, 0)),
            pl.BlockSpec((1, tile), lambda i: (0, i)),
        ],
        out_specs=[out, out],
        out_shape=[jax.ShapeDtypeStruct((rows, n), BF)] * 2,
        compiler_params=pltpu.CompilerParams(vmem_limit_bytes=VMEM_LIMIT),
        cost_estimate=pl.CostEstimate(
            flops=2 * rows * n * depth, bytes_accessed=2 * (rows + n) * depth + 4 * rows * n, transcendentals=rows * n
        ),
        name="hidden_forward",
    )(x, w, bias.reshape(1, n))


def hidden_back_kernel(g_ref, w_ref, slope_ref, out_ref, bias_ref):
    total = 0.0
    for part in row_parts(g_ref.shape[0]):
        grad = (nn(g_ref[part], w_ref[...]) * slope_ref[part].astype(F32)).astype(BF)
        out_ref[part] = grad
        total = total + jnp.sum(grad.astype(F32), axis=0, keepdims=True)
    bias_ref[...] = total


def hidden_backward(grad, w, slope):
    rows, depth = grad.shape
    n = w.shape[1]
    tile = math.gcd(n, 512)
    out = pl.BlockSpec((rows, tile), lambda i: (0, i))
    result, bias = pl.pallas_call(
        hidden_back_kernel,
        grid=(n // tile,),
        in_specs=[
            pl.BlockSpec((rows, depth), lambda i: (0, 0)),
            pl.BlockSpec((depth, tile), lambda i: (0, i)),
            out,
        ],
        out_specs=[out, pl.BlockSpec((1, tile), lambda i: (0, i))],
        out_shape=[jax.ShapeDtypeStruct((rows, n), BF), jax.ShapeDtypeStruct((1, n), F32)],
        compiler_params=pltpu.CompilerParams(vmem_limit_bytes=VMEM_LIMIT),
        cost_estimate=pl.CostEstimate(
            flops=2 * rows * n * depth, bytes_accessed=2 * (rows + n) * depth + 4 * rows * n, transcendentals=0
        ),
        name="hidden_backward",
    )(grad, w, slope)
    return result, bias[0]


def outer(left, right):
    return jnp.einsum("srn,srk->nk", left, right, preferred_element_type=F32).astype(BF)


def shard_outer_kernel(plan, counts, tile, split, spots_ref, *refs):
    outs = 2 if split else 1
    inputs, where = refs[: counts[0]], refs[counts[1] : counts[1] + outs]
    buffers = refs[counts[1] + outs : counts[1] + outs + len(plan["loads"])]
    acc, in_sems, out_sems = refs[counts[1] + outs + len(plan["loads"]) :]
    loads = []
    for n, (sources, start, size) in enumerate(plan["loads"]):
        row, copies = 0, []
        for m, source in enumerate(sources):
            rows = inputs[source].shape[0]
            window = inputs[source].at[:, pl.ds(start, size)]
            copies.append(pltpu.make_async_copy(window, buffers[n].at[pl.ds(row, rows)], in_sems.at[n, m]))
            copies[-1].start()
            row += rows
        loads.append(copies)
    ready = set()
    shipped = []
    unit = acc.shape[1]
    for left, right, base, ships in plan["parts"]:
        for n in (left, right):
            if n not in ready:
                for copy in loads[n]:
                    copy.wait()
                ready.add(n)
        width = buffers[left].shape[1]
        step = tile if width % tile == 0 else width

        @pl.loop(0, width // step)
        def _(t):
            block = buffers[left][:, pl.ds(pl.multiple_of(t * step, step), step)]
            product = lax.dot_general(
                block, buffers[right][...], (((0,), (0,)), ((), ())), preferred_element_type=F32
            )
            product = product.reshape(step // unit, unit, product.shape[1]).astype(BF)
            acc[pl.ds(base + t * (step // unit), step // unit)] = product

        for core, z, x, row, target, size in ships:
            spot = (z, x) if split else (z, x, core)
            places = [ref.at[(*spot, pl.ds(target, size))] for ref in where]
            copies = [
                pltpu.make_async_copy(acc.at[pl.ds(row, size)], each, out_sems.at[len(shipped)]) for each in places
            ]
            shipped.append((core, copies))
            on_own_core(split, spots_ref, core, [copy.start for copy in copies])
    for core, copies in shipped:
        on_own_core(split, spots_ref, core, [copy.wait for copy in copies])


def on_own_core(split, spots_ref, core, actions):
    if not split:
        actions[0]()
        return

    @pl.when(spots_ref[2] == core)
    def _():
        actions[0]()

    @pl.when(spots_ref[2] != core)
    def _():
        actions[1]()


def shard_outer(spots, inputs, loads, parts, zs, depth, unit, shard_units, deps=(), tile=384, split=True):
    dp = zs * 4
    plan_parts, base, row, placed = [], 0, 0, {}
    begun = {}
    for left, right, rows, first in parts:
        if first not in begun:
            begun[first] = (base, 0)
        start, shipped = begun[first]
        width = loads[left][2]
        size = rows // unit
        end = base + width // unit
        ships = []
        while shipped < dp and start + (shipped + 1) * size <= end:
            core, x, z = shipped % 2, shipped // 2 % 2, shipped // 4
            ships.append((core, z, x, start + shipped * size, first, size))
            shipped += 1
        begun[first] = (start, shipped)
        plan_parts.append((left, right, base, ships))
        base = end
    total = sum(len(part[3]) for part in plan_parts)
    shape = (zs, 2, shard_units, unit, depth) if split else (zs, 2, 2, shard_units, unit, depth)
    outs = [jax.ShapeDtypeStruct(shape, BF)] * (2 if split else 1)
    anywhere = pl.BlockSpec(memory_space=pl.ANY)
    heights = [sum(inputs[source].shape[0] for source in sources) for sources, _, _ in loads]
    flops = sum(2 * heights[p[0]] * loads[p[0]][2] * loads[p[1]][2] for p in parts)
    return pl.pallas_call(
        functools.partial(
            shard_outer_kernel, {"loads": loads, "parts": plan_parts}, (len(inputs), len(inputs) + len(deps)), tile, split
        ),
        out_shape=outs,
        in_specs=[pl.BlockSpec(memory_space=pltpu.SMEM)] + [anywhere] * (len(inputs) + len(deps)),
        out_specs=[anywhere] * len(outs),
        scratch_shapes=[pltpu.VMEM((height, load[2]), BF) for height, load in zip(heights, loads)]
        + [
            pltpu.VMEM((base, unit, depth), BF),
            pltpu.SemaphoreType.DMA((len(loads), max(len(load[0]) for load in loads))),
            pltpu.SemaphoreType.DMA((total,)),
        ],
        compiler_params=pltpu.CompilerParams(vmem_limit_bytes=VMEM_LIMIT),
        cost_estimate=pl.CostEstimate(flops=flops, bytes_accessed=2 * base * unit * depth, transcendentals=0),
        name="shard_outer",
    )(spots, *inputs, *deps)


LANES = 128
LOG2E = math.log2(math.e)


def padded(block, column=None):
    rows, depth = block.shape
    if column is None:
        return jnp.concatenate([block, jnp.zeros((rows, LANES - depth), block.dtype)], axis=1)
    rest = jnp.zeros((rows, LANES - depth - 1), block.dtype)
    return jnp.concatenate([block, column.astype(block.dtype), rest], axis=1)


def mask_column(lengths_ref, offsets_ref, sample, total, rows):
    place = lax.broadcasted_iota(jnp.int32, (total, 1), 0)
    position = place
    for s in range(total // rows):
        position = jnp.where(place // rows == s, place - s * rows + offsets_ref[s], position)
    return jnp.where(position < lengths_ref[sample], 0.0, MASKED)


def nt(left, right):
    return lax.dot_general(left, right, (((1,), (1,)), ((), ())), preferred_element_type=F32)


def nn(left, right):
    return jnp.dot(left, right, preferred_element_type=F32)


def without(kernel, start, count, *fixed):
    def run(*refs):
        kernel(*fixed, *refs[:start], *refs[start + count :])

    return run


def attend_kernel(heads, chunk, lengths_ref, offsets_ref, q_ref, k_ref, v_ref, o_ref, lse_ref, q_s, k_s, vt_s, o_s):
    rows, width = q_ref.shape[1:]
    total = k_ref.shape[1]
    depth = width // heads
    factor = depth**-0.5 * LOG2E
    mask = mask_column(lengths_ref, offsets_ref, pl.program_id(0), total, rows)
    q_blank = padded(jnp.zeros((rows, depth), BF), jnp.ones((rows, 1), F32))
    k_blank = padded(jnp.zeros((total, depth), BF), mask)
    turned = jnp.transpose(v_ref[0].astype(F32))
    for h in range(heads):
        span = slice(h * depth, (h + 1) * depth)
        q_s[h] = q_blank
        k_s[h] = k_blank
        q_s[h, :, :depth] = q_ref[0, :, span]
        k_s[h, :, :depth] = k_ref[0, :, span]
        vt_s[h] = turned[span].astype(BF)

    def one_head(h, carry):
        peak = jnp.full((1, rows), MASKED, F32)
        sums = jnp.zeros((1, rows), F32)
        mixed = jnp.zeros((depth, rows), F32)
        for c in range(total // chunk):
            part = slice(c * chunk, (c + 1) * chunk)
            scores = nt(k_s[h, part], q_s[h])
            higher = jnp.maximum(peak, jnp.max(scores, axis=0, keepdims=True))
            weights = jnp.exp2((scores - higher) * factor)
            if c == 0:
                sums = jnp.sum(weights, axis=0, keepdims=True)
                mixed = nn(vt_s[h, :, part], weights.astype(BF))
            else:
                shrink = jnp.exp2((peak - higher) * factor)
                sums = sums * shrink + jnp.sum(weights, axis=0, keepdims=True)
                mixed = mixed * shrink + nn(vt_s[h, :, part], weights.astype(BF))
            peak = higher
        o_s[h] = jnp.transpose(mixed / sums)
        lse_ref[0, h] = peak * factor + jnp.log2(sums)
        return carry

    lax.fori_loop(0, heads, one_head, 0, unroll=4)
    for h in range(heads):
        o_ref[0, :, h * depth : (h + 1) * depth] = o_s[h].astype(BF)


def attend(lengths, offsets, queries, keys_values, heads, tile, deps=()):
    count, rows, width = queries.shape
    total = keys_values.shape[1]
    depth = width // heads
    tile = min(tile, total)
    pick = lambda i, *_: (i, 0, 0)
    return pl.pallas_call(
        without(attend_kernel, 5, len(deps), heads, tile),
        grid_spec=pltpu.PrefetchScalarGridSpec(
            num_scalar_prefetch=2,
            grid=(count,),
            in_specs=[
                pl.BlockSpec((1, rows, width), pick),
                pl.BlockSpec((1, total, width), pick),
                pl.BlockSpec((1, total, width), lambda i, *_: (i, 0, 1)),
            ]
            + [pl.BlockSpec(memory_space=pl.ANY)] * len(deps),
            out_specs=[
                pl.BlockSpec((1, rows, width), pick),
                pl.BlockSpec((1, heads, 1, rows), lambda i, *_: (i, 0, 0, 0)),
            ],
            scratch_shapes=[
                pltpu.VMEM((heads, rows, LANES), BF),
                pltpu.VMEM((heads, total, LANES), BF),
                pltpu.VMEM((heads, depth, total), BF),
                pltpu.VMEM((heads, rows, depth), F32),
            ],
        ),
        out_shape=[
            jax.ShapeDtypeStruct((count, rows, width), BF),
            jax.ShapeDtypeStruct((count, heads, 1, rows), F32),
        ],
        compiler_params=pltpu.CompilerParams(vmem_limit_bytes=VMEM_LIMIT),
        cost_estimate=pl.CostEstimate(
            flops=4 * count * heads * rows * total * LANES,
            bytes_accessed=2 * count * width * (2 * rows + 2 * total),
            transcendentals=count * heads * rows * total,
        ),
        name="attend",
    )(lengths, offsets, queries, keys_values, keys_values, *deps)


def attend_back_kernel(
    heads, chunk, lengths_ref, offsets_ref, q_ref, k_ref, v_ref, o_ref, g_ref, lse_ref,
    dq_ref, dk_ref, dv_ref, q_s, k_s, kt_s, v_s, g_s, delta_s, dq_s, dk_s, dv_s
):
    rows, width = q_ref.shape[1:]
    total = k_ref.shape[1]
    depth = width // heads
    scale = depth**-0.5
    factor = scale * LOG2E
    mask = mask_column(lengths_ref, offsets_ref, pl.program_id(0), total, rows)
    ones = jnp.ones((rows, 1), F32)
    cross = jnp.transpose(g_ref[0].astype(F32) * o_ref[0].astype(F32))
    for h in range(heads):
        span = slice(h * depth, (h + 1) * depth)
        delta_s[h] = jnp.sum(cross[span], axis=0, keepdims=True)
        q_s[h] = padded(q_ref[0, :, span], ones)
        k_s[h] = padded(k_ref[0, :, span], mask)
        kt_s[h] = jnp.transpose(k_ref[0, :, span])
        g_s[h] = padded(g_ref[0, :, span])
        v_s[h] = padded(v_ref[0, :, span])

    def one_head(h, carry):
        dq = jnp.zeros((depth, rows), F32)
        for c in range(total // chunk):
            part = slice(c * chunk, (c + 1) * chunk)
            probs = jnp.exp2(nt(k_s[h, part], q_s[h]) * factor - lse_ref[0, h])
            slopes = (probs * (nt(v_s[h, part], g_s[h]) - delta_s[h])).astype(BF)
            dv_s[h, part] = nn(probs.astype(BF), g_s[h]).astype(BF)
            dk_s[h, part] = (nn(slopes, q_s[h]) * scale).astype(BF)
            dq = dq + nn(kt_s[h, :, part], slopes)
        dq_s[h] = jnp.transpose(dq * scale)
        return carry

    lax.fori_loop(0, heads, one_head, 0, unroll=4)
    for h in range(heads):
        span = slice(h * depth, (h + 1) * depth)
        dq_ref[0, :, span] = dq_s[h].astype(BF)
        dk_ref[0, :, span] = dk_s[h][:, :depth]
        dv_ref[0, :, span] = dv_s[h][:, :depth]


def attend_back(lengths, offsets, queries, keys_values, mixed, grads, sample, lse, heads, tile, deps=()):
    count, rows, width = queries.shape
    total = keys_values.shape[1]
    depth = width // heads
    tile = min(tile, total)
    pick = lambda i, *_: (i, 0, 0)
    near = pl.BlockSpec((1, rows, width), pick)
    picked = pl.BlockSpec((1, rows, width), lambda i, *_: (sample + i, 0, 0))
    far = pl.BlockSpec((1, total, width), pick)
    far_values = pl.BlockSpec((1, total, width), lambda i, *_: (i, 0, 1))
    return pl.pallas_call(
        without(attend_back_kernel, 8, len(deps), heads, tile),
        grid_spec=pltpu.PrefetchScalarGridSpec(
            num_scalar_prefetch=2,
            grid=(count,),
            in_specs=[near, far, far_values, near, picked, pl.BlockSpec((1, heads, 1, rows), lambda i, *_: (i, 0, 0, 0))]
            + [pl.BlockSpec(memory_space=pl.ANY)] * len(deps),
            out_specs=[near, far, far],
            scratch_shapes=[
                pltpu.VMEM((heads, rows, LANES), BF),
                pltpu.VMEM((heads, total, LANES), BF),
                pltpu.VMEM((heads, depth, total), BF),
                pltpu.VMEM((heads, total, LANES), BF),
                pltpu.VMEM((heads, rows, LANES), BF),
                pltpu.VMEM((heads, 1, rows), F32),
                pltpu.VMEM((heads, rows, depth), F32),
                pltpu.VMEM((heads, total, LANES), BF),
                pltpu.VMEM((heads, total, LANES), BF),
            ],
        ),
        out_shape=[
            jax.ShapeDtypeStruct((count, rows, width), BF),
            jax.ShapeDtypeStruct((count, total, width), BF),
            jax.ShapeDtypeStruct((count, total, width), BF),
        ],
        compiler_params=pltpu.CompilerParams(vmem_limit_bytes=VMEM_LIMIT),
        cost_estimate=pl.CostEstimate(
            flops=10 * count * heads * rows * total * LANES,
            bytes_accessed=2 * count * width * (4 * rows + 4 * total),
            transcendentals=count * heads * rows * total,
        ),
        name="attend_back",
    )(lengths, offsets, queries, keys_values, keys_values, mixed, grads, lse, *deps)


def block_spots(counts, spread):
    per, first = spread
    spots = []
    for matrix, count in enumerate(counts):
        for block in range(count):
            device, place_in = divmod(len(spots), per)
            device += first
            spots.append((matrix, block, device // 4, device // 2 % 2, device % 2, place_in))
    return spots


EXTRA = ROW_BLOCK - 128
PACKED = (ROW_BLOCK + EXTRA, 128)


def packed(block):
    corner = block[128:, 128:]
    corner = jnp.concatenate([corner, jnp.zeros((EXTRA, 128 - EXTRA), block.dtype)], axis=1)
    return jnp.concatenate([block[:, :128], corner], axis=0)


def unpacked(block):
    side = jnp.transpose(block[128:ROW_BLOCK])
    right = jnp.concatenate([side, block[ROW_BLOCK:, :EXTRA]], axis=0)
    return jnp.concatenate([block[:ROW_BLOCK], right], axis=1)


def precise(left, right, dims):
    return lax.dot_general(left, right, (dims, ((), ())), precision=PRECISE, preferred_element_type=F32)


def muon_gram_kernel(groups, spread, spots_ref, base_own, base_other, *refs):
    count = sum(groups)
    sums, momenta = refs[: len(groups)], refs[len(groups) : len(groups) + count]
    outs = refs[len(groups) + count : len(groups) + 2 * count]
    own_ref, other_ref, grams, sems = refs[len(groups) + 2 * count :]
    n = 0
    for matrices, sum_ref in zip(groups, sums):
        start = 0
        for _ in range(matrices):
            size = momenta[n].shape[0]
            outs[n][...] = MUON_DECAY * momenta[n][...] + sum_ref[start : start + size]
            start += size
            n += 1
    zs = own_ref.shape[1]
    spots = block_spots([out.shape[1] // ROW_BLOCK for out in outs], spread)
    copies = []
    for n, (matrix, block, z, x, core, place_in) in enumerate(spots):
        turned = outs[matrix][:, block * ROW_BLOCK : (block + 1) * ROW_BLOCK]
        grams[n] = packed(precise(turned, turned, ((0,), (0,))))
        away = (lax.rem(spots_ref[1] + x, 2), lax.rem(zs + z - spots_ref[0], zs), place_in)
        pair = [pltpu.make_async_copy(grams.at[n], ref.at[away], sems.at[n]) for ref in (own_ref, other_ref)]
        on_own_core(True, spots_ref, core, [copy.start for copy in pair])
        copies.append((core, pair))
    for core, pair in copies:
        on_own_core(True, spots_ref, core, [copy.wait for copy in pair])


def muon_gram(spots, groups, spread, base):
    momenta = [momentum for _, each in groups for momentum in each]
    terms = jax.ShapeDtypeStruct(base[0].shape, F32)
    vmem, anywhere = pl.BlockSpec(memory_space=pltpu.VMEM), pl.BlockSpec(memory_space=pl.ANY)
    blocks = len(block_spots([momentum.shape[1] // ROW_BLOCK for momentum in momenta], spread))
    outs = pl.pallas_call(
        functools.partial(muon_gram_kernel, [len(each) for _, each in groups], spread),
        out_shape=[jax.ShapeDtypeStruct(momentum.shape, F32) for momentum in momenta] + [terms, terms],
        in_specs=[pl.BlockSpec(memory_space=pltpu.SMEM), anywhere, anywhere]
        + [vmem] * (len(groups) + len(momenta)),
        out_specs=[vmem] * len(momenta) + [anywhere, anywhere],
        input_output_aliases={1: len(momenta), 2: len(momenta) + 1},
        scratch_shapes=[
            pltpu.VMEM((blocks,) + PACKED, F32),
            pltpu.SemaphoreType.DMA((blocks,)),
        ],
        compiler_params=pltpu.CompilerParams(vmem_limit_bytes=VMEM_LIMIT),
        name="muon_gram",
    )(spots, *base, *[group[0] for group in groups], *momenta)
    return outs[:-2], outs[-2], outs[-1]


def polynomial_kernel(count, *refs):
    out = refs[count]
    shape = (ROW_BLOCK, ROW_BLOCK)
    eye = (lax.broadcasted_iota(jnp.int32, shape, 0) == lax.broadcasted_iota(jnp.int32, shape, 1)).astype(F32)
    mul = lambda left, right: precise(left, right, ((1,), (0,)))
    blocks = range(out.shape[0])
    currents, scales, totals = [], [], []
    for n in blocks:
        gram = refs[0][n]
        for ref in refs[1:count]:
            gram = gram + ref[n]
        gram = unpacked(gram)
        square = jnp.sum(jnp.sum(gram * eye, axis=1, keepdims=True), axis=0, keepdims=True)
        scale = 1.0 / (jnp.sqrt(square) + NORM_EPS)
        scales.append(scale)
        currents.append(gram * (scale * scale))
    for step in range(NS_STEPS):
        factors = [NS_A * eye + NS_B * a + NS_C * mul(a, a) for a in currents]
        totals = factors if step == 0 else [mul(f, t) for f, t in zip(factors, totals)]
        if step + 1 < NS_STEPS:
            currents = [mul(f, a) for f, a in zip(factors, currents)]
            currents = [mul(a, f) for f, a in zip(factors, currents)]
    for n in blocks:
        out[n] = packed(totals[n] * scales[n])


def polynomial(parts):
    vmem = pl.BlockSpec(memory_space=pltpu.VMEM)
    return pl.pallas_call(
        functools.partial(polynomial_kernel, len(parts)),
        out_shape=jax.ShapeDtypeStruct(parts[0].shape, F32),
        in_specs=[vmem] * len(parts),
        out_specs=vmem,
        compiler_params=pltpu.CompilerParams(vmem_limit_bytes=VMEM_LIMIT),
        name="polynomial",
    )(*parts)


def muon_apply_kernel(rates, placed, spots_ref, *refs):
    count = len(rates)
    parts, momenta, masters = refs[:4], refs[4 : 4 + count], refs[4 + count : 4 + 2 * count]
    outs, factors = refs[4 + 2 * count : 4 + 3 * count], refs[4 + 3 * count]
    for n in range(4):
        factors[n] = parts[n][...]
    zs = factors.shape[1]
    for matrix, block, z, x, core, place_in in placed:
        part = slice(block * ROW_BLOCK, (block + 1) * ROW_BLOCK)
        away = 2 * lax.rem(spots_ref[2] + core, 2) + lax.rem(spots_ref[1] + x, 2)
        factor = unpacked(factors[away, lax.rem(zs + z - spots_ref[0], zs), place_in])
        direction = precise(momenta[matrix][:, part], factor, ((1,), (1,)))
        outs[matrix][:, part] = masters[matrix][:, part] * (1.0 - WEIGHT_SHRINK) - rates[matrix] * direction


def muon_apply(spots, factors, momenta, masters, rates, placed):
    vmem = pl.BlockSpec(memory_space=pltpu.VMEM)
    return pl.pallas_call(
        functools.partial(muon_apply_kernel, rates, placed),
        out_shape=[jax.ShapeDtypeStruct(master.shape, F32) for master in masters],
        in_specs=[pl.BlockSpec(memory_space=pltpu.SMEM)] + [vmem] * (4 + 2 * len(masters)),
        out_specs=[vmem] * len(masters),
        scratch_shapes=[pltpu.VMEM((4,) + factors[0].shape, F32)],
        compiler_params=pltpu.CompilerParams(vmem_limit_bytes=VMEM_LIMIT),
        name="muon_apply",
    )(spots, *factors, *momenta, *masters)


def body(net, tokens, conditioning, heights, widths, upstream, *state):
    masters, momenta = state[0:5], state[5:10]
    biases, bias_first, bias_second = state[10:13]
    w_qkv, w_proj, w_fc1, w_fc2, w_ada = masters
    micro, local, rows, width = tokens.shape
    count = micro * local
    head_dim = width // HEADS
    hidden = w_fc1.shape[1] * net.dp
    seq, dp = net.seq, net.dp
    y = net.y.digit()

    bounds = [0, 6 * width, 7 * width, 8 * width, 9 * width, 9 * width + hidden, 10 * width + hidden]

    n_qkv, n_proj, n_fc1, n_fc2 = [w.shape[1] for w in (w_qkv, w_proj, w_fc1, w_fc2)]
    unit = math.gcd(math.gcd(n_qkv, n_proj), 8)
    unit_qkv, layout_qkv = math.gcd(n_qkv, 8), [(n_qkv, 1)]
    own_tokens = tokens.reshape(count, rows, width)
    wires = net.y.gather(net.wire([w_qkv, w_proj]))

    ada_rows, ada_cols = w_ada.shape
    cond = conditioning.astype(F32).reshape(count, width)
    cond_act, silu_back = jax.vjp(sigmoid_linear, cond)
    cond_low = cond_act.astype(BF).astype(F32)
    cond_parts = jnp.transpose(cond_low.reshape(count, seq, ada_rows), (1, 0, 2)).reshape(seq, -1)
    parcel = jnp.concatenate([jnp.broadcast_to(biases, (seq,) + biases.shape), cond_parts], axis=1)
    parcel = net.to_all(tie(jnp.broadcast_to(parcel[None], (dp,) + parcel.shape), wires[0]))
    cond_all = parcel[:, 0, biases.shape[0] :].reshape(dp * count, ada_rows).astype(BF)
    first = Staged(net.gather_steps(net.joined(wires, unit, width), [(n_qkv, 1), (n_proj, 1)], 0.45))
    sent = first.advance()
    token_pieces = [net.y.gather(tie(own_tokens[0], *sent))]

    low_ada = w_ada.astype(BF)
    partial = jnp.dot(tie(cond_all, *sent), low_ada, preferred_element_type=F32).reshape(dp, 1, count, ada_cols)
    partial = jnp.broadcast_to(partial, (dp, seq, count, ada_cols))
    received = net.to_all(partial)
    first.advance(partial)
    sent = first.advance(received)
    received, parcel = tie(received, *sent), tie(parcel, *sent)
    received = jnp.sum(received, axis=1)
    bias_full = parcel[:, :, : biases.shape[0]].reshape(-1)
    b_ada, b_q, b_v, b_proj, b_fc1, b_fc2 = [bias_full[bounds[i] : bounds[i + 1]] for i in range(6)]
    modulation = jnp.transpose(received, (1, 0, 2)).reshape(count, dp * ada_cols) + b_ada
    shift_one, scale_one, gate_one, shift_two, scale_two, gate_two = jnp.split(
        modulation[:, None, :], 6, axis=-1
    )
    t_qkv, t_proj = first.finish(modulation)[0]
    wires = net.y.gather(tie(net.wire([w_fc1]), token_pieces[0][-1], *sent))
    wires = wires[:1] + [tie(wire, t_qkv) for wire in wires[1:]]
    t_fc1 = lax.all_gather(net.rows(wires), "dp", axis=0, tiled=True)
    for i in range(1, count):
        token_pieces.append(net.y.gather(tie(own_tokens[i], wires[-1])))

    lengths = (heights * widths).reshape(count).astype(jnp.int32)
    offsets = jnp.stack([((y + s) % seq) * rows for s in range(seq)]).astype(jnp.int32)
    normed_all, inverse_all, attn_all, queries, keys_values, attended, log_total = [[] for _ in range(7)]
    b_kv = jnp.concatenate([jnp.zeros_like(b_v), b_v])
    for i in range(count):
        normed, inverse = layer_norm(jnp.concatenate(token_pieces[i], axis=0).astype(F32))
        attn = (normed * (1.0 + scale_one[i]) + shift_one[i]).astype(BF)
        queries.append((dot_t(attn[None, :rows], t_qkv[:width]) + b_q).astype(BF))
        keys_values.append((dot_t(attn[None], t_qkv[width:]) + b_kv).astype(BF))
        mixed, lse = attend(lengths[i : i + 1], offsets, queries[i], keys_values[i], HEADS, 512)
        if i == 0:
            token_pieces[1:] = [each[:1] + [tie(a, mixed) for a in each[1:]] for each in token_pieces[1:]]
            last_piece = token_pieces[-1][-1] if count > 1 else mixed
            wires = net.y.gather(tie(net.wire([w_fc2]), last_piece))
        normed_all.append(normed[:rows])
        inverse_all.append(inverse[:rows])
        attn_all.append(attn)
        attended.append(mixed)
        log_total.append(lse)
    wires = wires[:1] + [tie(wire, keys_values[-1]) for wire in wires[1:]]
    t_fc2 = lax.all_gather(net.rows(wires), "dp", axis=0, tiled=True)
    attended_low = jnp.concatenate(attended, axis=0)

    inputs = own_tokens.astype(F32)
    branch_one = dot_t(attended_low, t_proj) + b_proj
    mixed_one = inputs + gate_one * branch_one
    normed_two, inverse_two = layer_norm(mixed_one)
    ffn_in = (normed_two * (1.0 + scale_two) + shift_two).astype(BF)
    flat = lambda array: array.reshape(-1, array.shape[-1])
    activated_low, slope = hidden_forward(flat(ffn_in), t_fc1, b_fc1)
    activated_low = activated_low.reshape(count, rows, hidden)
    grad_out = upstream.reshape(count, rows, width).astype(F32)
    grad_branch_two = (gate_two * grad_out).astype(BF)
    term_fc2 = outer(grad_branch_two, activated_low)
    sum_fc2 = net.scatter(term_fc2)
    branch_two = dot_t(tie(activated_low, term_fc2), t_fc2) + b_fc2
    grad_branch_two = tie(grad_branch_two, term_fc2)
    result = (mixed_one + gate_two * branch_two).astype(BF)

    grad_gate_two = jnp.sum(branch_two * grad_out, axis=1)
    bias_fc2 = jnp.sum(grad_branch_two.astype(F32), axis=(0, 1))
    grad_pre, bias_fc1 = hidden_backward(flat(grad_branch_two), t_fc2, slope)
    grad_pre = grad_pre.reshape(count, rows, hidden)
    grad_ffn_in = dot(grad_pre, t_fc1)
    grad_shift_two = jnp.sum(grad_ffn_in, axis=1)
    grad_scale_two = jnp.sum(grad_ffn_in * normed_two, axis=1)
    grad_mixed = grad_out + norm_back(normed_two, inverse_two, grad_ffn_in * (1.0 + scale_two))
    grad_gate_one = jnp.sum(branch_one * grad_mixed, axis=1)
    grad_branch_one = (gate_one * grad_mixed).astype(BF)
    bias_proj = jnp.sum(grad_branch_one.astype(F32), axis=(0, 1))
    grad_attended = dot(grad_branch_one, t_proj).astype(BF)
    unit_mid = math.gcd(math.gcd(n_proj, n_fc1), 8)
    own, other = shard_outer(
        net.spots(),
        [flat(grad_pre), flat(ffn_in), flat(grad_branch_one), flat(attended_low)],
        [([2], 0, width), ([3], 0, width), ([1], 0, width)]
        + [([0], j * width, width) for j in range(hidden // width)],
        [(0, 1, n_proj, 0)] + [(3 + j, 2, n_fc1, n_proj // unit_mid) for j in range(hidden // width)],
        net.z.size, width, unit_mid, (n_proj + n_fc1) // unit_mid,
    )
    term_mid = (own.astype(F32) + net.core.send(other, 1).astype(F32)).astype(BF)
    term_mid = tie(term_mid, sum_fc2, grad_attended)
    sum_mid = net.scatter_chips(term_mid.reshape(dp // 2 * (n_proj + n_fc1), width))
    grad_attended = tie(grad_attended, term_mid)

    def far_steps(dk, dv):
        part = dot(dk[:, rows:], t_qkv[width : 2 * width]) + dot(dv[:, rows:], t_qkv[2 * width :])
        part = part.astype(BF)[0]
        blank = jnp.zeros((rows, width), BF)
        return Staged(net.y.scatter_steps(lambda s: blank if s == 0 else part[(s - 1) * rows : s * rows]))

    grad_q, grad_k, grad_v, far_parts = [], [], [], []
    turned = [momentum.T for momentum in momenta]
    sent = []
    for i in range(count):
        dq, dk, dv = attend_back(
            lengths[i : i + 1], offsets, queries[i], keys_values[i], attended[i],
            grad_attended, i, log_total[i], HEADS, 512, sent,
        )
        sent = []
        grad_q.append(dq)
        grad_k.append(dk)
        grad_v.append(dv)
        if i + 1 < count:
            far_parts.append(far_steps(dk, dv))
            sent = sent + far_parts[-1].advance()
    unit_last = math.gcd(n_qkv, 8)
    (term_last,) = shard_outer(
        net.spots(),
        [flat(each) for each in grad_q + grad_k + grad_v]
        + [attn[:rows] for attn in attn_all]
        + attn_all,
        [([n * count + i for i in range(count)], 0, width) for n in range(5)],
        [(0, 3, n_qkv, 0), (1, 4, n_qkv, 0), (2, 4, n_qkv, 0)],
        net.z.size, width, unit_last, n_qkv // unit_last, sent, split=False,
    )
    sum_last = net.scatter(term_last.reshape(dp * n_qkv, width))
    grad_k[-1] = tie(grad_k[-1], term_last)
    far_parts.append(far_steps(grad_k[-1], grad_v[-1]))
    sent = far_parts[-1].advance()
    grad_q[0] = tie(grad_q[0], *sent)
    bias_q = sum(jnp.sum(each.astype(F32), axis=(0, 1)) for each in grad_q)
    bias_v = sum(jnp.sum(each.astype(F32), axis=(0, 1)) for each in grad_v)
    own_part = jnp.concatenate(
        [
            dot(grad_q[i], t_qkv[:width])
            + dot(grad_k[i][:, :rows], t_qkv[width : 2 * width])
            + dot(grad_v[i][:, :rows], t_qkv[2 * width :])
            for i in range(count)
        ],
        axis=0,
    )
    halves = Staged(lockstep(*[net.halves_steps(tie(each, own_part)) for each in (sum_fc2, sum_mid)]))
    halves.advance()
    matrices = (w_qkv, w_proj, w_fc1, w_fc2, w_ada)
    per = -(-sum(matrix.shape[0] // ROW_BLOCK for matrix in matrices) // dp)
    spread_early = (per, 0)
    early_blocks = (w_fc2.shape[0] + w_fc1.shape[0] + w_proj.shape[0]) // ROW_BLOCK
    spread_last = (per, -(-early_blocks // per))
    far_sum = jnp.stack([steps_of.finish() for steps_of in far_parts])
    grad_attn_in = own_part + far_sum
    normed_one, inverse_one = jnp.stack(normed_all), jnp.stack(inverse_all)
    grad_shift_one = jnp.sum(grad_attn_in, axis=1)
    grad_scale_one = jnp.sum(grad_attn_in * normed_one, axis=1)
    grad_inputs = grad_mixed + norm_back(normed_one, inverse_one, grad_attn_in * (1.0 + scale_one))
    grad_inputs = grad_inputs.astype(BF).reshape(tokens.shape)

    grad_mod_local = jnp.concatenate(
        [grad_shift_one, grad_scale_one, grad_gate_one, grad_shift_two, grad_scale_two, grad_gate_two], axis=-1
    )
    bias_ada = jnp.sum(grad_mod_local, axis=0)
    sent = jnp.transpose(grad_mod_local.reshape(count, dp, 1, ada_cols), (1, 2, 0, 3))
    sent = jnp.broadcast_to(sent, (dp, seq, count, ada_cols))
    mod_parts = net.to_all(sent)
    mod_parts = tie(mod_parts, sent)
    mod_cols = jnp.sum(mod_parts, axis=1).astype(BF).reshape(dp * count, ada_cols)
    shard_ada = jnp.einsum("sr,sc->cr", cond_all, mod_cols, preferred_element_type=F32)

    cond_part = jnp.einsum("sc,rc->sr", mod_cols, low_ada, preferred_element_type=F32)
    cond_part = jnp.broadcast_to(cond_part.reshape(dp, 1, -1), (dp, seq, count * ada_rows))
    term_bias = jnp.concatenate([bias_ada, bias_q, bias_v, bias_proj, bias_fc1, bias_fc2])
    parcel = jnp.concatenate([term_bias.reshape(dp, seq, -1), cond_part], axis=-1)
    got_parcel = net.to_all(parcel)

    sums = halves.finish(parcel)
    blank = jnp.zeros((2, net.z.size, per) + PACKED, F32)
    (next_fc2, next_proj, next_fc1), *early = muon_gram(
        net.spots(), [(sums[0], [turned[3]]), (sums[1], [turned[1], turned[2]])], spread_early, (blank, blank)
    )
    got_parcel = tie(got_parcel, early[0])
    halves = Staged(net.halves_steps(tie(sum_last, got_parcel)))
    sent = halves.advance()
    total = halves.finish(shard_ada)
    (next_qkv, next_ada), *grams = muon_gram(
        net.spots(), [(total, [turned[0]]), (shard_ada, [turned[4]])], spread_last, early
    )
    grams = Staged(net.gram_steps(*grams))
    sent = grams.advance()
    parcel = tie(got_parcel, *sent)
    while not grams.done:
        sent = grams.advance(sent[0])
    gathered = Staged(net.muon_gather_steps(grams.result))
    sent = gathered.advance()
    while not gathered.done:
        sent = gathered.advance(sent[0])
    momenta_in = [next_fc2, next_proj, next_fc1, next_qkv, next_ada]
    heights_of = [momentum.shape[1] // ROW_BLOCK for momentum in momenta_in]
    placed = block_spots(heights_of[:3], spread_early)
    placed += [(3 + spot[0],) + spot[1:] for spot in block_spots(heights_of[3:], spread_last)]
    new_fc2, new_proj, new_fc1, new_qkv, new_ada = muon_apply(
        net.spots(), gathered.result, momenta_in, [w.T for w in (w_fc2, w_proj, w_fc1, w_qkv, w_ada)],
        [math.sqrt(width / hidden), 1.0, math.sqrt(hidden / width), math.sqrt(3.0), math.sqrt(6.0)], placed,
    )

    size = biases.shape[0]
    grad_bias = jnp.sum(parcel[..., :size], axis=(0, 1))
    cond_part = jnp.sum(parcel[..., size:], axis=0).reshape(seq, count, ada_rows)
    grad_cond = silu_back(jnp.transpose(cond_part, (1, 0, 2)).reshape(count, width))[0]
    next_first = BETA_FIRST * bias_first + (1.0 - BETA_FIRST) * grad_bias
    next_second = BETA_SECOND * bias_second + (1.0 - BETA_SECOND) * grad_bias * grad_bias
    first_hat = next_first / (1.0 - BETA_FIRST**STEP_COUNT)
    second_hat = next_second / (1.0 - BETA_SECOND**STEP_COUNT)
    new_biases = biases * (1.0 - ADAM_RATE * ADAM_DECAY) - ADAM_RATE * first_hat / (
        jnp.sqrt(second_hat) + ADAM_EPS
    )
    return (
        result.reshape(tokens.shape),
        grad_inputs,
        grad_cond.reshape(conditioning.shape),
        new_qkv.T, new_proj.T, new_fc1.T, new_fc2.T, new_ada.T,
        next_qkv.T, next_proj.T, next_fc1.T, next_fc2.T, next_ada.T,
        new_biases,
        next_first,
        next_second,
    )


def solution(mesh):
    rows = P(None, "dp", "seq", None)
    matrix = P("seq", "dp")
    flat = P(("dp", "seq"))
    in_specs = (rows, P(None, "dp", None), P(None, "dp"), P(None, "dp"), rows) + (matrix,) * 10 + (flat,) * 3
    out_specs = (rows, rows, P(None, "dp", None)) + (matrix,) * 10 + (flat,) * 3
    return jax.shard_map(
        functools.partial(body, Net(mesh)), mesh=mesh, in_specs=in_specs, out_specs=out_specs, check_vma=False
    )
```

```python
import functools
import math

import jax
import jax.numpy as jnp
from jax import lax
from jax.experimental import pallas as pl
from jax.experimental.pallas import tpu as pltpu
from jax.sharding import PartitionSpec as P

HEADS = 16
ROW_BLOCK = 144
NS_STEPS = 5
STEP_COUNT = 10

PRECISE = lax.Precision.HIGHEST
LN_EPS = 1e-06
MASKED = -1e30
NS_A = 3.4445
NS_B = -4.775
NS_C = 2.0315
MUON_DECAY = 0.5
WEIGHT_SHRINK = 0.0001
NORM_EPS = 1e-07
BETA_FIRST = 0.9
BETA_SECOND = 0.999
ADAM_RATE = 0.1
ADAM_DECAY = 0.01
ADAM_EPS = 1e-08
BF = jnp.bfloat16
F32 = jnp.float32
VMEM_LIMIT = 60 * 2**20


class Ring:
    def __init__(self, name, total, stride, size):
        self.name, self.total, self.stride, self.size = name, total, stride, size

    def digit(self):
        return (lax.axis_index(self.name) // self.stride) % self.size

    def send(self, value, shift):
        pairs = []
        for i in range(self.total):
            d = (i // self.stride) % self.size
            pairs.append((i, i + ((d + shift) % self.size - d) * self.stride))
        return lax.ppermute(value, self.name, pairs)

    def gather(self, value, far=1):
        n = self.size
        blocks = [value] + [None] * (n - 1)
        if n == 2:
            blocks[1] = self.send(value, 1)
        elif n > 2:
            low = high = value
            for t in range(1, n // 2):
                low, high = self.send(low, 1), self.send(high, -1)
                blocks[n - t], blocks[t] = low, high
            blocks[n // 2] = self.send(low, 1) if far == 1 else self.send(high, -1)
        return blocks

    def gather_steps(self, value, far=1):
        n = self.size
        blocks = [value] + [None] * (n - 1)
        if n == 2:
            blocks[1] = self.send(value, 1)
            anchor = yield [value]
            blocks[1] = tie(blocks[1], anchor)
            return blocks
        low = high = value
        for t in range(1, n // 2):
            sent = [low, high]
            low, high = self.send(low, 1), self.send(high, -1)
            anchor = yield sent
            low, high = tie(low, anchor), tie(high, anchor)
            blocks[n - t], blocks[t] = low, high
        sent = [low if far == 1 else high]
        last = self.send(sent[0], far)
        anchor = yield sent
        blocks[n // 2] = tie(last, anchor)
        return blocks

    def scatter_steps(self, block_of, far=1):
        n = self.size
        if n == 1:
            return block_of(0).astype(F32)
        if n == 2:
            sent = block_of(1)
            got = self.send(sent, 1)
            anchor = yield [sent]
            return block_of(0).astype(F32) + tie(got, anchor).astype(F32)
        sent = block_of(n // 2)
        got = self.send(sent, far)
        anchor = yield [sent]
        low, high = (tie(got, anchor), None) if far == 1 else (None, tie(got, anchor))
        for t in range(n // 2 - 1, 0, -1):
            up, down = block_of(t), block_of(n - t)
            if low is not None:
                up = (up.astype(F32) + low.astype(F32)).astype(up.dtype)
            if high is not None:
                down = (down.astype(F32) + high.astype(F32)).astype(down.dtype)
            low, high = self.send(up, 1), self.send(down, -1)
            anchor = yield [up, down]
            low, high = tie(low, anchor), tie(high, anchor)
        return block_of(0).astype(F32) + low.astype(F32) + high.astype(F32)


def tie(value, *earlier):
    earlier = [array for array in earlier if array is not None]
    if not earlier:
        return value
    anywhere = pl.BlockSpec(memory_space=pl.ANY)
    return pl.pallas_call(
        lambda *refs: None,
        out_shape=jax.ShapeDtypeStruct(value.shape, value.dtype),
        in_specs=[anywhere] * (1 + len(earlier)),
        out_specs=anywhere,
        input_output_aliases={0: 0},
        name="tie",
    )(value, *earlier)


def lockstep(*steps):
    results = [None] * len(steps)
    alive = dict(enumerate(steps))
    anchor = None
    while alive:
        sent = []
        for n, step in list(alive.items()):
            try:
                sent += step.send(anchor)
            except StopIteration as stop:
                results[n] = stop.value
                del alive[n]
        if alive:
            anchor = yield sent
    return results


class Staged:
    def __init__(self, steps):
        self.steps, self.result, self.started, self.done = steps, None, False, False

    def advance(self, anchor=None):
        if self.done:
            return []
        try:
            sent = self.steps.send(anchor if self.started else None)
            self.started = True
            return sent
        except StopIteration as stop:
            self.result, self.done = stop.value, True
            return []

    def finish(self, anchor=None):
        while not self.done:
            self.advance(anchor)
        return self.result


def place_kernel(zs, ga, parts, count, outs, *refs):
    spots, sources = refs[0], refs[1 : 1 + count]
    outputs, (full, in_sems, out_sems) = refs[1 + count : 1 + count + outs], refs[1 + count + outs :]
    g = full.shape[3]
    half = count // 2
    shards = []
    for sc in range(2):
        for sx in range(2):
            for sz in range(zs):
                where = (lax.rem(spots[0] + sz, zs), lax.rem(spots[1] + sx, 2), lax.rem(spots[2] + sc, 2))
                n = 2 * len(shards)
                line, pair = sources[sc * half + sx].at[sz], sources[sc * half + 2 + sz].at[sx]
                copies = [
                    pltpu.make_async_copy(line, full.at[(*where, pl.ds(0, ga))], in_sems.at[n]),
                    pltpu.make_async_copy(pair, full.at[(*where, pl.ds(ga, g - ga))], in_sems.at[n + 1]),
                ]
                for copy in copies:
                    copy.start()
                shards.append((where, copies))
    exits = []
    for where, copies in shards:
        for copy in copies:
            copy.wait()
        for output, start, size, column, depth in parts:
            target = outputs[output].at[(*where, slice(None), slice(None), pl.ds(column, depth))]
            copy = pltpu.make_async_copy(
                full.at[(*where, pl.ds(start, size))], target, out_sems.at[len(exits)]
            )
            copy.start()
            exits.append(copy)
    for copy in exits:
        copy.wait()


def place(spots, sources, shape, ga, parts, shapes):
    zs = shape[0]
    moved = math.prod(shape) * 2
    return pl.pallas_call(
        functools.partial(place_kernel, zs, ga, parts, len(sources), len(shapes)),
        out_shape=[jax.ShapeDtypeStruct(each, BF) for each in shapes],
        in_specs=[pl.BlockSpec(memory_space=pltpu.SMEM)]
        + [pl.BlockSpec(memory_space=pl.ANY)] * len(sources),
        out_specs=[pl.BlockSpec(memory_space=pl.ANY)] * len(shapes),
        scratch_shapes=[
            pltpu.VMEM(shape, BF),
            pltpu.SemaphoreType.DMA((8 * zs,)),
            pltpu.SemaphoreType.DMA((4 * zs * len(parts),)),
        ],
        compiler_params=pltpu.CompilerParams(vmem_limit_bytes=VMEM_LIMIT),
        cost_estimate=pl.CostEstimate(flops=0, bytes_accessed=2 * moved, transcendentals=0),
        name="place",
    )(spots, *sources)


class Net:
    def __init__(self, mesh):
        dp, seq = mesh.shape["dp"], mesh.shape["seq"]
        self.dp, self.seq = dp, seq
        self.core = Ring("dp", dp, 1, 2)
        self.x = Ring("dp", dp, 2, 2)
        self.z = Ring("dp", dp, 4, dp // 4)
        self.y = Ring("seq", seq, 1, seq)

    def spots(self):
        return jnp.stack([self.z.digit(), self.x.digit(), self.core.digit()]).astype(jnp.int32)


    def wire(self, shards):
        turned = [shard.astype(BF).T for shard in shards]
        return turned[0] if len(turned) == 1 else jnp.concatenate(turned, axis=0)

    def rows(self, wires):
        if self.seq == 2:
            own, other = wires
            return jnp.where(
                self.y.digit() == 0,
                jnp.concatenate([own, other], axis=1),
                jnp.concatenate([other, own], axis=1),
            )
        order = (jnp.arange(self.seq) - self.y.digit()) % self.seq
        full = jnp.take(jnp.stack(wires), order, axis=0)
        return jnp.transpose(full, (1, 0, 2)).reshape(full.shape[1], -1)

    def joined(self, wires, unit, depth):
        full = self.rows(wires)
        return full.reshape(full.shape[0] // unit, unit, depth)

    def scatter(self, term):
        return lax.psum_scatter(term, "dp", scatter_dimension=0, tiled=True)

    def scatter_chips(self, term):
        groups = [list(range(core, self.dp, 2)) for core in range(2)]
        return lax.psum_scatter(term, "dp", scatter_dimension=0, tiled=True, axis_index_groups=groups)

    def halves_steps(self, term):
        y = self.y.digit()
        blocks = term.reshape(term.shape[0], self.seq, -1)
        return (
            yield from self.y.scatter_steps(
                lambda s: lax.dynamic_index_in_dim(blocks, (y + s) % self.seq, 1, keepdims=False)
            )
        )

    def gather_steps(self, units, layout, part):
        g, unit, depth = units.shape
        zs = self.z.size
        ga = max(1, int(part * g))
        first, second = units[:ga], units[ga:]

        def line_steps():
            blocks = yield from self.z.gather_steps(first, 1)
            line = jnp.stack(blocks)
            return (yield from self.x.gather_steps(line))

        def pair_steps():
            blocks = yield from self.x.gather_steps(second)
            return (yield from self.z.gather_steps(jnp.stack(blocks), -1))

        lines, pairs = yield from lockstep(line_steps(), pair_steps())
        pieces = lines + pairs
        others = [self.core.send(piece, 1) for piece in pieces]
        anchor = yield pieces
        sources = pieces + [tie(other, anchor) for other in others]
        parts, shapes, start = [], [], 0
        for n, (rows, blocks) in enumerate(layout):
            size = rows // unit
            shapes.append((zs, 2, 2, size, unit, blocks * depth))
            for j in range(blocks):
                parts.append((n, start, size, j * depth, depth))
                start += size
        full = place(self.spots(), sources, (zs, 2, 2, g, unit, depth), ga, parts, shapes)
        return [f.reshape(-1, f.shape[-1]) for f in full], lines[1:] + pairs[1:]


    def gram_steps(self, own, other):
        got = self.core.send(other, 1)
        anchor = yield [other]
        half = own + tie(got, anchor)
        sent = half[1]
        got = self.x.send(sent, 1)
        anchor = yield [sent]
        kept = half[0] + tie(got, anchor)
        sent = [kept[shift] for shift in range(1, self.z.size)]
        got = [self.z.send(each, shift) for shift, each in enumerate(sent, 1)]
        anchor = yield sent
        return [kept[0]] + [tie(each, anchor) for each in got]

    def muon_gather_steps(self, parts):
        factor = polynomial(parts)
        got = [self.z.send(factor, -shift) for shift in range(1, self.z.size)]
        anchor = yield [factor]
        line = jnp.stack([factor] + [tie(each, anchor) for each in got])
        got = self.x.send(line, 1)
        anchor = yield [line]
        pair = [line, tie(got, anchor)]
        others = [self.core.send(each, 1) for each in pair]
        anchor = yield pair
        return pair + [tie(each, anchor) for each in others]


    def to_all(self, value):
        flat = value.reshape((self.dp * self.seq,) + value.shape[2:])
        return lax.all_to_all(flat, ("dp", "seq"), 0, 0, tiled=True).reshape(value.shape)

    def to_dp(self, value):
        return lax.all_to_all(value, "dp", 0, 0, tiled=True)


def layer_norm(values):
    centered = values - jnp.mean(values, axis=-1, keepdims=True)
    inverse = lax.rsqrt(jnp.mean(centered * centered, axis=-1, keepdims=True) + LN_EPS)
    return (centered * inverse, inverse)


def norm_back(normed, inverse, grad):
    mean_grad = jnp.mean(grad, axis=-1, keepdims=True)
    mean_cross = jnp.mean(grad * normed, axis=-1, keepdims=True)
    return inverse * (grad - mean_grad - normed * mean_cross)


def sigmoid_linear(values):
    return values * jax.nn.sigmoid(values)


def dot_t(left, right):
    return jnp.einsum("srk,nk->srn", left, right, preferred_element_type=F32)


def dot(left, right):
    return jnp.einsum("srn,nk->srk", left, right, preferred_element_type=F32)


GELU_SCALE = math.sqrt(2.0 / math.pi)
GELU_CUBE = 0.044715


def row_parts(rows):
    step = rows // 4 if rows % 64 == 0 else rows
    return [slice(start, start + step) for start in range(0, rows, step)]


def hidden_kernel(x_ref, w_ref, b_ref, act_ref, slope_ref):
    for part in row_parts(x_ref.shape[0]):
        value = nt(x_ref[part], w_ref[...]) + b_ref[...]
        square = value * value
        bend = jnp.tanh(value * (GELU_SCALE + (GELU_SCALE * GELU_CUBE) * square))
        half = 0.5 + 0.5 * bend
        act_ref[part] = (value * half).astype(BF)
        steep = (0.5 * value) * (GELU_SCALE + (3.0 * GELU_SCALE * GELU_CUBE) * square)
        slope_ref[part] = (half + steep * (1.0 - bend * bend)).astype(BF)


def hidden_forward(x, w, bias):
    rows, depth = x.shape
    n = w.shape[0]
    tile = math.gcd(n, 512)
    out = pl.BlockSpec((rows, tile), lambda i: (0, i))
    return pl.pallas_call(
        hidden_kernel,
        grid=(n // tile,),
        in_specs=[
            pl.BlockSpec((rows, depth), lambda i: (0, 0)),
            pl.BlockSpec((tile, depth), lambda i: (i, 0)),
            pl.BlockSpec((1, tile), lambda i: (0, i)),
        ],
        out_specs=[out, out],
        out_shape=[jax.ShapeDtypeStruct((rows, n), BF)] * 2,
        compiler_params=pltpu.CompilerParams(vmem_limit_bytes=VMEM_LIMIT),
        cost_estimate=pl.CostEstimate(
            flops=2 * rows * n * depth, bytes_accessed=2 * (rows + n) * depth + 4 * rows * n, transcendentals=rows * n
        ),
        name="hidden_forward",
    )(x, w, bias.reshape(1, n))


def hidden_back_kernel(g_ref, w_ref, slope_ref, out_ref, bias_ref):
    total = 0.0
    for part in row_parts(g_ref.shape[0]):
        grad = (nn(g_ref[part], w_ref[...]) * slope_ref[part].astype(F32)).astype(BF)
        out_ref[part] = grad
        total = total + jnp.sum(grad.astype(F32), axis=0, keepdims=True)
    bias_ref[...] = total


def hidden_backward(grad, w, slope):
    rows, depth = grad.shape
    n = w.shape[1]
    tile = math.gcd(n, 512)
    out = pl.BlockSpec((rows, tile), lambda i: (0, i))
    result, bias = pl.pallas_call(
        hidden_back_kernel,
        grid=(n // tile,),
        in_specs=[
            pl.BlockSpec((rows, depth), lambda i: (0, 0)),
            pl.BlockSpec((depth, tile), lambda i: (0, i)),
            out,
        ],
        out_specs=[out, pl.BlockSpec((1, tile), lambda i: (0, i))],
        out_shape=[jax.ShapeDtypeStruct((rows, n), BF), jax.ShapeDtypeStruct((1, n), F32)],
        compiler_params=pltpu.CompilerParams(vmem_limit_bytes=VMEM_LIMIT),
        cost_estimate=pl.CostEstimate(
            flops=2 * rows * n * depth, bytes_accessed=2 * (rows + n) * depth + 4 * rows * n, transcendentals=0
        ),
        name="hidden_backward",
    )(grad, w, slope)
    return result, bias[0]


def outer(left, right):
    return jnp.einsum("srn,srk->nk", left, right, preferred_element_type=F32).astype(BF)


def shard_outer_kernel(plan, counts, tile, split, spots_ref, *refs):
    outs = 2 if split else 1
    inputs, where = refs[: counts[0]], refs[counts[1] : counts[1] + outs]
    buffers = refs[counts[1] + outs : counts[1] + outs + len(plan["loads"])]
    acc, in_sems, out_sems = refs[counts[1] + outs + len(plan["loads"]) :]
    loads = []
    for n, (sources, start, size) in enumerate(plan["loads"]):
        row, copies = 0, []
        for m, source in enumerate(sources):
            rows = inputs[source].shape[0]
            window = inputs[source].at[:, pl.ds(start, size)]
            copies.append(pltpu.make_async_copy(window, buffers[n].at[pl.ds(row, rows)], in_sems.at[n, m]))
            copies[-1].start()
            row += rows
        loads.append(copies)
    ready = set()
    shipped = []
    unit = acc.shape[1]
    for left, right, base, ships in plan["parts"]:
        for n in (left, right):
            if n not in ready:
                for copy in loads[n]:
                    copy.wait()
                ready.add(n)
        width = buffers[left].shape[1]
        step = tile if width % tile == 0 else width

        @pl.loop(0, width // step)
        def _(t):
            block = buffers[left][:, pl.ds(pl.multiple_of(t * step, step), step)]
            product = lax.dot_general(
                block, buffers[right][...], (((0,), (0,)), ((), ())), preferred_element_type=F32
            )
            product = product.reshape(step // unit, unit, product.shape[1]).astype(BF)
            acc[pl.ds(base + t * (step // unit), step // unit)] = product

        for core, z, x, row, target, size in ships:
            spot = (z, x) if split else (z, x, core)
            places = [ref.at[(*spot, pl.ds(target, size))] for ref in where]
            copies = [
                pltpu.make_async_copy(acc.at[pl.ds(row, size)], each, out_sems.at[len(shipped)]) for each in places
            ]
            shipped.append((core, copies))
            on_own_core(split, spots_ref, core, [copy.start for copy in copies])
    for core, copies in shipped:
        on_own_core(split, spots_ref, core, [copy.wait for copy in copies])


def on_own_core(split, spots_ref, core, actions):
    if not split:
        actions[0]()
        return

    @pl.when(spots_ref[2] == core)
    def _():
        actions[0]()

    @pl.when(spots_ref[2] != core)
    def _():
        actions[1]()


def shard_outer(spots, inputs, loads, parts, zs, depth, unit, shard_units, deps=(), tile=384, split=True):
    dp = zs * 4
    plan_parts, base, row, placed = [], 0, 0, {}
    begun = {}
    for left, right, rows, first in parts:
        if first not in begun:
            begun[first] = (base, 0)
        start, shipped = begun[first]
        width = loads[left][2]
        size = rows // unit
        end = base + width // unit
        ships = []
        while shipped < dp and start + (shipped + 1) * size <= end:
            core, x, z = shipped % 2, shipped // 2 % 2, shipped // 4
            ships.append((core, z, x, start + shipped * size, first, size))
            shipped += 1
        begun[first] = (start, shipped)
        plan_parts.append((left, right, base, ships))
        base = end
    total = sum(len(part[3]) for part in plan_parts)
    shape = (zs, 2, shard_units, unit, depth) if split else (zs, 2, 2, shard_units, unit, depth)
    outs = [jax.ShapeDtypeStruct(shape, BF)] * (2 if split else 1)
    anywhere = pl.BlockSpec(memory_space=pl.ANY)
    heights = [sum(inputs[source].shape[0] for source in sources) for sources, _, _ in loads]
    flops = sum(2 * heights[p[0]] * loads[p[0]][2] * loads[p[1]][2] for p in parts)
    return pl.pallas_call(
        functools.partial(
            shard_outer_kernel, {"loads": loads, "parts": plan_parts}, (len(inputs), len(inputs) + len(deps)), tile, split
        ),
        out_shape=outs,
        in_specs=[pl.BlockSpec(memory_space=pltpu.SMEM)] + [anywhere] * (len(inputs) + len(deps)),
        out_specs=[anywhere] * len(outs),
        scratch_shapes=[pltpu.VMEM((height, load[2]), BF) for height, load in zip(heights, loads)]
        + [
            pltpu.VMEM((base, unit, depth), BF),
            pltpu.SemaphoreType.DMA((len(loads), max(len(load[0]) for load in loads))),
            pltpu.SemaphoreType.DMA((total,)),
        ],
        compiler_params=pltpu.CompilerParams(vmem_limit_bytes=VMEM_LIMIT),
        cost_estimate=pl.CostEstimate(flops=flops, bytes_accessed=2 * base * unit * depth, transcendentals=0),
        name="shard_outer",
    )(spots, *inputs, *deps)


LANES = 128
LOG2E = math.log2(math.e)


def padded(block, column=None):
    rows, depth = block.shape
    if column is None:
        return jnp.concatenate([block, jnp.zeros((rows, LANES - depth), block.dtype)], axis=1)
    rest = jnp.zeros((rows, LANES - depth - 1), block.dtype)
    return jnp.concatenate([block, column.astype(block.dtype), rest], axis=1)


def mask_column(lengths_ref, offsets_ref, sample, total, rows):
    place = lax.broadcasted_iota(jnp.int32, (total, 1), 0)
    position = place
    for s in range(total // rows):
        position = jnp.where(place // rows == s, place - s * rows + offsets_ref[s], position)
    return jnp.where(position < lengths_ref[sample], 0.0, MASKED)


def nt(left, right):
    return lax.dot_general(left, right, (((1,), (1,)), ((), ())), preferred_element_type=F32)


def nn(left, right):
    return jnp.dot(left, right, preferred_element_type=F32)


def without(kernel, start, count, *fixed):
    def run(*refs):
        kernel(*fixed, *refs[:start], *refs[start + count :])

    return run


def attend_kernel(heads, chunk, lengths_ref, offsets_ref, q_ref, k_ref, v_ref, o_ref, lse_ref, q_s, k_s, vt_s, o_s):
    rows, width = q_ref.shape[1:]
    total = k_ref.shape[1]
    depth = width // heads
    factor = depth**-0.5 * LOG2E
    mask = mask_column(lengths_ref, offsets_ref, pl.program_id(0), total, rows)
    q_blank = padded(jnp.zeros((rows, depth), BF), jnp.ones((rows, 1), F32))
    k_blank = padded(jnp.zeros((total, depth), BF), mask)
    turned = jnp.transpose(v_ref[0].astype(F32))
    for h in range(heads):
        span = slice(h * depth, (h + 1) * depth)
        q_s[h] = q_blank
        k_s[h] = k_blank
        q_s[h, :, :depth] = q_ref[0, :, span]
        k_s[h, :, :depth] = k_ref[0, :, span]
        vt_s[h] = turned[span].astype(BF)

    def one_head(h, carry):
        peak = jnp.full((1, rows), MASKED, F32)
        sums = jnp.zeros((1, rows), F32)
        mixed = jnp.zeros((depth, rows), F32)
        for c in range(total // chunk):
            part = slice(c * chunk, (c + 1) * chunk)
            scores = nt(k_s[h, part], q_s[h])
            higher = jnp.maximum(peak, jnp.max(scores, axis=0, keepdims=True))
            weights = jnp.exp2((scores - higher) * factor)
            if c == 0:
                sums = jnp.sum(weights, axis=0, keepdims=True)
                mixed = nn(vt_s[h, :, part], weights.astype(BF))
            else:
                shrink = jnp.exp2((peak - higher) * factor)
                sums = sums * shrink + jnp.sum(weights, axis=0, keepdims=True)
                mixed = mixed * shrink + nn(vt_s[h, :, part], weights.astype(BF))
            peak = higher
        o_s[h] = jnp.transpose(mixed / sums)
        lse_ref[0, h] = peak * factor + jnp.log2(sums)
        return carry

    lax.fori_loop(0, heads, one_head, 0, unroll=4)
    for h in range(heads):
        o_ref[0, :, h * depth : (h + 1) * depth] = o_s[h].astype(BF)


def attend(lengths, offsets, queries, keys_values, heads, tile, deps=()):
    count, rows, width = queries.shape
    total = keys_values.shape[1]
    depth = width // heads
    tile = min(tile, total)
    pick = lambda i, *_: (i, 0, 0)
    return pl.pallas_call(
        without(attend_kernel, 5, len(deps), heads, tile),
        grid_spec=pltpu.PrefetchScalarGridSpec(
            num_scalar_prefetch=2,
            grid=(count,),
            in_specs=[
                pl.BlockSpec((1, rows, width), pick),
                pl.BlockSpec((1, total, width), pick),
                pl.BlockSpec((1, total, width), lambda i, *_: (i, 0, 1)),
            ]
            + [pl.BlockSpec(memory_space=pl.ANY)] * len(deps),
            out_specs=[
                pl.BlockSpec((1, rows, width), pick),
                pl.BlockSpec((1, heads, 1, rows), lambda i, *_: (i, 0, 0, 0)),
            ],
            scratch_shapes=[
                pltpu.VMEM((heads, rows, LANES), BF),
                pltpu.VMEM((heads, total, LANES), BF),
                pltpu.VMEM((heads, depth, total), BF),
                pltpu.VMEM((heads, rows, depth), F32),
            ],
        ),
        out_shape=[
            jax.ShapeDtypeStruct((count, rows, width), BF),
            jax.ShapeDtypeStruct((count, heads, 1, rows), F32),
        ],
        compiler_params=pltpu.CompilerParams(vmem_limit_bytes=VMEM_LIMIT),
        cost_estimate=pl.CostEstimate(
            flops=4 * count * heads * rows * total * LANES,
            bytes_accessed=2 * count * width * (2 * rows + 2 * total),
            transcendentals=count * heads * rows * total,
        ),
        name="attend",
    )(lengths, offsets, queries, keys_values, keys_values, *deps)


def attend_back_kernel(
    heads, chunk, lengths_ref, offsets_ref, q_ref, k_ref, v_ref, o_ref, g_ref, lse_ref,
    dq_ref, dk_ref, dv_ref, q_s, k_s, kt_s, v_s, g_s, delta_s, dq_s, dk_s, dv_s
):
    rows, width = q_ref.shape[1:]
    total = k_ref.shape[1]
    depth = width // heads
    scale = depth**-0.5
    factor = scale * LOG2E
    mask = mask_column(lengths_ref, offsets_ref, pl.program_id(0), total, rows)
    ones = jnp.ones((rows, 1), F32)
    cross = jnp.transpose(g_ref[0].astype(F32) * o_ref[0].astype(F32))
    for h in range(heads):
        span = slice(h * depth, (h + 1) * depth)
        delta_s[h] = jnp.sum(cross[span], axis=0, keepdims=True)
        q_s[h] = padded(q_ref[0, :, span], ones)
        k_s[h] = padded(k_ref[0, :, span], mask)
        kt_s[h] = jnp.transpose(k_ref[0, :, span])
        g_s[h] = padded(g_ref[0, :, span])
        v_s[h] = padded(v_ref[0, :, span])

    def one_head(h, carry):
        dq = jnp.zeros((depth, rows), F32)
        for c in range(total // chunk):
            part = slice(c * chunk, (c + 1) * chunk)
            probs = jnp.exp2(nt(k_s[h, part], q_s[h]) * factor - lse_ref[0, h])
            slopes = (probs * (nt(v_s[h, part], g_s[h]) - delta_s[h])).astype(BF)
            dv_s[h, part] = nn(probs.astype(BF), g_s[h]).astype(BF)
            dk_s[h, part] = (nn(slopes, q_s[h]) * scale).astype(BF)
            dq = dq + nn(kt_s[h, :, part], slopes)
        dq_s[h] = jnp.transpose(dq * scale)
        return carry

    lax.fori_loop(0, heads, one_head, 0, unroll=4)
    for h in range(heads):
        span = slice(h * depth, (h + 1) * depth)
        dq_ref[0, :, span] = dq_s[h].astype(BF)
        dk_ref[0, :, span] = dk_s[h][:, :depth]
        dv_ref[0, :, span] = dv_s[h][:, :depth]


def attend_back(lengths, offsets, queries, keys_values, mixed, grads, sample, lse, heads, tile, deps=()):
    count, rows, width = queries.shape
    total = keys_values.shape[1]
    depth = width // heads
    tile = min(tile, total)
    pick = lambda i, *_: (i, 0, 0)
    near = pl.BlockSpec((1, rows, width), pick)
    picked = pl.BlockSpec((1, rows, width), lambda i, *_: (sample + i, 0, 0))
    far = pl.BlockSpec((1, total, width), pick)
    far_values = pl.BlockSpec((1, total, width), lambda i, *_: (i, 0, 1))
    return pl.pallas_call(
        without(attend_back_kernel, 8, len(deps), heads, tile),
        grid_spec=pltpu.PrefetchScalarGridSpec(
            num_scalar_prefetch=2,
            grid=(count,),
            in_specs=[near, far, far_values, near, picked, pl.BlockSpec((1, heads, 1, rows), lambda i, *_: (i, 0, 0, 0))]
            + [pl.BlockSpec(memory_space=pl.ANY)] * len(deps),
            out_specs=[near, far, far],
            scratch_shapes=[
                pltpu.VMEM((heads, rows, LANES), BF),
                pltpu.VMEM((heads, total, LANES), BF),
                pltpu.VMEM((heads, depth, total), BF),
                pltpu.VMEM((heads, total, LANES), BF),
                pltpu.VMEM((heads, rows, LANES), BF),
                pltpu.VMEM((heads, 1, rows), F32),
                pltpu.VMEM((heads, rows, depth), F32),
                pltpu.VMEM((heads, total, LANES), BF),
                pltpu.VMEM((heads, total, LANES), BF),
            ],
        ),
        out_shape=[
            jax.ShapeDtypeStruct((count, rows, width), BF),
            jax.ShapeDtypeStruct((count, total, width), BF),
            jax.ShapeDtypeStruct((count, total, width), BF),
        ],
        compiler_params=pltpu.CompilerParams(vmem_limit_bytes=VMEM_LIMIT),
        cost_estimate=pl.CostEstimate(
            flops=10 * count * heads * rows * total * LANES,
            bytes_accessed=2 * count * width * (4 * rows + 4 * total),
            transcendentals=count * heads * rows * total,
        ),
        name="attend_back",
    )(lengths, offsets, queries, keys_values, keys_values, mixed, grads, lse, *deps)


def block_spots(counts, spread):
    per, first = spread
    spots = []
    for matrix, count in enumerate(counts):
        for block in range(count):
            device, place_in = divmod(len(spots), per)
            device += first
            spots.append((matrix, block, device // 4, device // 2 % 2, device % 2, place_in))
    return spots


EXTRA = ROW_BLOCK - 128
PACKED = (ROW_BLOCK + EXTRA, 128)


def packed(block):
    corner = block[128:, 128:]
    corner = jnp.concatenate([corner, jnp.zeros((EXTRA, 128 - EXTRA), block.dtype)], axis=1)
    return jnp.concatenate([block[:, :128], corner], axis=0)


def unpacked(block):
    side = jnp.transpose(block[128:ROW_BLOCK])
    right = jnp.concatenate([side, block[ROW_BLOCK:, :EXTRA]], axis=0)
    return jnp.concatenate([block[:ROW_BLOCK], right], axis=1)


def precise(left, right, dims):
    return lax.dot_general(left, right, (dims, ((), ())), precision=PRECISE, preferred_element_type=F32)


def muon_gram_kernel(groups, spread, spots_ref, base_own, base_other, *refs):
    count = sum(groups)
    sums, momenta = refs[: len(groups)], refs[len(groups) : len(groups) + count]
    outs = refs[len(groups) + count : len(groups) + 2 * count]
    own_ref, other_ref, grams, sems = refs[len(groups) + 2 * count :]
    n = 0
    for matrices, sum_ref in zip(groups, sums):
        start = 0
        for _ in range(matrices):
            size = momenta[n].shape[0]
            outs[n][...] = MUON_DECAY * momenta[n][...] + sum_ref[start : start + size]
            start += size
            n += 1
    zs = own_ref.shape[1]
    spots = block_spots([out.shape[1] // ROW_BLOCK for out in outs], spread)
    copies = []
    for n, (matrix, block, z, x, core, place_in) in enumerate(spots):
        turned = outs[matrix][:, block * ROW_BLOCK : (block + 1) * ROW_BLOCK]
        grams[n] = packed(precise(turned, turned, ((0,), (0,))))
        away = (lax.rem(spots_ref[1] + x, 2), lax.rem(zs + z - spots_ref[0], zs), place_in)
        pair = [pltpu.make_async_copy(grams.at[n], ref.at[away], sems.at[n]) for ref in (own_ref, other_ref)]
        on_own_core(True, spots_ref, core, [copy.start for copy in pair])
        copies.append((core, pair))
    for core, pair in copies:
        on_own_core(True, spots_ref, core, [copy.wait for copy in pair])


def muon_gram(spots, groups, spread, base):
    momenta = [momentum for _, each in groups for momentum in each]
    terms = jax.ShapeDtypeStruct(base[0].shape, F32)
    vmem, anywhere = pl.BlockSpec(memory_space=pltpu.VMEM), pl.BlockSpec(memory_space=pl.ANY)
    blocks = len(block_spots([momentum.shape[1] // ROW_BLOCK for momentum in momenta], spread))
    outs = pl.pallas_call(
        functools.partial(muon_gram_kernel, [len(each) for _, each in groups], spread),
        out_shape=[jax.ShapeDtypeStruct(momentum.shape, F32) for momentum in momenta] + [terms, terms],
        in_specs=[pl.BlockSpec(memory_space=pltpu.SMEM), anywhere, anywhere]
        + [vmem] * (len(groups) + len(momenta)),
        out_specs=[vmem] * len(momenta) + [anywhere, anywhere],
        input_output_aliases={1: len(momenta), 2: len(momenta) + 1},
        scratch_shapes=[
            pltpu.VMEM((blocks,) + PACKED, F32),
            pltpu.SemaphoreType.DMA((blocks,)),
        ],
        compiler_params=pltpu.CompilerParams(vmem_limit_bytes=VMEM_LIMIT),
        name="muon_gram",
    )(spots, *base, *[group[0] for group in groups], *momenta)
    return outs[:-2], outs[-2], outs[-1]


def polynomial_kernel(count, *refs):
    out = refs[count]
    shape = (ROW_BLOCK, ROW_BLOCK)
    eye = (lax.broadcasted_iota(jnp.int32, shape, 0) == lax.broadcasted_iota(jnp.int32, shape, 1)).astype(F32)
    mul = lambda left, right: precise(left, right, ((1,), (0,)))
    blocks = range(out.shape[0])
    currents, scales, totals = [], [], []
    for n in blocks:
        gram = refs[0][n]
        for ref in refs[1:count]:
            gram = gram + ref[n]
        gram = unpacked(gram)
        square = jnp.sum(jnp.sum(gram * eye, axis=1, keepdims=True), axis=0, keepdims=True)
        scale = 1.0 / (jnp.sqrt(square) + NORM_EPS)
        scales.append(scale)
        currents.append(gram * (scale * scale))
    for step in range(NS_STEPS):
        factors = [NS_A * eye + NS_B * a + NS_C * mul(a, a) for a in currents]
        totals = factors if step == 0 else [mul(f, t) for f, t in zip(factors, totals)]
        if step + 1 < NS_STEPS:
            currents = [mul(f, a) for f, a in zip(factors, currents)]
            currents = [mul(a, f) for f, a in zip(factors, currents)]
    for n in blocks:
        out[n] = packed(totals[n] * scales[n])


def polynomial(parts):
    vmem = pl.BlockSpec(memory_space=pltpu.VMEM)
    return pl.pallas_call(
        functools.partial(polynomial_kernel, len(parts)),
        out_shape=jax.ShapeDtypeStruct(parts[0].shape, F32),
        in_specs=[vmem] * len(parts),
        out_specs=vmem,
        compiler_params=pltpu.CompilerParams(vmem_limit_bytes=VMEM_LIMIT),
        name="polynomial",
    )(*parts)


def muon_apply_kernel(rates, placed, spots_ref, *refs):
    count = len(rates)
    parts, momenta, masters = refs[:4], refs[4 : 4 + count], refs[4 + count : 4 + 2 * count]
    outs, factors = refs[4 + 2 * count : 4 + 3 * count], refs[4 + 3 * count]
    for n in range(4):
        factors[n] = parts[n][...]
    zs = factors.shape[1]
    for matrix, block, z, x, core, place_in in placed:
        part = slice(block * ROW_BLOCK, (block + 1) * ROW_BLOCK)
        away = 2 * lax.rem(spots_ref[2] + core, 2) + lax.rem(spots_ref[1] + x, 2)
        factor = unpacked(factors[away, lax.rem(zs + z - spots_ref[0], zs), place_in])
        direction = precise(momenta[matrix][:, part], factor, ((1,), (1,)))
        outs[matrix][:, part] = masters[matrix][:, part] * (1.0 - WEIGHT_SHRINK) - rates[matrix] * direction


def muon_apply(spots, factors, momenta, masters, rates, placed):
    vmem = pl.BlockSpec(memory_space=pltpu.VMEM)
    return pl.pallas_call(
        functools.partial(muon_apply_kernel, rates, placed),
        out_shape=[jax.ShapeDtypeStruct(master.shape, F32) for master in masters],
        in_specs=[pl.BlockSpec(memory_space=pltpu.SMEM)] + [vmem] * (4 + 2 * len(masters)),
        out_specs=[vmem] * len(masters),
        scratch_shapes=[pltpu.VMEM((4,) + factors[0].shape, F32)],
        compiler_params=pltpu.CompilerParams(vmem_limit_bytes=VMEM_LIMIT),
        name="muon_apply",
    )(spots, *factors, *momenta, *masters)


def body(net, tokens, conditioning, heights, widths, upstream, *state):
    masters, momenta = state[0:5], state[5:10]
    biases, bias_first, bias_second = state[10:13]
    w_qkv, w_proj, w_fc1, w_fc2, w_ada = masters
    micro, local, rows, width = tokens.shape
    count = micro * local
    head_dim = width // HEADS
    hidden = w_fc1.shape[1] * net.dp
    seq, dp = net.seq, net.dp
    y = net.y.digit()

    bounds = [0, 6 * width, 7 * width, 8 * width, 9 * width, 9 * width + hidden, 10 * width + hidden]

    n_qkv, n_proj, n_fc1, n_fc2 = [w.shape[1] for w in (w_qkv, w_proj, w_fc1, w_fc2)]
    unit = math.gcd(math.gcd(n_qkv, n_proj), 8)
    unit_qkv, layout_qkv = math.gcd(n_qkv, 8), [(n_qkv, 1)]
    own_tokens = tokens.reshape(count, rows, width)
    wires = net.y.gather(net.wire([w_qkv, w_proj]))

    ada_rows, ada_cols = w_ada.shape
    cond = conditioning.astype(F32).reshape(count, width)
    cond_act, silu_back = jax.vjp(sigmoid_linear, cond)
    cond_low = cond_act.astype(BF).astype(F32)
    cond_parts = jnp.transpose(cond_low.reshape(count, seq, ada_rows), (1, 0, 2)).reshape(seq, -1)
    parcel = jnp.concatenate([jnp.broadcast_to(biases, (seq,) + biases.shape), cond_parts], axis=1)
    parcel = net.to_all(tie(jnp.broadcast_to(parcel[None], (dp,) + parcel.shape), wires[0]))
    cond_all = parcel[:, 0, biases.shape[0] :].reshape(dp * count, ada_rows).astype(BF)
    first = Staged(net.gather_steps(net.joined(wires, unit, width), [(n_qkv, 1), (n_proj, 1)], 0.45))
    sent = first.advance()
    token_pieces = [net.y.gather(tie(own_tokens[0], *sent))]

    low_ada = w_ada.astype(BF)
    partial = jnp.dot(tie(cond_all, *sent), low_ada, preferred_element_type=F32).reshape(dp, 1, count, ada_cols)
    partial = jnp.broadcast_to(partial, (dp, seq, count, ada_cols))
    received = net.to_all(partial)
    first.advance(partial)
    sent = first.advance(received)
    received, parcel = tie(received, *sent), tie(parcel, *sent)
    received = jnp.sum(received, axis=1)
    bias_full = parcel[:, :, : biases.shape[0]].reshape(-1)
    b_ada, b_q, b_v, b_proj, b_fc1, b_fc2 = [bias_full[bounds[i] : bounds[i + 1]] for i in range(6)]
    modulation = jnp.transpose(received, (1, 0, 2)).reshape(count, dp * ada_cols) + b_ada
    shift_one, scale_one, gate_one, shift_two, scale_two, gate_two = jnp.split(
        modulation[:, None, :], 6, axis=-1
    )
    t_qkv, t_proj = first.finish(modulation)[0]
    wires = net.y.gather(tie(net.wire([w_fc1]), token_pieces[0][-1], *sent))
    wires = wires[:1] + [tie(wire, t_qkv) for wire in wires[1:]]
    t_fc1 = lax.all_gather(net.rows(wires), "dp", axis=0, tiled=True)
    for i in range(1, count):
        token_pieces.append(net.y.gather(tie(own_tokens[i], wires[-1])))

    lengths = (heights * widths).reshape(count).astype(jnp.int32)
    offsets = jnp.stack([((y + s) % seq) * rows for s in range(seq)]).astype(jnp.int32)
    normed_all, inverse_all, attn_all, queries, keys_values, attended, log_total = [[] for _ in range(7)]
    b_kv = jnp.concatenate([jnp.zeros_like(b_v), b_v])
    for i in range(count):
        normed, inverse = layer_norm(jnp.concatenate(token_pieces[i], axis=0).astype(F32))
        attn = (normed * (1.0 + scale_one[i]) + shift_one[i]).astype(BF)
        queries.append((dot_t(attn[None, :rows], t_qkv[:width]) + b_q).astype(BF))
        keys_values.append((dot_t(attn[None], t_qkv[width:]) + b_kv).astype(BF))
        mixed, lse = attend(lengths[i : i + 1], offsets, queries[i], keys_values[i], HEADS, 512)
        if i == 0:
            token_pieces[1:] = [each[:1] + [tie(a, mixed) for a in each[1:]] for each in token_pieces[1:]]
            last_piece = token_pieces[-1][-1] if count > 1 else mixed
            wires = net.y.gather(tie(net.wire([w_fc2]), last_piece))
        normed_all.append(normed[:rows])
        inverse_all.append(inverse[:rows])
        attn_all.append(attn)
        attended.append(mixed)
        log_total.append(lse)
    wires = wires[:1] + [tie(wire, keys_values[-1]) for wire in wires[1:]]
    t_fc2 = lax.all_gather(net.rows(wires), "dp", axis=0, tiled=True)
    attended_low = jnp.concatenate(attended, axis=0)

    inputs = own_tokens.astype(F32)
    branch_one = dot_t(attended_low, t_proj) + b_proj
    mixed_one = inputs + gate_one * branch_one
    normed_two, inverse_two = layer_norm(mixed_one)
    ffn_in = (normed_two * (1.0 + scale_two) + shift_two).astype(BF)
    flat = lambda array: array.reshape(-1, array.shape[-1])
    activated_low, slope = hidden_forward(flat(ffn_in), t_fc1, b_fc1)
    activated_low = activated_low.reshape(count, rows, hidden)
    grad_out = upstream.reshape(count, rows, width).astype(F32)
    grad_branch_two = (gate_two * grad_out).astype(BF)
    term_fc2 = outer(grad_branch_two, activated_low)
    sum_fc2 = net.scatter(term_fc2)
    branch_two = dot_t(tie(activated_low, term_fc2), t_fc2) + b_fc2
    grad_branch_two = tie(grad_branch_two, term_fc2)
    result = (mixed_one + gate_two * branch_two).astype(BF)

    grad_gate_two = jnp.sum(branch_two * grad_out, axis=1)
    bias_fc2 = jnp.sum(grad_branch_two.astype(F32), axis=(0, 1))
    grad_pre, bias_fc1 = hidden_backward(flat(grad_branch_two), t_fc2, slope)
    grad_pre = grad_pre.reshape(count, rows, hidden)
    grad_ffn_in = dot(grad_pre, t_fc1)
    grad_shift_two = jnp.sum(grad_ffn_in, axis=1)
    grad_scale_two = jnp.sum(grad_ffn_in * normed_two, axis=1)
    grad_mixed = grad_out + norm_back(normed_two, inverse_two, grad_ffn_in * (1.0 + scale_two))
    grad_gate_one = jnp.sum(branch_one * grad_mixed, axis=1)
    grad_branch_one = (gate_one * grad_mixed).astype(BF)
    bias_proj = jnp.sum(grad_branch_one.astype(F32), axis=(0, 1))
    grad_attended = dot(grad_branch_one, t_proj).astype(BF)
    unit_mid = math.gcd(math.gcd(n_proj, n_fc1), 8)
    own, other = shard_outer(
        net.spots(),
        [flat(grad_pre), flat(ffn_in), flat(grad_branch_one), flat(attended_low)],
        [([2], 0, width), ([3], 0, width), ([1], 0, width)]
        + [([0], j * width, width) for j in range(hidden // width)],
        [(0, 1, n_proj, 0)] + [(3 + j, 2, n_fc1, n_proj // unit_mid) for j in range(hidden // width)],
        net.z.size, width, unit_mid, (n_proj + n_fc1) // unit_mid,
    )
    term_mid = (own.astype(F32) + net.core.send(other, 1).astype(F32)).astype(BF)
    term_mid = tie(term_mid, sum_fc2, grad_attended)
    sum_mid = net.scatter_chips(term_mid.reshape(dp // 2 * (n_proj + n_fc1), width))
    grad_attended = tie(grad_attended, term_mid)

    def far_steps(dk, dv):
        part = dot(dk[:, rows:], t_qkv[width : 2 * width]) + dot(dv[:, rows:], t_qkv[2 * width :])
        part = part.astype(BF)[0]
        blank = jnp.zeros((rows, width), BF)
        return Staged(net.y.scatter_steps(lambda s: blank if s == 0 else part[(s - 1) * rows : s * rows]))

    grad_q, grad_k, grad_v, far_parts = [], [], [], []
    turned = [momentum.T for momentum in momenta]
    sent = []
    for i in range(count):
        dq, dk, dv = attend_back(
            lengths[i : i + 1], offsets, queries[i], keys_values[i], attended[i],
            grad_attended, i, log_total[i], HEADS, 512, sent,
        )
        sent = []
        grad_q.append(dq)
        grad_k.append(dk)
        grad_v.append(dv)
        if i + 1 < count:
            far_parts.append(far_steps(dk, dv))
            sent = sent + far_parts[-1].advance()
    far_parts.append(far_steps(grad_k[-1], grad_v[-1]))
    sent = sent + far_parts[-1].advance()
    unit_last = math.gcd(n_qkv, 8)
    (term_last,) = shard_outer(
        net.spots(),
        [flat(each) for each in grad_q + grad_k + grad_v]
        + [attn[:rows] for attn in attn_all]
        + attn_all,
        [([n * count + i for i in range(count)], 0, width) for n in range(5)],
        [(0, 3, n_qkv, 0), (1, 4, n_qkv, 0), (2, 4, n_qkv, 0)],
        net.z.size, width, unit_last, n_qkv // unit_last, sent, split=False,
    )
    sum_last = net.scatter(term_last.reshape(dp * n_qkv, width))
    sent = [term_last]
    grad_q[0] = tie(grad_q[0], *sent)
    bias_q = sum(jnp.sum(each.astype(F32), axis=(0, 1)) for each in grad_q)
    bias_v = sum(jnp.sum(each.astype(F32), axis=(0, 1)) for each in grad_v)
    own_part = jnp.concatenate(
        [
            dot(grad_q[i], t_qkv[:width])
            + dot(grad_k[i][:, :rows], t_qkv[width : 2 * width])
            + dot(grad_v[i][:, :rows], t_qkv[2 * width :])
            for i in range(count)
        ],
        axis=0,
    )
    halves = Staged(lockstep(*[net.halves_steps(tie(each, own_part)) for each in (sum_fc2, sum_mid)]))
    halves.advance()
    matrices = (w_qkv, w_proj, w_fc1, w_fc2, w_ada)
    per = -(-sum(matrix.shape[0] // ROW_BLOCK for matrix in matrices) // dp)
    spread_early = (per, 0)
    early_blocks = (w_fc2.shape[0] + w_fc1.shape[0] + w_proj.shape[0]) // ROW_BLOCK
    spread_last = (per, -(-early_blocks // per))
    far_sum = jnp.stack([steps_of.finish() for steps_of in far_parts])
    grad_attn_in = own_part + far_sum
    normed_one, inverse_one = jnp.stack(normed_all), jnp.stack(inverse_all)
    grad_shift_one = jnp.sum(grad_attn_in, axis=1)
    grad_scale_one = jnp.sum(grad_attn_in * normed_one, axis=1)
    grad_inputs = grad_mixed + norm_back(normed_one, inverse_one, grad_attn_in * (1.0 + scale_one))
    grad_inputs = grad_inputs.astype(BF).reshape(tokens.shape)

    grad_mod_local = jnp.concatenate(
        [grad_shift_one, grad_scale_one, grad_gate_one, grad_shift_two, grad_scale_two, grad_gate_two], axis=-1
    )
    bias_ada = jnp.sum(grad_mod_local, axis=0)
    sent = jnp.transpose(grad_mod_local.reshape(count, dp, 1, ada_cols), (1, 2, 0, 3))
    sent = jnp.broadcast_to(sent, (dp, seq, count, ada_cols))
    mod_parts = net.to_all(sent)
    mod_parts = tie(mod_parts, sent)
    mod_cols = jnp.sum(mod_parts, axis=1).astype(BF).reshape(dp * count, ada_cols)
    shard_ada = jnp.einsum("sr,sc->cr", cond_all, mod_cols, preferred_element_type=F32)

    cond_part = jnp.einsum("sc,rc->sr", mod_cols, low_ada, preferred_element_type=F32)
    cond_part = jnp.broadcast_to(cond_part.reshape(dp, 1, -1), (dp, seq, count * ada_rows))
    term_bias = jnp.concatenate([bias_ada, bias_q, bias_v, bias_proj, bias_fc1, bias_fc2])
    parcel = jnp.concatenate([term_bias.reshape(dp, seq, -1), cond_part], axis=-1)
    got_parcel = net.to_all(parcel)

    sums = halves.finish(parcel)
    blank = jnp.zeros((2, net.z.size, per) + PACKED, F32)
    (next_fc2, next_proj, next_fc1), *early = muon_gram(
        net.spots(), [(sums[0], [turned[3]]), (sums[1], [turned[1], turned[2]])], spread_early, (blank, blank)
    )
    got_parcel = tie(got_parcel, early[0])
    halves = Staged(net.halves_steps(tie(sum_last, got_parcel)))
    sent = halves.advance()
    total = halves.finish(shard_ada)
    (next_qkv, next_ada), *grams = muon_gram(
        net.spots(), [(total, [turned[0]]), (shard_ada, [turned[4]])], spread_last, early
    )
    grams = Staged(net.gram_steps(*grams))
    sent = grams.advance()
    parcel = tie(got_parcel, *sent)
    while not grams.done:
        sent = grams.advance(sent[0])
    gathered = Staged(net.muon_gather_steps(grams.result))
    sent = gathered.advance()
    while not gathered.done:
        sent = gathered.advance(sent[0])
    momenta_in = [next_fc2, next_proj, next_fc1, next_qkv, next_ada]
    heights_of = [momentum.shape[1] // ROW_BLOCK for momentum in momenta_in]
    placed = block_spots(heights_of[:3], spread_early)
    placed += [(3 + spot[0],) + spot[1:] for spot in block_spots(heights_of[3:], spread_last)]
    new_fc2, new_proj, new_fc1, new_qkv, new_ada = muon_apply(
        net.spots(), gathered.result, momenta_in, [w.T for w in (w_fc2, w_proj, w_fc1, w_qkv, w_ada)],
        [math.sqrt(width / hidden), 1.0, math.sqrt(hidden / width), math.sqrt(3.0), math.sqrt(6.0)], placed,
    )

    size = biases.shape[0]
    grad_bias = jnp.sum(parcel[..., :size], axis=(0, 1))
    cond_part = jnp.sum(parcel[..., size:], axis=0).reshape(seq, count, ada_rows)
    grad_cond = silu_back(jnp.transpose(cond_part, (1, 0, 2)).reshape(count, width))[0]
    next_first = BETA_FIRST * bias_first + (1.0 - BETA_FIRST) * grad_bias
    next_second = BETA_SECOND * bias_second + (1.0 - BETA_SECOND) * grad_bias * grad_bias
    first_hat = next_first / (1.0 - BETA_FIRST**STEP_COUNT)
    second_hat = next_second / (1.0 - BETA_SECOND**STEP_COUNT)
    new_biases = biases * (1.0 - ADAM_RATE * ADAM_DECAY) - ADAM_RATE * first_hat / (
        jnp.sqrt(second_hat) + ADAM_EPS
    )
    return (
        result.reshape(tokens.shape),
        grad_inputs,
        grad_cond.reshape(conditioning.shape),
        new_qkv.T, new_proj.T, new_fc1.T, new_fc2.T, new_ada.T,
        next_qkv.T, next_proj.T, next_fc1.T, next_fc2.T, next_ada.T,
        new_biases,
        next_first,
        next_second,
    )


def solution(mesh):
    rows = P(None, "dp", "seq", None)
    matrix = P("seq", "dp")
    flat = P(("dp", "seq"))
    in_specs = (rows, P(None, "dp", None), P(None, "dp"), P(None, "dp"), rows) + (matrix,) * 10 + (flat,) * 3
    out_specs = (rows, rows, P(None, "dp", None)) + (matrix,) * 10 + (flat,) * 3
    return jax.shard_map(
        functools.partial(body, Net(mesh)), mesh=mesh, in_specs=in_specs, out_specs=out_specs, check_vma=False
    )
```
